32 devices in a mesh: wide: 8 (over y, x, core), narrow: 4 (over z).
Axes of the slice: x: 2, y: 2, z: 4, core: 2. Of those that a mesh axis runs over, the one named last changes fastest.
Arguments:
- tokens: bfloat16 [32, 512, 768], P(('wide', 'narrow')), may hold values from -6 to 6
- lengths: int32 [32], P(('wide', 'narrow')), may hold values from 20 to 512, as said below
- gain_one: bfloat16 [768], P(('wide', 'narrow')), may hold values from 0.5 to 1.5
- w_value: bfloat16 [768, 768], P(('wide', 'narrow')), may hold values from -0.21875 to 0.21875
- w_first: bfloat16 [12, 768, 768], P(None, ('wide', 'narrow')), may hold values from -0.21875 to 0.21875
- b_first: bfloat16 [12, 768], P(None, ('wide', 'narrow')), may hold values from -3 to 3
- w_second: bfloat16 [12, 768, 512], P(None, ('wide', 'narrow')), may hold values from -0.4375 to 0.4375
- b_second: bfloat16 [6144], P(('wide', 'narrow')), may hold values from -4 to 4
- w_out: bfloat16 [768, 768], P(('wide', 'narrow')), may hold values from -0.625 to 0.625
- gain_two: bfloat16 [768], P(('wide', 'narrow')), may hold values from 0.5 to 1.5
- w_up: bfloat16 [768, 3072], P(('wide', 'narrow')), may hold values from -0.21875 to 0.21875
- w_down: bfloat16 [3072, 768], P(('wide', 'narrow')), may hold values from -0.15625 to 0.15625
- grad_out: float32 [32, 512, 768], P(('wide', 'narrow')), may hold values from -6 to 6
Outputs:
- block_out: float32 [32, 512, 768], P(('wide', 'narrow'))
- grad_tokens: float32 [32, 512, 768], P(('wide', 'narrow'))
- grad_gain_one: float32 [768], P(('wide', 'narrow'))
- grad_w_value: float32 [768, 768], P(('wide', 'narrow'))
- grad_w_first: float32 [12, 768, 768], P(None, ('wide', 'narrow'))
- grad_b_first: float32 [12, 768], P(None, ('wide', 'narrow'))
- grad_w_second: float32 [12, 768, 512], P(None, ('wide', 'narrow'))
- grad_b_second: float32 [6144], P(('wide', 'narrow'))
- grad_w_out: float32 [768, 768], P(('wide', 'narrow'))
- grad_gain_two: float32 [768], P(('wide', 'narrow'))
- grad_w_up: float32 [768, 3072], P(('wide', 'narrow'))
- grad_w_down: float32 [3072, 768], P(('wide', 'narrow'))
The draws below stay inside these ranges and needn't reach their ends.
Inputs may be any that keep to these rules, and one draw needn't show every extreme that they name: `lengths`: some row holds an item of the full 512 slots.
All inputs are finite; a program needn't handle non-finite values.
Results may differ from the reference program's by a relative error of at most 0.013.
Values may be sent and summed in bfloat16 or wider, within the bound.
A program may use at most 256 MiB of HBM per device.

```python
import jax
import jax.numpy as jnp
from jax import lax

D = 768
H = 12
FF = 3072
SLOTS = 512
ROWS = 32


def draw_lengths(key, part):
    key = jax.random.fold_in(key, 11)
    first_key, second_key = jax.random.split(key)
    drawn = jax.random.randint(first_key, (ROWS,), 20, SLOTS + 1)
    chosen = jax.random.randint(second_key, (), 0, ROWS)
    return jnp.where(jnp.arange(ROWS) == chosen, SLOTS, drawn).astype(jnp.int32)


def level_of(key, dims, pieces, least, high):
    def one(axis_at, blocks):
        steps = jax.random.uniform(jax.random.fold_in(jax.random.fold_in(key, 6), axis_at), (blocks,), jnp.float32, least / len(pieces), high / len(pieces))
        return jnp.repeat(jnp.exp(steps), dims[axis_at] // blocks).reshape((-1,) + (1,) * (len(dims) - axis_at - 1))

    level = one(*pieces[0])
    for cut in pieces[1:]:
        level = level * one(*cut)
    return level


def bell_draw(rng, extent, width, bound, shards=(), kind=jnp.bfloat16):
    entries = jax.random.normal(rng, extent, jnp.float32) * width
    if len(shards) > 0:
        entries = level_of(rng, extent, shards, -0.22, 0.18) * entries
    return jnp.clip(entries, min=-bound, max=bound).astype(kind)


def setup_inputs(seed: int = 0) -> dict:
    key_list = jax.random.split(jax.random.key(seed), 14)
    tokens = bell_draw(key_list[0], (ROWS, SLOTS, D), 1.0, 6.0, ((0, 32),))
    lengths = draw_lengths(jax.random.fold_in(key_list[13], 71), 0)
    gain_one = jnp.clip(1.0 + 0.1 * jax.random.normal(key_list[2], (D,), jnp.float32), 0.5, 1.5).astype(jnp.bfloat16)
    w_value = bell_draw(key_list[3], (D, D), D ** -0.5, 0.21875, ((0, 32),))
    w_first = bell_draw(key_list[4], (H, D, D), D ** -0.5, 0.21875, ((1, 32),))
    b_first = bell_draw(key_list[5], (H, D), 0.5, 3.0, ((1, 32),))
    w_second = bell_draw(key_list[6], (H, D, SLOTS), (D // 4) ** -0.5, 0.4375, ((1, 32),))
    b_second = bell_draw(key_list[7], (H * SLOTS,), 1.0, 4.0, ((0, 32),))
    w_out = bell_draw(key_list[8], (D, D), (D // 8) ** -0.5, 0.625, ((0, 32),))
    gain_two = jnp.clip(1.0 + 0.1 * jax.random.normal(key_list[9], (D,), jnp.float32), 0.5, 1.5).astype(jnp.bfloat16)
    w_up = bell_draw(key_list[10], (D, FF), D ** -0.5, 0.21875, ((0, 32),))
    w_down = bell_draw(key_list[11], (FF, D), (FF // 2) ** -0.5, 0.15625, ((0, 32),))
    grad_out = bell_draw(key_list[12], (ROWS, SLOTS, D), 1.0, 6.0, ((0, 32),), jnp.float32)
    return dict(tokens=tokens, lengths=lengths, gain_one=gain_one, w_value=w_value, w_first=w_first, b_first=b_first, w_second=w_second, b_second=b_second, w_out=w_out, gain_two=gain_two, w_up=w_up, w_down=w_down, grad_out=grad_out)


@jax.custom_vjp
def low(v):
    return lax.optimization_barrier(v.astype(jnp.bfloat16)).astype(jnp.float32)

@jax.custom_vjp
def low_back(v):
    return v

def low_keep(v):
    return (low(v), None)

def low_pass(kept, grad):
    return (grad,)

def back_keep(v):
    return (v, None)

def back_low(kept, grad):
    return (low(grad),)
low.defvjp(low_keep, low_pass)
low_back.defvjp(back_keep, back_low)
highest = lax.Precision.HIGHEST
epsilon = 1e-05

def norm_rows(values, factor):
    average = lax.optimization_barrier(jnp.mean(values, axis=-1, keepdims=True))
    centred = values - average
    spread = lax.optimization_barrier(jnp.mean(centred * centred, axis=-1, keepdims=True))
    return centred * lax.rsqrt(spread + epsilon) * factor

def smooth(values):
    return jax.nn.gelu(values, approximate=False)

def attend_row(normed, length, w_value, w_first, b_first, w_second, b_second, w_out):
    values = low(low_back(jnp.dot(normed, w_value, precision=highest)))
    before = low_back(jnp.einsum('sd,hde->hse', normed, w_first, precision=highest) + b_first[:, None, :])
    hidden = low(smooth(before))
    logits = low_back(jnp.einsum('hse,hej->hsj', hidden, w_second, precision=highest) + b_second.reshape(H, SLOTS)[:, None, :])
    visible = jnp.arange(SLOTS) < length
    masked = jnp.where(visible[None, None, :], logits, jnp.float32(-1e+30))
    highest_score = lax.optimization_barrier(jnp.max(masked, axis=-1, keepdims=True))
    scaled = jnp.exp(masked - highest_score)
    probabilities = scaled / lax.optimization_barrier(jnp.sum(scaled, axis=-1, keepdims=True))
    weights = low(probabilities)
    per_head = values.reshape(SLOTS, H, D // H).transpose(1, 0, 2)
    mixture = jnp.einsum('hsj,hjc->hsc', weights, per_head, precision=highest)
    joined = low(low_back(mixture.transpose(1, 0, 2).reshape(SLOTS, D)))
    return low_back(jnp.dot(joined, w_out, precision=highest))

def reference(tokens, lengths, gain_one, w_value, w_first, b_first, w_second, b_second, w_out, gain_two, w_up, w_down, grad_out):
    floats = tuple((array.astype(jnp.float32) for array in (tokens, gain_one, w_value, w_first, b_first, w_second, b_second, w_out, gain_two, w_up, w_down)))

    def forward(inputs, gain_one, w_value, w_first, b_first, w_second, b_second, w_out, gain_two, w_up, w_down):
        normed_one = low(norm_rows(inputs, gain_one))

        def attend(row_pair):
            return attend_row(row_pair[0], row_pair[1], w_value, w_first, b_first, w_second, b_second, w_out)
        branch = lax.map(jax.checkpoint(attend), (normed_one, lengths))
        middle = inputs + branch
        normed_two = low(norm_rows(middle, gain_two))
        upward = low_back(jnp.einsum('rsd,df->rsf', normed_two, w_up, precision=highest))
        active = low(smooth(upward))
        downward = low_back(jnp.einsum('rsf,fd->rsd', active, w_down, precision=highest))
        return middle + downward
    result, pullback = jax.vjp(forward, *floats)
    grads = pullback(grad_out.astype(jnp.float32))
    return (result, grads[0], grads[1], grads[2], grads[3], grads[4], grads[5], grads[6], grads[7], grads[8], grads[9], grads[10])
```

```python
import jax
import jax.numpy as jnp
from jax import lax
from jax.sharding import Mesh
from jax.sharding import PartitionSpec as P

epsilon = 1e-05
f32 = jnp.float32
bf16 = jnp.bfloat16
GROUP = 4


def norm_rows(values, factor):
    average = jnp.mean(values, axis=-1, keepdims=True)
    centred = values - average
    spread = jnp.mean(centred * centred, axis=-1, keepdims=True)
    return centred * lax.rsqrt(spread + epsilon) * factor


def smooth(values):
    return jax.nn.gelu(values, approximate=False)


def mm(spec, a, b):
    return jnp.einsum(spec, a, b, preferred_element_type=f32)


REST = ("rep", "narrow")
ALL = ("tp", "rep", "narrow")


def to_heads(shard):
    heads, depth, width = shard.shape
    pieces = lax.all_to_all(shard.reshape(GROUP, heads // GROUP, depth, width), "tp", 0, 0)
    whole = lax.all_gather(pieces, REST, axis=0)
    return whole.transpose(2, 1, 0, 3, 4).reshape(heads // GROUP, -1, width)


def from_heads(grad):
    heads, depth, width = grad.shape
    n = lax.axis_size("rep") * lax.axis_size("narrow")
    pieces = grad.astype(bf16).reshape(heads, GROUP, n, depth // (GROUP * n), width).transpose(2, 1, 0, 3, 4)
    pieces = pieces.reshape((n * GROUP,) + pieces.shape[2:])
    share = lax.psum_scatter(pieces, REST, scatter_dimension=0, tiled=True)
    share = lax.all_to_all(share, "tp", 0, 0)
    return share.reshape(heads * GROUP, depth // (GROUP * n), width).astype(f32)


def on_device(tokens, lengths, gain_one, w_value, w_first, b_first, w_second, b_second, w_out, gain_two, w_up, w_down, grad_out):
    row_count, slots, width = tokens.shape
    heads_all = w_first.shape[0]
    heads = heads_all // GROUP
    head_size = width // heads_all
    me = lax.axis_index("tp")
    depth = w_value.shape[0]

    small = [gain_one, gain_two, b_second, b_first.reshape(-1)]
    gathered = lax.all_gather(jnp.concatenate(small), ALL, axis=0)
    n_all = gathered.shape[0]
    g1 = gathered[:, :depth].reshape(-1).astype(f32)
    g2 = gathered[:, depth : 2 * depth].reshape(-1).astype(f32)
    b2_len = b_second.shape[0]
    b2 = gathered[:, 2 * depth : 2 * depth + b2_len].reshape(heads_all, slots).astype(f32)
    b1 = gathered[:, 2 * depth + b2_len :].reshape(n_all, heads_all, depth).transpose(1, 0, 2).reshape(heads_all, width).astype(f32)
    b1 = lax.dynamic_slice_in_dim(b1, me * heads, heads, 0)
    b2 = lax.dynamic_slice_in_dim(b2, me * heads, heads, 0)

    wf = to_heads(w_first)
    ws = to_heads(w_second)
    wv = to_heads(w_value.reshape(depth, GROUP, width // GROUP).transpose(1, 0, 2))[0]
    rows = lax.all_gather(tokens, "tp", axis=0, tiled=True)
    lens = lax.all_gather(lengths, "tp", axis=0, tiled=True)
    n_rows = rows.shape[0]

    normed = norm_rows(rows.astype(f32), g1).astype(bf16)
    values = mm("rsd,de->rse", normed, wv).astype(bf16)
    per_head = values.reshape(n_rows, slots, heads, head_size).transpose(2, 0, 1, 3)
    before = mm("rsd,hde->hrse", normed, wf) + b1[:, None, None, :]
    hidden = smooth(before).astype(bf16)
    logits = mm("hrse,hej->hrsj", hidden, ws) + b2[:, None, None, :]
    visible = lax.broadcasted_iota(jnp.int32, (1, n_rows, 1, slots), 3) < lens[None, :, None, None]
    masked = jnp.where(visible, logits, f32(-1e30))
    scaled = jnp.exp(masked - jnp.max(masked, axis=-1, keepdims=True))
    probabilities = scaled / jnp.sum(scaled, axis=-1, keepdims=True)
    weights = probabilities.astype(bf16)
    mixture = mm("hrsj,hrjc->rshc", weights, per_head).astype(bf16)
    mixture = mixture.reshape(GROUP, row_count, slots, heads * head_size)
    joined = lax.all_to_all(mixture, "tp", 0, 0).transpose(1, 2, 0, 3).reshape(row_count * slots, width)

    wo = lax.all_gather(w_out, ALL, axis=0, tiled=True)
    wu = lax.all_gather(w_up, ALL, axis=0, tiled=True)
    wd = lax.all_gather(w_down, ALL, axis=0, tiled=True)
    inputs = tokens.astype(f32).reshape(-1, width)
    middle = inputs + mm("sd,de->se", joined, wo)
    normed_two, norm_two_back = jax.vjp(norm_rows, middle, g2)
    normed_two = normed_two.astype(bf16)
    upward = mm("td,df->tf", normed_two, wu)
    active, smooth_up_back = jax.vjp(smooth, upward)
    active = active.astype(bf16)
    result = middle + mm("tf,fd->td", active, wd)

    g_out = grad_out.reshape(-1, width)
    grad_branch = g_out.astype(bf16)
    grad_w_down = mm("tf,td->fd", active, grad_branch)
    grad_upward = smooth_up_back(mm("td,fd->tf", grad_branch, wd))[0].astype(bf16)
    grad_w_up = mm("td,tf->df", normed_two, grad_upward)
    grad_middle_norm, grad_gain_two = norm_two_back(mm("tf,df->td", grad_upward, wu))
    grad_middle = g_out + grad_middle_norm
    grad_attn = grad_middle.astype(bf16)
    grad_w_out = mm("sd,se->de", joined, grad_attn)
    grad_joined = mm("se,de->sd", grad_attn, wo).astype(bf16)

    grad_mixture = grad_joined.reshape(row_count, slots, GROUP, heads * head_size).transpose(2, 0, 1, 3)
    grad_mixture = lax.all_to_all(grad_mixture, "tp", 0, 0).reshape(n_rows, slots, heads, head_size).transpose(2, 0, 1, 3)
    grad_weights = mm("hrsc,hrjc->hrsj", grad_mixture, per_head)
    grad_values = mm("hrsj,hrsc->rjhc", weights, grad_mixture).astype(bf16).reshape(n_rows, slots, heads * head_size)
    centre = jnp.sum(probabilities * grad_weights, axis=-1, keepdims=True)
    grad_logits = (probabilities * (grad_weights - centre)).astype(bf16)
    grad_b_second = jnp.sum(grad_logits.astype(f32), axis=(1, 2))
    grad_w_second = mm("hrse,hrsj->hej", hidden, grad_logits)
    grad_hidden = mm("hrsj,hej->hrse", grad_logits, ws)
    smooth_value, smooth_back = jax.vjp(smooth, before)
    grad_before = smooth_back(grad_hidden)[0].astype(bf16)
    grad_b_first = jnp.sum(grad_before.astype(f32), axis=(1, 2))
    grad_w_first = mm("rsd,hrse->hde", normed, grad_before)
    grad_w_value = mm("rsd,rse->de", normed, grad_values)
    grad_normed = mm("hrse,hde->rsd", grad_before, wf) + mm("rse,de->rsd", grad_values, wv)
    grad_normed = lax.psum_scatter(grad_normed.astype(bf16), "tp", scatter_dimension=0, tiled=True)
    value, norm_one_back = jax.vjp(norm_rows, inputs, g1)
    grad_inputs_norm, grad_gain_one = norm_one_back(grad_normed.astype(f32).reshape(-1, width))
    grad_tokens = grad_middle + grad_inputs_norm

    out_first = from_heads(grad_w_first)
    out_second = from_heads(grad_w_second)
    out_value = from_heads(grad_w_value[None]).transpose(1, 0, 2).reshape(depth, width)

    def share(grad):
        return lax.psum_scatter(grad.astype(bf16), ALL, scatter_dimension=0, tiled=True).astype(f32)

    vec_tp = jnp.concatenate([grad_b_first.reshape(-1), grad_b_second.reshape(-1)])
    vec_tp = lax.dynamic_update_slice_in_dim(jnp.zeros((GROUP, vec_tp.shape[0]), f32), vec_tp[None], me, 0)
    vec = jnp.concatenate([vec_tp.reshape(-1), grad_gain_one, grad_gain_two])
    vec = lax.psum(vec, ALL)
    index = (me * lax.axis_size("rep") + lax.axis_index("rep")) * lax.axis_size("narrow") + lax.axis_index("narrow")
    n_tp = GROUP * (heads * width + heads * slots)
    tp_part = vec[:n_tp].reshape(GROUP, -1)
    gb1 = tp_part[:, : heads * width].reshape(heads_all, width)
    gb2 = tp_part[:, heads * width :].reshape(-1)
    gb1 = lax.dynamic_slice_in_dim(gb1, index * depth, depth, 1)
    gb2 = lax.dynamic_slice_in_dim(gb2, index * b2_len, b2_len, 0)
    gg1 = lax.dynamic_slice_in_dim(vec[n_tp : n_tp + width], index * depth, depth, 0)
    gg2 = lax.dynamic_slice_in_dim(vec[n_tp + width :], index * depth, depth, 0)
    shape = tokens.shape
    return (
        result.reshape(shape),
        grad_tokens.reshape(shape),
        gg1,
        out_value,
        out_first,
        gb1,
        out_second,
        gb2,
        share(grad_w_out),
        gg2,
        share(grad_w_up),
        share(grad_w_down),
    )


def solution(mesh):
    wide, narrow = mesh.shape["wide"], mesh.shape["narrow"]
    grouped = Mesh(mesh.devices.reshape(GROUP, wide // GROUP, narrow), ALL)
    vec = P(ALL)
    flat = P(ALL, None)
    mid = P(None, ALL, None)
    row = P(ALL, None, None)
    return jax.shard_map(
        on_device,
        mesh=grouped,
        in_specs=(row, vec, vec, flat, mid, P(None, ALL), mid, vec, flat, vec, flat, flat, row),
        out_specs=(row, row, vec, flat, mid, P(None, ALL), mid, vec, flat, vec, flat, flat),
        check_vma=False,
    )
```

```python
import jax
import jax.numpy as jnp
from jax import lax
from jax.experimental import pallas as pl
from jax.experimental.pallas import tpu as pltpu
from jax.sharding import Mesh
from jax.sharding import PartitionSpec as P

epsilon = 1e-05
f32 = jnp.float32
bf16 = jnp.bfloat16
GROUP = 4


def norm_rows(values, factor):
    average = jnp.mean(values, axis=-1, keepdims=True)
    centred = values - average
    spread = jnp.mean(centred * centred, axis=-1, keepdims=True)
    return centred * lax.rsqrt(spread + epsilon) * factor


def smooth(values):
    return jax.nn.gelu(values, approximate=False)


def mm(spec, a, b):
    return jnp.einsum(spec, a, b, preferred_element_type=f32)


REST = ("rep", "narrow")
ALL = ("tp", "rep", "narrow")


def to_heads(shard):
    heads, depth, width = shard.shape
    pieces = lax.all_to_all(shard.reshape(GROUP, heads // GROUP, depth, width), "tp", 0, 0)
    whole = lax.all_gather(pieces, REST, axis=0)
    return whole.transpose(2, 1, 0, 3, 4).reshape(heads // GROUP, -1, width)


def from_heads(grad):
    heads, depth, width = grad.shape
    n = lax.axis_size("rep") * lax.axis_size("narrow")
    pieces = grad.astype(bf16).reshape(heads, GROUP, n, depth // (GROUP * n), width).transpose(2, 1, 0, 3, 4)
    pieces = pieces.reshape((n * GROUP,) + pieces.shape[2:])
    share = lax.psum_scatter(pieces, REST, scatter_dimension=0, tiled=True)
    share = lax.all_to_all(share, "tp", 0, 0)
    return share.reshape(heads * GROUP, depth // (GROUP * n), width).astype(f32)


def on_device(tokens, lengths, gain_one, w_value, w_first, b_first, w_second, b_second, w_out, gain_two, w_up, w_down, grad_out):
    row_count, slots, width = tokens.shape
    heads_all = w_first.shape[0]
    heads = heads_all // GROUP
    head_size = width // heads_all
    me = lax.axis_index("tp")
    depth = w_value.shape[0]

    small = [gain_one, gain_two, b_second, b_first.reshape(-1)]
    gathered = lax.all_gather(jnp.concatenate(small), ALL, axis=0)
    n_all = gathered.shape[0]
    g1 = gathered[:, :depth].reshape(-1).astype(f32)
    g2 = gathered[:, depth : 2 * depth].reshape(-1).astype(f32)
    b2_len = b_second.shape[0]
    b2 = gathered[:, 2 * depth : 2 * depth + b2_len].reshape(heads_all, slots).astype(f32)
    b1 = gathered[:, 2 * depth + b2_len :].reshape(n_all, heads_all, depth).transpose(1, 0, 2).reshape(heads_all, width).astype(f32)
    b1 = lax.dynamic_slice_in_dim(b1, me * heads, heads, 0)
    b2 = lax.dynamic_slice_in_dim(b2, me * heads, heads, 0)

    wf = to_heads(w_first)
    ws = to_heads(w_second)
    wv = to_heads(w_value.reshape(depth, GROUP, width // GROUP).transpose(1, 0, 2))[0]
    rows = lax.all_gather(tokens, "tp", axis=0, tiled=True)
    lens = lax.all_gather(lengths, "tp", axis=0, tiled=True)
    n_rows = rows.shape[0]

    normed = norm_rows(rows.astype(f32), g1).astype(bf16)
    values = mm("rsd,de->rse", normed, wv).astype(bf16)
    per_head = values.reshape(n_rows, slots, heads, head_size).transpose(2, 0, 1, 3)
    before = mm("rsd,hde->hrse", normed, wf) + b1[:, None, None, :]
    hidden = smooth(before).astype(bf16)
    logits = mm("hrse,hej->hrsj", hidden, ws) + b2[:, None, None, :]
    visible = lax.broadcasted_iota(jnp.int32, (1, n_rows, 1, slots), 3) < lens[None, :, None, None]
    masked = jnp.where(visible, logits, f32(-1e30))
    scaled = jnp.exp(masked - jnp.max(masked, axis=-1, keepdims=True))
    probabilities = scaled / jnp.sum(scaled, axis=-1, keepdims=True)
    weights = probabilities.astype(bf16)
    mixture = mm("hrsj,hrjc->rshc", weights, per_head).astype(bf16)
    mixture = mixture.reshape(GROUP, row_count, slots, heads * head_size)
    joined = lax.all_to_all(mixture, "tp", 0, 0).transpose(1, 2, 0, 3).reshape(row_count * slots, width)

    wo = lax.all_gather(w_out, ALL, axis=0, tiled=True)
    wu = lax.all_gather(w_up, ALL, axis=0, tiled=True)
    wd = lax.all_gather(w_down, ALL, axis=0, tiled=True)
    inputs = tokens.astype(f32).reshape(-1, width)
    middle = inputs + mm("sd,de->se", joined, wo)
    normed_two, norm_two_back = jax.vjp(norm_rows, middle, g2)
    normed_two = normed_two.astype(bf16)
    upward = mm("td,df->tf", normed_two, wu)
    active, smooth_up_back = jax.vjp(smooth, upward)
    active = active.astype(bf16)
    result = middle + mm("tf,fd->td", active, wd)

    g_out = grad_out.reshape(-1, width)
    grad_branch = g_out.astype(bf16)
    grad_w_down = mm("tf,td->fd", active, grad_branch)
    grad_upward = smooth_up_back(mm("td,fd->tf", grad_branch, wd))[0].astype(bf16)
    grad_w_up = mm("td,tf->df", normed_two, grad_upward)
    grad_middle_norm, grad_gain_two = norm_two_back(mm("tf,df->td", grad_upward, wu))
    grad_middle = g_out + grad_middle_norm
    grad_attn = grad_middle.astype(bf16)
    grad_w_out = mm("sd,se->de", joined, grad_attn)
    grad_joined = mm("se,de->sd", grad_attn, wo).astype(bf16)

    grad_mixture = grad_joined.reshape(row_count, slots, GROUP, heads * head_size).transpose(2, 0, 1, 3)
    grad_mixture = lax.all_to_all(grad_mixture, "tp", 0, 0).reshape(n_rows, slots, heads, head_size).transpose(2, 0, 1, 3)
    grad_weights = mm("hrsc,hrjc->hrsj", grad_mixture, per_head)
    grad_values = mm("hrsj,hrsc->rjhc", weights, grad_mixture).astype(bf16).reshape(n_rows, slots, heads * head_size)
    centre = jnp.sum(probabilities * grad_weights, axis=-1, keepdims=True)
    grad_logits = (probabilities * (grad_weights - centre)).astype(bf16)
    grad_b_second = jnp.sum(grad_logits.astype(f32), axis=(1, 2))
    grad_w_second = mm("hrse,hrsj->hej", hidden, grad_logits)
    grad_hidden = mm("hrsj,hej->hrse", grad_logits, ws)
    smooth_value, smooth_back = jax.vjp(smooth, before)
    grad_before = smooth_back(grad_hidden)[0].astype(bf16)
    grad_b_first = jnp.sum(grad_before.astype(f32), axis=(1, 2))
    grad_w_first = mm("rsd,hrse->hde", normed, grad_before)
    grad_w_value = mm("rsd,rse->de", normed, grad_values)
    grad_normed = mm("hrse,hde->rsd", grad_before, wf) + mm("rse,de->rsd", grad_values, wv)
    grad_normed = lax.psum_scatter(grad_normed.astype(bf16), "tp", scatter_dimension=0, tiled=True)
    value, norm_one_back = jax.vjp(norm_rows, inputs, g1)
    grad_inputs_norm, grad_gain_one = norm_one_back(grad_normed.astype(f32).reshape(-1, width))
    grad_tokens = grad_middle + grad_inputs_norm

    out_first = from_heads(grad_w_first)
    out_second = from_heads(grad_w_second)
    out_value = from_heads(grad_w_value[None]).transpose(1, 0, 2).reshape(depth, width)

    def share(grad):
        return lax.psum_scatter(grad.astype(bf16), ALL, scatter_dimension=0, tiled=True).astype(f32)

    vec_tp = jnp.concatenate([grad_b_first.reshape(-1), grad_b_second.reshape(-1)])
    vec_tp = lax.dynamic_update_slice_in_dim(jnp.zeros((GROUP, vec_tp.shape[0]), f32), vec_tp[None], me, 0)
    vec = jnp.concatenate([vec_tp.reshape(-1), grad_gain_one, grad_gain_two])
    vec = lax.psum(vec, ALL)
    index = (me * lax.axis_size("rep") + lax.axis_index("rep")) * lax.axis_size("narrow") + lax.axis_index("narrow")
    n_tp = GROUP * (heads * width + heads * slots)
    tp_part = vec[:n_tp].reshape(GROUP, -1)
    gb1 = tp_part[:, : heads * width].reshape(heads_all, width)
    gb2 = tp_part[:, heads * width :].reshape(-1)
    gb1 = lax.dynamic_slice_in_dim(gb1, index * depth, depth, 1)
    gb2 = lax.dynamic_slice_in_dim(gb2, index * b2_len, b2_len, 0)
    gg1 = lax.dynamic_slice_in_dim(vec[n_tp : n_tp + width], index * depth, depth, 0)
    gg2 = lax.dynamic_slice_in_dim(vec[n_tp + width :], index * depth, depth, 0)
    shape = tokens.shape
    return (
        result.reshape(shape),
        grad_tokens.reshape(shape),
        gg1,
        out_value,
        out_first,
        gb1,
        out_second,
        gb2,
        share(grad_w_out),
        gg2,
        share(grad_w_up),
        share(grad_w_down),
    )


MESH = pl.DeviceIdType.MESH
VMEM_LIMIT = 60 * 2**20
ANY = pl.BlockSpec(memory_space=pl.ANY)
FULL = pl.BlockSpec(memory_space=pltpu.VMEM)
DMA = pltpu.SemaphoreType.DMA


def shape_of(dims, kind):
    return jax.ShapeDtypeStruct(dims, kind)


def dot_nt(a, b):
    return lax.dot_general(a, b, (((1,), (1,)), ((), ())), preferred_element_type=f32)


def dot_tn(a, b):
    return lax.dot_general(a, b, (((0,), (0,)), ((), ())), preferred_element_type=f32)


def dot_nn(a, b):
    return lax.dot_general(a, b, (((1,), (0,)), ((), ())), preferred_element_type=f32)


def place():
    return lax.axis_index("tp"), lax.axis_index("rep"), lax.axis_index("narrow")


def group_peers():
    t, c, z = place()
    along_x = t + 1 - 2 * (t % 2)
    along_y = (t + 2) % GROUP
    return [along_x, along_y, GROUP - 1 - t]


def line_peers():
    z = lax.axis_index("narrow")
    return [(z + k) % 4 for k in (1, 2, 3)]


def greet(devices):
    barrier = pltpu.get_barrier_semaphore()
    for device in devices:
        pl.semaphore_signal(barrier, inc=1, device_id=device, device_id_type=MESH)
    pl.semaphore_wait(barrier, len(devices))


def remote(src, dst, send, recv, device):
    copy = pltpu.make_async_remote_copy(
        src_ref=src, dst_ref=dst, send_sem=send, recv_sem=recv, device_id=device, device_id_type=MESH
    )
    copy.start()
    return copy


def local(src, dst, sem):
    copy = pltpu.make_async_copy(src, dst, sem)
    copy.start()
    return copy


def gather_kernel(pa, pt, pf, la, lt, lf, own, s1, r1, s2, r2, s3, r3, st, rt, sf, rf):
    t, c, z = place()
    sibling = (t, 1 - c, z)
    tps, zs = group_peers(), line_peers()
    greet([(p, c, z) for p in tps] + [(t, c, p) for p in zs] + [sibling])
    y, x = t // 2, t % 2
    slow, fast = (1 - c) * y + c * x, (1 - c) * x + c * y
    fast_peer = (1 - c) * tps[0] + c * tps[1]
    slow_peer = (1 - c) * tps[1] + c * tps[0]
    heads = la.shape[0]
    mine = [local(pa.at[t, h], la.at[h, c, z, t], own.at[h]) for h in range(heads)]
    mine_f = local(pf, lf.at[c, slow, fast, z], own.at[heads])
    mine_t = local(pt, lt.at[t], own.at[heads + 1])
    one, two, three = [], [], []
    for h in range(heads):
        one.append(
            [remote(pa.at[p, h], la.at[h, c, z, t], s1.at[h, k], r1.at[h, k], (p, c, z)) for k, p in enumerate(tps)]
        )
    f1 = [remote(pf, lf.at[c, slow, fast, z], sf.at[k], rf.at[k], (t, c, p)) for k, p in enumerate(zs)]
    toks = [remote(pt, lt.at[t], st.at[k], rt.at[k], (p, c, z)) for k, p in enumerate(tps)]
    for h in range(heads):
        mine[h].wait()
        for copy in one[h]:
            copy.wait()
        two.append(
            [remote(la.at[h, c, z], la.at[h, c, z], s2.at[h, k], r2.at[h, k], (t, c, p)) for k, p in enumerate(zs)]
        )
    mine_f.wait()
    for copy in f1:
        copy.wait()
    f2 = remote(lf.at[c, slow, fast], lf.at[c, slow, fast], sf.at[3], rf.at[3], (fast_peer, c, z))
    for h in range(heads):
        if h == 1:
            f2.wait()
            f3 = remote(lf.at[c, slow], lf.at[c, slow], sf.at[4], rf.at[4], (slow_peer, c, z))
        for copy in two[h]:
            copy.wait()
        three.append(remote(la.at[h, c], la.at[h, c], s3.at[h], r3.at[h], sibling))
    f3.wait()
    f4 = remote(lf.at[c], lf.at[c], sf.at[5], rf.at[5], sibling)
    mine_t.wait()
    for copy in toks + three + [f4]:
        copy.wait()


def gather_call(pa, pt, pf):
    heads = pa.shape[1]
    return pl.pallas_call(
        gather_kernel,
        out_shape=(
            shape_of((heads, 2, 4, GROUP) + pa.shape[2:], bf16),
            shape_of((GROUP,) + pt.shape, bf16),
            shape_of((2, 2, 2, 4) + pf.shape, bf16),
        ),
        in_specs=[ANY] * 3,
        out_specs=(ANY,) * 3,
        scratch_shapes=[
            DMA((heads + 2,)),
            DMA((heads, 3)),
            DMA((heads, 3)),
            DMA((heads, 3)),
            DMA((heads, 3)),
            DMA((heads,)),
            DMA((heads,)),
            DMA((3,)),
            DMA((3,)),
            DMA((6,)),
            DMA((6,)),
        ],
        compiler_params=pltpu.CompilerParams(collective_id=1, has_side_effects=True),
    )(pa, pt, pf)


def trade_kernel(src, dst, own, send, recv):
    t, c, z = place()
    tps = group_peers()
    greet([(p, c, z) for p in tps])
    mine = local(src.at[t], dst.at[t], own)
    copies = [remote(src.at[p], dst.at[t], send.at[k], recv.at[k], (p, c, z)) for k, p in enumerate(tps)]
    mine.wait()
    for copy in copies:
        copy.wait()


def trade_call(pieces, collective_id):
    return pl.pallas_call(
        lambda *refs: trade_kernel(*refs),
        out_shape=shape_of(pieces.shape, pieces.dtype),
        in_specs=[ANY],
        out_specs=ANY,
        scratch_shapes=[DMA, DMA((3,)), DMA((3,))],
        compiler_params=pltpu.CompilerParams(collective_id=collective_id, has_side_effects=True),
    )(pieces)


def gelu_pair(v):
    cdf = 0.5 * (1.0 + lax.erf(v * 0.7071067811865476))
    return v * cdf, cdf + v * (jnp.exp(-0.5 * v * v) * 0.3989422804014327)


def centre_rows(v):
    shifted = v - jnp.mean(v, axis=-1, keepdims=True)
    scale = lax.rsqrt(jnp.mean(shifted * shifted, axis=-1, keepdims=True) + epsilon)
    return shifted * scale, scale


def attend_kernel(la, lt, b2, wf, ws, wv, small, normed, values, hid, slope, prob, join, nrm, val, cols):
    h, r = pl.program_id(0), pl.program_id(1)
    width = wf.shape[-1]

    @pl.when(r == 0)
    def _():
        def unpack(t, carry):
            for c in range(2):
                for z in range(0, 4, 2):
                    tops, lows = [], []
                    for k in range(2):
                        tops.append(la[0, c, z + k, t, 0:32, :].astype(f32)[0:24])
                        lows.append(la[0, c, z + k, t, 16:48, :].astype(f32)[8:32])
                    top, low = jnp.concatenate(tops, 0), jnp.concatenate(lows, 0)
                    at = pl.ds(pl.multiple_of((t * 8 + c * 4 + z) * 24, 48), 48)
                    wf[0, at, :] = top.astype(bf16)
                    ws[0, at, :] = low[:, :512].astype(bf16)

                    @pl.when(h == 0)
                    def _():
                        last = low[:, 640:768]
                        cols[at, :] = last
                        lane = lax.broadcasted_iota(jnp.int32, last.shape, 1)
                        wv[at, 0:128] = low[:, 512:640].astype(bf16)
                        wv[at, 128:256] = jnp.where(lane < 64, last, 0.0).astype(bf16)

            return carry

        lax.fori_loop(0, GROUP, unpack, 0)

        @pl.when(h == 0)
        def _():
            small[...] = cols[...].T[64:72]

    @pl.when(h == 0)
    def _():
        unit, _ = centre_rows(lt[0, 0:512, :].astype(f32))
        out = (unit * small[3:4]).astype(bf16)
        nrm[r] = out
        normed[0] = out
        v = dot_nn(out, wv[...]).astype(bf16)
        val[r] = v
        values[0] = v

    mask = lt[0, 512:528, 0:512].astype(f32)[0:1]
    row = lax.broadcasted_iota(jnp.int32, (8, width), 0)
    b1 = jnp.sum(jnp.where(row == h, small[...], 0.0), axis=0, keepdims=True)
    row = lax.broadcasted_iota(jnp.int32, b2.shape, 0)
    shift = jnp.sum(jnp.where(row == h, b2[...], 0.0), axis=0, keepdims=True) + mask
    tile = pl.ds(pl.multiple_of((h // 2) * 128, 128), 128)
    step = 256
    for m in range(0, 512, step):
        at = slice(m, m + step)
        before = dot_nn(nrm[r, at, :], wf[0]) + b1
        out, grad = gelu_pair(before)
        hidden = out.astype(bf16)
        hid[0, 0, at, :] = hidden
        slope[0, 0, at, :] = grad.astype(bf16)
        logits = dot_nn(hidden, ws[0]) + shift
        e = jnp.exp(logits - jnp.max(logits, axis=-1, keepdims=True))
        p = (e / jnp.sum(e, axis=-1, keepdims=True)).astype(bf16)
        prob[0, 0, at, :] = p
        mix = dot_nn(p, val[r, :, tile])
        lane = lax.broadcasted_iota(jnp.int32, mix.shape, 1)
        old = join[r, at, tile].astype(f32)
        join[r, at, tile] = jnp.where((h == 1) & (lane < 64), old, mix).astype(bf16)


def attend_call(la, lt, b2):
    heads, width = la.shape[0], la.shape[-1]
    slots = 512
    by_row = lambda h, r: (jnp.where(h == 0, r, GROUP - 1), 0, 0)
    by_head = lambda h, r: (h, 0, 0)
    both = lambda h, r: (h, r, 0, 0)
    return pl.pallas_call(
        attend_kernel,
        grid=(heads, GROUP),
        out_shape=(
            shape_of((heads, width, width), bf16),
            shape_of((heads, width, slots), bf16),
            shape_of((width, 256), bf16),
            shape_of((8, width), f32),
            shape_of((GROUP, slots, width), bf16),
            shape_of((GROUP, slots, 256), bf16),
            shape_of((heads, GROUP, slots, width), bf16),
            shape_of((heads, GROUP, slots, width), bf16),
            shape_of((heads, GROUP, slots, slots), bf16),
            shape_of((GROUP, slots, 256), bf16),
        ),
        in_specs=[
            pl.BlockSpec((1,) + la.shape[1:], lambda h, r: (h, 0, 0, 0, 0, 0)),
            pl.BlockSpec((1,) + lt.shape[1:], lambda h, r: (r, 0, 0)),
            pl.BlockSpec(b2.shape, lambda h, r: (0, 0)),
        ],
        out_specs=(
            pl.BlockSpec((1, width, width), by_head),
            pl.BlockSpec((1, width, slots), by_head),
            pl.BlockSpec((width, 256), lambda h, r: (0, 0)),
            pl.BlockSpec((8, width), lambda h, r: (0, 0)),
            pl.BlockSpec((1, slots, width), by_row),
            pl.BlockSpec((1, slots, 256), by_row),
            pl.BlockSpec((1, 1, slots, width), both),
            pl.BlockSpec((1, 1, slots, width), both),
            pl.BlockSpec((1, 1, slots, slots), both),
            pl.BlockSpec((GROUP, slots, 256), lambda h, r: (0, 0, 0)),
        ),
        scratch_shapes=[
            pltpu.VMEM((GROUP, slots, width), bf16),
            pltpu.VMEM((GROUP, slots, 256), bf16),
            pltpu.VMEM((width, 128), f32),
        ],
        compiler_params=pltpu.CompilerParams(vmem_limit_bytes=VMEM_LIMIT),
    )(la, lt, b2)


def slab(t, c, z):
    y, x = t // 2, t % 2
    return (0, y, x, z) if c == 0 else (1, x, y, z)


def ffn_kernel(lf, joined, tokens, small, gout, result, gmid, gj, gf, gg2, wu, wo, n2, acc, gn2, gwu):
    width = tokens.shape[-1]
    wo[...] = jnp.zeros_like(wo)
    for t in range(GROUP):
        for c in range(2):
            for z in range(0, 4, 2):
                pair = [lf[slab(t, c, z + k)][96:128].astype(f32)[0:24] for k in range(2)]
                wo[t, (c * 4 + z) * 24 : (c * 4 + z) * 24 + 48, :] = jnp.concatenate(pair, 0).astype(bf16)
    middle = tokens[...].astype(f32)
    for t in range(GROUP):
        middle = middle + dot_nn(joined[t], wo[t])
    acc[...] = middle
    g2 = small[4:5]
    unit, _ = centre_rows(middle)
    n2[...] = (unit * g2).astype(bf16)
    gn2[...] = jnp.zeros_like(gn2)

    def block(p, carry):
        rows = pl.ds(pl.multiple_of(p * 48, 16), 48)
        for t in range(GROUP):
            for c in range(2):
                for z in range(0, 4, 2):
                    ends = [lf[slab(t, c, z + k) + (rows,)].astype(f32) for k in range(2)]
                    at = (t * 8 + c * 4 + z) * 24
                    for k in range(2):
                        both = jnp.concatenate([e[24 * k : 24 * k + 24] for e in ends], 0)
                        wu[k, at : at + 48, :] = both.astype(bf16)
        branch = gout[...].astype(bf16)
        for k in range(2):
            wd = jnp.concatenate(
                [lf[0, p, k, :, 128:224, :].reshape(384, width), lf[1, k, p, :, 128:224, :].reshape(384, width)], 0
            )
            up = dot_nn(n2[...], wu[k])
            act, slope = gelu_pair(up)
            act = act.astype(bf16)
            acc[...] += dot_nn(act, wd)
            gup = (dot_nt(branch, wd) * slope).astype(bf16)
            gwd = dot_tn(act, branch).astype(bf16)
            gf[0, p, k, :, 128:224, :] = gwd[:384].reshape(4, 96, width)
            gf[1, k, p, :, 128:224, :] = gwd[384:].reshape(4, 96, width)
            gwu[k] = dot_tn(n2[...], gup)
            gn2[...] += dot_nt(gup, wu[k])
        for t in range(GROUP):
            for c in range(2):
                for z in range(4):
                    at = (t * 8 + c * 4 + z) * 24
                    both = jnp.concatenate([gwu[0, at : at + 24, :], gwu[1, at : at + 24, :]], 0)
                    gf[slab(t, c, z) + (rows,)] = both.astype(bf16)
        return carry

    lax.fori_loop(0, 2, block, 0)
    result[...] = acc[...]
    middle = tokens[...].astype(f32)
    for t in range(GROUP):
        middle = middle + dot_nn(joined[t], wo[t])
    unit, scale = centre_rows(middle)
    gn = gn2[...]
    gg2[...] = jnp.sum((gn * unit).reshape(-1, 8, width), axis=0)
    gu = gn * g2
    back = scale * (
        gu - jnp.mean(gu, axis=-1, keepdims=True) - unit * jnp.mean(gu * unit, axis=-1, keepdims=True)
    )
    gm = gout[...] + back
    gmid[...] = gm
    ga = gm.astype(bf16)
    for t in range(GROUP):
        gj[t] = dot_nt(ga, wo[t]).astype(bf16)
        gwo = dot_tn(joined[t], ga)
        for c in range(2):
            for z in range(4):
                at = (c * 4 + z) * 24
                padded = jnp.concatenate([gwo[at : at + 24, :], jnp.zeros((8, width), f32)], 0)
                gf[slab(t, c, z) + (slice(96, 128),)] = padded.astype(bf16)


def ffn_call(lf, joined, tokens, small, gout):
    slots, width = tokens.shape
    return pl.pallas_call(
        ffn_kernel,
        out_shape=(
            shape_of((slots, width), f32),
            shape_of((slots, width), f32),
            shape_of(joined.shape, bf16),
            shape_of(lf.shape, bf16),
            shape_of((8, width), f32),
        ),
        in_specs=[FULL] * 5,
        out_specs=(FULL,) * 5,
        scratch_shapes=[
            pltpu.VMEM((2, width, width), bf16),
            pltpu.VMEM((GROUP, 256, width), bf16),
            pltpu.VMEM((slots, width), bf16),
            pltpu.VMEM((slots, width), f32),
            pltpu.VMEM((slots, width), f32),
            pltpu.VMEM((2, width, width), f32),
        ],
        compiler_params=pltpu.CompilerParams(vmem_limit_bytes=VMEM_LIMIT),
    )(lf, joined, tokens, small, gout)


def back_kernel(
    wf, ws, wv, normed, values, hid, slope, prob, gmix, lt, gg2, ga, gs, gn_out, awf, aws, ab1, ab2, gn, gv, awv, ag1
):
    h, r = pl.program_id(0), pl.program_id(1)
    width = wf.shape[-1]

    @pl.when(r == 0)
    def _():
        awf[...] = jnp.zeros_like(awf)
        aws[...] = jnp.zeros_like(aws)
        ab1[...] = jnp.zeros_like(ab1)
        ab2[h] = jnp.zeros(ab2.shape[1:], f32)

    tile = pl.ds(pl.multiple_of((h // 2) * 128, 128), 128)
    lane = lax.broadcasted_iota(jnp.int32, (512, 128), 1)
    gm = jnp.where(lane // 64 == h % 2, gmix[0, :, tile].astype(f32), 0.0).astype(bf16)
    gw = dot_nt(gm, values[0, :, tile])
    p = prob[0, 0]
    p32 = p.astype(f32)
    gl = (p32 * (gw - jnp.sum(p32 * gw, axis=-1, keepdims=True))).astype(bf16)
    ab2[h] += jnp.sum(gl.astype(f32).reshape(-1, 8, 512), axis=0)
    gvh = dot_tn(p, gm)

    @pl.when(h != 1)
    def _():
        gv[r, :, tile] = gvh

    @pl.when(h == 1)
    def _():
        gv[r, :, tile] += gvh

    aws[...] += dot_tn(hid[0, 0], gl)
    gb = (dot_nt(gl, ws[0]) * slope[0, 0].astype(f32)).astype(bf16)
    ab1[...] += jnp.sum(gb.astype(f32).reshape(-1, 8, width), axis=0)
    awf[...] += dot_tn(normed[0], gb)
    part = dot_nt(gb, wf[0])

    @pl.when(h == 0)
    def _():
        gn[r] = part

    @pl.when(h == 1)
    def _():
        gn[r] += part

    @pl.when(h == 2)
    def _():
        gvb = gv[r].astype(bf16)
        total = gn[r] + part + dot_nt(gvb, wv[...])
        gn_out[0] = total.astype(bf16)
        unit, _ = centre_rows(lt[0, 0:512, :].astype(f32))
        first = jnp.where(r == 0, 0.0, 1.0)
        ag1[...] = jnp.where(r == 0, 0.0, ag1[...]) + jnp.sum((total * unit).reshape(-1, 8, width), axis=0)
        more = dot_tn(normed[0], gvb)

        @pl.when(r == 0)
        def _():
            awv[...] = more

        @pl.when(r != 0)
        def _():
            awv[...] += more

    @pl.when(r == GROUP - 1)
    def _():
        last = h == 2
        row = lax.broadcasted_iota(jnp.int32, (128, width), 0)
        stack = jnp.where(row == 64, jnp.sum(ab1[...], axis=0, keepdims=True), 0.0)
        stack = jnp.where(last & (row == 65), jnp.sum(ag1[...], axis=0, keepdims=True), stack)
        stack = jnp.where(last & (row == 66), jnp.sum(gg2[...], axis=0, keepdims=True), stack)
        cols = stack.T
        lane = lax.broadcasted_iota(jnp.int32, (width, 128), 1)

        @pl.when(jnp.logical_not(last))
        def _():
            awv[:, 0:128] = jnp.zeros((width, 128), f32)
            awv[:, 128:256] = cols

        @pl.when(last)
        def _():
            awv[:, 128:256] = jnp.where(lane < 64, awv[:, 128:256], cols)

        def pack(t, carry):
            for c in range(2):
                for z in range(4):
                    at = pl.ds(pl.multiple_of((t * 8 + c * 4 + z) * 24, 8), 24)
                    low = jnp.concatenate([aws[at, :], awv[at, :]], 1)
                    ga[0, c, z, t] = jnp.concatenate([awf[at, :], low], 0).astype(bf16)
            return carry

        lax.fori_loop(0, GROUP, pack, 0)

        @pl.when(last)
        def _():
            flat = jnp.concatenate([jnp.sum(ab2[k], axis=0, keepdims=True) for k in range(3)], 1)
            flat = jnp.broadcast_to(flat, (8, 1536))
            for c in range(2):
                for z in range(4):
                    s = (c * 4 + z) * 192
                    gs[c, z] = (pltpu.roll(flat, 1536 - s, 1) if s else flat)[:, 0:256]


def back_call(wf, ws, wv, normed, values, hid, slope, prob, gmix, lt, gg2):
    heads, width, slots = ws.shape
    by_head = lambda h, r: (h, 0, 0)
    row = lambda h, r: (r, 0, 0)
    both = lambda h, r: (h, r, 0, 0)
    return pl.pallas_call(
        back_kernel,
        grid=(heads, GROUP),
        out_shape=(
            shape_of((heads, 2, 4, GROUP, 48, width), bf16),
            shape_of((2, 4, 8, 256), f32),
            shape_of((GROUP, slots, width), bf16),
        ),
        in_specs=[
            pl.BlockSpec((1, width, width), by_head),
            pl.BlockSpec((1, width, slots), by_head),
            pl.BlockSpec((width, 256), lambda h, r: (0, 0)),
            pl.BlockSpec((1, slots, width), row),
            pl.BlockSpec((1, slots, 256), row),
            pl.BlockSpec((1, 1, slots, width), both),
            pl.BlockSpec((1, 1, slots, width), both),
            pl.BlockSpec((1, 1, slots, slots), both),
            pl.BlockSpec((1, slots, 256), row),
            pl.BlockSpec((1,) + lt.shape[1:], lambda h, r: (jnp.where(h == 2, r, 0), 0, 0)),
            pl.BlockSpec((8, width), lambda h, r: (0, 0)),
        ],
        out_specs=(
            pl.BlockSpec((1, 2, 4, GROUP, 48, width), lambda h, r: (h, 0, 0, 0, 0, 0)),
            pl.BlockSpec((2, 4, 8, 256), lambda h, r: (0, 0, 0, 0)),
            pl.BlockSpec((1, slots, width), lambda h, r: (jnp.where(h == 2, r, 0), 0, 0)),
        ),
        scratch_shapes=[
            pltpu.VMEM((width, width), f32),
            pltpu.VMEM((width, slots), f32),
            pltpu.VMEM((8, width), f32),
            pltpu.VMEM((heads, 8, slots), f32),
            pltpu.VMEM((GROUP, slots, width), f32),
            pltpu.VMEM((GROUP, slots, 256), f32),
            pltpu.VMEM((width, 256), f32),
            pltpu.VMEM((8, width), f32),
        ],
        compiler_params=pltpu.CompilerParams(vmem_limit_bytes=VMEM_LIMIT),
    )(wf, ws, wv, normed, values, hid, slope, prob, gmix, lt, gg2)


def add_into(total, more, count):
    def one(i, carry):
        total[i] = (total[i].astype(f32) + more[i].astype(f32)).astype(bf16)
        return carry

    lax.fori_loop(0, count, one, 0)


def reduce_kernel(
    gf, ga, gs, gn, tokens, gmid, small, out_f, out_a, out_s, gtok,
    fs, fb1, fb2, fb3, fb4, asum, ab1, ab2, ss, sb1, sb2, nb, own, s1, r1, s2, r2, s3, r3, sn, rn, sf, rf, sv, rv,
):
    t, c, z = place()
    sibling = (t, 1 - c, z)
    tps, zs = group_peers(), line_peers()
    greet([(p, c, z) for p in tps] + [(t, c, p) for p in zs] + [sibling])
    y, x = t // 2, t % 2
    slow, fast = (1 - c) * y + c * x, (1 - c) * x + c * y
    fast_peer = (1 - c) * tps[0] + c * tps[1]
    slow_peer = (1 - c) * tps[1] + c * tps[0]
    heads = ga.shape[0]
    one = [remote(ga.at[h, 1 - c], ab1.at[h], s1.at[h], r1.at[h], sibling) for h in range(heads)]
    v1 = remote(gs.at[1 - c], sb1, sv.at[0], rv.at[0], sibling)
    f1 = remote(gf.at[1 - c], fb1, sf.at[0], rf.at[0], sibling)
    mine = [local(ga.at[h, c], asum.at[h], own.at[h]) for h in range(heads)]
    mine_s = local(gs.at[c], ss, own.at[heads])
    mine_f = local(gf.at[c], fs, own.at[heads + 1])
    mine_n = local(gn.at[t], nb.at[3], own.at[heads + 2])
    parts = [remote(gn.at[p], nb.at[k], sn.at[k], rn.at[k], (p, c, z)) for k, p in enumerate(tps)]
    two = []
    for h in range(heads):
        mine[h].wait()
        one[h].wait()

        def line(i, carry):
            add_into(asum.at[h, i], ab1.at[h, i], GROUP)
            return carry

        lax.fori_loop(0, 4, line, 0)
        two.append(
            [remote(asum.at[h, p], ab2.at[h, k], s2.at[h, k], r2.at[h, k], (t, c, p)) for k, p in enumerate(zs)]
        )
        if h == 0:
            mine_s.wait()
            v1.wait()
            ss[...] += sb1[...]
            v2 = [remote(ss.at[p], sb2.at[k], sv.at[1 + k], rv.at[1 + k], (t, c, p)) for k, p in enumerate(zs)]
    mine_f.wait()
    f1.wait()

    for which in (1 - slow, slow):
        for j in range(2):
            add_into(fs.at[which, j], fb1.at[which, j], 4)
        if which is not slow:
            f2 = remote(fs.at[1 - slow], fb2, sf.at[1], rf.at[1], (slow_peer, c, z))
    mine_n.wait()
    for copy in parts:
        copy.wait()

    def ln_back(i, carry):
        at = pl.ds(pl.multiple_of(i * 128, 128), 128)
        g = nb[0, at, :].astype(f32) + nb[1, at, :].astype(f32) + nb[2, at, :].astype(f32) + nb[3, at, :].astype(f32)
        unit, scale = centre_rows(tokens[at, :].astype(f32))
        gu = g * small[3:4]
        back = scale * (
            gu - jnp.mean(gu, axis=-1, keepdims=True) - unit * jnp.mean(gu * unit, axis=-1, keepdims=True)
        )
        gtok[at, :] = gmid[at, :] + back
        return carry

    lax.fori_loop(0, 4, ln_back, 0)
    f2.wait()
    for which in (1 - fast, fast):
        add_into(fs.at[slow, which], fb2.at[which], 4)
        if which is not fast:
            f3 = remote(fs.at[slow, 1 - fast], fb3, sf.at[2], rf.at[2], (fast_peer, c, z))
    f3.wait()
    add_into(fs.at[slow, fast], fb3, 4)
    f4 = [
        remote(fs.at[slow, fast, p], fb4.at[k], sf.at[3 + k], rf.at[3 + k], (t, c, p)) for k, p in enumerate(zs)
    ]
    three, mine_a = [], []
    for h in range(heads):
        for copy in two[h]:
            copy.wait()

        def fold(i, carry):
            total = asum[h, z, i].astype(f32)
            for k in range(3):
                total = total + ab2[h, k, i].astype(f32)
            asum[h, z, i] = total.astype(bf16)
            return carry

        lax.fori_loop(0, GROUP, fold, 0)
        mine_a.append(local(asum.at[h, z, t], out_a.at[h, t], own.at[h]))
        three.append(
            [remote(asum.at[h, z, p], out_a.at[h, t], s3.at[h, k], r3.at[h, k], (p, c, z)) for k, p in enumerate(tps)]
        )
    for copy in v2:
        copy.wait()
    out_s[...] = ss[z] + sb2[0] + sb2[1] + sb2[2]
    for copy in f4:
        copy.wait()
    total = fs[slow, fast, z].astype(f32)
    for k in range(3):
        total = total + fb4[k].astype(f32)
    out_f[...] = total
    for copy in mine_a:
        copy.wait()
    for copies in three:
        for copy in copies:
            copy.wait()


def reduce_call(gf, ga, gs, gn, tokens, gmid, small):
    heads, width = ga.shape[0], ga.shape[-1]
    rows = gf.shape[-2]
    return pl.pallas_call(
        reduce_kernel,
        out_shape=(
            shape_of((rows, width), f32),
            shape_of((heads, GROUP, 48, width), bf16),
            shape_of((8, 256), f32),
            shape_of(tokens.shape, f32),
        ),
        in_specs=[ANY] * 4 + [FULL] * 3,
        out_specs=(FULL, ANY, FULL, FULL),
        scratch_shapes=[
            pltpu.VMEM((2, 2, 4, rows, width), bf16),
            pltpu.VMEM((2, 2, 4, rows, width), bf16),
            pltpu.VMEM((2, 4, rows, width), bf16),
            pltpu.VMEM((4, rows, width), bf16),
            pltpu.VMEM((3, rows, width), bf16),
            pltpu.VMEM((heads, 4, GROUP, 48, width), bf16),
            pltpu.VMEM((heads, 4, GROUP, 48, width), bf16),
            pltpu.VMEM((heads, 3, GROUP, 48, width), bf16),
            pltpu.VMEM((4, 8, 256), f32),
            pltpu.VMEM((4, 8, 256), f32),
            pltpu.VMEM((3, 8, 256), f32),
            pltpu.VMEM((4,) + tokens.shape, bf16),
            DMA((heads + 3,)),
            DMA((heads,)),
            DMA((heads,)),
            DMA((heads, 3)),
            DMA((heads, 3)),
            DMA((heads, 3)),
            DMA((heads, 3)),
            DMA((3,)),
            DMA((3,)),
            DMA((6,)),
            DMA((6,)),
            DMA((4,)),
            DMA((4,)),
        ],
        compiler_params=pltpu.CompilerParams(collective_id=4, has_side_effects=True, vmem_limit_bytes=VMEM_LIMIT),
    )(gf, ga, gs, gn, tokens, gmid, small)


def pack_inputs(tokens, lengths, gain_one, w_value, w_first, b_first, w_second, b_second, w_out, gain_two, w_up, w_down):
    _, slots, width = tokens.shape
    heads_all, depth, _ = w_first.shape
    heads = heads_all // GROUP
    split = lambda v: v.reshape((GROUP, heads) + v.shape[1:])
    cols = jnp.concatenate(
        [
            b_first.reshape(GROUP, heads, depth).transpose(0, 2, 1),
            jnp.broadcast_to(jnp.stack([gain_one, gain_two], 1), (GROUP, depth, 2)),
            jnp.zeros((GROUP, depth, 59), bf16),
        ],
        2,
    )
    head_zero = jnp.concatenate([w_value.reshape(depth, GROUP, -1).transpose(1, 0, 2), cols], 2)
    head_one = jnp.broadcast_to(jnp.pad(b_second[None, :], ((0, depth - 1), (0, 256 - b_second.shape[0]))), head_zero.shape)
    extra = jnp.stack([head_zero, head_one, jnp.zeros_like(head_zero)], 1)
    low = jnp.concatenate([split(w_second), extra], 3)
    pa = jnp.concatenate([split(w_first), low], 2)
    spot = lax.broadcasted_iota(jnp.int32, (16, width), 1)
    mask = jnp.where(spot < lengths[0], 0.0, -1e30).astype(bf16)
    pt = jnp.concatenate([tokens[0], mask], 0)
    ups = [w_up[:, k * width : (k + 1) * width] for k in range(w_up.shape[1] // width)]
    pf = jnp.concatenate(ups + [w_out, jnp.zeros((8, width), bf16), w_down], 0)
    return pa, pt, pf


def on_device_fast(tokens, lengths, gain_one, w_value, w_first, b_first, w_second, b_second, w_out, gain_two, w_up, w_down, grad_out):
    _, slots, width = tokens.shape
    heads_all, depth, _ = w_first.shape
    heads = heads_all // GROUP
    me = lax.axis_index("tp")
    pa, pt, pf = pack_inputs(
        tokens, lengths, gain_one, w_value, w_first, b_first, w_second, b_second, w_out, gain_two, w_up, w_down
    )
    la, lt, lf = gather_call(pa, pt, pf)
    b2 = lax.dynamic_index_in_dim(la[1, :, :, :, 24, 512:704], me, 2, False).reshape(heads, slots).astype(f32)
    wf, ws, wv, small, normed, values, hid, slope, prob, join = attend_call(la, lt, b2)
    joined = trade_call(join, 2)
    result, gmid, gj, gf, gg2 = ffn_call(lf, joined, tokens[0], small, grad_out[0])
    gmix = trade_call(gj, 3)
    ga, gs, gn = back_call(wf, ws, wv, normed, values, hid, slope, prob, gmix, lt, gg2)
    out_f, out_a, out_s, gtok = reduce_call(gf, ga, gs, gn, tokens[0], gmid, small)
    low = out_a[:, :, 24:].astype(f32)
    to_all = lambda v: v.transpose((1, 0) + tuple(range(2, v.ndim))).reshape((heads_all,) + v.shape[2:])
    gb1 = to_all(low[:, :, :, 704])
    gains = jnp.sum(low[2, :, :, 705:707], axis=0)
    return (
        result[None],
        gtok[None],
        gains[:, 0],
        low[2, :, :, 512:704].transpose(1, 0, 2).reshape(depth, width),
        to_all(out_a[:, :, :24].astype(f32)),
        gb1,
        to_all(low[:, :, :, :512]),
        out_s[0, : b_second.shape[0]],
        out_f[4 * depth : 5 * depth],
        gains[:, 1],
        out_f[: 4 * depth].reshape(4, depth, width).transpose(1, 0, 2).reshape(depth, 4 * width),
        out_f[128:],
    )


def solution(mesh):
    wide, narrow = mesh.shape["wide"], mesh.shape["narrow"]
    grouped = Mesh(mesh.devices.reshape(GROUP, wide // GROUP, narrow), ALL)
    vec = P(ALL)
    flat = P(ALL, None)
    mid = P(None, ALL, None)
    row = P(ALL, None, None)
    body = on_device_fast if (wide, narrow) == (8, 4) else on_device
    return jax.shard_map(
        body,
        mesh=grouped,
        in_specs=(row, vec, vec, flat, mid, P(None, ALL), mid, vec, flat, vec, flat, flat, row),
        out_specs=(row, row, vec, flat, mid, P(None, ALL), mid, vec, flat, vec, flat, flat),
        check_vma=False,
    )
```

```python
import jax
import jax.numpy as jnp
from jax import lax
from jax.experimental import pallas as pl
from jax.experimental.pallas import tpu as pltpu
from jax.sharding import Mesh
from jax.sharding import PartitionSpec as P

epsilon = 1e-05
f32 = jnp.float32
bf16 = jnp.bfloat16
GROUP = 4


def norm_rows(values, factor):
    average = jnp.mean(values, axis=-1, keepdims=True)
    centred = values - average
    spread = jnp.mean(centred * centred, axis=-1, keepdims=True)
    return centred * lax.rsqrt(spread + epsilon) * factor


def smooth(values):
    return jax.nn.gelu(values, approximate=False)


def mm(spec, a, b):
    return jnp.einsum(spec, a, b, preferred_element_type=f32)


REST = ("rep", "narrow")
ALL = ("tp", "rep", "narrow")


def to_heads(shard):
    heads, depth, width = shard.shape
    pieces = lax.all_to_all(shard.reshape(GROUP, heads // GROUP, depth, width), "tp", 0, 0)
    whole = lax.all_gather(pieces, REST, axis=0)
    return whole.transpose(2, 1, 0, 3, 4).reshape(heads // GROUP, -1, width)


def from_heads(grad):
    heads, depth, width = grad.shape
    n = lax.axis_size("rep") * lax.axis_size("narrow")
    pieces = grad.astype(bf16).reshape(heads, GROUP, n, depth // (GROUP * n), width).transpose(2, 1, 0, 3, 4)
    pieces = pieces.reshape((n * GROUP,) + pieces.shape[2:])
    share = lax.psum_scatter(pieces, REST, scatter_dimension=0, tiled=True)
    share = lax.all_to_all(share, "tp", 0, 0)
    return share.reshape(heads * GROUP, depth // (GROUP * n), width).astype(f32)


def on_device(tokens, lengths, gain_one, w_value, w_first, b_first, w_second, b_second, w_out, gain_two, w_up, w_down, grad_out):
    row_count, slots, width = tokens.shape
    heads_all = w_first.shape[0]
    heads = heads_all // GROUP
    head_size = width // heads_all
    me = lax.axis_index("tp")
    depth = w_value.shape[0]

    small = [gain_one, gain_two, b_second, b_first.reshape(-1)]
    gathered = lax.all_gather(jnp.concatenate(small), ALL, axis=0)
    n_all = gathered.shape[0]
    g1 = gathered[:, :depth].reshape(-1).astype(f32)
    g2 = gathered[:, depth : 2 * depth].reshape(-1).astype(f32)
    b2_len = b_second.shape[0]
    b2 = gathered[:, 2 * depth : 2 * depth + b2_len].reshape(heads_all, slots).astype(f32)
    b1 = gathered[:, 2 * depth + b2_len :].reshape(n_all, heads_all, depth).transpose(1, 0, 2).reshape(heads_all, width).astype(f32)
    b1 = lax.dynamic_slice_in_dim(b1, me * heads, heads, 0)
    b2 = lax.dynamic_slice_in_dim(b2, me * heads, heads, 0)

    wf = to_heads(w_first)
    ws = to_heads(w_second)
    wv = to_heads(w_value.reshape(depth, GROUP, width // GROUP).transpose(1, 0, 2))[0]
    rows = lax.all_gather(tokens, "tp", axis=0, tiled=True)
    lens = lax.all_gather(lengths, "tp", axis=0, tiled=True)
    n_rows = rows.shape[0]

    normed = norm_rows(rows.astype(f32), g1).astype(bf16)
    values = mm("rsd,de->rse", normed, wv).astype(bf16)
    per_head = values.reshape(n_rows, slots, heads, head_size).transpose(2, 0, 1, 3)
    before = mm("rsd,hde->hrse", normed, wf) + b1[:, None, None, :]
    hidden = smooth(before).astype(bf16)
    logits = mm("hrse,hej->hrsj", hidden, ws) + b2[:, None, None, :]
    visible = lax.broadcasted_iota(jnp.int32, (1, n_rows, 1, slots), 3) < lens[None, :, None, None]
    masked = jnp.where(visible, logits, f32(-1e30))
    scaled = jnp.exp(masked - jnp.max(masked, axis=-1, keepdims=True))
    probabilities = scaled / jnp.sum(scaled, axis=-1, keepdims=True)
    weights = probabilities.astype(bf16)
    mixture = mm("hrsj,hrjc->rshc", weights, per_head).astype(bf16)
    mixture = mixture.reshape(GROUP, row_count, slots, heads * head_size)
    joined = lax.all_to_all(mixture, "tp", 0, 0).transpose(1, 2, 0, 3).reshape(row_count * slots, width)

    wo = lax.all_gather(w_out, ALL, axis=0, tiled=True)
    wu = lax.all_gather(w_up, ALL, axis=0, tiled=True)
    wd = lax.all_gather(w_down, ALL, axis=0, tiled=True)
    inputs = tokens.astype(f32).reshape(-1, width)
    middle = inputs + mm("sd,de->se", joined, wo)
    normed_two, norm_two_back = jax.vjp(norm_rows, middle, g2)
    normed_two = normed_two.astype(bf16)
    upward = mm("td,df->tf", normed_two, wu)
    active, smooth_up_back = jax.vjp(smooth, upward)
    active = active.astype(bf16)
    result = middle + mm("tf,fd->td", active, wd)

    g_out = grad_out.reshape(-1, width)
    grad_branch = g_out.astype(bf16)
    grad_w_down = mm("tf,td->fd", active, grad_branch)
    grad_upward = smooth_up_back(mm("td,fd->tf", grad_branch, wd))[0].astype(bf16)
    grad_w_up = mm("td,tf->df", normed_two, grad_upward)
    grad_middle_norm, grad_gain_two = norm_two_back(mm("tf,df->td", grad_upward, wu))
    grad_middle = g_out + grad_middle_norm
    grad_attn = grad_middle.astype(bf16)
    grad_w_out = mm("sd,se->de", joined, grad_attn)
    grad_joined = mm("se,de->sd", grad_attn, wo).astype(bf16)

    grad_mixture = grad_joined.reshape(row_count, slots, GROUP, heads * head_size).transpose(2, 0, 1, 3)
    grad_mixture = lax.all_to_all(grad_mixture, "tp", 0, 0).reshape(n_rows, slots, heads, head_size).transpose(2, 0, 1, 3)
    grad_weights = mm("hrsc,hrjc->hrsj", grad_mixture, per_head)
    grad_values = mm("hrsj,hrsc->rjhc", weights, grad_mixture).astype(bf16).reshape(n_rows, slots, heads * head_size)
    centre = jnp.sum(probabilities * grad_weights, axis=-1, keepdims=True)
    grad_logits = (probabilities * (grad_weights - centre)).astype(bf16)
    grad_b_second = jnp.sum(grad_logits.astype(f32), axis=(1, 2))
    grad_w_second = mm("hrse,hrsj->hej", hidden, grad_logits)
    grad_hidden = mm("hrsj,hej->hrse", grad_logits, ws)
    smooth_value, smooth_back = jax.vjp(smooth, before)
    grad_before = smooth_back(grad_hidden)[0].astype(bf16)
    grad_b_first = jnp.sum(grad_before.astype(f32), axis=(1, 2))
    grad_w_first = mm("rsd,hrse->hde", normed, grad_before)
    grad_w_value = mm("rsd,rse->de", normed, grad_values)
    grad_normed = mm("hrse,hde->rsd", grad_before, wf) + mm("rse,de->rsd", grad_values, wv)
    grad_normed = lax.psum_scatter(grad_normed.astype(bf16), "tp", scatter_dimension=0, tiled=True)
    value, norm_one_back = jax.vjp(norm_rows, inputs, g1)
    grad_inputs_norm, grad_gain_one = norm_one_back(grad_normed.astype(f32).reshape(-1, width))
    grad_tokens = grad_middle + grad_inputs_norm

    out_first = from_heads(grad_w_first)
    out_second = from_heads(grad_w_second)
    out_value = from_heads(grad_w_value[None]).transpose(1, 0, 2).reshape(depth, width)

    def share(grad):
        return lax.psum_scatter(grad.astype(bf16), ALL, scatter_dimension=0, tiled=True).astype(f32)

    vec_tp = jnp.concatenate([grad_b_first.reshape(-1), grad_b_second.reshape(-1)])
    vec_tp = lax.dynamic_update_slice_in_dim(jnp.zeros((GROUP, vec_tp.shape[0]), f32), vec_tp[None], me, 0)
    vec = jnp.concatenate([vec_tp.reshape(-1), grad_gain_one, grad_gain_two])
    vec = lax.psum(vec, ALL)
    index = (me * lax.axis_size("rep") + lax.axis_index("rep")) * lax.axis_size("narrow") + lax.axis_index("narrow")
    n_tp = GROUP * (heads * width + heads * slots)
    tp_part = vec[:n_tp].reshape(GROUP, -1)
    gb1 = tp_part[:, : heads * width].reshape(heads_all, width)
    gb2 = tp_part[:, heads * width :].reshape(-1)
    gb1 = lax.dynamic_slice_in_dim(gb1, index * depth, depth, 1)
    gb2 = lax.dynamic_slice_in_dim(gb2, index * b2_len, b2_len, 0)
    gg1 = lax.dynamic_slice_in_dim(vec[n_tp : n_tp + width], index * depth, depth, 0)
    gg2 = lax.dynamic_slice_in_dim(vec[n_tp + width :], index * depth, depth, 0)
    shape = tokens.shape
    return (
        result.reshape(shape),
        grad_tokens.reshape(shape),
        gg1,
        out_value,
        out_first,
        gb1,
        out_second,
        gb2,
        share(grad_w_out),
        gg2,
        share(grad_w_up),
        share(grad_w_down),
    )


MESH = pl.DeviceIdType.MESH
VMEM_LIMIT = 60 * 2**20
ANY = pl.BlockSpec(memory_space=pl.ANY)
FULL = pl.BlockSpec(memory_space=pltpu.VMEM)
DMA = pltpu.SemaphoreType.DMA


def shape_of(dims, kind):
    return jax.ShapeDtypeStruct(dims, kind)


def dot_nt(a, b):
    return lax.dot_general(a, b, (((1,), (1,)), ((), ())), preferred_element_type=f32)


def dot_tn(a, b):
    return lax.dot_general(a, b, (((0,), (0,)), ((), ())), preferred_element_type=f32)


def dot_nn(a, b):
    return lax.dot_general(a, b, (((1,), (0,)), ((), ())), preferred_element_type=f32)


def place():
    return lax.axis_index("tp"), lax.axis_index("rep"), lax.axis_index("narrow")


def group_peers():
    t, c, z = place()
    along_x = t + 1 - 2 * (t % 2)
    along_y = (t + 2) % GROUP
    return [along_x, along_y, GROUP - 1 - t]


def line_peers():
    z = lax.axis_index("narrow")
    return [(z + k) % 4 for k in (1, 2, 3)]


def greet(devices):
    barrier = pltpu.get_barrier_semaphore()
    for device in devices:
        pl.semaphore_signal(barrier, inc=1, device_id=device, device_id_type=MESH)
    pl.semaphore_wait(barrier, len(devices))


def remote(src, dst, send, recv, device):
    return pltpu.make_async_remote_copy(
        src_ref=src, dst_ref=dst, send_sem=send, recv_sem=recv, device_id=device, device_id_type=MESH
    )


def local(src, dst, sem):
    return pltpu.make_async_copy(src, dst, sem)


def start(copies):
    for copy in copies:
        copy.start()


def wait(copies):
    for copy in copies:
        copy.wait()


def square():
    t, c, z = place()
    y, x = t // 2, t % 2
    tps = group_peers()
    slow, fast = (1 - c) * y + c * x, (1 - c) * x + c * y
    fast_peer = (1 - c) * tps[0] + c * tps[1]
    slow_peer = (1 - c) * tps[1] + c * tps[0]
    return slow, fast, (slow_peer, c, z), (fast_peer, c, z)


def gelu_pair(v):
    cdf = 0.5 * (1.0 + lax.erf(v * 0.7071067811865476))
    return v * cdf, cdf + v * (jnp.exp(-0.5 * v * v) * 0.3989422804014327)


def centre_rows(v):
    shifted = v - jnp.mean(v, axis=-1, keepdims=True)
    scale = lax.rsqrt(jnp.mean(shifted * shifted, axis=-1, keepdims=True) + epsilon)
    return shifted * scale, scale


def attend_kernel(
    pa, pt, pf, wf, ws, wv, small, normed, values, hid, slope, prob, joined, lf,
    la, lt, nrm, val, cols, b2, join, own, s1, r1, s2, r2, s3, r3, st, rt, sf, rf, sj, rj,
):
    h, r = pl.program_id(0), pl.program_id(1)
    width = wf.shape[-1]
    heads = la.shape[0]
    t, c, z = place()
    sibling = (t, 1 - c, z)
    tps, zs = group_peers(), line_peers()
    slow, fast, slow_dev, fast_dev = square()

    a1 = lambda i: [
        remote(pa.at[p, i], la.at[i, c, z, t], s1.at[i, k], r1.at[i, k], (p, c, z)) for k, p in enumerate(tps)
    ]
    a2 = lambda i: [
        remote(la.at[i, c, z], la.at[i, c, z], s2.at[i, k], r2.at[i, k], (t, c, p)) for k, p in enumerate(zs)
    ]
    a3 = lambda i: [remote(la.at[i, c], la.at[i, c], s3.at[i], r3.at[i], sibling)]
    mine = lambda i: [local(pa.at[t, i], la.at[i, c, z, t], own.at[i])]
    mine_t = lambda: [local(pt, lt.at[3], own.at[heads])]
    mine_f = lambda: [local(pf, lf.at[c, slow, fast, z], own.at[heads + 1])]
    mine_j = lambda: [local(join.at[3], joined.at[t], own.at[heads + 2])]
    toks = lambda: [remote(pt, lt.at[k], st.at[k], rt.at[k], (p, c, z)) for k, p in enumerate(tps)]
    f1 = lambda: [remote(pf, lf.at[c, slow, fast, z], sf.at[k], rf.at[k], (t, c, p)) for k, p in enumerate(zs)]
    f2 = lambda: [remote(lf.at[c, slow, fast], lf.at[c, slow, fast], sf.at[3], rf.at[3], fast_dev)]
    f3 = lambda: [remote(lf.at[c, slow], lf.at[c, slow], sf.at[4], rf.at[4], slow_dev)]
    f4 = lambda: [remote(lf.at[c, slow], lf.at[c, slow], sf.at[5], rf.at[5], sibling)]
    f5 = lambda: [remote(lf.at[c, 1 - slow], lf.at[c, 1 - slow], sf.at[6], rf.at[6], sibling)]
    out_j = lambda k: [remote(join.at[k], joined.at[t], sj.at[k], rj.at[k], (tps[k], c, z))]

    def at_step(i, j):
        return pl.when((h == i) & (r == j))

    @at_step(0, 0)
    def _():
        greet([(p, c, z) for p in tps] + [(t, c, p) for p in zs] + [sibling])
        for i in range(heads):
            start(mine(i) + a1(i))
        start(mine_f() + f1() + mine_t() + toks())
        for i in range(heads):
            wait(mine(i) + a1(i))
            start(a2(i))
        wait(a2(0))
        start(a3(0))
        wait(mine_t() + toks() + a3(0))

    @at_step(0, 1)
    def _():
        wait(mine_f() + f1())
        start(f2())

    @at_step(1, 0)
    def _():
        wait(a2(1))
        start(a3(1))
        wait(a3(1))

    @at_step(1, 1)
    def _():
        wait(f2())
        start(f3() + f4())

    @at_step(2, 0)
    def _():
        wait(a2(2))
        start(a3(2))
        wait(a3(2))

    @pl.when(r == 0)
    def _():
        def unpack(i, carry):
            for cc in range(2):
                for zz in range(0, 4, 2):
                    tops, lows = [], []
                    for k in range(2):
                        tops.append(la[h, cc, zz + k, i, 0:32, :].astype(f32)[0:24])
                        lows.append(la[h, cc, zz + k, i, 16:48, :].astype(f32)[8:32])
                    top, low = jnp.concatenate(tops, 0), jnp.concatenate(lows, 0)
                    at = pl.ds(pl.multiple_of((i * 8 + cc * 4 + zz) * 24, 48), 48)
                    wf[0, at, :] = top.astype(bf16)
                    ws[0, at, :] = low[:, :512].astype(bf16)

                    @pl.when(h == 0)
                    def _():
                        last = low[:, 640:768]
                        cols[at, :] = last
                        lane = lax.broadcasted_iota(jnp.int32, last.shape, 1)
                        wv[at, 0:128] = low[:, 512:640].astype(bf16)
                        wv[at, 128:256] = jnp.where(lane < 64, last, 0.0).astype(bf16)

            return carry

        lax.fori_loop(0, GROUP, unpack, 0)

        @pl.when(h == 0)
        def _():
            small[...] = cols[...].T[64:72]
            mine_rows = cols[pl.ds(pl.multiple_of(t * 192, 192), 192), :].astype(bf16)
            lane = lax.broadcasted_iota(jnp.int32, (128, 512), 0)
            spot = lax.broadcasted_iota(jnp.int32, (128, 512), 1)
            spread = dot_nn(mine_rows, jnp.where(lane - 69 == spot % 8, 1.0, 0.0).astype(bf16))
            row = lax.broadcasted_iota(jnp.int32, (64, 512), 0)
            spot = lax.broadcasted_iota(jnp.int32, (64, 512), 1)
            for i in range(heads):
                picked = jnp.where(row == spot // 8, spread[64 * i : 64 * i + 64], 0.0)
                b2[i] = jnp.broadcast_to(jnp.sum(picked, axis=0, keepdims=True), (8, 512))

    @pl.when(h == 0)
    def _():
        unit, _ = centre_rows(lt[r, 0:512, :].astype(f32))
        out = (unit * small[3:4]).astype(bf16)
        nrm[r] = out
        normed[0] = out
        v = dot_nn(out, wv[...]).astype(bf16)
        val[r] = v
        values[0] = v

    mask = lt[r, 512:528, 0:512].astype(f32)[0:1]
    row = lax.broadcasted_iota(jnp.int32, (8, width), 0)
    b1 = jnp.sum(jnp.where(row == h, small[...], 0.0), axis=0, keepdims=True)
    shift = b2[h, 0:1] + mask
    tile = pl.ds(pl.multiple_of((h // 2) * 128, 128), 128)
    step = 256
    for m in range(0, 512, step):
        at = slice(m, m + step)
        before = dot_nn(nrm[r, at, :], wf[0]) + b1
        out, grad = gelu_pair(before)
        hidden = out.astype(bf16)
        hid[0, 0, at, :] = hidden
        slope[0, 0, at, :] = grad.astype(bf16)
        logits = dot_nn(hidden, ws[0]) + shift
        e = jnp.exp(logits - jnp.max(logits, axis=-1, keepdims=True))
        p = (e / jnp.sum(e, axis=-1, keepdims=True)).astype(bf16)
        prob[0, 0, at, :] = p
        mix = dot_nn(p, val[r, :, tile])
        lane = lax.broadcasted_iota(jnp.int32, mix.shape, 1)
        old = join[r, at, tile].astype(f32)
        join[r, at, tile] = jnp.where((h == 1) & (lane < 64), old, mix).astype(bf16)

    for k in range(3):

        @at_step(2, k)
        def _():
            start(out_j(k))

    @at_step(2, 2)
    def _():
        wait(f3())
        start(f5())

    @at_step(2, 3)
    def _():
        start(mine_j())
        for k in range(3):
            wait(out_j(k))
        wait(mine_j() + f4() + f5())


def attend_call(pa, pt, pf):
    heads, width = pa.shape[1], pa.shape[-1]
    slots = 512
    by_row = lambda h, r: (jnp.where(h == 0, r, GROUP - 1), 0, 0)
    by_head = lambda h, r: (h, 0, 0)
    both = lambda h, r: (h, r, 0, 0)
    return pl.pallas_call(
        attend_kernel,
        grid=(heads, GROUP),
        out_shape=(
            shape_of((heads, width, width), bf16),
            shape_of((heads, width, slots), bf16),
            shape_of((width, 256), bf16),
            shape_of((8, width), f32),
            shape_of((GROUP, slots, width), bf16),
            shape_of((GROUP, slots, 256), bf16),
            shape_of((heads, GROUP, slots, width), bf16),
            shape_of((heads, GROUP, slots, width), bf16),
            shape_of((heads, GROUP, slots, slots), bf16),
            shape_of((GROUP, slots, 256), bf16),
            shape_of((2, 2, 2, 4) + pf.shape, bf16),
        ),
        in_specs=[ANY] * 3,
        out_specs=(
            pl.BlockSpec((1, width, width), by_head),
            pl.BlockSpec((1, width, slots), by_head),
            pl.BlockSpec((width, 256), lambda h, r: (0, 0)),
            pl.BlockSpec((8, width), lambda h, r: (0, 0)),
            pl.BlockSpec((1, slots, width), by_row),
            pl.BlockSpec((1, slots, 256), by_row),
            pl.BlockSpec((1, 1, slots, width), both),
            pl.BlockSpec((1, 1, slots, width), both),
            pl.BlockSpec((1, 1, slots, slots), both),
            ANY,
            ANY,
        ),
        scratch_shapes=[
            pltpu.VMEM((heads, 2, 4, GROUP) + pa.shape[2:], bf16),
            pltpu.VMEM((GROUP,) + pt.shape, bf16),
            pltpu.VMEM((GROUP, slots, width), bf16),
            pltpu.VMEM((GROUP, slots, 256), bf16),
            pltpu.VMEM((width, 128), f32),
            pltpu.VMEM((heads, 8, slots), f32),
            pltpu.VMEM((GROUP, slots, 256), bf16),
            DMA((heads + 3,)),
            DMA((heads, 3)),
            DMA((heads, 3)),
            DMA((heads, 3)),
            DMA((heads, 3)),
            DMA((heads,)),
            DMA((heads,)),
            DMA((3,)),
            DMA((3,)),
            DMA((7,)),
            DMA((7,)),
            DMA((3,)),
            DMA((3,)),
        ],
        compiler_params=pltpu.CompilerParams(collective_id=1, has_side_effects=True, vmem_limit_bytes=VMEM_LIMIT),
    )(pa, pt, pf)


def slab(t, c, z):
    y, x = t // 2, t % 2
    return (0, y, x, z) if c == 0 else (1, x, y, z)


def ffn_kernel(
    lf, joined, tokens, small, gout, result, gmid, gmix, half, gg2,
    gf, gj, more, wu, wo, n2, acc, gn2, gwu, own, sg, rg, sx, rx,
):
    width = tokens.shape[-1]
    me, core, z_me = place()
    tps = group_peers()
    sibling = (me, 1 - core, z_me)
    parts = (slice(0, 96), slice(128, 224), slice(96, 128))
    cross = lambda k: [
        remote(
            gf.at[1 - core, :, :, :, parts[k], :], more.at[:, :, :, parts[k], :], sx.at[k], rx.at[k], sibling
        )
    ]
    out_g = lambda k: [remote(gj.at[tps[k]], gmix.at[k], sg.at[k], rg.at[k], (tps[k], core, z_me))]
    greet([(p, core, z_me) for p in tps] + [sibling])
    wo[...] = jnp.zeros_like(wo)
    for t in range(GROUP):
        for c in range(2):
            for z in range(0, 4, 2):
                pair = [lf[slab(t, c, z + k)][96:128].astype(f32)[0:24] for k in range(2)]
                wo[t, (c * 4 + z) * 24 : (c * 4 + z) * 24 + 48, :] = jnp.concatenate(pair, 0).astype(bf16)
    middle = tokens[...].astype(f32)
    for t in range(GROUP):
        middle = middle + dot_nn(joined[t], wo[t])
    acc[...] = middle
    g2 = small[4:5]
    unit, _ = centre_rows(middle)
    n2[...] = (unit * g2).astype(bf16)
    gn2[...] = jnp.zeros_like(gn2)

    def block(p, carry):
        rows = pl.ds(pl.multiple_of(p * 48, 16), 48)
        for t in range(GROUP):
            for c in range(2):
                for z in range(0, 4, 2):
                    ends = [lf[slab(t, c, z + k) + (rows,)].astype(f32) for k in range(2)]
                    at = (t * 8 + c * 4 + z) * 24
                    for k in range(2):
                        both = jnp.concatenate([e[24 * k : 24 * k + 24] for e in ends], 0)
                        wu[k, at : at + 48, :] = both.astype(bf16)
        branch = gout[...].astype(bf16)
        for k in range(2):
            wd = jnp.concatenate(
                [lf[0, p, k, :, 128:224, :].reshape(384, width), lf[1, k, p, :, 128:224, :].reshape(384, width)], 0
            )
            up = dot_nn(n2[...], wu[k])
            act, slope = gelu_pair(up)
            act = act.astype(bf16)
            acc[...] += dot_nn(act, wd)
            gup = (dot_nt(branch, wd) * slope).astype(bf16)
            gwd = dot_tn(act, branch).astype(bf16)
            gf[0, p, k, :, 128:224, :] = gwd[:384].reshape(4, 96, width)
            gf[1, k, p, :, 128:224, :] = gwd[384:].reshape(4, 96, width)
            gwu[k] = dot_tn(n2[...], gup)
            gn2[...] += dot_nt(gup, wu[k])
        for t in range(GROUP):
            for c in range(2):
                for z in range(4):
                    at = (t * 8 + c * 4 + z) * 24
                    both = jnp.concatenate([gwu[0, at : at + 24, :], gwu[1, at : at + 24, :]], 0)
                    gf[slab(t, c, z) + (rows,)] = both.astype(bf16)
        return carry

    lax.fori_loop(0, 2, block, 0)
    start(cross(0) + cross(1))
    result[...] = acc[...]
    middle = tokens[...].astype(f32)
    for t in range(GROUP):
        middle = middle + dot_nn(joined[t], wo[t])
    unit, scale = centre_rows(middle)
    gn = gn2[...]
    gg2[...] = jnp.sum((gn * unit).reshape(-1, 8, width), axis=0)
    gu = gn * g2
    back = scale * (
        gu - jnp.mean(gu, axis=-1, keepdims=True) - unit * jnp.mean(gu * unit, axis=-1, keepdims=True)
    )
    gm = gout[...] + back
    gmid[...] = gm
    ga = gm.astype(bf16)
    for t in range(GROUP):
        gj[t] = dot_nt(ga, wo[t]).astype(bf16)
    for k in range(3):
        start(out_g(k))
    mine = local(gj.at[me], gmix.at[3], own)
    mine.start()
    for t in range(GROUP):
        gwo = dot_tn(joined[t], ga)
        for c in range(2):
            for z in range(4):
                at = (c * 4 + z) * 24
                padded = jnp.concatenate([gwo[at : at + 24, :], jnp.zeros((8, width), f32)], 0)
                gf[slab(t, c, z) + (slice(96, 128),)] = padded.astype(bf16)
    start(cross(2))
    for k in range(3):
        wait(cross(k))

        def fold(i, carry):
            for j in range(2):
                for z in range(4):
                    spot = (i, j, z, parts[k])
                    half[spot] = (gf[(core,) + spot].astype(f32) + more[spot].astype(f32)).astype(bf16)
            return carry

        lax.fori_loop(0, 2, fold, 0)
    for k in range(3):
        wait(out_g(k))
    mine.wait()


def ffn_call(lf, joined, tokens, small, gout):
    slots, width = tokens.shape
    return pl.pallas_call(
        ffn_kernel,
        out_shape=(
            shape_of((slots, width), f32),
            shape_of((slots, width), f32),
            shape_of(joined.shape, bf16),
            shape_of(lf.shape[1:], bf16),
            shape_of((8, width), f32),
        ),
        in_specs=[FULL] * 5,
        out_specs=(FULL, FULL, ANY, FULL, FULL),
        scratch_shapes=[
            pltpu.VMEM(lf.shape, bf16),
            pltpu.VMEM(joined.shape, bf16),
            pltpu.VMEM(lf.shape[1:], bf16),
            pltpu.VMEM((2, width, width), bf16),
            pltpu.VMEM((GROUP, 256, width), bf16),
            pltpu.VMEM((slots, width), bf16),
            pltpu.VMEM((slots, width), f32),
            pltpu.VMEM((slots, width), f32),
            pltpu.VMEM((2, width, width), f32),
            DMA,
            DMA((3,)),
            DMA((3,)),
            DMA((3,)),
            DMA((3,)),
        ],
        compiler_params=pltpu.CompilerParams(collective_id=2, has_side_effects=True, vmem_limit_bytes=VMEM_LIMIT),
    )(lf, joined, tokens, small, gout)


def back_kernel(
    wf, ws, wv, normed, values, hid, slope, prob, gmix, gg2, half, tokens, gmid, small, out_f, out_a, out_s, gtok,
    awf, aws, ab1, ab2, gn, gv, awv, ag1, ga, gs, gnb, nb, fs, fb2, fb3, fb4, cb1, cb2, sb1, sb2,
    own, s1, r1, s2, r2, s3, r3, sn, rn, sf, rf, sv, rv,
):
    h, r = pl.program_id(0), pl.program_id(1)
    width = wf.shape[-1]
    heads = ga.shape[0]
    t, c, z = place()
    sibling = (t, 1 - c, z)
    tps, zs = group_peers(), line_peers()
    slow, fast, slow_dev, fast_dev = square()

    a1 = lambda i: [remote(ga.at[i, 1 - c], cb1.at[i], s1.at[i], r1.at[i], sibling)]
    a2 = lambda i: [
        remote(ga.at[i, c, p], cb2.at[i, k], s2.at[i, k], r2.at[i, k], (t, c, p)) for k, p in enumerate(zs)
    ]
    a3 = lambda i: [
        remote(ga.at[i, c, z, p], out_a.at[i, t], s3.at[i, k], r3.at[i, k], (p, c, z)) for k, p in enumerate(tps)
    ]
    mine = lambda i: [local(ga.at[i, c, z, t], out_a.at[i, t], own.at[i])]
    mine_f = lambda: [local(half.at[slow], fs, own.at[heads])]
    v1 = lambda: [remote(gs.at[1 - c], sb1, sv.at[0], rv.at[0], sibling)]
    v2 = lambda: [remote(gs.at[c, p], sb2.at[k], sv.at[1 + k], rv.at[1 + k], (t, c, p)) for k, p in enumerate(zs)]
    f2 = lambda: [remote(half.at[1 - slow], fb2, sf.at[0], rf.at[0], slow_dev)]
    f3 = lambda: [remote(fs.at[1 - fast], fb3, sf.at[1], rf.at[1], fast_dev)]
    f4 = lambda: [
        remote(fs.at[fast, p], fb4.at[k], sf.at[2 + k], rf.at[2 + k], (t, c, p)) for k, p in enumerate(zs)
    ]
    out_n = lambda k: [remote(gnb.at[k], nb.at[k], sn.at[k], rn.at[k], (tps[k], c, z))]

    def at_step(i, j):
        return pl.when((h == i) & (r == j))

    def meet(i):
        wait(a1(i))

        def line(k, carry):
            for j in range(GROUP):
                ga[i, c, k, j] = (ga[i, c, k, j].astype(f32) + cb1[i, k, j].astype(f32)).astype(bf16)
            return carry

        lax.fori_loop(0, 4, line, 0)
        start(a2(i))

    def deal(i):
        wait(a2(i))

        def fold(j, carry):
            total = ga[i, c, z, j].astype(f32)
            for k in range(3):
                total = total + cb2[i, k, j].astype(f32)
            ga[i, c, z, j] = total.astype(bf16)
            return carry

        lax.fori_loop(0, GROUP, fold, 0)
        start(mine(i) + a3(i))

    def add_slabs(total, more):
        def one(k, carry):
            fs[total, k] = (fs[total, k].astype(f32) + more[k].astype(f32)).astype(bf16)
            return carry

        lax.fori_loop(0, 4, one, 0)

    @at_step(0, 0)
    def _():
        greet([(p, c, z) for p in tps] + [(t, c, p) for p in zs] + [sibling])
        start(f2() + mine_f())

    @at_step(1, 0)
    def _():
        meet(0)

    @at_step(1, 3)
    def _():
        wait(f2() + mine_f())
        add_slabs(1 - fast, fb2.at[1 - fast])
        start(f3())
        add_slabs(fast, fb2.at[fast])

    @at_step(2, 0)
    def _():
        meet(1)

    @at_step(2, 3)
    def _():
        wait(f3())
        add_slabs(fast, fb3)
        start(f4())

    @pl.when(r == 0)
    def _():
        awf[...] = jnp.zeros_like(awf)
        aws[...] = jnp.zeros_like(aws)
        ab1[...] = jnp.zeros_like(ab1)
        ab2[h] = jnp.zeros(ab2.shape[1:], f32)

    tile = pl.ds(pl.multiple_of((h // 2) * 128, 128), 128)
    lane = lax.broadcasted_iota(jnp.int32, (512, 128), 1)
    gm = jnp.where(lane // 64 == h % 2, gmix[0, :, tile].astype(f32), 0.0).astype(bf16)
    gw = dot_nt(gm, values[0, :, tile])
    p = prob[0, 0]
    p32 = p.astype(f32)
    gl = (p32 * (gw - jnp.sum(p32 * gw, axis=-1, keepdims=True))).astype(bf16)
    ab2[h] += jnp.sum(gl.astype(f32).reshape(-1, 8, 512), axis=0)
    gvh = dot_tn(p, gm)

    @pl.when(h != 1)
    def _():
        gv[r, :, tile] = gvh

    @pl.when(h == 1)
    def _():
        gv[r, :, tile] += gvh

    aws[...] += dot_tn(hid[0, 0], gl)
    gb = (dot_nt(gl, ws[0]) * slope[0, 0].astype(f32)).astype(bf16)
    ab1[...] += jnp.sum(gb.astype(f32).reshape(-1, 8, width), axis=0)
    awf[...] += dot_tn(normed[0], gb)
    part = dot_nt(gb, wf[0])

    @pl.when(h == 0)
    def _():
        gn[r] = part

    @pl.when(h == 1)
    def _():
        gn[r] += part

    @pl.when(h == 2)
    def _():
        gvb = gv[r].astype(bf16)
        total = gn[r] + part + dot_nt(gvb, wv[...])
        gn[r] = total
        both = (total * normed[0].astype(f32)).reshape(-1, 8, width)
        ag1[...] = jnp.where(r == 0, 0.0, ag1[...]) + jnp.sum(both, axis=0)
        more = dot_tn(normed[0], gvb)

        @pl.when(r == 0)
        def _():
            awv[...] = more

        @pl.when(r != 0)
        def _():
            awv[...] += more

        for k in range(3):

            @pl.when(r == k)
            def _():
                gnb[k] = total.astype(bf16)
                start(out_n(k))

    @pl.when(r == GROUP - 1)
    def _():
        last = h == 2
        row = lax.broadcasted_iota(jnp.int32, (128, width), 0)
        stack = jnp.where(row == 64, jnp.sum(ab1[...], axis=0, keepdims=True), 0.0)
        gains = jnp.sum(ag1[...], axis=0, keepdims=True) / small[3:4]
        stack = jnp.where(last & (row == 65), gains, stack)
        stack = jnp.where(last & (row == 66), jnp.sum(gg2[...], axis=0, keepdims=True), stack)
        cols = stack.T
        lane = lax.broadcasted_iota(jnp.int32, (width, 128), 1)

        @pl.when(jnp.logical_not(last))
        def _():
            awv[:, 0:128] = jnp.zeros((width, 128), f32)
            awv[:, 128:256] = cols

        @pl.when(last)
        def _():
            awv[:, 128:256] = jnp.where(lane < 64, awv[:, 128:256], cols)

        def pack(i, carry):
            for cc in range(2):
                for zz in range(4):
                    at = pl.ds(pl.multiple_of((i * 8 + cc * 4 + zz) * 24, 8), 24)
                    low = jnp.concatenate([aws[at, :], awv[at, :]], 1)
                    ga[h, cc, zz, i] = jnp.concatenate([awf[at, :], low], 0).astype(bf16)
            return carry

        lax.fori_loop(0, GROUP, pack, 0)

    for i in range(heads):

        @at_step(i, 3)
        def _():
            start(a1(i))

    @at_step(2, 3)
    def _():
        flat = jnp.concatenate([jnp.sum(ab2[k], axis=0, keepdims=True) for k in range(3)], 1)
        flat = jnp.broadcast_to(flat, (8, 1536))
        for cc in range(2):
            for zz in range(4):
                s = (cc * 4 + zz) * 192
                gs[cc, zz] = (pltpu.roll(flat, 1536 - s, 1) if s else flat)[:, 0:256]
        start(v1())
        meet(2)
        wait(v1())
        gs[c] += sb1[...]
        start(v2())
        deal(0)
        for k in range(3):
            wait(out_n(k))

        def ln_back(i, carry):
            at = pl.ds(pl.multiple_of(i * 128, 128), 128)
            g = gn[3, at, :] + nb[0, at, :].astype(f32) + nb[1, at, :].astype(f32) + nb[2, at, :].astype(f32)
            unit, scale = centre_rows(tokens[at, :].astype(f32))
            gu = g * small[3:4]
            back = scale * (
                gu - jnp.mean(gu, axis=-1, keepdims=True) - unit * jnp.mean(gu * unit, axis=-1, keepdims=True)
            )
            gtok[at, :] = gmid[at, :] + back
            return carry

        lax.fori_loop(0, 4, ln_back, 0)
        deal(1)
        wait(f4())
        total = fs[fast, z].astype(f32)
        for k in range(3):
            total = total + fb4[k].astype(f32)
        out_f[...] = total
        wait(v2())
        out_s[...] = gs[c, z] + sb2[0] + sb2[1] + sb2[2]
        deal(2)
        for i in range(heads):
            wait(mine(i) + a3(i))


def back_call(wf, ws, wv, normed, values, hid, slope, prob, gmix, gg2, half, tokens, gmid, small):
    heads, width, slots = ws.shape
    rows = half.shape[-2]
    by_head = lambda h, r: (h, 0, 0)
    row = lambda h, r: (r, 0, 0)
    both = lambda h, r: (h, r, 0, 0)
    flat = lambda h, r: (0, 0)
    return pl.pallas_call(
        back_kernel,
        grid=(heads, GROUP),
        out_shape=(
            shape_of((rows, width), f32),
            shape_of((heads, GROUP, 48, width), bf16),
            shape_of((8, 256), f32),
            shape_of(tokens.shape, f32),
        ),
        in_specs=[
            pl.BlockSpec((1, width, width), by_head),
            pl.BlockSpec((1, width, slots), by_head),
            pl.BlockSpec((width, 256), flat),
            pl.BlockSpec((1, slots, width), row),
            pl.BlockSpec((1, slots, 256), row),
            pl.BlockSpec((1, 1, slots, width), both),
            pl.BlockSpec((1, 1, slots, width), both),
            pl.BlockSpec((1, 1, slots, slots), both),
            pl.BlockSpec((1, slots, 256), row),
            pl.BlockSpec((8, width), flat),
            ANY,
            FULL,
            FULL,
            pl.BlockSpec((8, width), flat),
        ],
        out_specs=(FULL, ANY, FULL, FULL),
        scratch_shapes=[
            pltpu.VMEM((width, width), f32),
            pltpu.VMEM((width, slots), f32),
            pltpu.VMEM((8, width), f32),
            pltpu.VMEM((heads, 8, slots), f32),
            pltpu.VMEM((GROUP, slots, width), f32),
            pltpu.VMEM((GROUP, slots, 256), f32),
            pltpu.VMEM((width, 256), f32),
            pltpu.VMEM((8, width), f32),
            pltpu.VMEM((heads, 2, 4, GROUP, 48, width), bf16),
            pltpu.VMEM((2, 4, 8, 256), f32),
            pltpu.VMEM((3, slots, width), bf16),
            pltpu.VMEM((3, slots, width), bf16),
            pltpu.VMEM((2, 4, rows, width), bf16),
            pltpu.VMEM((2, 4, rows, width), bf16),
            pltpu.VMEM((4, rows, width), bf16),
            pltpu.VMEM((3, rows, width), bf16),
            pltpu.VMEM((heads, 4, GROUP, 48, width), bf16),
            pltpu.VMEM((heads, 3, GROUP, 48, width), bf16),
            pltpu.VMEM((4, 8, 256), f32),
            pltpu.VMEM((3, 8, 256), f32),
            DMA((heads + 1,)),
            DMA((heads,)),
            DMA((heads,)),
            DMA((heads, 3)),
            DMA((heads, 3)),
            DMA((heads, 3)),
            DMA((heads, 3)),
            DMA((3,)),
            DMA((3,)),
            DMA((5,)),
            DMA((5,)),
            DMA((4,)),
            DMA((4,)),
        ],
        compiler_params=pltpu.CompilerParams(collective_id=3, has_side_effects=True, vmem_limit_bytes=VMEM_LIMIT),
    )(wf, ws, wv, normed, values, hid, slope, prob, gmix, gg2, half, tokens, gmid, small)


def pack_inputs(tokens, lengths, gain_one, w_value, w_first, b_first, w_second, b_second, w_out, gain_two, w_up, w_down):
    _, slots, width = tokens.shape
    heads_all, depth, _ = w_first.shape
    heads = heads_all // GROUP
    split = lambda v: v.reshape((GROUP, heads) + v.shape[1:])
    cols = jnp.concatenate(
        [
            b_first.reshape(GROUP, heads, depth).transpose(0, 2, 1),
            jnp.broadcast_to(jnp.stack([gain_one, gain_two], 1), (GROUP, depth, 2)),
            jnp.broadcast_to(b_second.reshape(depth, 8), (GROUP, depth, 8)),
            jnp.zeros((GROUP, depth, 51), bf16),
        ],
        2,
    )
    head_zero = jnp.concatenate([w_value.reshape(depth, GROUP, -1).transpose(1, 0, 2), cols], 2)
    extra = jnp.pad(head_zero[:, None], ((0, 0), (0, heads - 1), (0, 0), (0, 0)))
    low = jnp.concatenate([split(w_second), extra], 3)
    pa = jnp.concatenate([split(w_first), low], 2)
    spot = lax.broadcasted_iota(jnp.int32, (16, width), 1)
    mask = jnp.where(spot < lengths[0], 0.0, -1e30).astype(bf16)
    pt = jnp.concatenate([tokens[0], mask], 0)
    ups = [w_up[:, k * width : (k + 1) * width] for k in range(w_up.shape[1] // width)]
    pf = jnp.concatenate(ups + [w_out, jnp.zeros((8, width), bf16), w_down], 0)
    return pa, pt, pf


def on_device_fast(tokens, lengths, gain_one, w_value, w_first, b_first, w_second, b_second, w_out, gain_two, w_up, w_down, grad_out):
    _, slots, width = tokens.shape
    heads_all, depth, _ = w_first.shape
    heads = heads_all // GROUP
    pa, pt, pf = pack_inputs(
        tokens, lengths, gain_one, w_value, w_first, b_first, w_second, b_second, w_out, gain_two, w_up, w_down
    )
    wf, ws, wv, small, normed, values, hid, slope, prob, joined, lf = attend_call(pa, pt, pf)
    result, gmid, gmix, half, gg2 = ffn_call(lf, joined, tokens[0], small, grad_out[0])
    out_f, out_a, out_s, gtok = back_call(
        wf, ws, wv, normed, values, hid, slope, prob, gmix, gg2, half, tokens[0], gmid, small
    )
    low = out_a[:, :, 24:].astype(f32)
    to_all = lambda v: v.transpose((1, 0) + tuple(range(2, v.ndim))).reshape((heads_all,) + v.shape[2:])
    gb1 = to_all(low[:, :, :, 704])
    gains = jnp.sum(low[2, :, :, 705:707], axis=0)
    return (
        result[None],
        gtok[None],
        gains[:, 0],
        low[2, :, :, 512:704].transpose(1, 0, 2).reshape(depth, width),
        to_all(out_a[:, :, :24].astype(f32)),
        gb1,
        to_all(low[:, :, :, :512]),
        out_s[0, : b_second.shape[0]],
        out_f[4 * depth : 5 * depth],
        gains[:, 1],
        out_f[: 4 * depth].reshape(4, depth, width).transpose(1, 0, 2).reshape(depth, 4 * width),
        out_f[128:],
    )


def solution(mesh):
    wide, narrow = mesh.shape["wide"], mesh.shape["narrow"]
    grouped = Mesh(mesh.devices.reshape(GROUP, wide // GROUP, narrow), ALL)
    vec = P(ALL)
    flat = P(ALL, None)
    mid = P(None, ALL, None)
    row = P(ALL, None, None)
    body = on_device_fast if (wide, narrow) == (8, 4) else on_device
    return jax.shard_map(
        body,
        mesh=grouped,
        in_specs=(row, vec, vec, flat, mid, P(None, ALL), mid, vec, flat, vec, flat, flat, row),
        out_specs=(row, row, vec, flat, mid, P(None, ALL), mid, vec, flat, vec, flat, flat),
        check_vma=False,
    )
```

```python
import jax
import jax.numpy as jnp
from jax import lax
from jax.experimental import pallas as pl
from jax.experimental.pallas import tpu as pltpu
from jax.sharding import Mesh
from jax.sharding import PartitionSpec as P

epsilon = 1e-05
f32 = jnp.float32
bf16 = jnp.bfloat16
GROUP = 4


def norm_rows(values, factor):
    average = jnp.mean(values, axis=-1, keepdims=True)
    centred = values - average
    spread = jnp.mean(centred * centred, axis=-1, keepdims=True)
    return centred * lax.rsqrt(spread + epsilon) * factor


def smooth(values):
    return jax.nn.gelu(values, approximate=False)


def mm(spec, a, b):
    return jnp.einsum(spec, a, b, preferred_element_type=f32)


REST = ("rep", "narrow")
ALL = ("tp", "rep", "narrow")


def to_heads(shard):
    heads, depth, width = shard.shape
    pieces = lax.all_to_all(shard.reshape(GROUP, heads // GROUP, depth, width), "tp", 0, 0)
    whole = lax.all_gather(pieces, REST, axis=0)
    return whole.transpose(2, 1, 0, 3, 4).reshape(heads // GROUP, -1, width)


def from_heads(grad):
    heads, depth, width = grad.shape
    n = lax.axis_size("rep") * lax.axis_size("narrow")
    pieces = grad.astype(bf16).reshape(heads, GROUP, n, depth // (GROUP * n), width).transpose(2, 1, 0, 3, 4)
    pieces = pieces.reshape((n * GROUP,) + pieces.shape[2:])
    share = lax.psum_scatter(pieces, REST, scatter_dimension=0, tiled=True)
    share = lax.all_to_all(share, "tp", 0, 0)
    return share.reshape(heads * GROUP, depth // (GROUP * n), width).astype(f32)


def on_device(tokens, lengths, gain_one, w_value, w_first, b_first, w_second, b_second, w_out, gain_two, w_up, w_down, grad_out):
    row_count, slots, width = tokens.shape
    heads_all = w_first.shape[0]
    heads = heads_all // GROUP
    head_size = width // heads_all
    me = lax.axis_index("tp")
    depth = w_value.shape[0]

    small = [gain_one, gain_two, b_second, b_first.reshape(-1)]
    gathered = lax.all_gather(jnp.concatenate(small), ALL, axis=0)
    n_all = gathered.shape[0]
    g1 = gathered[:, :depth].reshape(-1).astype(f32)
    g2 = gathered[:, depth : 2 * depth].reshape(-1).astype(f32)
    b2_len = b_second.shape[0]
    b2 = gathered[:, 2 * depth : 2 * depth + b2_len].reshape(heads_all, slots).astype(f32)
    b1 = gathered[:, 2 * depth + b2_len :].reshape(n_all, heads_all, depth).transpose(1, 0, 2).reshape(heads_all, width).astype(f32)
    b1 = lax.dynamic_slice_in_dim(b1, me * heads, heads, 0)
    b2 = lax.dynamic_slice_in_dim(b2, me * heads, heads, 0)

    wf = to_heads(w_first)
    ws = to_heads(w_second)
    wv = to_heads(w_value.reshape(depth, GROUP, width // GROUP).transpose(1, 0, 2))[0]
    rows = lax.all_gather(tokens, "tp", axis=0, tiled=True)
    lens = lax.all_gather(lengths, "tp", axis=0, tiled=True)
    n_rows = rows.shape[0]

    normed = norm_rows(rows.astype(f32), g1).astype(bf16)
    values = mm("rsd,de->rse", normed, wv).astype(bf16)
    per_head = values.reshape(n_rows, slots, heads, head_size).transpose(2, 0, 1, 3)
    before = mm("rsd,hde->hrse", normed, wf) + b1[:, None, None, :]
    hidden = smooth(before).astype(bf16)
    logits = mm("hrse,hej->hrsj", hidden, ws) + b2[:, None, None, :]
    visible = lax.broadcasted_iota(jnp.int32, (1, n_rows, 1, slots), 3) < lens[None, :, None, None]
    masked = jnp.where(visible, logits, f32(-1e30))
    scaled = jnp.exp(masked - jnp.max(masked, axis=-1, keepdims=True))
    probabilities = scaled / jnp.sum(scaled, axis=-1, keepdims=True)
    weights = probabilities.astype(bf16)
    mixture = mm("hrsj,hrjc->rshc", weights, per_head).astype(bf16)
    mixture = mixture.reshape(GROUP, row_count, slots, heads * head_size)
    joined = lax.all_to_all(mixture, "tp", 0, 0).transpose(1, 2, 0, 3).reshape(row_count * slots, width)

    wo = lax.all_gather(w_out, ALL, axis=0, tiled=True)
    wu = lax.all_gather(w_up, ALL, axis=0, tiled=True)
    wd = lax.all_gather(w_down, ALL, axis=0, tiled=True)
    inputs = tokens.astype(f32).reshape(-1, width)
    middle = inputs + mm("sd,de->se", joined, wo)
    normed_two, norm_two_back = jax.vjp(norm_rows, middle, g2)
    normed_two = normed_two.astype(bf16)
    upward = mm("td,df->tf", normed_two, wu)
    active, smooth_up_back = jax.vjp(smooth, upward)
    active = active.astype(bf16)
    result = middle + mm("tf,fd->td", active, wd)

    g_out = grad_out.reshape(-1, width)
    grad_branch = g_out.astype(bf16)
    grad_w_down = mm("tf,td->fd", active, grad_branch)
    grad_upward = smooth_up_back(mm("td,fd->tf", grad_branch, wd))[0].astype(bf16)
    grad_w_up = mm("td,tf->df", normed_two, grad_upward)
    grad_middle_norm, grad_gain_two = norm_two_back(mm("tf,df->td", grad_upward, wu))
    grad_middle = g_out + grad_middle_norm
    grad_attn = grad_middle.astype(bf16)
    grad_w_out = mm("sd,se->de", joined, grad_attn)
    grad_joined = mm("se,de->sd", grad_attn, wo).astype(bf16)

    grad_mixture = grad_joined.reshape(row_count, slots, GROUP, heads * head_size).transpose(2, 0, 1, 3)
    grad_mixture = lax.all_to_all(grad_mixture, "tp", 0, 0).reshape(n_rows, slots, heads, head_size).transpose(2, 0, 1, 3)
    grad_weights = mm("hrsc,hrjc->hrsj", grad_mixture, per_head)
    grad_values = mm("hrsj,hrsc->rjhc", weights, grad_mixture).astype(bf16).reshape(n_rows, slots, heads * head_size)
    centre = jnp.sum(probabilities * grad_weights, axis=-1, keepdims=True)
    grad_logits = (probabilities * (grad_weights - centre)).astype(bf16)
    grad_b_second = jnp.sum(grad_logits.astype(f32), axis=(1, 2))
    grad_w_second = mm("hrse,hrsj->hej", hidden, grad_logits)
    grad_hidden = mm("hrsj,hej->hrse", grad_logits, ws)
    smooth_value, smooth_back = jax.vjp(smooth, before)
    grad_before = smooth_back(grad_hidden)[0].astype(bf16)
    grad_b_first = jnp.sum(grad_before.astype(f32), axis=(1, 2))
    grad_w_first = mm("rsd,hrse->hde", normed, grad_before)
    grad_w_value = mm("rsd,rse->de", normed, grad_values)
    grad_normed = mm("hrse,hde->rsd", grad_before, wf) + mm("rse,de->rsd", grad_values, wv)
    grad_normed = lax.psum_scatter(grad_normed.astype(bf16), "tp", scatter_dimension=0, tiled=True)
    value, norm_one_back = jax.vjp(norm_rows, inputs, g1)
    grad_inputs_norm, grad_gain_one = norm_one_back(grad_normed.astype(f32).reshape(-1, width))
    grad_tokens = grad_middle + grad_inputs_norm

    out_first = from_heads(grad_w_first)
    out_second = from_heads(grad_w_second)
    out_value = from_heads(grad_w_value[None]).transpose(1, 0, 2).reshape(depth, width)

    def share(grad):
        return lax.psum_scatter(grad.astype(bf16), ALL, scatter_dimension=0, tiled=True).astype(f32)

    vec_tp = jnp.concatenate([grad_b_first.reshape(-1), grad_b_second.reshape(-1)])
    vec_tp = lax.dynamic_update_slice_in_dim(jnp.zeros((GROUP, vec_tp.shape[0]), f32), vec_tp[None], me, 0)
    vec = jnp.concatenate([vec_tp.reshape(-1), grad_gain_one, grad_gain_two])
    vec = lax.psum(vec, ALL)
    index = (me * lax.axis_size("rep") + lax.axis_index("rep")) * lax.axis_size("narrow") + lax.axis_index("narrow")
    n_tp = GROUP * (heads * width + heads * slots)
    tp_part = vec[:n_tp].reshape(GROUP, -1)
    gb1 = tp_part[:, : heads * width].reshape(heads_all, width)
    gb2 = tp_part[:, heads * width :].reshape(-1)
    gb1 = lax.dynamic_slice_in_dim(gb1, index * depth, depth, 1)
    gb2 = lax.dynamic_slice_in_dim(gb2, index * b2_len, b2_len, 0)
    gg1 = lax.dynamic_slice_in_dim(vec[n_tp : n_tp + width], index * depth, depth, 0)
    gg2 = lax.dynamic_slice_in_dim(vec[n_tp + width :], index * depth, depth, 0)
    shape = tokens.shape
    return (
        result.reshape(shape),
        grad_tokens.reshape(shape),
        gg1,
        out_value,
        out_first,
        gb1,
        out_second,
        gb2,
        share(grad_w_out),
        gg2,
        share(grad_w_up),
        share(grad_w_down),
    )


MESH = pl.DeviceIdType.MESH
VMEM_LIMIT = 60 * 2**20
ANY = pl.BlockSpec(memory_space=pl.ANY)
FULL = pl.BlockSpec(memory_space=pltpu.VMEM)
DMA = pltpu.SemaphoreType.DMA


def shape_of(dims, kind):
    return jax.ShapeDtypeStruct(dims, kind)


def dot_nt(a, b):
    return lax.dot_general(a, b, (((1,), (1,)), ((), ())), preferred_element_type=f32)


def dot_tn(a, b):
    return lax.dot_general(a, b, (((0,), (0,)), ((), ())), preferred_element_type=f32)


def dot_nn(a, b):
    return lax.dot_general(a, b, (((1,), (0,)), ((), ())), preferred_element_type=f32)


def place():
    return lax.axis_index("tp"), lax.axis_index("rep"), lax.axis_index("narrow")


def group_peers():
    t, c, z = place()
    along_x = t + 1 - 2 * (t % 2)
    along_y = (t + 2) % GROUP
    return [along_x, along_y, GROUP - 1 - t]


def line_peers():
    z = lax.axis_index("narrow")
    return [(z + k) % 4 for k in (1, 2, 3)]


def line_place():
    z = lax.axis_index("narrow")
    side = z // 2
    end, inner = 3 * side, 1 + side
    return end, inner, 2 - side, 3 - 3 * side, end + inner - z, z == inner


class Spread:
    def __init__(self, slabs, send, recv):
        t, c, z = place()
        end, inner, other, far, near, is_inner = line_place()
        self.is_inner = is_inner
        move = lambda o, k, to: remote(slabs(o), slabs(o), send.at[k], recv.at[o], (t, c, to))
        self.own = lambda: [move(z, 0, other), move(z, 1, near)]
        self.on = lambda: [move(other, 2, end), move(far, 3, end)]
        self.near = lambda: move(near, 0, near)

    def begin(self):
        start(self.own())

    def forward(self):
        @pl.when(self.is_inner)
        def _():
            for copy in self.on():
                copy.wait_recv()
            start(self.on())

    def finish(self):
        self.near().wait_recv()

        @pl.when(jnp.logical_not(self.is_inner))
        def _():
            for copy in self.on():
                copy.wait_recv()

        for copy in self.own():
            copy.wait_send()

        @pl.when(self.is_inner)
        def _():
            for copy in self.on():
                copy.wait_send()


class Gather:
    def __init__(self, slabs, land, add, send, recv):
        t, c, z = place()
        end, inner, other, far, near, is_inner = line_place()
        self.is_inner, self.add, self.z = is_inner, add, z
        self.other, self.far = other, far
        move = lambda o, slot, k, to: remote(slabs(o), land(slot), send.at[k], recv.at[slot], (t, c, to))
        self.out = lambda: [move(far, 2, 0, inner), move(other, 1, 1, inner), move(inner, 0, 2, inner)]
        self.back = lambda: [move(end, 0, 2, end)]
        self.on_far = lambda: [move(far, 1, 0, far)]
        self.on_other = lambda: [move(other, 3, 1, other)]
        self.got = lambda slot: move(z, slot, 0, near).wait_recv()

    def begin(self):
        @pl.when(self.is_inner)
        def _():
            start(self.back())

        @pl.when(jnp.logical_not(self.is_inner))
        def _():
            start(self.out())

    def forward(self):
        @pl.when(self.is_inner)
        def _():
            self.got(2)
            self.add(self.far, 2)
            start(self.on_far())
            self.got(1)
            self.add(self.other, 1)
            start(self.on_other())

    def finish(self):
        self.got(0)
        self.add(self.z, 0)

        @pl.when(self.is_inner)
        def _():
            self.got(3)
            self.add(self.z, 3)
            for copy in self.back() + self.on_far() + self.on_other():
                copy.wait_send()

        @pl.when(jnp.logical_not(self.is_inner))
        def _():
            self.got(1)
            self.add(self.z, 1)
            for copy in self.out():
                copy.wait_send()


def greet(devices):
    barrier = pltpu.get_barrier_semaphore()
    for device in devices:
        pl.semaphore_signal(barrier, inc=1, device_id=device, device_id_type=MESH)
    pl.semaphore_wait(barrier, len(devices))


def remote(src, dst, send, recv, device):
    return pltpu.make_async_remote_copy(
        src_ref=src, dst_ref=dst, send_sem=send, recv_sem=recv, device_id=device, device_id_type=MESH
    )


def local(src, dst, sem):
    return pltpu.make_async_copy(src, dst, sem)


def start(copies):
    for copy in copies:
        copy.start()


def wait(copies):
    for copy in copies:
        copy.wait()


def square():
    t, c, z = place()
    y, x = t // 2, t % 2
    tps = group_peers()
    slow, fast = (1 - c) * y + c * x, (1 - c) * x + c * y
    fast_peer = (1 - c) * tps[0] + c * tps[1]
    slow_peer = (1 - c) * tps[1] + c * tps[0]
    return slow, fast, (slow_peer, c, z), (fast_peer, c, z)


def gelu_pair(v):
    cdf = 0.5 * (1.0 + lax.erf(v * 0.7071067811865476))
    return v * cdf, cdf + v * (jnp.exp(-0.5 * v * v) * 0.3989422804014327)


def centre_rows(v):
    shifted = v - jnp.mean(v, axis=-1, keepdims=True)
    scale = lax.rsqrt(jnp.mean(shifted * shifted, axis=-1, keepdims=True) + epsilon)
    return shifted * scale, scale


def attend_kernel(
    pa, pt, pf, wf, ws, wv, small, normed, values, hid, slope, prob, joined, lf,
    la, lt, nrm, val, cols, b2, join, own, s1, r1, s2, r2, s3, r3, st, rt, s1f, r1f, sf, rf, sj, rj,
):
    h, r = pl.program_id(0), pl.program_id(1)
    width = wf.shape[-1]
    heads = la.shape[0]
    t, c, z = place()
    sibling = (t, 1 - c, z)
    tps, zs = group_peers(), line_peers()
    slow, fast, slow_dev, fast_dev = square()

    a1 = lambda i: [
        remote(pa.at[p, i], la.at[i, c, z, t], s1.at[i, k], r1.at[i, k], (p, c, z)) for k, p in enumerate(tps)
    ]
    a2 = lambda i: Spread(lambda o: la.at[i, c, o], s2.at[i], r2.at[i])
    a3 = lambda i: [remote(la.at[i, c], la.at[i, c], s3.at[i], r3.at[i], sibling)]
    mine = lambda i: [local(pa.at[t, i], la.at[i, c, z, t], own.at[i])]
    mine_t = lambda: [local(pt, lt.at[3], own.at[heads])]
    mine_f = lambda: [local(pf, lf.at[c, slow, fast, z], own.at[heads + 1])]
    mine_j = lambda: [local(join.at[3], joined.at[t], own.at[heads + 2])]
    toks = lambda: [remote(pt, lt.at[k], st.at[k], rt.at[k], (p, c, z)) for k, p in enumerate(tps)]
    f1 = lambda: Spread(lambda o: lf.at[c, slow, fast, o], s1f, r1f)
    f2 = lambda: [remote(lf.at[c, slow, fast], lf.at[c, slow, fast], sf.at[0], rf.at[0], fast_dev)]
    f3 = lambda: [remote(lf.at[c, slow], lf.at[c, slow], sf.at[1], rf.at[1], slow_dev)]
    f4 = lambda: [remote(lf.at[c, slow], lf.at[c, slow], sf.at[2], rf.at[2], sibling)]
    f5 = lambda: [remote(lf.at[c, 1 - slow], lf.at[c, 1 - slow], sf.at[3], rf.at[3], sibling)]
    out_j = lambda k: [remote(join.at[k], joined.at[t], sj.at[k], rj.at[k], (tps[k], c, z))]

    def at_step(i, j):
        return pl.when((h == i) & (r == j))

    @at_step(0, 0)
    def _():
        greet([(p, c, z) for p in tps] + [(t, c, p) for p in zs] + [sibling])
        start(mine_f())
        for i in range(heads):
            start(mine(i) + a1(i))
        start(mine_t())
        wait(mine_f())
        f1().begin()
        start(toks())
        for i in range(heads):
            wait(mine(i) + a1(i))
        a2(0).begin()
        f1().forward()
        a2(1).begin()
        f1().finish()
        start(f2())
        a2(0).forward()
        a2(0).finish()
        start(a3(0))
        a2(1).forward()
        a2(2).begin()
        wait(mine_t() + toks() + a3(0))

    @at_step(1, 0)
    def _():
        a2(1).finish()
        start(a3(1))
        a2(2).forward()
        wait(a3(1))

    @at_step(1, 1)
    def _():
        wait(f2())
        start(f3() + f4())

    @at_step(2, 0)
    def _():
        a2(2).finish()
        start(a3(2))
        wait(a3(2))

    @pl.when(r == 0)
    def _():
        def unpack(i, carry):
            for cc in range(2):
                for zz in range(0, 4, 2):
                    tops, lows = [], []
                    for k in range(2):
                        tops.append(la[h, cc, zz + k, i, 0:32, :].astype(f32)[0:24])
                        lows.append(la[h, cc, zz + k, i, 16:48, :].astype(f32)[8:32])
                    top, low = jnp.concatenate(tops, 0), jnp.concatenate(lows, 0)
                    at = pl.ds(pl.multiple_of((i * 8 + cc * 4 + zz) * 24, 48), 48)
                    wf[0, at, :] = top.astype(bf16)
                    ws[0, at, :] = low[:, :512].astype(bf16)

                    @pl.when(h == 0)
                    def _():
                        last = low[:, 640:768]
                        cols[at, :] = last
                        lane = lax.broadcasted_iota(jnp.int32, last.shape, 1)
                        wv[at, 0:128] = low[:, 512:640].astype(bf16)
                        wv[at, 128:256] = jnp.where(lane < 64, last, 0.0).astype(bf16)

            return carry

        lax.fori_loop(0, GROUP, unpack, 0)

        @pl.when(h == 0)
        def _():
            small[...] = cols[...].T[64:72]
            mine_rows = cols[pl.ds(pl.multiple_of(t * 192, 192), 192), :].astype(bf16)
            lane = lax.broadcasted_iota(jnp.int32, (128, 512), 0)
            spot = lax.broadcasted_iota(jnp.int32, (128, 512), 1)
            spread = dot_nn(mine_rows, jnp.where(lane - 69 == spot % 8, 1.0, 0.0).astype(bf16))
            row = lax.broadcasted_iota(jnp.int32, (64, 512), 0)
            spot = lax.broadcasted_iota(jnp.int32, (64, 512), 1)
            for i in range(heads):
                picked = jnp.where(row == spot // 8, spread[64 * i : 64 * i + 64], 0.0)
                b2[i] = jnp.broadcast_to(jnp.sum(picked, axis=0, keepdims=True), (8, 512))

    @pl.when(h == 0)
    def _():
        unit, _ = centre_rows(lt[r, 0:512, :].astype(f32))
        out = (unit * small[3:4]).astype(bf16)
        nrm[r] = out
        normed[0] = out
        v = dot_nn(out, wv[...]).astype(bf16)
        val[r] = v
        values[0] = v

    mask = lt[r, 512:528, 0:512].astype(f32)[0:1]
    row = lax.broadcasted_iota(jnp.int32, (8, width), 0)
    b1 = jnp.sum(jnp.where(row == h, small[...], 0.0), axis=0, keepdims=True)
    shift = b2[h, 0:1] + mask
    tile = pl.ds(pl.multiple_of((h // 2) * 128, 128), 128)
    step = 256
    for m in range(0, 512, step):
        at = slice(m, m + step)
        before = dot_nn(nrm[r, at, :], wf[0]) + b1
        out, grad = gelu_pair(before)
        hidden = out.astype(bf16)
        hid[0, 0, at, :] = hidden
        slope[0, 0, at, :] = grad.astype(bf16)
        logits = dot_nn(hidden, ws[0]) + shift
        e = jnp.exp(logits - jnp.max(logits, axis=-1, keepdims=True))
        p = (e / jnp.sum(e, axis=-1, keepdims=True)).astype(bf16)
        prob[0, 0, at, :] = p
        mix = dot_nn(p, val[r, :, tile])
        lane = lax.broadcasted_iota(jnp.int32, mix.shape, 1)
        old = join[r, at, tile].astype(f32)
        join[r, at, tile] = jnp.where((h == 1) & (lane < 64), old, mix).astype(bf16)

    for k in range(3):

        @at_step(2, k)
        def _():
            start(out_j(k))

    @at_step(2, 2)
    def _():
        wait(f3())
        start(f5())

    @at_step(2, 3)
    def _():
        start(mine_j())
        for k in range(3):
            wait(out_j(k))
        wait(mine_j() + f4() + f5())


def attend_call(pa, pt, pf):
    heads, width = pa.shape[1], pa.shape[-1]
    slots = 512
    by_row = lambda h, r: (jnp.where(h == 0, r, GROUP - 1), 0, 0)
    by_head = lambda h, r: (h, 0, 0)
    both = lambda h, r: (h, r, 0, 0)
    return pl.pallas_call(
        attend_kernel,
        grid=(heads, GROUP),
        out_shape=(
            shape_of((heads, width, width), bf16),
            shape_of((heads, width, slots), bf16),
            shape_of((width, 256), bf16),
            shape_of((8, width), f32),
            shape_of((GROUP, slots, width), bf16),
            shape_of((GROUP, slots, 256), bf16),
            shape_of((heads, GROUP, slots, width), bf16),
            shape_of((heads, GROUP, slots, width), bf16),
            shape_of((heads, GROUP, slots, slots), bf16),
            shape_of((GROUP, slots, 256), bf16),
            shape_of((2, 2, 2, 4) + pf.shape, bf16),
        ),
        in_specs=[ANY] * 3,
        out_specs=(
            pl.BlockSpec((1, width, width), by_head),
            pl.BlockSpec((1, width, slots), by_head),
            pl.BlockSpec((width, 256), lambda h, r: (0, 0)),
            pl.BlockSpec((8, width), lambda h, r: (0, 0)),
            pl.BlockSpec((1, slots, width), by_row),
            pl.BlockSpec((1, slots, 256), by_row),
            pl.BlockSpec((1, 1, slots, width), both),
            pl.BlockSpec((1, 1, slots, width), both),
            pl.BlockSpec((1, 1, slots, slots), both),
            ANY,
            ANY,
        ),
        scratch_shapes=[
            pltpu.VMEM((heads, 2, 4, GROUP) + pa.shape[2:], bf16),
            pltpu.VMEM((GROUP,) + pt.shape, bf16),
            pltpu.VMEM((GROUP, slots, width), bf16),
            pltpu.VMEM((GROUP, slots, 256), bf16),
            pltpu.VMEM((width, 128), f32),
            pltpu.VMEM((heads, 8, slots), f32),
            pltpu.VMEM((GROUP, slots, 256), bf16),
            DMA((heads + 3,)),
            DMA((heads, 3)),
            DMA((heads, 3)),
            DMA((heads, 4)),
            DMA((heads, 4)),
            DMA((heads,)),
            DMA((heads,)),
            DMA((3,)),
            DMA((3,)),
            DMA((4,)),
            DMA((4,)),
            DMA((4,)),
            DMA((4,)),
            DMA((3,)),
            DMA((3,)),
        ],
        compiler_params=pltpu.CompilerParams(collective_id=1, has_side_effects=True, vmem_limit_bytes=VMEM_LIMIT),
    )(pa, pt, pf)


def slab(t, c, z):
    y, x = t // 2, t % 2
    return (0, y, x, z) if c == 0 else (1, x, y, z)


def ffn_kernel(
    lf, joined, tokens, small, gout, result, gmid, gmix, half, gg2,
    gf, gj, more, wu, wo, n2, acc, gn2, gwu, own, sg, rg, sx, rx,
):
    width = tokens.shape[-1]
    me, core, z_me = place()
    tps = group_peers()
    sibling = (me, 1 - core, z_me)
    parts = (slice(0, 96), slice(128, 224), slice(96, 128))
    cross = lambda k: [
        remote(
            gf.at[1 - core, :, :, :, parts[k], :], more.at[:, :, :, parts[k], :], sx.at[k], rx.at[k], sibling
        )
    ]
    out_g = lambda k: [remote(gj.at[tps[k]], gmix.at[k], sg.at[k], rg.at[k], (tps[k], core, z_me))]
    greet([(p, core, z_me) for p in tps] + [sibling])
    wo[...] = jnp.zeros_like(wo)
    for t in range(GROUP):
        for c in range(2):
            for z in range(0, 4, 2):
                pair = [lf[slab(t, c, z + k)][96:128].astype(f32)[0:24] for k in range(2)]
                wo[t, (c * 4 + z) * 24 : (c * 4 + z) * 24 + 48, :] = jnp.concatenate(pair, 0).astype(bf16)
    middle = tokens[...].astype(f32)
    for t in range(GROUP):
        middle = middle + dot_nn(joined[t], wo[t])
    acc[...] = middle
    g2 = small[4:5]
    unit, _ = centre_rows(middle)
    n2[...] = (unit * g2).astype(bf16)
    gn2[...] = jnp.zeros_like(gn2)

    def block(p, carry):
        rows = pl.ds(pl.multiple_of(p * 48, 16), 48)
        for t in range(GROUP):
            for c in range(2):
                for z in range(0, 4, 2):
                    ends = [lf[slab(t, c, z + k) + (rows,)].astype(f32) for k in range(2)]
                    at = (t * 8 + c * 4 + z) * 24
                    for k in range(2):
                        both = jnp.concatenate([e[24 * k : 24 * k + 24] for e in ends], 0)
                        wu[k, at : at + 48, :] = both.astype(bf16)
        branch = gout[...].astype(bf16)
        for k in range(2):
            wd = jnp.concatenate(
                [lf[0, p, k, :, 128:224, :].reshape(384, width), lf[1, k, p, :, 128:224, :].reshape(384, width)], 0
            )
            up = dot_nn(n2[...], wu[k])
            act, slope = gelu_pair(up)
            act = act.astype(bf16)
            acc[...] += dot_nn(act, wd)
            gup = (dot_nt(branch, wd) * slope).astype(bf16)
            gwd = dot_tn(act, branch).astype(bf16)
            gf[0, p, k, :, 128:224, :] = gwd[:384].reshape(4, 96, width)
            gf[1, k, p, :, 128:224, :] = gwd[384:].reshape(4, 96, width)
            gwu[k] = dot_tn(n2[...], gup)
            gn2[...] += dot_nt(gup, wu[k])
        for t in range(GROUP):
            for c in range(2):
                for z in range(4):
                    at = (t * 8 + c * 4 + z) * 24
                    both = jnp.concatenate([gwu[0, at : at + 24, :], gwu[1, at : at + 24, :]], 0)
                    gf[slab(t, c, z) + (rows,)] = both.astype(bf16)
        return carry

    lax.fori_loop(0, 2, block, 0)
    start(cross(0) + cross(1))
    result[...] = acc[...]
    middle = tokens[...].astype(f32)
    for t in range(GROUP):
        middle = middle + dot_nn(joined[t], wo[t])
    unit, scale = centre_rows(middle)
    gn = gn2[...]
    gg2[...] = jnp.sum((gn * unit).reshape(-1, 8, width), axis=0)
    gu = gn * g2
    back = scale * (
        gu - jnp.mean(gu, axis=-1, keepdims=True) - unit * jnp.mean(gu * unit, axis=-1, keepdims=True)
    )
    gm = gout[...] + back
    gmid[...] = gm
    ga = gm.astype(bf16)
    for t in range(GROUP):
        gj[t] = dot_nt(ga, wo[t]).astype(bf16)
    for k in range(3):
        start(out_g(k))
    mine = local(gj.at[me], gmix.at[3], own)
    mine.start()
    for t in range(GROUP):
        gwo = dot_tn(joined[t], ga)
        for c in range(2):
            for z in range(4):
                at = (c * 4 + z) * 24
                padded = jnp.concatenate([gwo[at : at + 24, :], jnp.zeros((8, width), f32)], 0)
                gf[slab(t, c, z) + (slice(96, 128),)] = padded.astype(bf16)
    start(cross(2))
    for k in range(3):
        wait(cross(k))

        def fold(i, carry):
            for j in range(2):
                for z in range(4):
                    spot = (i, j, z, parts[k])
                    half[spot] = (gf[(core,) + spot].astype(f32) + more[spot].astype(f32)).astype(bf16)
            return carry

        lax.fori_loop(0, 2, fold, 0)
    for k in range(3):
        wait(out_g(k))
    mine.wait()


def ffn_call(lf, joined, tokens, small, gout):
    slots, width = tokens.shape
    return pl.pallas_call(
        ffn_kernel,
        out_shape=(
            shape_of((slots, width), f32),
            shape_of((slots, width), f32),
            shape_of(joined.shape, bf16),
            shape_of(lf.shape[1:], bf16),
            shape_of((8, width), f32),
        ),
        in_specs=[FULL] * 5,
        out_specs=(FULL, FULL, ANY, FULL, FULL),
        scratch_shapes=[
            pltpu.VMEM(lf.shape, bf16),
            pltpu.VMEM(joined.shape, bf16),
            pltpu.VMEM(lf.shape[1:], bf16),
            pltpu.VMEM((2, width, width), bf16),
            pltpu.VMEM((GROUP, 256, width), bf16),
            pltpu.VMEM((slots, width), bf16),
            pltpu.VMEM((slots, width), f32),
            pltpu.VMEM((slots, width), f32),
            pltpu.VMEM((2, width, width), f32),
            DMA,
            DMA((3,)),
            DMA((3,)),
            DMA((3,)),
            DMA((3,)),
        ],
        compiler_params=pltpu.CompilerParams(collective_id=2, has_side_effects=True, vmem_limit_bytes=VMEM_LIMIT),
    )(lf, joined, tokens, small, gout)


def back_kernel(
    wf, ws, wv, normed, values, hid, slope, prob, gmix, gg2, half, tokens, gmid, small, out_f, out_a, out_s, gtok,
    awf, aws, ab1, ab2, gn, gv, awv, ag1, ga, gs, gnb, nb, fs, fb2, fb3, fb4, cb1, cb2, sb1, sb2,
    own, s1, r1, s2, r2, s3, r3, sn, rn, sf, rf, s4, r4, sv, rv,
):
    h, r = pl.program_id(0), pl.program_id(1)
    width = wf.shape[-1]
    heads = ga.shape[0]
    t, c, z = place()
    sibling = (t, 1 - c, z)
    tps, zs = group_peers(), line_peers()
    slow, fast, slow_dev, fast_dev = square()

    a1 = lambda i: [remote(ga.at[i, 1 - c], cb1.at[i], s1.at[i], r1.at[i], sibling)]
    def add_heads(i):
        def add(o, slot):
            def one(j, carry):
                ga[i, c, o, j] = (ga[i, c, o, j].astype(f32) + cb2[i, slot, j].astype(f32)).astype(bf16)
                return carry

            lax.fori_loop(0, GROUP, one, 0)

        return add

    def add_f(o, slot):
        fs[fast, o] = (fs[fast, o].astype(f32) + fb4[slot].astype(f32)).astype(bf16)

    a2 = lambda i: Gather(lambda o: ga.at[i, c, o], lambda k: cb2.at[i, k], add_heads(i), s2.at[i], r2.at[i])
    a3 = lambda i: [
        remote(ga.at[i, c, z, p], out_a.at[i, t], s3.at[i, k], r3.at[i, k], (p, c, z)) for k, p in enumerate(tps)
    ]
    mine = lambda i: [local(ga.at[i, c, z, t], out_a.at[i, t], own.at[i])]
    mine_f = lambda: [local(half.at[slow], fs, own.at[heads])]
    v1 = lambda: [remote(gs.at[1 - c], sb1, sv.at[0], rv.at[0], sibling)]
    v2 = lambda: [remote(gs.at[c, p], sb2.at[k], sv.at[1 + k], rv.at[1 + k], (t, c, p)) for k, p in enumerate(zs)]
    f2 = lambda: [remote(half.at[1 - slow], fb2, sf.at[0], rf.at[0], slow_dev)]
    f3 = lambda: [remote(fs.at[1 - fast], fb3, sf.at[1], rf.at[1], fast_dev)]
    f4 = lambda: Gather(lambda o: fs.at[fast, o], lambda k: fb4.at[k], add_f, s4, r4)
    out_n = lambda k: [remote(gnb.at[k], nb.at[k], sn.at[k], rn.at[k], (tps[k], c, z))]

    def at_step(i, j):
        return pl.when((h == i) & (r == j))

    def meet(i):
        wait(a1(i))

        def line(k, carry):
            for j in range(GROUP):
                ga[i, c, k, j] = (ga[i, c, k, j].astype(f32) + cb1[i, k, j].astype(f32)).astype(bf16)
            return carry

        lax.fori_loop(0, 4, line, 0)
        a2(i).begin()

    def deal(i):
        a2(i).finish()
        start(mine(i) + a3(i))

    def add_slabs(total, more):
        def one(k, carry):
            fs[total, k] = (fs[total, k].astype(f32) + more[k].astype(f32)).astype(bf16)
            return carry

        lax.fori_loop(0, 4, one, 0)

    @at_step(0, 0)
    def _():
        greet([(p, c, z) for p in tps] + [(t, c, p) for p in zs] + [sibling])
        start(f2() + mine_f())

    @at_step(1, 0)
    def _():
        meet(0)

    @at_step(1, 3)
    def _():
        wait(f2() + mine_f())
        add_slabs(1 - fast, fb2.at[1 - fast])
        start(f3())
        add_slabs(fast, fb2.at[fast])

    @at_step(1, 2)
    def _():
        a2(0).forward()

    @at_step(2, 0)
    def _():
        meet(1)

    @at_step(2, 1)
    def _():
        deal(0)

    @at_step(2, 2)
    def _():
        a2(1).forward()

    @at_step(2, 3)
    def _():
        wait(f3())
        add_slabs(fast, fb3)
        f4().begin()

    @pl.when(r == 0)
    def _():
        awf[...] = jnp.zeros_like(awf)
        aws[...] = jnp.zeros_like(aws)
        ab1[...] = jnp.zeros_like(ab1)
        ab2[h] = jnp.zeros(ab2.shape[1:], f32)

    tile = pl.ds(pl.multiple_of((h // 2) * 128, 128), 128)
    lane = lax.broadcasted_iota(jnp.int32, (512, 128), 1)
    gm = jnp.where(lane // 64 == h % 2, gmix[0, :, tile].astype(f32), 0.0).astype(bf16)
    gw = dot_nt(gm, values[0, :, tile])
    p = prob[0, 0]
    p32 = p.astype(f32)
    gl = (p32 * (gw - jnp.sum(p32 * gw, axis=-1, keepdims=True))).astype(bf16)
    ab2[h] += jnp.sum(gl.astype(f32).reshape(-1, 8, 512), axis=0)
    gvh = dot_tn(p, gm)

    @pl.when(h != 1)
    def _():
        gv[r, :, tile] = gvh

    @pl.when(h == 1)
    def _():
        gv[r, :, tile] += gvh

    aws[...] += dot_tn(hid[0, 0], gl)
    gb = (dot_nt(gl, ws[0]) * slope[0, 0].astype(f32)).astype(bf16)
    ab1[...] += jnp.sum(gb.astype(f32).reshape(-1, 8, width), axis=0)
    awf[...] += dot_tn(normed[0], gb)
    part = dot_nt(gb, wf[0])

    @pl.when(h == 0)
    def _():
        gn[r] = part

    @pl.when(h == 1)
    def _():
        gn[r] += part

    @pl.when(h == 2)
    def _():
        gvb = gv[r].astype(bf16)
        total = gn[r] + part + dot_nt(gvb, wv[...])
        gn[r] = total
        both = (total * normed[0].astype(f32)).reshape(-1, 8, width)
        ag1[...] = jnp.where(r == 0, 0.0, ag1[...]) + jnp.sum(both, axis=0)
        more = dot_tn(normed[0], gvb)

        @pl.when(r == 0)
        def _():
            awv[...] = more

        @pl.when(r != 0)
        def _():
            awv[...] += more

        for k in range(3):

            @pl.when(r == k)
            def _():
                gnb[k] = total.astype(bf16)
                start(out_n(k))

    @pl.when(r == GROUP - 1)
    def _():
        last = h == 2
        row = lax.broadcasted_iota(jnp.int32, (128, width), 0)
        stack = jnp.where(row == 64, jnp.sum(ab1[...], axis=0, keepdims=True), 0.0)
        gains = jnp.sum(ag1[...], axis=0, keepdims=True) / small[3:4]
        stack = jnp.where(last & (row == 65), gains, stack)
        stack = jnp.where(last & (row == 66), jnp.sum(gg2[...], axis=0, keepdims=True), stack)
        cols = stack.T
        lane = lax.broadcasted_iota(jnp.int32, (width, 128), 1)

        @pl.when(jnp.logical_not(last))
        def _():
            awv[:, 0:128] = jnp.zeros((width, 128), f32)
            awv[:, 128:256] = cols

        @pl.when(last)
        def _():
            awv[:, 128:256] = jnp.where(lane < 64, awv[:, 128:256], cols)

        def pack(i, carry):
            for cc in range(2):
                for zz in range(4):
                    at = pl.ds(pl.multiple_of((i * 8 + cc * 4 + zz) * 24, 8), 24)
                    low = jnp.concatenate([aws[at, :], awv[at, :]], 1)
                    ga[h, cc, zz, i] = jnp.concatenate([awf[at, :], low], 0).astype(bf16)
            return carry

        lax.fori_loop(0, GROUP, pack, 0)

    for i in range(heads):

        @at_step(i, 3)
        def _():
            start(a1(i))

    @at_step(2, 3)
    def _():
        flat = jnp.concatenate([jnp.sum(ab2[k], axis=0, keepdims=True) for k in range(3)], 1)
        flat = jnp.broadcast_to(flat, (8, 1536))
        for cc in range(2):
            for zz in range(4):
                s = (cc * 4 + zz) * 192
                gs[cc, zz] = (pltpu.roll(flat, 1536 - s, 1) if s else flat)[:, 0:256]
        start(v1())
        meet(2)
        wait(v1())
        gs[c] += sb1[...]
        start(v2())
        f4().forward()
        for k in range(3):
            wait(out_n(k))
        a2(2).forward()

        def ln_back(i, carry):
            at = pl.ds(pl.multiple_of(i * 128, 128), 128)
            g = gn[3, at, :] + nb[0, at, :].astype(f32) + nb[1, at, :].astype(f32) + nb[2, at, :].astype(f32)
            unit, scale = centre_rows(tokens[at, :].astype(f32))
            gu = g * small[3:4]
            back = scale * (
                gu - jnp.mean(gu, axis=-1, keepdims=True) - unit * jnp.mean(gu * unit, axis=-1, keepdims=True)
            )
            gtok[at, :] = gmid[at, :] + back
            return carry

        lax.fori_loop(0, 4, ln_back, 0)
        deal(1)
        f4().finish()
        out_f[...] = fs[fast, z].astype(f32)
        wait(v2())
        out_s[...] = gs[c, z] + sb2[0] + sb2[1] + sb2[2]
        deal(2)
        for i in range(heads):
            wait(mine(i) + a3(i))


def back_call(wf, ws, wv, normed, values, hid, slope, prob, gmix, gg2, half, tokens, gmid, small):
    heads, width, slots = ws.shape
    rows = half.shape[-2]
    by_head = lambda h, r: (h, 0, 0)
    row = lambda h, r: (r, 0, 0)
    both = lambda h, r: (h, r, 0, 0)
    flat = lambda h, r: (0, 0)
    return pl.pallas_call(
        back_kernel,
        grid=(heads, GROUP),
        out_shape=(
            shape_of((rows, width), f32),
            shape_of((heads, GROUP, 48, width), bf16),
            shape_of((8, 256), f32),
            shape_of(tokens.shape, f32),
        ),
        in_specs=[
            pl.BlockSpec((1, width, width), by_head),
            pl.BlockSpec((1, width, slots), by_head),
            pl.BlockSpec((width, 256), flat),
            pl.BlockSpec((1, slots, width), row),
            pl.BlockSpec((1, slots, 256), row),
            pl.BlockSpec((1, 1, slots, width), both),
            pl.BlockSpec((1, 1, slots, width), both),
            pl.BlockSpec((1, 1, slots, slots), both),
            pl.BlockSpec((1, slots, 256), row),
            pl.BlockSpec((8, width), flat),
            ANY,
            FULL,
            FULL,
            pl.BlockSpec((8, width), flat),
        ],
        out_specs=(FULL, ANY, FULL, FULL),
        scratch_shapes=[
            pltpu.VMEM((width, width), f32),
            pltpu.VMEM((width, slots), f32),
            pltpu.VMEM((8, width), f32),
            pltpu.VMEM((heads, 8, slots), f32),
            pltpu.VMEM((GROUP, slots, width), f32),
            pltpu.VMEM((GROUP, slots, 256), f32),
            pltpu.VMEM((width, 256), f32),
            pltpu.VMEM((8, width), f32),
            pltpu.VMEM((heads, 2, 4, GROUP, 48, width), bf16),
            pltpu.VMEM((2, 4, 8, 256), f32),
            pltpu.VMEM((3, slots, width), bf16),
            pltpu.VMEM((3, slots, width), bf16),
            pltpu.VMEM((2, 4, rows, width), bf16),
            pltpu.VMEM((2, 4, rows, width), bf16),
            pltpu.VMEM((4, rows, width), bf16),
            pltpu.VMEM((4, rows, width), bf16),
            pltpu.VMEM((heads, 4, GROUP, 48, width), bf16),
            pltpu.VMEM((heads, 4, GROUP, 48, width), bf16),
            pltpu.VMEM((4, 8, 256), f32),
            pltpu.VMEM((3, 8, 256), f32),
            DMA((heads + 1,)),
            DMA((heads,)),
            DMA((heads,)),
            DMA((heads, 3)),
            DMA((heads, 4)),
            DMA((heads, 3)),
            DMA((heads, 3)),
            DMA((3,)),
            DMA((3,)),
            DMA((2,)),
            DMA((2,)),
            DMA((3,)),
            DMA((4,)),
            DMA((4,)),
            DMA((4,)),
        ],
        compiler_params=pltpu.CompilerParams(collective_id=3, has_side_effects=True, vmem_limit_bytes=VMEM_LIMIT),
    )(wf, ws, wv, normed, values, hid, slope, prob, gmix, gg2, half, tokens, gmid, small)


def pack_inputs(tokens, lengths, gain_one, w_value, w_first, b_first, w_second, b_second, w_out, gain_two, w_up, w_down):
    _, slots, width = tokens.shape
    heads_all, depth, _ = w_first.shape
    heads = heads_all // GROUP
    split = lambda v: v.reshape((GROUP, heads) + v.shape[1:])
    cols = jnp.concatenate(
        [
            b_first.reshape(GROUP, heads, depth).transpose(0, 2, 1),
            jnp.broadcast_to(jnp.stack([gain_one, gain_two], 1), (GROUP, depth, 2)),
            jnp.broadcast_to(b_second.reshape(depth, 8), (GROUP, depth, 8)),
            jnp.zeros((GROUP, depth, 51), bf16),
        ],
        2,
    )
    head_zero = jnp.concatenate([w_value.reshape(depth, GROUP, -1).transpose(1, 0, 2), cols], 2)
    extra = jnp.pad(head_zero[:, None], ((0, 0), (0, heads - 1), (0, 0), (0, 0)))
    low = jnp.concatenate([split(w_second), extra], 3)
    pa = jnp.concatenate([split(w_first), low], 2)
    spot = lax.broadcasted_iota(jnp.int32, (16, width), 1)
    mask = jnp.where(spot < lengths[0], 0.0, -1e30).astype(bf16)
    pt = jnp.concatenate([tokens[0], mask], 0)
    ups = [w_up[:, k * width : (k + 1) * width] for k in range(w_up.shape[1] // width)]
    pf = jnp.concatenate(ups + [w_out, jnp.zeros((8, width), bf16), w_down], 0)
    return pa, pt, pf


def on_device_fast(tokens, lengths, gain_one, w_value, w_first, b_first, w_second, b_second, w_out, gain_two, w_up, w_down, grad_out):
    _, slots, width = tokens.shape
    heads_all, depth, _ = w_first.shape
    heads = heads_all // GROUP
    pa, pt, pf = pack_inputs(
        tokens, lengths, gain_one, w_value, w_first, b_first, w_second, b_second, w_out, gain_two, w_up, w_down
    )
    wf, ws, wv, small, normed, values, hid, slope, prob, joined, lf = attend_call(pa, pt, pf)
    result, gmid, gmix, half, gg2 = ffn_call(lf, joined, tokens[0], small, grad_out[0])
    out_f, out_a, out_s, gtok = back_call(
        wf, ws, wv, normed, values, hid, slope, prob, gmix, gg2, half, tokens[0], gmid, small
    )
    low = out_a[:, :, 24:].astype(f32)
    to_all = lambda v: v.transpose((1, 0) + tuple(range(2, v.ndim))).reshape((heads_all,) + v.shape[2:])
    gb1 = to_all(low[:, :, :, 704])
    gains = jnp.sum(low[2, :, :, 705:707], axis=0)
    return (
        result[None],
        gtok[None],
        gains[:, 0],
        low[2, :, :, 512:704].transpose(1, 0, 2).reshape(depth, width),
        to_all(out_a[:, :, :24].astype(f32)),
        gb1,
        to_all(low[:, :, :, :512]),
        out_s[0, : b_second.shape[0]],
        out_f[4 * depth : 5 * depth],
        gains[:, 1],
        out_f[: 4 * depth].reshape(4, depth, width).transpose(1, 0, 2).reshape(depth, 4 * width),
        out_f[128:],
    )


def solution(mesh):
    wide, narrow = mesh.shape["wide"], mesh.shape["narrow"]
    grouped = Mesh(mesh.devices.reshape(GROUP, wide // GROUP, narrow), ALL)
    vec = P(ALL)
    flat = P(ALL, None)
    mid = P(None, ALL, None)
    row = P(ALL, None, None)
    body = on_device_fast if (wide, narrow) == (8, 4) else on_device
    return jax.shard_map(
        body,
        mesh=grouped,
        in_specs=(row, vec, vec, flat, mid, P(None, ALL), mid, vec, flat, vec, flat, flat, row),
        out_specs=(row, row, vec, flat, mid, P(None, ALL), mid, vec, flat, vec, flat, flat),
        check_vma=False,
    )
```

```python
import jax
import jax.numpy as jnp
from jax import lax
from jax.experimental import pallas as pl
from jax.experimental.pallas import tpu as pltpu
from jax.sharding import Mesh
from jax.sharding import PartitionSpec as P

epsilon = 1e-05
f32 = jnp.float32
bf16 = jnp.bfloat16
GROUP = 4


def norm_rows(values, factor):
    average = jnp.mean(values, axis=-1, keepdims=True)
    centred = values - average
    spread = jnp.mean(centred * centred, axis=-1, keepdims=True)
    return centred * lax.rsqrt(spread + epsilon) * factor


def smooth(values):
    return jax.nn.gelu(values, approximate=False)


def mm(spec, a, b):
    return jnp.einsum(spec, a, b, preferred_element_type=f32)


REST = ("rep", "narrow")
ALL = ("tp", "rep", "narrow")


def to_heads(shard):
    heads, depth, width = shard.shape
    pieces = lax.all_to_all(shard.reshape(GROUP, heads // GROUP, depth, width), "tp", 0, 0)
    whole = lax.all_gather(pieces, REST, axis=0)
    return whole.transpose(2, 1, 0, 3, 4).reshape(heads // GROUP, -1, width)


def from_heads(grad):
    heads, depth, width = grad.shape
    n = lax.axis_size("rep") * lax.axis_size("narrow")
    pieces = grad.astype(bf16).reshape(heads, GROUP, n, depth // (GROUP * n), width).transpose(2, 1, 0, 3, 4)
    pieces = pieces.reshape((n * GROUP,) + pieces.shape[2:])
    share = lax.psum_scatter(pieces, REST, scatter_dimension=0, tiled=True)
    share = lax.all_to_all(share, "tp", 0, 0)
    return share.reshape(heads * GROUP, depth // (GROUP * n), width).astype(f32)


def on_device(tokens, lengths, gain_one, w_value, w_first, b_first, w_second, b_second, w_out, gain_two, w_up, w_down, grad_out):
    row_count, slots, width = tokens.shape
    heads_all = w_first.shape[0]
    heads = heads_all // GROUP
    head_size = width // heads_all
    me = lax.axis_index("tp")
    depth = w_value.shape[0]

    small = [gain_one, gain_two, b_second, b_first.reshape(-1)]
    gathered = lax.all_gather(jnp.concatenate(small), ALL, axis=0)
    n_all = gathered.shape[0]
    g1 = gathered[:, :depth].reshape(-1).astype(f32)
    g2 = gathered[:, depth : 2 * depth].reshape(-1).astype(f32)
    b2_len = b_second.shape[0]
    b2 = gathered[:, 2 * depth : 2 * depth + b2_len].reshape(heads_all, slots).astype(f32)
    b1 = gathered[:, 2 * depth + b2_len :].reshape(n_all, heads_all, depth).transpose(1, 0, 2).reshape(heads_all, width).astype(f32)
    b1 = lax.dynamic_slice_in_dim(b1, me * heads, heads, 0)
    b2 = lax.dynamic_slice_in_dim(b2, me * heads, heads, 0)

    wf = to_heads(w_first)
    ws = to_heads(w_second)
    wv = to_heads(w_value.reshape(depth, GROUP, width // GROUP).transpose(1, 0, 2))[0]
    rows = lax.all_gather(tokens, "tp", axis=0, tiled=True)
    lens = lax.all_gather(lengths, "tp", axis=0, tiled=True)
    n_rows = rows.shape[0]

    normed = norm_rows(rows.astype(f32), g1).astype(bf16)
    values = mm("rsd,de->rse", normed, wv).astype(bf16)
    per_head = values.reshape(n_rows, slots, heads, head_size).transpose(2, 0, 1, 3)
    before = mm("rsd,hde->hrse", normed, wf) + b1[:, None, None, :]
    hidden = smooth(before).astype(bf16)
    logits = mm("hrse,hej->hrsj", hidden, ws) + b2[:, None, None, :]
    visible = lax.broadcasted_iota(jnp.int32, (1, n_rows, 1, slots), 3) < lens[None, :, None, None]
    masked = jnp.where(visible, logits, f32(-1e30))
    scaled = jnp.exp(masked - jnp.max(masked, axis=-1, keepdims=True))
    probabilities = scaled / jnp.sum(scaled, axis=-1, keepdims=True)
    weights = probabilities.astype(bf16)
    mixture = mm("hrsj,hrjc->rshc", weights, per_head).astype(bf16)
    mixture = mixture.reshape(GROUP, row_count, slots, heads * head_size)
    joined = lax.all_to_all(mixture, "tp", 0, 0).transpose(1, 2, 0, 3).reshape(row_count * slots, width)

    wo = lax.all_gather(w_out, ALL, axis=0, tiled=True)
    wu = lax.all_gather(w_up, ALL, axis=0, tiled=True)
    wd = lax.all_gather(w_down, ALL, axis=0, tiled=True)
    inputs = tokens.astype(f32).reshape(-1, width)
    middle = inputs + mm("sd,de->se", joined, wo)
    normed_two, norm_two_back = jax.vjp(norm_rows, middle, g2)
    normed_two = normed_two.astype(bf16)
    upward = mm("td,df->tf", normed_two, wu)
    active, smooth_up_back = jax.vjp(smooth, upward)
    active = active.astype(bf16)
    result = middle + mm("tf,fd->td", active, wd)

    g_out = grad_out.reshape(-1, width)
    grad_branch = g_out.astype(bf16)
    grad_w_down = mm("tf,td->fd", active, grad_branch)
    grad_upward = smooth_up_back(mm("td,fd->tf", grad_branch, wd))[0].astype(bf16)
    grad_w_up = mm("td,tf->df", normed_two, grad_upward)
    grad_middle_norm, grad_gain_two = norm_two_back(mm("tf,df->td", grad_upward, wu))
    grad_middle = g_out + grad_middle_norm
    grad_attn = grad_middle.astype(bf16)
    grad_w_out = mm("sd,se->de", joined, grad_attn)
    grad_joined = mm("se,de->sd", grad_attn, wo).astype(bf16)

    grad_mixture = grad_joined.reshape(row_count, slots, GROUP, heads * head_size).transpose(2, 0, 1, 3)
    grad_mixture = lax.all_to_all(grad_mixture, "tp", 0, 0).reshape(n_rows, slots, heads, head_size).transpose(2, 0, 1, 3)
    grad_weights = mm("hrsc,hrjc->hrsj", grad_mixture, per_head)
    grad_values = mm("hrsj,hrsc->rjhc", weights, grad_mixture).astype(bf16).reshape(n_rows, slots, heads * head_size)
    centre = jnp.sum(probabilities * grad_weights, axis=-1, keepdims=True)
    grad_logits = (probabilities * (grad_weights - centre)).astype(bf16)
    grad_b_second = jnp.sum(grad_logits.astype(f32), axis=(1, 2))
    grad_w_second = mm("hrse,hrsj->hej", hidden, grad_logits)
    grad_hidden = mm("hrsj,hej->hrse", grad_logits, ws)
    smooth_value, smooth_back = jax.vjp(smooth, before)
    grad_before = smooth_back(grad_hidden)[0].astype(bf16)
    grad_b_first = jnp.sum(grad_before.astype(f32), axis=(1, 2))
    grad_w_first = mm("rsd,hrse->hde", normed, grad_before)
    grad_w_value = mm("rsd,rse->de", normed, grad_values)
    grad_normed = mm("hrse,hde->rsd", grad_before, wf) + mm("rse,de->rsd", grad_values, wv)
    grad_normed = lax.psum_scatter(grad_normed.astype(bf16), "tp", scatter_dimension=0, tiled=True)
    value, norm_one_back = jax.vjp(norm_rows, inputs, g1)
    grad_inputs_norm, grad_gain_one = norm_one_back(grad_normed.astype(f32).reshape(-1, width))
    grad_tokens = grad_middle + grad_inputs_norm

    out_first = from_heads(grad_w_first)
    out_second = from_heads(grad_w_second)
    out_value = from_heads(grad_w_value[None]).transpose(1, 0, 2).reshape(depth, width)

    def share(grad):
        return lax.psum_scatter(grad.astype(bf16), ALL, scatter_dimension=0, tiled=True).astype(f32)

    vec_tp = jnp.concatenate([grad_b_first.reshape(-1), grad_b_second.reshape(-1)])
    vec_tp = lax.dynamic_update_slice_in_dim(jnp.zeros((GROUP, vec_tp.shape[0]), f32), vec_tp[None], me, 0)
    vec = jnp.concatenate([vec_tp.reshape(-1), grad_gain_one, grad_gain_two])
    vec = lax.psum(vec, ALL)
    index = (me * lax.axis_size("rep") + lax.axis_index("rep")) * lax.axis_size("narrow") + lax.axis_index("narrow")
    n_tp = GROUP * (heads * width + heads * slots)
    tp_part = vec[:n_tp].reshape(GROUP, -1)
    gb1 = tp_part[:, : heads * width].reshape(heads_all, width)
    gb2 = tp_part[:, heads * width :].reshape(-1)
    gb1 = lax.dynamic_slice_in_dim(gb1, index * depth, depth, 1)
    gb2 = lax.dynamic_slice_in_dim(gb2, index * b2_len, b2_len, 0)
    gg1 = lax.dynamic_slice_in_dim(vec[n_tp : n_tp + width], index * depth, depth, 0)
    gg2 = lax.dynamic_slice_in_dim(vec[n_tp + width :], index * depth, depth, 0)
    shape = tokens.shape
    return (
        result.reshape(shape),
        grad_tokens.reshape(shape),
        gg1,
        out_value,
        out_first,
        gb1,
        out_second,
        gb2,
        share(grad_w_out),
        gg2,
        share(grad_w_up),
        share(grad_w_down),
    )


MESH = pl.DeviceIdType.MESH
VMEM_LIMIT = 60 * 2**20
ANY = pl.BlockSpec(memory_space=pl.ANY)
FULL = pl.BlockSpec(memory_space=pltpu.VMEM)
DMA = pltpu.SemaphoreType.DMA


def shape_of(dims, kind):
    return jax.ShapeDtypeStruct(dims, kind)


def dot_nt(a, b):
    return lax.dot_general(a, b, (((1,), (1,)), ((), ())), preferred_element_type=f32)


def dot_tn(a, b):
    return lax.dot_general(a, b, (((0,), (0,)), ((), ())), preferred_element_type=f32)


def dot_nn(a, b):
    return lax.dot_general(a, b, (((1,), (0,)), ((), ())), preferred_element_type=f32)


def place():
    return lax.axis_index("tp"), lax.axis_index("rep"), lax.axis_index("narrow")


def group_peers():
    t, c, z = place()
    along_x = t + 1 - 2 * (t % 2)
    along_y = (t + 2) % GROUP
    return [along_x, along_y, GROUP - 1 - t]


def line_peers():
    z = lax.axis_index("narrow")
    return [(z + k) % 4 for k in (1, 2, 3)]


def line_place():
    z = lax.axis_index("narrow")
    side = z // 2
    end, inner = 3 * side, 1 + side
    return end, inner, 2 - side, 3 - 3 * side, end + inner - z, z == inner


class Spread:
    def __init__(self, slabs, send, recv, source=None):
        t, c, z = place()
        end, inner, other, far, near, is_inner = line_place()
        self.is_inner = is_inner
        move = lambda o, k, to: remote(slabs(o), slabs(o), send.at[k], recv.at[o], (t, c, to))
        source = slabs(z) if source is None else source
        give = lambda k, to: remote(source, slabs(z), send.at[k], recv.at[z], (t, c, to))
        self.own = lambda: [give(0, other), give(1, near)]
        self.on = lambda: [move(other, 2, end), move(far, 3, end)]
        self.near = lambda: move(near, 0, near)

    def begin(self):
        start(self.own())

    def forward(self):
        @pl.when(self.is_inner)
        def _():
            for copy in self.on():
                copy.wait_recv()
            start(self.on())

    def finish(self):
        self.near().wait_recv()

        @pl.when(jnp.logical_not(self.is_inner))
        def _():
            for copy in self.on():
                copy.wait_recv()

        for copy in self.own():
            copy.wait_send()

        @pl.when(self.is_inner)
        def _():
            for copy in self.on():
                copy.wait_send()


class Gather:
    def __init__(self, slabs, land, add, send, recv):
        t, c, z = place()
        end, inner, other, far, near, is_inner = line_place()
        self.is_inner, self.add, self.z = is_inner, add, z
        self.other, self.far = other, far
        move = lambda o, slot, k, to: remote(slabs(o), land(slot), send.at[k], recv.at[slot], (t, c, to))
        self.out = lambda: [move(far, 2, 0, inner), move(other, 1, 1, inner), move(inner, 0, 2, inner)]
        self.back = lambda: [move(end, 0, 2, end)]
        self.on_far = lambda: [move(far, 1, 0, far)]
        self.on_other = lambda: [move(other, 3, 1, other)]
        self.got = lambda slot: move(z, slot, 0, near).wait_recv()

    def begin(self):
        @pl.when(self.is_inner)
        def _():
            start(self.back())

        @pl.when(jnp.logical_not(self.is_inner))
        def _():
            start(self.out())

    def forward(self):
        @pl.when(self.is_inner)
        def _():
            self.got(2)
            self.add(self.far, 2)
            start(self.on_far())
            self.got(1)
            self.add(self.other, 1)
            start(self.on_other())

    def finish(self):
        self.got(0)
        self.add(self.z, 0)

        @pl.when(self.is_inner)
        def _():
            self.got(3)
            self.add(self.z, 3)
            for copy in self.back() + self.on_far() + self.on_other():
                copy.wait_send()

        @pl.when(jnp.logical_not(self.is_inner))
        def _():
            self.got(1)
            self.add(self.z, 1)
            for copy in self.out():
                copy.wait_send()


def greet(devices):
    barrier = pltpu.get_barrier_semaphore()
    for device in devices:
        pl.semaphore_signal(barrier, inc=1, device_id=device, device_id_type=MESH)


def met(count):
    pl.semaphore_wait(pltpu.get_barrier_semaphore(), count)


def remote(src, dst, send, recv, device):
    return pltpu.make_async_remote_copy(
        src_ref=src, dst_ref=dst, send_sem=send, recv_sem=recv, device_id=device, device_id_type=MESH
    )


def local(src, dst, sem):
    return pltpu.make_async_copy(src, dst, sem)


def start(copies):
    for copy in copies:
        copy.start()


def wait(copies):
    for copy in copies:
        copy.wait()


def square():
    t, c, z = place()
    y, x = t // 2, t % 2
    tps = group_peers()
    slow, fast = (1 - c) * y + c * x, (1 - c) * x + c * y
    fast_peer = (1 - c) * tps[0] + c * tps[1]
    slow_peer = (1 - c) * tps[1] + c * tps[0]
    return slow, fast, (slow_peer, c, z), (fast_peer, c, z)


def gelu_pair(v):
    cdf = 0.5 * (1.0 + lax.erf(v * 0.7071067811865476))
    return v * cdf, cdf + v * (jnp.exp(-0.5 * v * v) * 0.3989422804014327)


def centre_rows(v):
    shifted = v - jnp.mean(v, axis=-1, keepdims=True)
    scale = lax.rsqrt(jnp.mean(shifted * shifted, axis=-1, keepdims=True) + epsilon)
    return shifted * scale, scale


ROWS = ((0, 144), (144, 272), (272, 384))


def part(i):
    return slice(*ROWS[i])


def attend_kernel(
    tokens, extra, w_first, w_second, w_out, w_up, w_down,
    wf, ws, wv, small, normed, values, hid, slope, prob, joined, lf,
    pa, pf, la, lt, nrm, val, cols, b2, masks, join, own, s1, r1, s2, r2, s3, r3, st, rt, s1f, r1f, sf, rf, sj, rj,
):
    h, r = pl.program_id(0), pl.program_id(1)
    width = wf.shape[-1]
    heads = w_first.shape[0] // GROUP
    t, c, z = place()
    sibling = (t, 1 - c, z)
    tps, zs = group_peers(), line_peers()
    slow, fast, slow_dev, fast_dev = square()

    a1 = lambda i: [
        remote(pa.at[p, part(i)], la.at[c, z, t, part(i)], s1.at[i, k], r1.at[i, k], (p, c, z))
        for k, p in enumerate(tps)
    ]
    a2 = lambda i: Spread(lambda o: la.at[c, o, :, part(i)], s2.at[i], r2.at[i])
    a3 = lambda i: [remote(la.at[c, :, :, part(i)], la.at[c, :, :, part(i)], s3.at[i], r3.at[i], sibling)]
    mine = lambda i: [local(pa.at[t, part(i)], la.at[c, z, t, part(i)], own.at[i])]
    mine_t = lambda: [local(tokens.at[0], lt.at[3], own.at[heads])]
    mine_f = lambda: [local(pf, lf.at[c, slow, fast, z], own.at[heads + 1])]
    mine_j = lambda: [local(join.at[3], joined.at[t], own.at[heads + 2])]
    toks = lambda: [remote(tokens.at[0], lt.at[k], st.at[k], rt.at[k], (p, c, z)) for k, p in enumerate(tps)]
    f1 = lambda: Spread(lambda o: lf.at[c, slow, fast, o], s1f, r1f, pf)
    f2 = lambda: [remote(lf.at[c, slow, fast], lf.at[c, slow, fast], sf.at[0], rf.at[0], fast_dev)]
    f3 = lambda: [remote(lf.at[c, slow], lf.at[c, slow], sf.at[1], rf.at[1], slow_dev)]
    f4 = lambda: [remote(lf.at[c, slow], lf.at[c, slow], sf.at[2], rf.at[2], sibling)]
    f5 = lambda: [remote(lf.at[c, 1 - slow], lf.at[c, 1 - slow], sf.at[3], rf.at[3], sibling)]
    out_j = lambda k: [remote(join.at[k], joined.at[t], sj.at[k], rj.at[k], (tps[k], c, z))]

    def at_step(i, j):
        return pl.when((h == i) & (r == j))

    @at_step(0, 0)
    def _():
        greet([(p, c, z) for p in tps] + [(t, c, p) for p in zs] + [sibling])
        blocks = lambda v: [v[:, k : k + 256] for k in range(0, v.shape[1], 256)]
        ups = [w_up[:, k : k + width].astype(f32) for k in range(0, w_up.shape[1], width)]
        pf[0:96] = jnp.concatenate(ups, 0).astype(bf16)
        pf[96:128] = jnp.concatenate([w_out[...].astype(f32), jnp.zeros((8, width), f32)], 0).astype(bf16)
        pf[128:224] = w_down[...]
        for p in range(GROUP):
            stack = [extra[p].astype(f32)]
            for i in range(heads):
                stack += blocks(w_first[heads * p + i].astype(f32)) + blocks(w_second[heads * p + i].astype(f32))
            pa[p] = jnp.concatenate(stack, 0).astype(bf16)
        met(7)
        f1().begin()
        for i in range(heads):
            start(mine(i) + a1(i))
        start(mine_f() + mine_t())
        wait(mine(0) + a1(0))
        a2(0).begin()
        wait(mine(1) + a1(1))
        wait(mine(2) + a1(2))
        start(toks())
        f1().forward()
        a2(1).begin()
        a2(0).forward()
        f1().finish()
        wait(mine_f())
        start(f2())
        a2(2).begin()
        a2(0).finish()
        start(a3(0))
        a2(1).forward()
        wait(mine_t() + toks() + a3(0))

    @at_step(0, 2)
    def _():
        a2(2).forward()

    @at_step(1, 0)
    def _():
        a2(1).finish()
        start(a3(1))
        wait(f2())
        start(f3() + f4())
        wait(a3(1))

    @at_step(2, 0)
    def _():
        a2(2).finish()
        start(a3(2))
        wait(a3(2))

    def unpack(i):
        def one(tt, carry):
            for cc in range(2):
                for zz in range(0, 4, 2):
                    at = pl.ds(pl.multiple_of((tt * 8 + cc * 4 + zz) * 24, 48), 48)

                    def block(first):
                        low = first // 16 * 16
                        both = [la[cc, zz + k, tt, low : low + 32].astype(f32)[first - low :][:24] for k in range(2)]
                        return jnp.concatenate(both, 0)

                    base = 24 + 120 * i
                    for j in range(3):
                        wf[0, at, 256 * j : 256 * j + 256] = block(base + 24 * j).astype(bf16)
                    for j in range(2):
                        ws[0, at, 256 * j : 256 * j + 256] = block(base + 72 + 24 * j).astype(bf16)
                    if i == 0:
                        both = block(0)
                        cols[at, :] = both[:, 128:256]
                        lane = lax.broadcasted_iota(jnp.int32, both.shape, 1)
                        wv[at, :] = jnp.where(lane < 192, both, 0.0).astype(bf16)

            return carry

        lax.fori_loop(0, GROUP, one, 0)

    for i in range(heads):

        @at_step(i, 0)
        def _():
            unpack(i)

    @at_step(0, 0)
    def _():
        small[...] = cols[...].T[64:72]
        mine_rows = cols[pl.ds(pl.multiple_of(t * 192, 192), 192), :].astype(bf16)
        lane = lax.broadcasted_iota(jnp.int32, (128, 512), 0)
        spot = lax.broadcasted_iota(jnp.int32, (128, 512), 1)
        spread = dot_nn(mine_rows, jnp.where(lane - 69 == spot % 8, 1.0, 0.0).astype(bf16))
        row = lax.broadcasted_iota(jnp.int32, (64, 512), 0)
        spot = lax.broadcasted_iota(jnp.int32, (64, 512), 1)
        for i in range(heads):
            picked = jnp.where(row == spot // 8, spread[64 * i : 64 * i + 64], 0.0)
            b2[i] = jnp.broadcast_to(jnp.sum(picked, axis=0, keepdims=True), (8, 512))
        for k, p in enumerate(tps + [t]):
            line = cols[pl.ds(pl.multiple_of((p * 8 + c * 4 + z) * 24, 8), 8), :]
            lane = lax.broadcasted_iota(jnp.int32, line.shape, 1)
            digits = jnp.where(lane == 77, 16.0 * line, jnp.where(lane == 78, line, 0.0))
            length = jnp.sum(digits, axis=1, keepdims=True)
            spot = lax.broadcasted_iota(jnp.int32, (8, 512), 1).astype(f32)
            masks[k] = jnp.where(spot < length, 0.0, -1e30)

    @pl.when(h == 0)
    def _():
        unit, _ = centre_rows(lt[r].astype(f32))
        out = (unit * small[3:4]).astype(bf16)
        nrm[r] = out
        normed[0] = out
        v = dot_nn(out, wv[...]).astype(bf16)
        val[r] = v
        values[0] = v

    row = lax.broadcasted_iota(jnp.int32, (8, width), 0)
    b1 = jnp.sum(jnp.where(row == h, small[...], 0.0), axis=0, keepdims=True)
    shift = b2[h, 0:1] + masks[r, 0:1]
    tile = pl.ds(pl.multiple_of((h // 2) * 128, 128), 128)
    step = 256
    for m in range(0, 512, step):
        at = slice(m, m + step)
        before = dot_nn(nrm[r, at, :], wf[0]) + b1
        out, grad = gelu_pair(before)
        hidden = out.astype(bf16)
        hid[0, 0, at, :] = hidden
        slope[0, 0, at, :] = grad.astype(bf16)
        logits = dot_nn(hidden, ws[0]) + shift
        e = jnp.exp(logits - jnp.max(logits, axis=-1, keepdims=True))
        p = (e / jnp.sum(e, axis=-1, keepdims=True)).astype(bf16)
        prob[0, 0, at, :] = p
        mix = dot_nn(p, val[r, :, tile])
        lane = lax.broadcasted_iota(jnp.int32, mix.shape, 1)
        old = join[r, at, tile].astype(f32)
        join[r, at, tile] = jnp.where((h == 1) & (lane < 64), old, mix).astype(bf16)

    for k in range(3):

        @at_step(2, k)
        def _():
            start(out_j(k))

    @at_step(2, 1)
    def _():
        wait(f3())
        start(f5())

    @at_step(2, 3)
    def _():
        start(mine_j())
        for k in range(3):
            wait(out_j(k))
        wait(mine_j() + f4() + f5())


def attend_call(tokens, extra, w_first, w_second, w_out, w_up, w_down):
    _, slots, width = tokens.shape
    heads = w_first.shape[0] // GROUP
    by_row = lambda h, r: (jnp.where(h == 0, r, GROUP - 1), 0, 0)
    by_head = lambda h, r: (h, 0, 0)
    both = lambda h, r: (h, r, 0, 0)
    rows_f = 2 * w_down.shape[0] + 32
    return pl.pallas_call(
        attend_kernel,
        grid=(heads, GROUP),
        out_shape=(
            shape_of((heads, width, width), bf16),
            shape_of((heads, width, slots), bf16),
            shape_of((width, 256), bf16),
            shape_of((8, width), f32),
            shape_of((GROUP, slots, width), bf16),
            shape_of((GROUP, slots, 256), bf16),
            shape_of((heads, GROUP, slots, width), bf16),
            shape_of((heads, GROUP, slots, width), bf16),
            shape_of((heads, GROUP, slots, slots), bf16),
            shape_of((GROUP, slots, 256), bf16),
            shape_of((2, 2, 2, 4, rows_f, width), bf16),
        ),
        in_specs=[ANY] + [FULL] * 6,
        out_specs=(
            pl.BlockSpec((1, width, width), by_head),
            pl.BlockSpec((1, width, slots), by_head),
            pl.BlockSpec((width, 256), lambda h, r: (0, 0)),
            pl.BlockSpec((8, width), lambda h, r: (0, 0)),
            pl.BlockSpec((1, slots, width), by_row),
            pl.BlockSpec((1, slots, 256), by_row),
            pl.BlockSpec((1, 1, slots, width), both),
            pl.BlockSpec((1, 1, slots, width), both),
            pl.BlockSpec((1, 1, slots, slots), both),
            ANY,
            ANY,
        ),
        scratch_shapes=[
            pltpu.VMEM((GROUP, 384, 256), bf16),
            pltpu.VMEM((rows_f, width), bf16),
            pltpu.VMEM((2, 4, GROUP, 384, 256), bf16),
            pltpu.VMEM((GROUP, slots, width), bf16),
            pltpu.VMEM((GROUP, slots, width), bf16),
            pltpu.VMEM((GROUP, slots, 256), bf16),
            pltpu.VMEM((width, 128), f32),
            pltpu.VMEM((heads, 8, slots), f32),
            pltpu.VMEM((GROUP, 8, slots), f32),
            pltpu.VMEM((GROUP, slots, 256), bf16),
            DMA((heads + 3,)),
            DMA((heads, 3)),
            DMA((heads, 3)),
            DMA((heads, 4)),
            DMA((heads, 4)),
            DMA((heads,)),
            DMA((heads,)),
            DMA((3,)),
            DMA((3,)),
            DMA((4,)),
            DMA((4,)),
            DMA((4,)),
            DMA((4,)),
            DMA((3,)),
            DMA((3,)),
        ],
        compiler_params=pltpu.CompilerParams(collective_id=1, has_side_effects=True, vmem_limit_bytes=VMEM_LIMIT),
    )(tokens, extra, w_first, w_second, w_out, w_up, w_down)


def slab(t, c, z):
    y, x = t // 2, t % 2
    return (0, y, x, z) if c == 0 else (1, x, y, z)


def ffn_kernel(
    lf_far, joined, tokens, small, gout, result, gmid, gmix, half, gg2,
    lf, loads, middles, gf, gj, more, wu, wo, n2, acc, gn2, gwu, own, sg, rg, sx, rx,
):
    width = tokens.shape[-1]
    me, core, z_me = place()
    tps = group_peers()
    sibling = (me, 1 - core, z_me)
    parts = (slice(0, 96), slice(128, 224), slice(96, 128))
    cross = lambda k: [
        remote(
            gf.at[1 - core, :, :, :, parts[k], :], more.at[:, :, :, parts[k], :], sx.at[k], rx.at[k], sibling
        )
    ]
    out_g = lambda k: [remote(gj.at[tps[k]], gmix.at[k], sg.at[k], rg.at[k], (tps[k], core, z_me))]
    greet([(p, core, z_me) for p in tps] + [sibling])
    load = lambda k: local(lf_far.at[:, :, :, :, parts[k], :], lf.at[:, :, :, :, parts[k], :], loads.at[k])
    for k in (2, 0, 1):
        load(k).start()
    load(2).wait()
    wo[...] = jnp.zeros_like(wo)
    for t in range(GROUP):
        for c in range(2):
            for z in range(0, 4, 2):
                pair = [lf[slab(t, c, z + k) + (slice(96, 128),)].astype(f32)[0:24] for k in range(2)]
                wo[t, (c * 4 + z) * 24 : (c * 4 + z) * 24 + 48, :] = jnp.concatenate(pair, 0).astype(bf16)
    middle = tokens[...].astype(f32)
    for t in range(GROUP):
        middle = middle + dot_nn(joined[t], wo[t])
    acc[...] = middle
    middles[...] = middle
    g2 = small[4:5]
    unit, _ = centre_rows(middle)
    n2[...] = (unit * g2).astype(bf16)
    gn2[...] = jnp.zeros_like(gn2)
    load(0).wait()
    load(1).wait()

    def block(p, carry):
        rows = pl.ds(pl.multiple_of(p * 48, 16), 48)
        for t in range(GROUP):
            for c in range(2):
                for z in range(0, 4, 2):
                    ends = [lf[slab(t, c, z + k) + (rows,)].astype(f32) for k in range(2)]
                    at = (t * 8 + c * 4 + z) * 24
                    for k in range(2):
                        both = jnp.concatenate([e[24 * k : 24 * k + 24] for e in ends], 0)
                        wu[k, at : at + 48, :] = both.astype(bf16)
        branch = gout[...].astype(bf16)
        for k in range(2):
            wd = jnp.concatenate(
                [lf[0, p, k, :, 128:224, :].reshape(384, width), lf[1, k, p, :, 128:224, :].reshape(384, width)], 0
            )
            up = dot_nn(n2[...], wu[k])
            act, slope = gelu_pair(up)
            act = act.astype(bf16)
            acc[...] += dot_nn(act, wd)
            gup = (dot_nt(branch, wd) * slope).astype(bf16)
            gwd = dot_tn(act, branch).astype(bf16)
            gf[0, p, k, :, 128:224, :] = gwd[:384].reshape(4, 96, width)
            gf[1, k, p, :, 128:224, :] = gwd[384:].reshape(4, 96, width)
            gwu[k] = dot_tn(n2[...], gup)
            gn2[...] += dot_nt(gup, wu[k])
        for t in range(GROUP):
            for c in range(2):
                for z in range(4):
                    at = (t * 8 + c * 4 + z) * 24
                    both = jnp.concatenate([gwu[0, at : at + 24, :], gwu[1, at : at + 24, :]], 0)
                    gf[slab(t, c, z) + (rows,)] = both.astype(bf16)
        return carry

    lax.fori_loop(0, 2, block, 0)
    met(4)
    start(cross(0) + cross(1))
    result[...] = acc[...]
    unit, scale = centre_rows(middles[...])
    gn = gn2[...]
    gg2[...] = jnp.sum((gn * unit).reshape(-1, 8, width), axis=0)
    gu = gn * g2
    back = scale * (
        gu - jnp.mean(gu, axis=-1, keepdims=True) - unit * jnp.mean(gu * unit, axis=-1, keepdims=True)
    )
    gm = gout[...] + back
    gmid[...] = gm
    ga = gm.astype(bf16)
    for t in range(GROUP):
        gj[t] = dot_nt(ga, wo[t]).astype(bf16)
    for k in range(3):
        start(out_g(k))
    mine = local(gj.at[me], gmix.at[3], own)
    mine.start()
    for t in range(GROUP):
        gwo = dot_tn(joined[t], ga)
        for c in range(2):
            for z in range(4):
                at = (c * 4 + z) * 24
                padded = jnp.concatenate([gwo[at : at + 24, :], jnp.zeros((8, width), f32)], 0)
                gf[slab(t, c, z) + (slice(96, 128),)] = padded.astype(bf16)
    start(cross(2))
    for k in range(3):
        wait(cross(k))

        def fold(i, carry):
            for j in range(2):
                for z in range(4):
                    spot = (i, j, z, parts[k])
                    half[spot] = (gf[(core,) + spot].astype(f32) + more[spot].astype(f32)).astype(bf16)
            return carry

        lax.fori_loop(0, 2, fold, 0)
    for k in range(3):
        wait(out_g(k))
    mine.wait()


def ffn_call(lf, joined, tokens, small, gout):
    slots, width = tokens.shape
    return pl.pallas_call(
        ffn_kernel,
        out_shape=(
            shape_of((slots, width), f32),
            shape_of((slots, width), f32),
            shape_of(joined.shape, bf16),
            shape_of(lf.shape[1:], bf16),
            shape_of((8, width), f32),
        ),
        in_specs=[ANY] + [FULL] * 4,
        out_specs=(FULL, FULL, ANY, FULL, FULL),
        scratch_shapes=[
            pltpu.VMEM(lf.shape, bf16),
            DMA((3,)),
            pltpu.VMEM((slots, width), f32),
            pltpu.VMEM(lf.shape, bf16),
            pltpu.VMEM(joined.shape, bf16),
            pltpu.VMEM(lf.shape[1:], bf16),
            pltpu.VMEM((2, width, width), bf16),
            pltpu.VMEM((GROUP, 256, width), bf16),
            pltpu.VMEM((slots, width), bf16),
            pltpu.VMEM((slots, width), f32),
            pltpu.VMEM((slots, width), f32),
            pltpu.VMEM((2, width, width), f32),
            DMA,
            DMA((3,)),
            DMA((3,)),
            DMA((3,)),
            DMA((3,)),
        ],
        compiler_params=pltpu.CompilerParams(collective_id=2, has_side_effects=True, vmem_limit_bytes=VMEM_LIMIT),
    )(lf, joined, tokens, small, gout)


def back_kernel(
    wf, ws, wv, normed, values, hid, slope, prob, gmix, gg2, half, tokens, gmid, small, out_f, out_a, out_s, gtok,
    awf, aws, ab1, ab2, gn, gv, awv, ag1, stash, ga, gs, gnb, nb, fs, fb2, fb3, fb4, cb1, cb2, sb1, sb2,
    own, s1, r1, s2, r2, s3, r3, sn, rn, sf, rf, s4, r4, sv, rv,
):
    step, r = pl.program_id(0), pl.program_id(1)
    width = wf.shape[-1]
    heads = ab1.shape[0]
    h = heads - 1 - step
    t, c, z = place()
    sibling = (t, 1 - c, z)
    tps, zs = group_peers(), line_peers()
    slow, fast, slow_dev, fast_dev = square()

    a1 = lambda i: [remote(ga.at[1 - c, :, :, part(i)], cb1.at[:, :, part(i)], s1.at[i], r1.at[i], sibling)]
    def add_heads(i):
        def add(o, slot):
            def one(j, carry):
                here = ga[c, o, j, part(i)].astype(f32) + cb2[slot, j, part(i)].astype(f32)
                ga[c, o, j, part(i)] = here.astype(bf16)
                return carry

            lax.fori_loop(0, GROUP, one, 0)

        return add

    def add_f(o, slot):
        fs[fast, o] = (fs[fast, o].astype(f32) + fb4[slot].astype(f32)).astype(bf16)

    a2 = lambda i: Gather(
        lambda o: ga.at[c, o, :, part(i)], lambda k: cb2.at[k, :, part(i)], add_heads(i), s2.at[i], r2.at[i]
    )
    a3 = lambda i: [
        remote(ga.at[c, z, p, part(i)], out_a.at[t, part(i)], s3.at[i, k], r3.at[i, k], (p, c, z))
        for k, p in enumerate(tps)
    ]
    mine = lambda i: [local(ga.at[c, z, t, part(i)], out_a.at[t, part(i)], own.at[i])]
    mine_f = lambda: [local(half.at[slow], fs, own.at[heads])]
    v1 = lambda: [remote(gs.at[1 - c], sb1, sv.at[0], rv.at[0], sibling)]
    v2 = lambda: [remote(gs.at[c, p], sb2.at[k], sv.at[1 + k], rv.at[1 + k], (t, c, p)) for k, p in enumerate(zs)]
    f2 = lambda: [remote(half.at[1 - slow], fb2, sf.at[0], rf.at[0], slow_dev)]
    f3 = lambda: [remote(fs.at[1 - fast], fb3, sf.at[1], rf.at[1], fast_dev)]
    f4 = lambda: Gather(lambda o: fs.at[fast, o], lambda k: fb4.at[k], add_f, s4, r4)
    out_n = lambda k: [remote(gnb.at[k], nb.at[k], sn.at[k], rn.at[k], (tps[k], c, z))]

    def at_step(i, j):
        return pl.when((step == i) & (r == j))

    def meet(i):
        wait(a1(i))

        def line(k, carry):
            for j in range(GROUP):
                here = ga[c, k, j, part(i)].astype(f32) + cb1[k, j, part(i)].astype(f32)
                ga[c, k, j, part(i)] = here.astype(bf16)
            return carry

        lax.fori_loop(0, 4, line, 0)
        a2(i).begin()

    def deal(i):
        a2(i).finish()
        start(mine(i) + a3(i))

    def add_slabs(total, more):
        def one(k, carry):
            fs[total, k] = (fs[total, k].astype(f32) + more[k].astype(f32)).astype(bf16)
            return carry

        lax.fori_loop(0, 4, one, 0)

    @at_step(0, 0)
    def _():
        greet([(p, c, z) for p in tps] + [(t, c, p) for p in zs] + [sibling])
        met(7)
        start(f2() + mine_f())

    @at_step(1, 0)
    def _():
        meet(2)

    @at_step(1, 2)
    def _():
        a2(2).forward()

    @at_step(1, 3)
    def _():
        wait(f2() + mine_f())
        add_slabs(1 - fast, fb2.at[1 - fast])
        start(f3())
        add_slabs(fast, fb2.at[fast])

    @at_step(2, 0)
    def _():
        meet(1)

    @at_step(2, 1)
    def _():
        deal(2)

    @at_step(2, 2)
    def _():
        a2(1).forward()

    @at_step(2, 3)
    def _():
        wait(f3())
        add_slabs(fast, fb3)
        f4().begin()

    @pl.when(r == 0)
    def _():
        awf[...] = jnp.zeros_like(awf)
        aws[...] = jnp.zeros_like(aws)
        ab1[h] = jnp.zeros(ab1.shape[1:], f32)
        ab2[h] = jnp.zeros(ab2.shape[1:], f32)

    tile = pl.ds(pl.multiple_of((h // 2) * 128, 128), 128)
    lane = lax.broadcasted_iota(jnp.int32, (512, 128), 1)
    gm = jnp.where(lane // 64 == h % 2, gmix[0, :, tile].astype(f32), 0.0).astype(bf16)
    gw = dot_nt(gm, values[0, :, tile])
    p = prob[0, 0]
    p32 = p.astype(f32)
    gl = (p32 * (gw - jnp.sum(p32 * gw, axis=-1, keepdims=True))).astype(bf16)
    ab2[h] += jnp.sum(gl.astype(f32).reshape(-1, 8, 512), axis=0)
    gvh = dot_tn(p, gm)

    @pl.when(h != 0)
    def _():
        gv[r, :, tile] = gvh

    @pl.when(h == 0)
    def _():
        gv[r, :, tile] += gvh

    aws[...] += dot_tn(hid[0, 0], gl)
    gb = (dot_nt(gl, ws[0]) * slope[0, 0].astype(f32)).astype(bf16)
    ab1[h] += jnp.sum(gb.astype(f32).reshape(-1, 8, width), axis=0)
    awf[...] += dot_tn(normed[0], gb)
    more_gn = dot_nt(gb, wf[0])

    @pl.when(step == 0)
    def _():
        gn[r] = more_gn

    @pl.when(step == 1)
    def _():
        gn[r] += more_gn

    @pl.when(step == 2)
    def _():
        gvb = gv[r].astype(bf16)
        total = gn[r] + more_gn + dot_nt(gvb, wv[...])
        gn[r] = total
        both = (total * normed[0].astype(f32)).reshape(-1, 8, width)
        ag1[...] = jnp.where(r == 0, 0.0, ag1[...]) + jnp.sum(both, axis=0)
        more = dot_tn(normed[0], gvb)

        @pl.when(r == 0)
        def _():
            awv[...] = more

        @pl.when(r != 0)
        def _():
            awv[...] += more

        for k in range(3):

            @pl.when(r == k)
            def _():
                gnb[k] = total.astype(bf16)
                start(out_n(k))

    def pack(i):
        def one(tt, carry):
            for cc in range(2):
                for zz in range(4):
                    at = pl.ds(pl.multiple_of((tt * 8 + cc * 4 + zz) * 24, 8), 24)
                    stack = [awf[at, 256 * j : 256 * j + 256] for j in range(3)]
                    stack += [aws[at, 256 * j : 256 * j + 256] for j in range(2)]
                    if i == 0:
                        stack = [awv[at, :]] + stack
                    if i == 1:
                        stack = stack + [stash[cc, zz, tt]]
                    whole = jnp.concatenate(stack, 0)
                    if i == 2:
                        stash[cc, zz, tt] = whole[0:8]
                        whole = whole[8:]
                    ga[cc, zz, tt, part(i)] = whole.astype(bf16)
            return carry

        lax.fori_loop(0, GROUP, one, 0)
        start(a1(i))

    @at_step(0, 3)
    def _():
        pack(2)

    @at_step(1, 3)
    def _():
        pack(1)

    @at_step(2, 3)
    def _():
        row = lax.broadcasted_iota(jnp.int32, (128, width), 0)
        stack = jnp.zeros((128, width), f32)
        gains = jnp.sum(ag1[...], axis=0, keepdims=True) / small[3:4]
        lines = [jnp.sum(ab1[i], axis=0, keepdims=True) for i in range(heads)]
        for k, line in enumerate(lines + [gains, jnp.sum(gg2[...], axis=0, keepdims=True)]):
            stack = jnp.where(row == 64 + k, line, stack)
        lane = lax.broadcasted_iota(jnp.int32, (width, 128), 1)
        awv[:, 128:256] = jnp.where(lane < 64, awv[:, 128:256], stack.T)
        pack(0)

    @at_step(2, 3)
    def _():
        flat = jnp.concatenate([jnp.sum(ab2[k], axis=0, keepdims=True) for k in range(3)], 1)
        flat = jnp.broadcast_to(flat, (8, 1536))
        for cc in range(2):
            for zz in range(4):
                s = (cc * 4 + zz) * 192
                gs[cc, zz] = (pltpu.roll(flat, 1536 - s, 1) if s else flat)[:, 0:256]
        start(v1())
        meet(0)
        wait(v1())
        gs[c] += sb1[...]
        start(v2())
        f4().forward()
        for k in range(3):
            wait(out_n(k))
        a2(0).forward()

        def ln_back(i, carry):
            at = pl.ds(pl.multiple_of(i * 128, 128), 128)
            g = gn[3, at, :] + nb[0, at, :].astype(f32) + nb[1, at, :].astype(f32) + nb[2, at, :].astype(f32)
            unit, scale = centre_rows(tokens[at, :].astype(f32))
            gu = g * small[3:4]
            back = scale * (
                gu - jnp.mean(gu, axis=-1, keepdims=True) - unit * jnp.mean(gu * unit, axis=-1, keepdims=True)
            )
            gtok[at, :] = gmid[at, :] + back
            return carry

        lax.fori_loop(0, 4, ln_back, 0)
        deal(1)
        f4().finish()
        out_f[...] = fs[fast, z].astype(f32)
        wait(v2())
        out_s[...] = gs[c, z] + sb2[0] + sb2[1] + sb2[2]
        deal(0)
        for i in range(heads):
            wait(mine(i) + a3(i))


def back_call(wf, ws, wv, normed, values, hid, slope, prob, gmix, gg2, half, tokens, gmid, small):
    heads, width, slots = ws.shape
    rows = half.shape[-2]
    by_head = lambda h, r: (heads - 1 - h, 0, 0)
    row = lambda h, r: (r, 0, 0)
    both = lambda h, r: (heads - 1 - h, r, 0, 0)
    flat = lambda h, r: (0, 0)
    return pl.pallas_call(
        back_kernel,
        grid=(heads, GROUP),
        out_shape=(
            shape_of((rows, width), f32),
            shape_of((GROUP, 384, 256), bf16),
            shape_of((8, 256), f32),
            shape_of(tokens.shape, f32),
        ),
        in_specs=[
            pl.BlockSpec((1, width, width), by_head),
            pl.BlockSpec((1, width, slots), by_head),
            pl.BlockSpec((width, 256), flat),
            pl.BlockSpec((1, slots, width), row),
            pl.BlockSpec((1, slots, 256), row),
            pl.BlockSpec((1, 1, slots, width), both),
            pl.BlockSpec((1, 1, slots, width), both),
            pl.BlockSpec((1, 1, slots, slots), both),
            pl.BlockSpec((1, slots, 256), row),
            pl.BlockSpec((8, width), flat),
            ANY,
            FULL,
            FULL,
            pl.BlockSpec((8, width), flat),
        ],
        out_specs=(FULL, ANY, FULL, FULL),
        scratch_shapes=[
            pltpu.VMEM((width, width), f32),
            pltpu.VMEM((width, slots), f32),
            pltpu.VMEM((heads, 8, width), f32),
            pltpu.VMEM((heads, 8, slots), f32),
            pltpu.VMEM((GROUP, slots, width), f32),
            pltpu.VMEM((GROUP, slots, 256), f32),
            pltpu.VMEM((width, 256), f32),
            pltpu.VMEM((8, width), f32),
            pltpu.VMEM((2, 4, GROUP, 8, 256), f32),
            pltpu.VMEM((2, 4, GROUP, 384, 256), bf16),
            pltpu.VMEM((2, 4, 8, 256), f32),
            pltpu.VMEM((3, slots, width), bf16),
            pltpu.VMEM((3, slots, width), bf16),
            pltpu.VMEM((2, 4, rows, width), bf16),
            pltpu.VMEM((2, 4, rows, width), bf16),
            pltpu.VMEM((4, rows, width), bf16),
            pltpu.VMEM((4, rows, width), bf16),
            pltpu.VMEM((4, GROUP, 384, 256), bf16),
            pltpu.VMEM((4, GROUP, 384, 256), bf16),
            pltpu.VMEM((4, 8, 256), f32),
            pltpu.VMEM((3, 8, 256), f32),
            DMA((heads + 1,)),
            DMA((heads,)),
            DMA((heads,)),
            DMA((heads, 3)),
            DMA((heads, 4)),
            DMA((heads, 3)),
            DMA((heads, 3)),
            DMA((3,)),
            DMA((3,)),
            DMA((2,)),
            DMA((2,)),
            DMA((3,)),
            DMA((4,)),
            DMA((4,)),
            DMA((4,)),
        ],
        compiler_params=pltpu.CompilerParams(collective_id=3, has_side_effects=True, vmem_limit_bytes=VMEM_LIMIT),
    )(wf, ws, wv, normed, values, hid, slope, prob, gmix, gg2, half, tokens, gmid, small)


def on_device_fast(tokens, lengths, gain_one, w_value, w_first, b_first, w_second, b_second, w_out, gain_two, w_up, w_down, grad_out):
    _, slots, width = tokens.shape
    heads_all, depth, _ = w_first.shape
    heads = heads_all // GROUP
    digits = jnp.stack([lengths[0] // 16, lengths[0] % 16]).astype(bf16)
    extra = jnp.concatenate(
        [
            w_value.reshape(depth, GROUP, -1).transpose(1, 0, 2),
            b_first.reshape(GROUP, heads, depth).transpose(0, 2, 1),
            jnp.broadcast_to(jnp.stack([gain_one, gain_two], 1), (GROUP, depth, 2)),
            jnp.broadcast_to(b_second.reshape(depth, 8), (GROUP, depth, 8)),
            jnp.broadcast_to(digits, (GROUP, depth, 2)),
            jnp.zeros((GROUP, depth, 49), bf16),
        ],
        2,
    )
    wf, ws, wv, small, normed, values, hid, slope, prob, joined, lf = attend_call(
        tokens, extra, w_first, w_second, w_out, w_up, w_down
    )
    result, gmid, gmix, half, gg2 = ffn_call(lf, joined, tokens[0], small, grad_out[0])
    out_f, out_a, out_s, gtok = back_call(
        wf, ws, wv, normed, values, hid, slope, prob, gmix, gg2, half, tokens[0], gmid, small
    )
    side = out_a[:, :depth].astype(f32)
    blocks = out_a[:, depth:].reshape(GROUP, heads, 5, depth, 256)
    widen = lambda v: v.transpose(0, 1, 3, 2, 4).reshape(heads_all, depth, -1).astype(f32)
    gains = jnp.sum(side[:, :, 195:197], axis=0)
    return (
        result[None],
        gtok[None],
        gains[:, 0],
        side[:, :, :192].transpose(1, 0, 2).reshape(depth, width),
        widen(blocks[:, :, :3]),
        side[:, :, 192:195].transpose(0, 2, 1).reshape(heads_all, depth),
        widen(blocks[:, :, 3:]),
        out_s[0, : b_second.shape[0]],
        out_f[4 * depth : 5 * depth],
        gains[:, 1],
        out_f[: 4 * depth].reshape(4, depth, width).transpose(1, 0, 2).reshape(depth, 4 * width),
        out_f[128:],
    )


def solution(mesh):
    wide, narrow = mesh.shape["wide"], mesh.shape["narrow"]
    grouped = Mesh(mesh.devices.reshape(GROUP, wide // GROUP, narrow), ALL)
    vec = P(ALL)
    flat = P(ALL, None)
    mid = P(None, ALL, None)
    row = P(ALL, None, None)
    body = on_device_fast if (wide, narrow) == (8, 4) else on_device
    return jax.shard_map(
        body,
        mesh=grouped,
        in_specs=(row, vec, vec, flat, mid, P(None, ALL), mid, vec, flat, vec, flat, flat, row),
        out_specs=(row, row, vec, flat, mid, P(None, ALL), mid, vec, flat, vec, flat, flat),
        check_vma=False,
    )
```

```python
import jax
import jax.numpy as jnp
from jax import lax
from jax.experimental import pallas as pl
from jax.experimental.pallas import tpu as pltpu
from jax.sharding import Mesh
from jax.sharding import PartitionSpec as P

epsilon = 1e-05
f32 = jnp.float32
bf16 = jnp.bfloat16
GROUP = 4


def norm_rows(values, factor):
    average = jnp.mean(values, axis=-1, keepdims=True)
    centred = values - average
    spread = jnp.mean(centred * centred, axis=-1, keepdims=True)
    return centred * lax.rsqrt(spread + epsilon) * factor


def smooth(values):
    return jax.nn.gelu(values, approximate=False)


def mm(spec, a, b):
    return jnp.einsum(spec, a, b, preferred_element_type=f32)


REST = ("rep", "narrow")
ALL = ("tp", "rep", "narrow")


def to_heads(shard):
    heads, depth, width = shard.shape
    pieces = lax.all_to_all(shard.reshape(GROUP, heads // GROUP, depth, width), "tp", 0, 0)
    whole = lax.all_gather(pieces, REST, axis=0)
    return whole.transpose(2, 1, 0, 3, 4).reshape(heads // GROUP, -1, width)


def from_heads(grad):
    heads, depth, width = grad.shape
    n = lax.axis_size("rep") * lax.axis_size("narrow")
    pieces = grad.astype(bf16).reshape(heads, GROUP, n, depth // (GROUP * n), width).transpose(2, 1, 0, 3, 4)
    pieces = pieces.reshape((n * GROUP,) + pieces.shape[2:])
    share = lax.psum_scatter(pieces, REST, scatter_dimension=0, tiled=True)
    share = lax.all_to_all(share, "tp", 0, 0)
    return share.reshape(heads * GROUP, depth // (GROUP * n), width).astype(f32)


def on_device(tokens, lengths, gain_one, w_value, w_first, b_first, w_second, b_second, w_out, gain_two, w_up, w_down, grad_out):
    row_count, slots, width = tokens.shape
    heads_all = w_first.shape[0]
    heads = heads_all // GROUP
    head_size = width // heads_all
    me = lax.axis_index("tp")
    depth = w_value.shape[0]

    small = [gain_one, gain_two, b_second, b_first.reshape(-1)]
    gathered = lax.all_gather(jnp.concatenate(small), ALL, axis=0)
    n_all = gathered.shape[0]
    g1 = gathered[:, :depth].reshape(-1).astype(f32)
    g2 = gathered[:, depth : 2 * depth].reshape(-1).astype(f32)
    b2_len = b_second.shape[0]
    b2 = gathered[:, 2 * depth : 2 * depth + b2_len].reshape(heads_all, slots).astype(f32)
    b1 = gathered[:, 2 * depth + b2_len :].reshape(n_all, heads_all, depth).transpose(1, 0, 2).reshape(heads_all, width).astype(f32)
    b1 = lax.dynamic_slice_in_dim(b1, me * heads, heads, 0)
    b2 = lax.dynamic_slice_in_dim(b2, me * heads, heads, 0)

    wf = to_heads(w_first)
    ws = to_heads(w_second)
    wv = to_heads(w_value.reshape(depth, GROUP, width // GROUP).transpose(1, 0, 2))[0]
    rows = lax.all_gather(tokens, "tp", axis=0, tiled=True)
    lens = lax.all_gather(lengths, "tp", axis=0, tiled=True)
    n_rows = rows.shape[0]

    normed = norm_rows(rows.astype(f32), g1).astype(bf16)
    values = mm("rsd,de->rse", normed, wv).astype(bf16)
    per_head = values.reshape(n_rows, slots, heads, head_size).transpose(2, 0, 1, 3)
    before = mm("rsd,hde->hrse", normed, wf) + b1[:, None, None, :]
    hidden = smooth(before).astype(bf16)
    logits = mm("hrse,hej->hrsj", hidden, ws) + b2[:, None, None, :]
    visible = lax.broadcasted_iota(jnp.int32, (1, n_rows, 1, slots), 3) < lens[None, :, None, None]
    masked = jnp.where(visible, logits, f32(-1e30))
    scaled = jnp.exp(masked - jnp.max(masked, axis=-1, keepdims=True))
    probabilities = scaled / jnp.sum(scaled, axis=-1, keepdims=True)
    weights = probabilities.astype(bf16)
    mixture = mm("hrsj,hrjc->rshc", weights, per_head).astype(bf16)
    mixture = mixture.reshape(GROUP, row_count, slots, heads * head_size)
    joined = lax.all_to_all(mixture, "tp", 0, 0).transpose(1, 2, 0, 3).reshape(row_count * slots, width)

    wo = lax.all_gather(w_out, ALL, axis=0, tiled=True)
    wu = lax.all_gather(w_up, ALL, axis=0, tiled=True)
    wd = lax.all_gather(w_down, ALL, axis=0, tiled=True)
    inputs = tokens.astype(f32).reshape(-1, width)
    middle = inputs + mm("sd,de->se", joined, wo)
    normed_two, norm_two_back = jax.vjp(norm_rows, middle, g2)
    normed_two = normed_two.astype(bf16)
    upward = mm("td,df->tf", normed_two, wu)
    active, smooth_up_back = jax.vjp(smooth, upward)
    active = active.astype(bf16)
    result = middle + mm("tf,fd->td", active, wd)

    g_out = grad_out.reshape(-1, width)
    grad_branch = g_out.astype(bf16)
    grad_w_down = mm("tf,td->fd", active, grad_branch)
    grad_upward = smooth_up_back(mm("td,fd->tf", grad_branch, wd))[0].astype(bf16)
    grad_w_up = mm("td,tf->df", normed_two, grad_upward)
    grad_middle_norm, grad_gain_two = norm_two_back(mm("tf,df->td", grad_upward, wu))
    grad_middle = g_out + grad_middle_norm
    grad_attn = grad_middle.astype(bf16)
    grad_w_out = mm("sd,se->de", joined, grad_attn)
    grad_joined = mm("se,de->sd", grad_attn, wo).astype(bf16)

    grad_mixture = grad_joined.reshape(row_count, slots, GROUP, heads * head_size).transpose(2, 0, 1, 3)
    grad_mixture = lax.all_to_all(grad_mixture, "tp", 0, 0).reshape(n_rows, slots, heads, head_size).transpose(2, 0, 1, 3)
    grad_weights = mm("hrsc,hrjc->hrsj", grad_mixture, per_head)
    grad_values = mm("hrsj,hrsc->rjhc", weights, grad_mixture).astype(bf16).reshape(n_rows, slots, heads * head_size)
    centre = jnp.sum(probabilities * grad_weights, axis=-1, keepdims=True)
    grad_logits = (probabilities * (grad_weights - centre)).astype(bf16)
    grad_b_second = jnp.sum(grad_logits.astype(f32), axis=(1, 2))
    grad_w_second = mm("hrse,hrsj->hej", hidden, grad_logits)
    grad_hidden = mm("hrsj,hej->hrse", grad_logits, ws)
    smooth_value, smooth_back = jax.vjp(smooth, before)
    grad_before = smooth_back(grad_hidden)[0].astype(bf16)
    grad_b_first = jnp.sum(grad_before.astype(f32), axis=(1, 2))
    grad_w_first = mm("rsd,hrse->hde", normed, grad_before)
    grad_w_value = mm("rsd,rse->de", normed, grad_values)
    grad_normed = mm("hrse,hde->rsd", grad_before, wf) + mm("rse,de->rsd", grad_values, wv)
    grad_normed = lax.psum_scatter(grad_normed.astype(bf16), "tp", scatter_dimension=0, tiled=True)
    value, norm_one_back = jax.vjp(norm_rows, inputs, g1)
    grad_inputs_norm, grad_gain_one = norm_one_back(grad_normed.astype(f32).reshape(-1, width))
    grad_tokens = grad_middle + grad_inputs_norm

    out_first = from_heads(grad_w_first)
    out_second = from_heads(grad_w_second)
    out_value = from_heads(grad_w_value[None]).transpose(1, 0, 2).reshape(depth, width)

    def share(grad):
        return lax.psum_scatter(grad.astype(bf16), ALL, scatter_dimension=0, tiled=True).astype(f32)

    vec_tp = jnp.concatenate([grad_b_first.reshape(-1), grad_b_second.reshape(-1)])
    vec_tp = lax.dynamic_update_slice_in_dim(jnp.zeros((GROUP, vec_tp.shape[0]), f32), vec_tp[None], me, 0)
    vec = jnp.concatenate([vec_tp.reshape(-1), grad_gain_one, grad_gain_two])
    vec = lax.psum(vec, ALL)
    index = (me * lax.axis_size("rep") + lax.axis_index("rep")) * lax.axis_size("narrow") + lax.axis_index("narrow")
    n_tp = GROUP * (heads * width + heads * slots)
    tp_part = vec[:n_tp].reshape(GROUP, -1)
    gb1 = tp_part[:, : heads * width].reshape(heads_all, width)
    gb2 = tp_part[:, heads * width :].reshape(-1)
    gb1 = lax.dynamic_slice_in_dim(gb1, index * depth, depth, 1)
    gb2 = lax.dynamic_slice_in_dim(gb2, index * b2_len, b2_len, 0)
    gg1 = lax.dynamic_slice_in_dim(vec[n_tp : n_tp + width], index * depth, depth, 0)
    gg2 = lax.dynamic_slice_in_dim(vec[n_tp + width :], index * depth, depth, 0)
    shape = tokens.shape
    return (
        result.reshape(shape),
        grad_tokens.reshape(shape),
        gg1,
        out_value,
        out_first,
        gb1,
        out_second,
        gb2,
        share(grad_w_out),
        gg2,
        share(grad_w_up),
        share(grad_w_down),
    )


MESH = pl.DeviceIdType.MESH
VMEM_LIMIT = 60 * 2**20
ANY = pl.BlockSpec(memory_space=pl.ANY)
FULL = pl.BlockSpec(memory_space=pltpu.VMEM)
DMA = pltpu.SemaphoreType.DMA


def shape_of(dims, kind):
    return jax.ShapeDtypeStruct(dims, kind)


def dot_nt(a, b):
    return lax.dot_general(a, b, (((1,), (1,)), ((), ())), preferred_element_type=f32)


def dot_tn(a, b):
    return lax.dot_general(a, b, (((0,), (0,)), ((), ())), preferred_element_type=f32)


def dot_nn(a, b):
    return lax.dot_general(a, b, (((1,), (0,)), ((), ())), preferred_element_type=f32)


def place():
    return lax.axis_index("tp"), lax.axis_index("rep"), lax.axis_index("narrow")


def group_peers():
    t, c, z = place()
    along_x = t + 1 - 2 * (t % 2)
    along_y = (t + 2) % GROUP
    return [along_x, along_y, GROUP - 1 - t]


def line_peers():
    z = lax.axis_index("narrow")
    return [(z + k) % 4 for k in (1, 2, 3)]


def line_place():
    z = lax.axis_index("narrow")
    side = z // 2
    end, inner = 3 * side, 1 + side
    return end, inner, 2 - side, 3 - 3 * side, end + inner - z, z == inner


class Spread:
    def __init__(self, slabs, send, recv, source=None):
        t, c, z = place()
        end, inner, other, far, near, is_inner = line_place()
        self.is_inner = is_inner
        move = lambda o, k, to: remote(slabs(o), slabs(o), send.at[k], recv.at[o], (t, c, to))
        source = slabs(z) if source is None else source
        give = lambda k, to: remote(source, slabs(z), send.at[k], recv.at[z], (t, c, to))
        self.own = lambda: [give(0, other), give(1, near)]
        self.on = lambda: [move(other, 2, end), move(far, 3, end)]
        self.near = lambda: move(near, 0, near)

    def begin(self):
        start(self.own())

    def forward(self):
        @pl.when(self.is_inner)
        def _():
            for copy in self.on():
                copy.wait_recv()
            start(self.on())

    def finish(self):
        self.near().wait_recv()

        @pl.when(jnp.logical_not(self.is_inner))
        def _():
            for copy in self.on():
                copy.wait_recv()

        for copy in self.own():
            copy.wait_send()

        @pl.when(self.is_inner)
        def _():
            for copy in self.on():
                copy.wait_send()


class Gather:
    def __init__(self, slabs, land, add, send, recv):
        t, c, z = place()
        end, inner, other, far, near, is_inner = line_place()
        self.is_inner, self.add, self.z = is_inner, add, z
        self.other, self.far = other, far
        move = lambda o, slot, k, to: remote(slabs(o), land(slot), send.at[k], recv.at[slot], (t, c, to))
        self.out = lambda: [move(far, 2, 0, inner), move(other, 1, 1, inner), move(inner, 0, 2, inner)]
        self.back = lambda: [move(end, 0, 2, end)]
        self.on_far = lambda: [move(far, 1, 0, far)]
        self.on_other = lambda: [move(other, 3, 1, other)]
        self.got = lambda slot: move(z, slot, 0, near).wait_recv()

    def begin(self):
        @pl.when(self.is_inner)
        def _():
            start(self.back())

        @pl.when(jnp.logical_not(self.is_inner))
        def _():
            start(self.out())

    def forward(self):
        @pl.when(self.is_inner)
        def _():
            self.got(2)
            self.add(self.far, 2)
            start(self.on_far())
            self.got(1)
            self.add(self.other, 1)
            start(self.on_other())

    def finish(self):
        self.got(0)
        self.add(self.z, 0)

        @pl.when(self.is_inner)
        def _():
            self.got(3)
            self.add(self.z, 3)
            for copy in self.back() + self.on_far() + self.on_other():
                copy.wait_send()

        @pl.when(jnp.logical_not(self.is_inner))
        def _():
            self.got(1)
            self.add(self.z, 1)
            for copy in self.out():
                copy.wait_send()


def greet(devices):
    barrier = pltpu.get_barrier_semaphore()
    for device in devices:
        pl.semaphore_signal(barrier, inc=1, device_id=device, device_id_type=MESH)


def met(count):
    pl.semaphore_wait(pltpu.get_barrier_semaphore(), count)


def remote(src, dst, send, recv, device):
    return pltpu.make_async_remote_copy(
        src_ref=src, dst_ref=dst, send_sem=send, recv_sem=recv, device_id=device, device_id_type=MESH
    )


def local(src, dst, sem):
    return pltpu.make_async_copy(src, dst, sem)


def start(copies):
    for copy in copies:
        copy.start()


def wait(copies):
    for copy in copies:
        copy.wait()


def square():
    t, c, z = place()
    y, x = t // 2, t % 2
    tps = group_peers()
    slow, fast = (1 - c) * y + c * x, (1 - c) * x + c * y
    fast_peer = (1 - c) * tps[0] + c * tps[1]
    slow_peer = (1 - c) * tps[1] + c * tps[0]
    return slow, fast, (slow_peer, c, z), (fast_peer, c, z)


def gelu_pair(v):
    cdf = 0.5 * (1.0 + lax.erf(v * 0.7071067811865476))
    return v * cdf, cdf + v * (jnp.exp(-0.5 * v * v) * 0.3989422804014327)


def centre_rows(v):
    shifted = v - jnp.mean(v, axis=-1, keepdims=True)
    scale = lax.rsqrt(jnp.mean(shifted * shifted, axis=-1, keepdims=True) + epsilon)
    return shifted * scale, scale


ROWS = ((0, 144), (144, 272), (272, 384))


def part(i):
    return slice(*ROWS[i])


def attend_kernel(
    tokens, extra, w_first, w_second, w_out, w_up, w_down,
    wf, ws, wv, small, normed, values, hid, slope, prob, joined, lf,
    pa, pf, la, lt, nrm, val, cols, b2, masks, join, own, s1, r1, s2, r2, s3, r3, st, rt, s1f, r1f, sf, rf, sj, rj,
):
    h, r = pl.program_id(0), pl.program_id(1)
    width = wf.shape[-1]
    heads = w_first.shape[0] // GROUP
    t, c, z = place()
    sibling = (t, 1 - c, z)
    tps, zs = group_peers(), line_peers()
    slow, fast, slow_dev, fast_dev = square()

    a1 = lambda i: [
        remote(pa.at[p, part(i)], la.at[c, z, t, part(i)], s1.at[i, k], r1.at[i, k], (p, c, z))
        for k, p in enumerate(tps)
    ]
    a2 = lambda i: Spread(lambda o: la.at[c, o, :, part(i)], s2.at[i], r2.at[i])
    a3 = lambda i: [remote(la.at[c, :, :, part(i)], la.at[c, :, :, part(i)], s3.at[i], r3.at[i], sibling)]
    mine = lambda i: [local(pa.at[t, part(i)], la.at[c, z, t, part(i)], own.at[i])]
    mine_t = lambda: [local(tokens.at[0], lt.at[3], own.at[heads])]
    mine_f = lambda: [local(pf, lf.at[c, slow, fast, z], own.at[heads + 1])]
    mine_j = lambda: [local(join.at[3], joined.at[t], own.at[heads + 2])]
    tok_fast = lambda: remote(tokens.at[0], lt.at[c], st.at[0], rt.at[0], fast_dev)
    tok_slow = lambda: remote(tokens.at[0], lt.at[1 - c], st.at[1], rt.at[1], slow_dev)
    tok_on = lambda: remote(lt.at[c], lt.at[2], st.at[2], rt.at[2], slow_dev)
    cut = lambda k: slice(*((0, 128), (128, 224))[k])
    f1 = lambda k: Spread(lambda o: lf.at[c, slow, fast, o, cut(k)], s1f.at[k], r1f.at[k], pf.at[cut(k)])

    def whole(k, spot, n, device):
        piece = lf.at[spot + (slice(None),) * (4 - len(spot)) + (cut(k),)]
        return [remote(piece, piece, sf.at[k, n], rf.at[k, n], device)]

    f2 = lambda k: whole(k, (c, slow, fast), 0, fast_dev)
    f3 = lambda k: whole(k, (c, slow), 1, slow_dev)
    f4 = lambda k: whole(k, (c, slow), 2, sibling)
    f5 = lambda k: whole(k, (c, 1 - slow), 3, sibling)
    out_j = lambda k: [remote(join.at[k], joined.at[t], sj.at[k], rj.at[k], (tps[k], c, z))]

    def at_step(i, j):
        return pl.when((h == i) & (r == j))

    @at_step(0, 0)
    def _():
        greet([(p, c, z) for p in tps] + [(t, c, p) for p in zs] + [sibling])
        blocks = lambda v: [v[:, k : k + 256] for k in range(0, v.shape[1], 256)]
        ups = [w_up[:, k : k + width].astype(f32) for k in range(0, w_up.shape[1], width)]
        pf[0:96] = jnp.concatenate(ups, 0).astype(bf16)
        pf[96:128] = jnp.concatenate([w_out[...].astype(f32), jnp.zeros((8, width), f32)], 0).astype(bf16)
        pf[128:224] = w_down[...]
        for p in range(GROUP):
            stack = [extra[p].astype(f32)]
            for i in range(heads):
                stack += blocks(w_first[heads * p + i].astype(f32)) + blocks(w_second[heads * p + i].astype(f32))
            pa[p] = jnp.concatenate(stack, 0).astype(bf16)
        met(7)
        f1(0).begin()
        for i in range(heads):
            start(mine(i) + a1(i))
        start(mine_f() + mine_t())
        wait(mine(0) + a1(0))
        a2(0).begin()
        wait(mine(1) + a1(1))
        wait(mine(2) + a1(2))
        start([tok_fast(), tok_slow()])
        f1(0).forward()
        f1(1).begin()
        a2(0).forward()
        a2(1).begin()
        tok_fast().wait_recv()
        tok_on().start()
        f1(0).finish()
        wait(mine_f())
        start(f2(0))
        a2(0).finish()
        start(a3(0))
        f1(1).forward()
        a2(1).forward()
        a2(2).begin()
        wait(mine_t() + a3(0))
        tok_fast().wait_send()
        tok_slow().wait()
        tok_on().wait()

    @at_step(0, 1)
    def _():
        wait(f2(0))
        start(f3(0) + f4(0))
        f1(1).finish()
        start(f2(1))

    @at_step(0, 3)
    def _():
        a2(2).forward()

    @at_step(1, 0)
    def _():
        a2(1).finish()
        start(a3(1))
        wait(a3(1))

    @at_step(1, 1)
    def _():
        wait(f2(1))
        start(f3(1) + f4(1))

    @at_step(2, 0)
    def _():
        a2(2).finish()
        start(a3(2))
        wait(f3(0))
        start(f5(0))
        wait(a3(2))

    def unpack(i):
        def one(tt, carry):
            for cc in range(2):
                for zz in range(0, 4, 2):
                    at = pl.ds(pl.multiple_of((tt * 8 + cc * 4 + zz) * 24, 48), 48)

                    def block(first):
                        low = first // 16 * 16
                        both = [la[cc, zz + k, tt, low : low + 32].astype(f32)[first - low :][:24] for k in range(2)]
                        return jnp.concatenate(both, 0)

                    base = 24 + 120 * i
                    for j in range(3):
                        wf[0, at, 256 * j : 256 * j + 256] = block(base + 24 * j).astype(bf16)
                    for j in range(2):
                        ws[0, at, 256 * j : 256 * j + 256] = block(base + 72 + 24 * j).astype(bf16)
                    if i == 0:
                        both = block(0)
                        cols[at, :] = both[:, 128:256]
                        lane = lax.broadcasted_iota(jnp.int32, both.shape, 1)
                        wv[at, :] = jnp.where(lane < 192, both, 0.0).astype(bf16)

            return carry

        lax.fori_loop(0, GROUP, one, 0)

    for i in range(heads):

        @at_step(i, 0)
        def _():
            unpack(i)

    @at_step(0, 0)
    def _():
        small[...] = cols[...].T[64:72]
        mine_rows = cols[pl.ds(pl.multiple_of(t * 192, 192), 192), :].astype(bf16)
        lane = lax.broadcasted_iota(jnp.int32, (128, 512), 0)
        spot = lax.broadcasted_iota(jnp.int32, (128, 512), 1)
        spread = dot_nn(mine_rows, jnp.where(lane - 69 == spot % 8, 1.0, 0.0).astype(bf16))
        row = lax.broadcasted_iota(jnp.int32, (64, 512), 0)
        spot = lax.broadcasted_iota(jnp.int32, (64, 512), 1)
        for i in range(heads):
            picked = jnp.where(row == spot // 8, spread[64 * i : 64 * i + 64], 0.0)
            b2[i] = jnp.broadcast_to(jnp.sum(picked, axis=0, keepdims=True), (8, 512))
        for k, p in enumerate(tps + [t]):
            line = cols[pl.ds(pl.multiple_of((p * 8 + c * 4 + z) * 24, 8), 8), :]
            lane = lax.broadcasted_iota(jnp.int32, line.shape, 1)
            digits = jnp.where(lane == 77, 16.0 * line, jnp.where(lane == 78, line, 0.0))
            length = jnp.sum(digits, axis=1, keepdims=True)
            spot = lax.broadcasted_iota(jnp.int32, (8, 512), 1).astype(f32)
            masks[k] = jnp.where(spot < length, 0.0, -1e30)

    @pl.when(h == 0)
    def _():
        unit, _ = centre_rows(lt[r].astype(f32))
        out = (unit * small[3:4]).astype(bf16)
        nrm[r] = out
        normed[0] = out
        v = dot_nn(out, wv[...]).astype(bf16)
        val[r] = v
        values[0] = v

    row = lax.broadcasted_iota(jnp.int32, (8, width), 0)
    b1 = jnp.sum(jnp.where(row == h, small[...], 0.0), axis=0, keepdims=True)
    shift = b2[h, 0:1] + masks[r, 0:1]
    tile = pl.ds(pl.multiple_of((h // 2) * 128, 128), 128)
    step = 256
    for m in range(0, 512, step):
        at = slice(m, m + step)
        before = dot_nn(nrm[r, at, :], wf[0]) + b1
        out, grad = gelu_pair(before)
        hidden = out.astype(bf16)
        hid[0, 0, at, :] = hidden
        slope[0, 0, at, :] = grad.astype(bf16)
        logits = dot_nn(hidden, ws[0]) + shift
        e = jnp.exp(logits - jnp.max(logits, axis=-1, keepdims=True))
        p = (e * (1.0 / jnp.sum(e, axis=-1, keepdims=True))).astype(bf16)
        prob[0, 0, at, :] = p
        mix = dot_nn(p, val[r, :, tile])
        lane = lax.broadcasted_iota(jnp.int32, mix.shape, 1)
        old = join[r, at, tile].astype(f32)
        join[r, at, tile] = jnp.where((h == 1) & (lane < 64), old, mix).astype(bf16)

    for k in range(3):

        @at_step(2, k)
        def _():
            start(out_j(k))

    @at_step(2, 2)
    def _():
        wait(f3(1))
        start(f5(1))

    @at_step(2, 3)
    def _():
        start(mine_j())
        for k in range(2):
            wait(f4(k) + f5(k))
        for k in range(3):
            wait(out_j(k))
        wait(mine_j())


def attend_call(tokens, extra, w_first, w_second, w_out, w_up, w_down):
    _, slots, width = tokens.shape
    heads = w_first.shape[0] // GROUP
    by_row = lambda h, r: (jnp.where(h == 0, r, GROUP - 1), 0, 0)
    by_head = lambda h, r: (h, 0, 0)
    both = lambda h, r: (h, r, 0, 0)
    rows_f = 2 * w_down.shape[0] + 32
    return pl.pallas_call(
        attend_kernel,
        grid=(heads, GROUP),
        out_shape=(
            shape_of((heads, width, width), bf16),
            shape_of((heads, width, slots), bf16),
            shape_of((width, 256), bf16),
            shape_of((8, width), f32),
            shape_of((GROUP, slots, width), bf16),
            shape_of((GROUP, slots, 256), bf16),
            shape_of((heads, GROUP, slots, width), bf16),
            shape_of((heads, GROUP, slots, width), bf16),
            shape_of((heads, GROUP, slots, slots), bf16),
            shape_of((GROUP, slots, 256), bf16),
            shape_of((2, 2, 2, 4, rows_f, width), bf16),
        ),
        in_specs=[ANY] + [FULL] * 6,
        out_specs=(
            pl.BlockSpec((1, width, width), by_head),
            pl.BlockSpec((1, width, slots), by_head),
            pl.BlockSpec((width, 256), lambda h, r: (0, 0)),
            pl.BlockSpec((8, width), lambda h, r: (0, 0)),
            pl.BlockSpec((1, slots, width), by_row),
            pl.BlockSpec((1, slots, 256), by_row),
            pl.BlockSpec((1, 1, slots, width), both),
            pl.BlockSpec((1, 1, slots, width), both),
            pl.BlockSpec((1, 1, slots, slots), both),
            ANY,
            ANY,
        ),
        scratch_shapes=[
            pltpu.VMEM((GROUP, 384, 256), bf16),
            pltpu.VMEM((rows_f, width), bf16),
            pltpu.VMEM((2, 4, GROUP, 384, 256), bf16),
            pltpu.VMEM((GROUP, slots, width), bf16),
            pltpu.VMEM((GROUP, slots, width), bf16),
            pltpu.VMEM((GROUP, slots, 256), bf16),
            pltpu.VMEM((width, 128), f32),
            pltpu.VMEM((heads, 8, slots), f32),
            pltpu.VMEM((GROUP, 8, slots), f32),
            pltpu.VMEM((GROUP, slots, 256), bf16),
            DMA((heads + 3,)),
            DMA((heads, 3)),
            DMA((heads, 3)),
            DMA((heads, 4)),
            DMA((heads, 4)),
            DMA((heads,)),
            DMA((heads,)),
            DMA((3,)),
            DMA((3,)),
            DMA((2, 4)),
            DMA((2, 4)),
            DMA((2, 4)),
            DMA((2, 4)),
            DMA((3,)),
            DMA((3,)),
        ],
        compiler_params=pltpu.CompilerParams(collective_id=1, has_side_effects=True, vmem_limit_bytes=VMEM_LIMIT),
    )(tokens, extra, w_first, w_second, w_out, w_up, w_down)


def slab(t, c, z):
    y, x = t // 2, t % 2
    return (0, y, x, z) if c == 0 else (1, x, y, z)


def ffn_kernel(
    lf_far, joined, tokens, small, gout, result, gmid, gmix, half, gg2,
    lf, loads, middles, gf, gj, more, wu, wo, n2, acc, gn2, gwu, own, sg, rg, sx, rx,
):
    width = tokens.shape[-1]
    me, core, z_me = place()
    tps = group_peers()
    sibling = (me, 1 - core, z_me)
    parts = (slice(0, 96), slice(128, 224), slice(96, 128))
    cross = lambda k: [
        remote(
            gf.at[1 - core, :, :, :, parts[k], :], more.at[:, :, :, parts[k], :], sx.at[k], rx.at[k], sibling
        )
    ]
    out_g = lambda k: [remote(gj.at[tps[k]], gmix.at[k], sg.at[k], rg.at[k], (tps[k], core, z_me))]
    greet([(p, core, z_me) for p in tps] + [sibling])
    load = lambda k: local(lf_far.at[:, :, :, :, parts[k], :], lf.at[:, :, :, :, parts[k], :], loads.at[k])
    for k in (2, 0, 1):
        load(k).start()
    load(2).wait()
    wo[...] = jnp.zeros_like(wo)
    for t in range(GROUP):
        for c in range(2):
            for z in range(0, 4, 2):
                pair = [lf[slab(t, c, z + k) + (slice(96, 128),)].astype(f32)[0:24] for k in range(2)]
                wo[t, (c * 4 + z) * 24 : (c * 4 + z) * 24 + 48, :] = jnp.concatenate(pair, 0).astype(bf16)
    middle = tokens[...].astype(f32)
    for t in range(GROUP):
        middle = middle + dot_nn(joined[t], wo[t])
    acc[...] = middle
    middles[...] = middle
    g2 = small[4:5]
    unit, _ = centre_rows(middle)
    n2[...] = (unit * g2).astype(bf16)
    gn2[...] = jnp.zeros_like(gn2)
    load(0).wait()
    load(1).wait()

    def block(p, carry):
        rows = pl.ds(pl.multiple_of(p * 48, 16), 48)
        for t in range(GROUP):
            for c in range(2):
                for z in range(0, 4, 2):
                    ends = [lf[slab(t, c, z + k) + (rows,)].astype(f32) for k in range(2)]
                    at = (t * 8 + c * 4 + z) * 24
                    for k in range(2):
                        both = jnp.concatenate([e[24 * k : 24 * k + 24] for e in ends], 0)
                        wu[k, at : at + 48, :] = both.astype(bf16)
        branch = gout[...].astype(bf16)
        for k in range(2):
            wd = jnp.concatenate(
                [lf[0, p, k, :, 128:224, :].reshape(384, width), lf[1, k, p, :, 128:224, :].reshape(384, width)], 0
            )
            up = dot_nn(n2[...], wu[k])
            act, slope = gelu_pair(up)
            act = act.astype(bf16)
            acc[...] += dot_nn(act, wd)
            gup = (dot_nt(branch, wd) * slope).astype(bf16)
            gwd = dot_tn(act, branch).astype(bf16)
            gf[0, p, k, :, 128:224, :] = gwd[:384].reshape(4, 96, width)
            gf[1, k, p, :, 128:224, :] = gwd[384:].reshape(4, 96, width)
            gwu[k] = dot_tn(n2[...], gup)
            gn2[...] += dot_nt(gup, wu[k])
        for t in range(GROUP):
            for c in range(2):
                for z in range(4):
                    at = (t * 8 + c * 4 + z) * 24
                    both = jnp.concatenate([gwu[0, at : at + 24, :], gwu[1, at : at + 24, :]], 0)
                    gf[slab(t, c, z) + (rows,)] = both.astype(bf16)
        return carry

    lax.fori_loop(0, 2, block, 0)
    met(4)
    start(cross(0) + cross(1))
    result[...] = acc[...]
    unit, scale = centre_rows(middles[...])
    gn = gn2[...]
    gg2[...] = jnp.sum((gn * unit).reshape(-1, 8, width), axis=0)
    gu = gn * g2
    back = scale * (
        gu - jnp.mean(gu, axis=-1, keepdims=True) - unit * jnp.mean(gu * unit, axis=-1, keepdims=True)
    )
    gm = gout[...] + back
    gmid[...] = gm
    ga = gm.astype(bf16)
    for t in range(GROUP):
        gj[t] = dot_nt(ga, wo[t]).astype(bf16)
    for k in range(3):
        start(out_g(k))
    mine = local(gj.at[me], gmix.at[3], own)
    mine.start()
    for t in range(GROUP):
        gwo = dot_tn(joined[t], ga)
        for c in range(2):
            for z in range(4):
                at = (c * 4 + z) * 24
                padded = jnp.concatenate([gwo[at : at + 24, :], jnp.zeros((8, width), f32)], 0)
                gf[slab(t, c, z) + (slice(96, 128),)] = padded.astype(bf16)
    start(cross(2))
    for k in range(3):
        wait(cross(k))

        def fold(i, carry):
            for j in range(2):
                for z in range(4):
                    spot = (i, j, z, parts[k])
                    half[spot] = (gf[(core,) + spot].astype(f32) + more[spot].astype(f32)).astype(bf16)
            return carry

        lax.fori_loop(0, 2, fold, 0)
    for k in range(3):
        wait(out_g(k))
    mine.wait()


def ffn_call(lf, joined, tokens, small, gout):
    slots, width = tokens.shape
    return pl.pallas_call(
        ffn_kernel,
        out_shape=(
            shape_of((slots, width), f32),
            shape_of((slots, width), f32),
            shape_of(joined.shape, bf16),
            shape_of(lf.shape[1:], bf16),
            shape_of((8, width), f32),
        ),
        in_specs=[ANY] + [FULL] * 4,
        out_specs=(FULL, FULL, ANY, FULL, FULL),
        scratch_shapes=[
            pltpu.VMEM(lf.shape, bf16),
            DMA((3,)),
            pltpu.VMEM((slots, width), f32),
            pltpu.VMEM(lf.shape, bf16),
            pltpu.VMEM(joined.shape, bf16),
            pltpu.VMEM(lf.shape[1:], bf16),
            pltpu.VMEM((2, width, width), bf16),
            pltpu.VMEM((GROUP, 256, width), bf16),
            pltpu.VMEM((slots, width), bf16),
            pltpu.VMEM((slots, width), f32),
            pltpu.VMEM((slots, width), f32),
            pltpu.VMEM((2, width, width), f32),
            DMA,
            DMA((3,)),
            DMA((3,)),
            DMA((3,)),
            DMA((3,)),
        ],
        compiler_params=pltpu.CompilerParams(collective_id=2, has_side_effects=True, vmem_limit_bytes=VMEM_LIMIT),
    )(lf, joined, tokens, small, gout)


def back_kernel(
    wf, ws, wv, normed, values, hid, slope, prob, gmix, gg2, half, tokens, gmid, small, out_f, out_a, out_s, gtok,
    awf, aws, ab1, ab2, gn, gv, awv, ag1, stash, ga, gs, gnb, nb, fs, fb2, fb3, fb4, cb1, cb2, sb1, sb2,
    own, s1, r1, s2, r2, s3, r3, sn, rn, sf, rf, s4, r4, sv, rv,
):
    step, r = pl.program_id(0), pl.program_id(1)
    width = wf.shape[-1]
    heads = ab1.shape[0]
    h = heads - 1 - step
    t, c, z = place()
    sibling = (t, 1 - c, z)
    tps, zs = group_peers(), line_peers()
    slow, fast, slow_dev, fast_dev = square()

    a1 = lambda i: [remote(ga.at[1 - c, :, :, part(i)], cb1.at[:, :, part(i)], s1.at[i], r1.at[i], sibling)]
    def add_heads(i):
        def add(o, slot):
            def one(j, carry):
                here = ga[c, o, j, part(i)].astype(f32) + cb2[slot, j, part(i)].astype(f32)
                ga[c, o, j, part(i)] = here.astype(bf16)
                return carry

            lax.fori_loop(0, GROUP, one, 0)

        return add

    def add_f(o, slot):
        fs[fast, o] = (fs[fast, o].astype(f32) + fb4[slot].astype(f32)).astype(bf16)

    a2 = lambda i: Gather(
        lambda o: ga.at[c, o, :, part(i)], lambda k: cb2.at[k, :, part(i)], add_heads(i), s2.at[i], r2.at[i]
    )
    a3 = lambda i: [
        remote(ga.at[c, z, p, part(i)], out_a.at[t, part(i)], s3.at[i, k], r3.at[i, k], (p, c, z))
        for k, p in enumerate(tps)
    ]
    mine = lambda i: [local(ga.at[c, z, t, part(i)], out_a.at[t, part(i)], own.at[i])]
    mine_f = lambda: [local(half.at[slow], fs, own.at[heads])]
    v1 = lambda: [remote(gs.at[1 - c], sb1, sv.at[0], rv.at[0], sibling)]
    v2 = lambda: [remote(gs.at[c, p], sb2.at[k], sv.at[1 + k], rv.at[1 + k], (t, c, p)) for k, p in enumerate(zs)]
    f2 = lambda: [remote(half.at[1 - slow], fb2, sf.at[0], rf.at[0], slow_dev)]
    f3 = lambda: [remote(fs.at[1 - fast], fb3, sf.at[1], rf.at[1], fast_dev)]
    f4 = lambda: Gather(lambda o: fs.at[fast, o], lambda k: fb4.at[k], add_f, s4, r4)
    out_n = lambda k: [remote(gnb.at[k], nb.at[k], sn.at[k], rn.at[k], (tps[k], c, z))]

    def at_step(i, j):
        return pl.when((step == i) & (r == j))

    def meet(i):
        wait(a1(i))

        def line(k, carry):
            for j in range(GROUP):
                here = ga[c, k, j, part(i)].astype(f32) + cb1[k, j, part(i)].astype(f32)
                ga[c, k, j, part(i)] = here.astype(bf16)
            return carry

        lax.fori_loop(0, 4, line, 0)
        a2(i).begin()

    def deal(i):
        a2(i).finish()
        start(mine(i) + a3(i))

    def add_slabs(total, more):
        def one(k, carry):
            fs[total, k] = (fs[total, k].astype(f32) + more[k].astype(f32)).astype(bf16)
            return carry

        lax.fori_loop(0, 4, one, 0)

    @at_step(0, 0)
    def _():
        greet([(p, c, z) for p in tps] + [(t, c, p) for p in zs] + [sibling])
        met(7)
        start(f2() + mine_f())

    @at_step(1, 0)
    def _():
        meet(2)

    @at_step(1, 2)
    def _():
        a2(2).forward()

    @at_step(1, 3)
    def _():
        wait(f2() + mine_f())
        add_slabs(1 - fast, fb2.at[1 - fast])
        start(f3())
        add_slabs(fast, fb2.at[fast])

    @at_step(2, 0)
    def _():
        meet(1)

    @at_step(2, 1)
    def _():
        deal(2)

    @at_step(2, 2)
    def _():
        a2(1).forward()

    @at_step(2, 3)
    def _():
        wait(f3())
        add_slabs(fast, fb3)
        f4().begin()

    @pl.when(r == 0)
    def _():
        awf[...] = jnp.zeros_like(awf)
        aws[...] = jnp.zeros_like(aws)
        ab1[h] = jnp.zeros(ab1.shape[1:], f32)
        ab2[h] = jnp.zeros(ab2.shape[1:], f32)

    tile = pl.ds(pl.multiple_of((h // 2) * 128, 128), 128)
    lane = lax.broadcasted_iota(jnp.int32, (512, 128), 1)
    gm = jnp.where(lane // 64 == h % 2, gmix[0, :, tile].astype(f32), 0.0).astype(bf16)
    gw = dot_nt(gm, values[0, :, tile])
    p = prob[0, 0]
    p32 = p.astype(f32)
    gl = (p32 * (gw - jnp.sum(p32 * gw, axis=-1, keepdims=True))).astype(bf16)
    ab2[h] += jnp.sum(gl.astype(f32).reshape(-1, 8, 512), axis=0)
    gvh = dot_tn(p, gm)

    @pl.when(h != 0)
    def _():
        gv[r, :, tile] = gvh

    @pl.when(h == 0)
    def _():
        gv[r, :, tile] += gvh

    aws[...] += dot_tn(hid[0, 0], gl)
    gb = (dot_nt(gl, ws[0]) * slope[0, 0].astype(f32)).astype(bf16)
    ab1[h] += jnp.sum(gb.astype(f32).reshape(-1, 8, width), axis=0)
    awf[...] += dot_tn(normed[0], gb)
    more_gn = dot_nt(gb, wf[0])

    @pl.when(step == 0)
    def _():
        gn[r] = more_gn

    @pl.when(step == 1)
    def _():
        gn[r] += more_gn

    @pl.when(step == 2)
    def _():
        gvb = gv[r].astype(bf16)
        total = gn[r] + more_gn + dot_nt(gvb, wv[...])
        gn[r] = total
        both = (total * normed[0].astype(f32)).reshape(-1, 8, width)
        ag1[...] = jnp.where(r == 0, 0.0, ag1[...]) + jnp.sum(both, axis=0)
        more = dot_tn(normed[0], gvb)

        @pl.when(r == 0)
        def _():
            awv[...] = more

        @pl.when(r != 0)
        def _():
            awv[...] += more

        for k in range(3):

            @pl.when(r == k)
            def _():
                gnb[k] = total.astype(bf16)
                start(out_n(k))

    def pack(i):
        def one(tt, carry):
            for cc in range(2):
                for zz in range(4):
                    at = pl.ds(pl.multiple_of((tt * 8 + cc * 4 + zz) * 24, 8), 24)
                    stack = [awf[at, 256 * j : 256 * j + 256] for j in range(3)]
                    stack += [aws[at, 256 * j : 256 * j + 256] for j in range(2)]
                    if i == 0:
                        stack = [awv[at, :]] + stack
                    if i == 1:
                        stack = stack + [stash[cc, zz, tt]]
                    whole = jnp.concatenate(stack, 0)
                    if i == 2:
                        stash[cc, zz, tt] = whole[0:8]
                        whole = whole[8:]
                    ga[cc, zz, tt, part(i)] = whole.astype(bf16)
            return carry

        lax.fori_loop(0, GROUP, one, 0)
        start(a1(i))

    @at_step(0, 3)
    def _():
        pack(2)

    @at_step(1, 3)
    def _():
        pack(1)

    @at_step(2, 3)
    def _():
        row = lax.broadcasted_iota(jnp.int32, (128, width), 0)
        stack = jnp.zeros((128, width), f32)
        gains = jnp.sum(ag1[...], axis=0, keepdims=True) / small[3:4]
        lines = [jnp.sum(ab1[i], axis=0, keepdims=True) for i in range(heads)]
        for k, line in enumerate(lines + [gains, jnp.sum(gg2[...], axis=0, keepdims=True)]):
            stack = jnp.where(row == 64 + k, line, stack)
        lane = lax.broadcasted_iota(jnp.int32, (width, 128), 1)
        awv[:, 128:256] = jnp.where(lane < 64, awv[:, 128:256], stack.T)
        pack(0)

    @at_step(2, 3)
    def _():
        flat = jnp.concatenate([jnp.sum(ab2[k], axis=0, keepdims=True) for k in range(3)], 1)
        flat = jnp.broadcast_to(flat, (8, 1536))
        for cc in range(2):
            for zz in range(4):
                s = (cc * 4 + zz) * 192
                gs[cc, zz] = (pltpu.roll(flat, 1536 - s, 1) if s else flat)[:, 0:256]
        start(v1())
        meet(0)
        wait(v1())
        gs[c] += sb1[...]
        start(v2())
        f4().forward()
        for k in range(3):
            wait(out_n(k))
        a2(0).forward()

        def ln_back(i, carry):
            at = pl.ds(pl.multiple_of(i * 128, 128), 128)
            g = gn[3, at, :] + nb[0, at, :].astype(f32) + nb[1, at, :].astype(f32) + nb[2, at, :].astype(f32)
            unit, scale = centre_rows(tokens[at, :].astype(f32))
            gu = g * small[3:4]
            back = scale * (
                gu - jnp.mean(gu, axis=-1, keepdims=True) - unit * jnp.mean(gu * unit, axis=-1, keepdims=True)
            )
            gtok[at, :] = gmid[at, :] + back
            return carry

        lax.fori_loop(0, 4, ln_back, 0)
        deal(1)
        f4().finish()
        out_f[...] = fs[fast, z].astype(f32)
        wait(v2())
        out_s[...] = gs[c, z] + sb2[0] + sb2[1] + sb2[2]
        deal(0)
        for i in range(heads):
            wait(mine(i) + a3(i))


def back_call(wf, ws, wv, normed, values, hid, slope, prob, gmix, gg2, half, tokens, gmid, small):
    heads, width, slots = ws.shape
    rows = half.shape[-2]
    by_head = lambda h, r: (heads - 1 - h, 0, 0)
    row = lambda h, r: (r, 0, 0)
    both = lambda h, r: (heads - 1 - h, r, 0, 0)
    flat = lambda h, r: (0, 0)
    return pl.pallas_call(
        back_kernel,
        grid=(heads, GROUP),
        out_shape=(
            shape_of((rows, width), f32),
            shape_of((GROUP, 384, 256), bf16),
            shape_of((8, 256), f32),
            shape_of(tokens.shape, f32),
        ),
        in_specs=[
            pl.BlockSpec((1, width, width), by_head),
            pl.BlockSpec((1, width, slots), by_head),
            pl.BlockSpec((width, 256), flat),
            pl.BlockSpec((1, slots, width), row),
            pl.BlockSpec((1, slots, 256), row),
            pl.BlockSpec((1, 1, slots, width), both),
            pl.BlockSpec((1, 1, slots, width), both),
            pl.BlockSpec((1, 1, slots, slots), both),
            pl.BlockSpec((1, slots, 256), row),
            pl.BlockSpec((8, width), flat),
            ANY,
            FULL,
            FULL,
            pl.BlockSpec((8, width), flat),
        ],
        out_specs=(FULL, ANY, FULL, FULL),
        scratch_shapes=[
            pltpu.VMEM((width, width), f32),
            pltpu.VMEM((width, slots), f32),
            pltpu.VMEM((heads, 8, width), f32),
            pltpu.VMEM((heads, 8, slots), f32),
            pltpu.VMEM((GROUP, slots, width), f32),
            pltpu.VMEM((GROUP, slots, 256), f32),
            pltpu.VMEM((width, 256), f32),
            pltpu.VMEM((8, width), f32),
            pltpu.VMEM((2, 4, GROUP, 8, 256), f32),
            pltpu.VMEM((2, 4, GROUP, 384, 256), bf16),
            pltpu.VMEM((2, 4, 8, 256), f32),
            pltpu.VMEM((3, slots, width), bf16),
            pltpu.VMEM((3, slots, width), bf16),
            pltpu.VMEM((2, 4, rows, width), bf16),
            pltpu.VMEM((2, 4, rows, width), bf16),
            pltpu.VMEM((4, rows, width), bf16),
            pltpu.VMEM((4, rows, width), bf16),
            pltpu.VMEM((4, GROUP, 384, 256), bf16),
            pltpu.VMEM((4, GROUP, 384, 256), bf16),
            pltpu.VMEM((4, 8, 256), f32),
            pltpu.VMEM((3, 8, 256), f32),
            DMA((heads + 1,)),
            DMA((heads,)),
            DMA((heads,)),
            DMA((heads, 3)),
            DMA((heads, 4)),
            DMA((heads, 3)),
            DMA((heads, 3)),
            DMA((3,)),
            DMA((3,)),
            DMA((2,)),
            DMA((2,)),
            DMA((3,)),
            DMA((4,)),
            DMA((4,)),
            DMA((4,)),
        ],
        compiler_params=pltpu.CompilerParams(collective_id=3, has_side_effects=True, vmem_limit_bytes=VMEM_LIMIT),
    )(wf, ws, wv, normed, values, hid, slope, prob, gmix, gg2, half, tokens, gmid, small)


def on_device_fast(tokens, lengths, gain_one, w_value, w_first, b_first, w_second, b_second, w_out, gain_two, w_up, w_down, grad_out):
    _, slots, width = tokens.shape
    heads_all, depth, _ = w_first.shape
    heads = heads_all // GROUP
    digits = jnp.stack([lengths[0] // 16, lengths[0] % 16]).astype(bf16)
    extra = jnp.concatenate(
        [
            w_value.reshape(depth, GROUP, -1).transpose(1, 0, 2),
            b_first.reshape(GROUP, heads, depth).transpose(0, 2, 1),
            jnp.broadcast_to(jnp.stack([gain_one, gain_two], 1), (GROUP, depth, 2)),
            jnp.broadcast_to(b_second.reshape(depth, 8), (GROUP, depth, 8)),
            jnp.broadcast_to(digits, (GROUP, depth, 2)),
            jnp.zeros((GROUP, depth, 49), bf16),
        ],
        2,
    )
    wf, ws, wv, small, normed, values, hid, slope, prob, joined, lf = attend_call(
        tokens, extra, w_first, w_second, w_out, w_up, w_down
    )
    result, gmid, gmix, half, gg2 = ffn_call(lf, joined, tokens[0], small, grad_out[0])
    out_f, out_a, out_s, gtok = back_call(
        wf, ws, wv, normed, values, hid, slope, prob, gmix, gg2, half, tokens[0], gmid, small
    )
    side = out_a[:, :depth].astype(f32)
    blocks = out_a[:, depth:].reshape(GROUP, heads, 5, depth, 256)
    widen = lambda v: v.transpose(0, 1, 3, 2, 4).reshape(heads_all, depth, -1).astype(f32)
    gains = jnp.sum(side[:, :, 195:197], axis=0)
    return (
        result[None],
        gtok[None],
        gains[:, 0],
        side[:, :, :192].transpose(1, 0, 2).reshape(depth, width),
        widen(blocks[:, :, :3]),
        side[:, :, 192:195].transpose(0, 2, 1).reshape(heads_all, depth),
        widen(blocks[:, :, 3:]),
        out_s[0, : b_second.shape[0]],
        out_f[4 * depth : 5 * depth],
        gains[:, 1],
        out_f[: 4 * depth].reshape(4, depth, width).transpose(1, 0, 2).reshape(depth, 4 * width),
        out_f[128:],
    )


def solution(mesh):
    wide, narrow = mesh.shape["wide"], mesh.shape["narrow"]
    grouped = Mesh(mesh.devices.reshape(GROUP, wide // GROUP, narrow), ALL)
    vec = P(ALL)
    flat = P(ALL, None)
    mid = P(None, ALL, None)
    row = P(ALL, None, None)
    body = on_device_fast if (wide, narrow) == (8, 4) else on_device
    return jax.shard_map(
        body,
        mesh=grouped,
        in_specs=(row, vec, vec, flat, mid, P(None, ALL), mid, vec, flat, vec, flat, flat, row),
        out_specs=(row, row, vec, flat, mid, P(None, ALL), mid, vec, flat, vec, flat, flat),
        check_vma=False,
    )
```

```python
import jax
import jax.numpy as jnp
from jax import lax
from jax.experimental import pallas as pl
from jax.experimental.pallas import tpu as pltpu
from jax.sharding import Mesh
from jax.sharding import PartitionSpec as P

epsilon = 1e-05
f32 = jnp.float32
bf16 = jnp.bfloat16
GROUP = 4


def norm_rows(values, factor):
    average = jnp.mean(values, axis=-1, keepdims=True)
    centred = values - average
    spread = jnp.mean(centred * centred, axis=-1, keepdims=True)
    return centred * lax.rsqrt(spread + epsilon) * factor


def smooth(values):
    return jax.nn.gelu(values, approximate=False)


def mm(spec, a, b):
    return jnp.einsum(spec, a, b, preferred_element_type=f32)


REST = ("rep", "narrow")
ALL = ("tp", "rep", "narrow")


def to_heads(shard):
    heads, depth, width = shard.shape
    pieces = lax.all_to_all(shard.reshape(GROUP, heads // GROUP, depth, width), "tp", 0, 0)
    whole = lax.all_gather(pieces, REST, axis=0)
    return whole.transpose(2, 1, 0, 3, 4).reshape(heads // GROUP, -1, width)


def from_heads(grad):
    heads, depth, width = grad.shape
    n = lax.axis_size("rep") * lax.axis_size("narrow")
    pieces = grad.astype(bf16).reshape(heads, GROUP, n, depth // (GROUP * n), width).transpose(2, 1, 0, 3, 4)
    pieces = pieces.reshape((n * GROUP,) + pieces.shape[2:])
    share = lax.psum_scatter(pieces, REST, scatter_dimension=0, tiled=True)
    share = lax.all_to_all(share, "tp", 0, 0)
    return share.reshape(heads * GROUP, depth // (GROUP * n), width).astype(f32)


def on_device(tokens, lengths, gain_one, w_value, w_first, b_first, w_second, b_second, w_out, gain_two, w_up, w_down, grad_out):
    row_count, slots, width = tokens.shape
    heads_all = w_first.shape[0]
    heads = heads_all // GROUP
    head_size = width // heads_all
    me = lax.axis_index("tp")
    depth = w_value.shape[0]

    small = [gain_one, gain_two, b_second, b_first.reshape(-1)]
    gathered = lax.all_gather(jnp.concatenate(small), ALL, axis=0)
    n_all = gathered.shape[0]
    g1 = gathered[:, :depth].reshape(-1).astype(f32)
    g2 = gathered[:, depth : 2 * depth].reshape(-1).astype(f32)
    b2_len = b_second.shape[0]
    b2 = gathered[:, 2 * depth : 2 * depth + b2_len].reshape(heads_all, slots).astype(f32)
    b1 = gathered[:, 2 * depth + b2_len :].reshape(n_all, heads_all, depth).transpose(1, 0, 2).reshape(heads_all, width).astype(f32)
    b1 = lax.dynamic_slice_in_dim(b1, me * heads, heads, 0)
    b2 = lax.dynamic_slice_in_dim(b2, me * heads, heads, 0)

    wf = to_heads(w_first)
    ws = to_heads(w_second)
    wv = to_heads(w_value.reshape(depth, GROUP, width // GROUP).transpose(1, 0, 2))[0]
    rows = lax.all_gather(tokens, "tp", axis=0, tiled=True)
    lens = lax.all_gather(lengths, "tp", axis=0, tiled=True)
    n_rows = rows.shape[0]

    normed = norm_rows(rows.astype(f32), g1).astype(bf16)
    values = mm("rsd,de->rse", normed, wv).astype(bf16)
    per_head = values.reshape(n_rows, slots, heads, head_size).transpose(2, 0, 1, 3)
    before = mm("rsd,hde->hrse", normed, wf) + b1[:, None, None, :]
    hidden = smooth(before).astype(bf16)
    logits = mm("hrse,hej->hrsj", hidden, ws) + b2[:, None, None, :]
    visible = lax.broadcasted_iota(jnp.int32, (1, n_rows, 1, slots), 3) < lens[None, :, None, None]
    masked = jnp.where(visible, logits, f32(-1e30))
    scaled = jnp.exp(masked - jnp.max(masked, axis=-1, keepdims=True))
    probabilities = scaled / jnp.sum(scaled, axis=-1, keepdims=True)
    weights = probabilities.astype(bf16)
    mixture = mm("hrsj,hrjc->rshc", weights, per_head).astype(bf16)
    mixture = mixture.reshape(GROUP, row_count, slots, heads * head_size)
    joined = lax.all_to_all(mixture, "tp", 0, 0).transpose(1, 2, 0, 3).reshape(row_count * slots, width)

    wo = lax.all_gather(w_out, ALL, axis=0, tiled=True)
    wu = lax.all_gather(w_up, ALL, axis=0, tiled=True)
    wd = lax.all_gather(w_down, ALL, axis=0, tiled=True)
    inputs = tokens.astype(f32).reshape(-1, width)
    middle = inputs + mm("sd,de->se", joined, wo)
    normed_two, norm_two_back = jax.vjp(norm_rows, middle, g2)
    normed_two = normed_two.astype(bf16)
    upward = mm("td,df->tf", normed_two, wu)
    active, smooth_up_back = jax.vjp(smooth, upward)
    active = active.astype(bf16)
    result = middle + mm("tf,fd->td", active, wd)

    g_out = grad_out.reshape(-1, width)
    grad_branch = g_out.astype(bf16)
    grad_w_down = mm("tf,td->fd", active, grad_branch)
    grad_upward = smooth_up_back(mm("td,fd->tf", grad_branch, wd))[0].astype(bf16)
    grad_w_up = mm("td,tf->df", normed_two, grad_upward)
    grad_middle_norm, grad_gain_two = norm_two_back(mm("tf,df->td", grad_upward, wu))
    grad_middle = g_out + grad_middle_norm
    grad_attn = grad_middle.astype(bf16)
    grad_w_out = mm("sd,se->de", joined, grad_attn)
    grad_joined = mm("se,de->sd", grad_attn, wo).astype(bf16)

    grad_mixture = grad_joined.reshape(row_count, slots, GROUP, heads * head_size).transpose(2, 0, 1, 3)
    grad_mixture = lax.all_to_all(grad_mixture, "tp", 0, 0).reshape(n_rows, slots, heads, head_size).transpose(2, 0, 1, 3)
    grad_weights = mm("hrsc,hrjc->hrsj", grad_mixture, per_head)
    grad_values = mm("hrsj,hrsc->rjhc", weights, grad_mixture).astype(bf16).reshape(n_rows, slots, heads * head_size)
    centre = jnp.sum(probabilities * grad_weights, axis=-1, keepdims=True)
    grad_logits = (probabilities * (grad_weights - centre)).astype(bf16)
    grad_b_second = jnp.sum(grad_logits.astype(f32), axis=(1, 2))
    grad_w_second = mm("hrse,hrsj->hej", hidden, grad_logits)
    grad_hidden = mm("hrsj,hej->hrse", grad_logits, ws)
    smooth_value, smooth_back = jax.vjp(smooth, before)
    grad_before = smooth_back(grad_hidden)[0].astype(bf16)
    grad_b_first = jnp.sum(grad_before.astype(f32), axis=(1, 2))
    grad_w_first = mm("rsd,hrse->hde", normed, grad_before)
    grad_w_value = mm("rsd,rse->de", normed, grad_values)
    grad_normed = mm("hrse,hde->rsd", grad_before, wf) + mm("rse,de->rsd", grad_values, wv)
    grad_normed = lax.psum_scatter(grad_normed.astype(bf16), "tp", scatter_dimension=0, tiled=True)
    value, norm_one_back = jax.vjp(norm_rows, inputs, g1)
    grad_inputs_norm, grad_gain_one = norm_one_back(grad_normed.astype(f32).reshape(-1, width))
    grad_tokens = grad_middle + grad_inputs_norm

    out_first = from_heads(grad_w_first)
    out_second = from_heads(grad_w_second)
    out_value = from_heads(grad_w_value[None]).transpose(1, 0, 2).reshape(depth, width)

    def share(grad):
        return lax.psum_scatter(grad.astype(bf16), ALL, scatter_dimension=0, tiled=True).astype(f32)

    vec_tp = jnp.concatenate([grad_b_first.reshape(-1), grad_b_second.reshape(-1)])
    vec_tp = lax.dynamic_update_slice_in_dim(jnp.zeros((GROUP, vec_tp.shape[0]), f32), vec_tp[None], me, 0)
    vec = jnp.concatenate([vec_tp.reshape(-1), grad_gain_one, grad_gain_two])
    vec = lax.psum(vec, ALL)
    index = (me * lax.axis_size("rep") + lax.axis_index("rep")) * lax.axis_size("narrow") + lax.axis_index("narrow")
    n_tp = GROUP * (heads * width + heads * slots)
    tp_part = vec[:n_tp].reshape(GROUP, -1)
    gb1 = tp_part[:, : heads * width].reshape(heads_all, width)
    gb2 = tp_part[:, heads * width :].reshape(-1)
    gb1 = lax.dynamic_slice_in_dim(gb1, index * depth, depth, 1)
    gb2 = lax.dynamic_slice_in_dim(gb2, index * b2_len, b2_len, 0)
    gg1 = lax.dynamic_slice_in_dim(vec[n_tp : n_tp + width], index * depth, depth, 0)
    gg2 = lax.dynamic_slice_in_dim(vec[n_tp + width :], index * depth, depth, 0)
    shape = tokens.shape
    return (
        result.reshape(shape),
        grad_tokens.reshape(shape),
        gg1,
        out_value,
        out_first,
        gb1,
        out_second,
        gb2,
        share(grad_w_out),
        gg2,
        share(grad_w_up),
        share(grad_w_down),
    )


MESH = pl.DeviceIdType.MESH
VMEM_LIMIT = 60 * 2**20
ANY = pl.BlockSpec(memory_space=pl.ANY)
FULL = pl.BlockSpec(memory_space=pltpu.VMEM)
DMA = pltpu.SemaphoreType.DMA


def shape_of(dims, kind):
    return jax.ShapeDtypeStruct(dims, kind)


def dot_nt(a, b):
    return lax.dot_general(a, b, (((1,), (1,)), ((), ())), preferred_element_type=f32)


def dot_tn(a, b):
    return lax.dot_general(a, b, (((0,), (0,)), ((), ())), preferred_element_type=f32)


def dot_nn(a, b):
    return lax.dot_general(a, b, (((1,), (0,)), ((), ())), preferred_element_type=f32)


def place():
    return lax.axis_index("tp"), lax.axis_index("rep"), lax.axis_index("narrow")


def group_peers():
    t, c, z = place()
    along_x = t + 1 - 2 * (t % 2)
    along_y = (t + 2) % GROUP
    return [GROUP - 1 - t, (1 - c) * along_x + c * along_y, (1 - c) * along_y + c * along_x]


def line_peers():
    z = lax.axis_index("narrow")
    return [(z + k) % 4 for k in (1, 2, 3)]


def line_place():
    z = lax.axis_index("narrow")
    side = z // 2
    end, inner = 3 * side, 1 + side
    return end, inner, 2 - side, 3 - 3 * side, end + inner - z, z == inner


class Spread:
    def __init__(self, slabs, send, recv, source=None):
        t, c, z = place()
        end, inner, other, far, near, is_inner = line_place()
        self.is_inner = is_inner
        move = lambda o, k, to: remote(slabs(o), slabs(o), send.at[k], recv.at[o], (t, c, to))
        source = slabs(z) if source is None else source
        give = lambda k, to: remote(source, slabs(z), send.at[k], recv.at[z], (t, c, to))
        self.own = lambda: [give(0, other), give(1, near)]
        self.on = lambda: [move(other, 2, end), move(far, 3, end)]
        self.near = lambda: move(near, 0, near)

    def begin(self):
        start(self.own())

    def forward(self):
        @pl.when(self.is_inner)
        def _():
            for copy in self.on():
                copy.wait_recv()
            start(self.on())

    def finish(self):
        self.near().wait_recv()

        @pl.when(jnp.logical_not(self.is_inner))
        def _():
            for copy in self.on():
                copy.wait_recv()

        for copy in self.own():
            copy.wait_send()

        @pl.when(self.is_inner)
        def _():
            for copy in self.on():
                copy.wait_send()


class Gather:
    def __init__(self, slabs, land, add, send, recv):
        t, c, z = place()
        end, inner, other, far, near, is_inner = line_place()
        self.is_inner, self.add, self.z = is_inner, add, z
        self.other, self.far = other, far
        move = lambda o, slot, k, to: remote(slabs(o), land(slot), send.at[k], recv.at[slot], (t, c, to))
        self.out = lambda: [move(far, 2, 0, inner), move(other, 1, 1, inner), move(inner, 0, 2, inner)]
        self.back = lambda: [move(end, 0, 2, end)]
        self.on_far = lambda: [move(far, 1, 0, far)]
        self.on_other = lambda: [move(other, 3, 1, other)]
        self.got = lambda slot: move(z, slot, 0, near).wait_recv()

    def begin(self):
        @pl.when(self.is_inner)
        def _():
            start(self.back())

        @pl.when(jnp.logical_not(self.is_inner))
        def _():
            start(self.out())

    def forward(self):
        @pl.when(self.is_inner)
        def _():
            self.got(2)
            self.add(self.far, 2)
            start(self.on_far())
            self.got(1)
            self.add(self.other, 1)
            start(self.on_other())

    def finish(self):
        self.got(0)
        self.add(self.z, 0)

        @pl.when(self.is_inner)
        def _():
            self.got(3)
            self.add(self.z, 3)
            for copy in self.back() + self.on_far() + self.on_other():
                copy.wait_send()

        @pl.when(jnp.logical_not(self.is_inner))
        def _():
            self.got(1)
            self.add(self.z, 1)
            for copy in self.out():
                copy.wait_send()


def greet(devices):
    barrier = pltpu.get_barrier_semaphore()
    for device in devices:
        pl.semaphore_signal(barrier, inc=1, device_id=device, device_id_type=MESH)


def met(count):
    pl.semaphore_wait(pltpu.get_barrier_semaphore(), count)


def remote(src, dst, send, recv, device):
    return pltpu.make_async_remote_copy(
        src_ref=src, dst_ref=dst, send_sem=send, recv_sem=recv, device_id=device, device_id_type=MESH
    )


def local(src, dst, sem):
    return pltpu.make_async_copy(src, dst, sem)


def start(copies):
    for copy in copies:
        copy.start()


def wait(copies):
    for copy in copies:
        copy.wait()


def square():
    t, c, z = place()
    y, x = t // 2, t % 2
    tps = group_peers()
    slow, fast = (1 - c) * y + c * x, (1 - c) * x + c * y
    return slow, fast, (tps[2], c, z), (tps[1], c, z)


def gelu_pair(v):
    cdf = 0.5 * (1.0 + lax.erf(v * 0.7071067811865476))
    return v * cdf, cdf + v * (jnp.exp(-0.5 * v * v) * 0.3989422804014327)


def centre_rows(v):
    shifted = v - jnp.mean(v, axis=-1, keepdims=True)
    scale = lax.rsqrt(jnp.mean(shifted * shifted, axis=-1, keepdims=True) + epsilon)
    return shifted * scale, scale


ROWS = ((0, 144), (144, 272), (272, 384))


def part(i):
    return slice(*ROWS[i])


def attend_kernel(
    tokens, extra, w_first, w_second, w_out, w_up, w_down,
    wf, ws, wv, small, normed, values, hid, slope, prob, joined, lf,
    pa, pf, la, lt, nrm, val, cols, b2, masks, join, own, s1, r1, s2, r2, s3, r3, st, rt, s1f, r1f, sf, rf, sj, rj,
):
    h, r = pl.program_id(0), pl.program_id(1)
    width = wf.shape[-1]
    heads = w_first.shape[0] // GROUP
    t, c, z = place()
    sibling = (t, 1 - c, z)
    tps, zs = group_peers(), line_peers()
    slow, fast, slow_dev, fast_dev = square()

    a1 = lambda i: [
        remote(pa.at[p, part(i)], la.at[c, z, t, part(i)], s1.at[i, k], r1.at[i, k], (p, c, z))
        for k, p in enumerate(tps)
    ]
    a2 = lambda i: Spread(lambda o: la.at[c, o, :, part(i)], s2.at[i], r2.at[i])
    a3 = lambda i: [remote(la.at[c, :, :, part(i)], la.at[c, :, :, part(i)], s3.at[i], r3.at[i], sibling)]
    mine = lambda i: [local(pa.at[t, part(i)], la.at[c, z, t, part(i)], own.at[i])]
    mine_t = lambda: [local(tokens.at[0], lt.at[3], own.at[heads])]
    mine_f = lambda: [local(pf, lf.at[c, slow, fast, z], own.at[heads + 1])]
    mine_j = lambda: [local(join.at[3], joined.at[t], own.at[heads + 2])]
    tok_fast = lambda: remote(tokens.at[0], lt.at[1], st.at[0], rt.at[0], fast_dev)
    tok_slow = lambda: remote(tokens.at[0], lt.at[2], st.at[1], rt.at[1], slow_dev)
    tok_on = lambda: remote(lt.at[1], lt.at[0], st.at[2], rt.at[2], slow_dev)
    f1 = lambda k: Spread(lambda o: lf.at[c, slow, fast, o, cut(k)], s1f.at[k], r1f.at[k], pf.at[cut(k)])

    def whole(k, spot, n, device):
        piece = lf.at[spot + (slice(None),) * (4 - len(spot)) + (cut(k),)]
        return [remote(piece, piece, sf.at[k, n], rf.at[k, n], device)]

    f2 = lambda k: whole(k, (c, slow, fast), 0, fast_dev)
    f3 = lambda k: whole(k, (c, slow), 1, slow_dev)
    f4 = lambda k: whole(k, (c, slow), 2, sibling)
    f5 = lambda k: whole(k, (c, 1 - slow), 3, sibling)
    out_j = lambda k: [remote(join.at[k], joined.at[t], sj.at[k], rj.at[k], (tps[k], c, z))]

    def at_step(i, j):
        return pl.when((h == i) & (r == j))

    @at_step(0, 0)
    def _():
        greet([(p, c, z) for p in tps] + [(t, c, p) for p in zs] + [sibling])
        blocks = lambda v: [v[:, k : k + 256] for k in range(0, v.shape[1], 256)]
        ups = [w_up[:, k : k + width].astype(f32) for k in range(0, w_up.shape[1], width)]
        pf[0:96] = jnp.concatenate(ups, 0).astype(bf16)
        pf[96:128] = jnp.concatenate([w_out[...].astype(f32), jnp.zeros((8, width), f32)], 0).astype(bf16)
        pf[128:224] = w_down[...]
        for p in range(GROUP):
            stack = [extra[p].astype(f32)]
            for i in range(heads):
                stack += blocks(w_first[heads * p + i].astype(f32)) + blocks(w_second[heads * p + i].astype(f32))
            pa[p] = jnp.concatenate(stack, 0).astype(bf16)
        met(7)
        f1(0).begin()
        for i in range(heads):
            start(mine(i) + a1(i))
        start(mine_f() + mine_t())
        wait(mine(0) + a1(0))
        a2(0).begin()
        wait(mine(1) + a1(1))
        wait(mine(2) + a1(2))
        start([tok_fast(), tok_slow()])
        f1(0).forward()
        f1(1).begin()
        a2(0).forward()
        a2(1).begin()
        tok_fast().wait_recv()
        tok_on().start()
        f1(0).finish()
        wait(mine_f())
        start(f2(0))
        a2(0).finish()
        start(a3(0))
        f1(1).forward()
        a2(1).forward()
        a2(2).begin()
        wait(mine_t() + a3(0))
        tok_fast().wait_send()
        tok_slow().wait()
        tok_on().wait()

    @at_step(0, 1)
    def _():
        wait(f2(0))
        start(f3(0) + f4(0))
        f1(1).finish()
        start(f2(1))

    @at_step(0, 3)
    def _():
        a2(2).forward()

    @at_step(1, 0)
    def _():
        a2(1).finish()
        start(a3(1))
        wait(a3(1))

    @at_step(1, 1)
    def _():
        wait(f2(1))
        start(f3(1) + f4(1))

    @at_step(2, 0)
    def _():
        a2(2).finish()
        start(a3(2))
        wait(f3(0))
        start(f5(0))
        wait(a3(2))

    def unpack(i):
        def one(tt, carry):
            for cc in range(2):
                for zz in range(0, 4, 2):
                    at = pl.ds(pl.multiple_of((tt * 8 + cc * 4 + zz) * 24, 48), 48)

                    def block(first):
                        low = first // 16 * 16
                        both = [la[cc, zz + k, tt, low : low + 32].astype(f32)[first - low :][:24] for k in range(2)]
                        return jnp.concatenate(both, 0)

                    base = 24 + 120 * i
                    for j in range(3):
                        wf[0, at, 256 * j : 256 * j + 256] = block(base + 24 * j).astype(bf16)
                    for j in range(2):
                        ws[0, at, 256 * j : 256 * j + 256] = block(base + 72 + 24 * j).astype(bf16)
                    if i == 0:
                        both = block(0)
                        cols[at, :] = both[:, 128:256]
                        lane = lax.broadcasted_iota(jnp.int32, both.shape, 1)
                        wv[at, :] = jnp.where(lane < 192, both, 0.0).astype(bf16)

            return carry

        lax.fori_loop(0, GROUP, one, 0)

    for i in range(heads):

        @at_step(i, 0)
        def _():
            unpack(i)

    @at_step(0, 0)
    def _():
        small[...] = cols[...].T[64:72]
        mine_rows = cols[pl.ds(pl.multiple_of(t * 192, 192), 192), :].astype(bf16)
        lane = lax.broadcasted_iota(jnp.int32, (128, 512), 0)
        spot = lax.broadcasted_iota(jnp.int32, (128, 512), 1)
        spread = dot_nn(mine_rows, jnp.where(lane - 69 == spot % 8, 1.0, 0.0).astype(bf16))
        row = lax.broadcasted_iota(jnp.int32, (64, 512), 0)
        spot = lax.broadcasted_iota(jnp.int32, (64, 512), 1)
        for i in range(heads):
            picked = jnp.where(row == spot // 8, spread[64 * i : 64 * i + 64], 0.0)
            b2[i] = jnp.broadcast_to(jnp.sum(picked, axis=0, keepdims=True), (8, 512))
        for k, p in enumerate(tps + [t]):
            line = cols[pl.ds(pl.multiple_of((p * 8 + c * 4 + z) * 24, 8), 8), :]
            lane = lax.broadcasted_iota(jnp.int32, line.shape, 1)
            digits = jnp.where(lane == 77, 16.0 * line, jnp.where(lane == 78, line, 0.0))
            length = jnp.sum(digits, axis=1, keepdims=True)
            spot = lax.broadcasted_iota(jnp.int32, (8, 512), 1).astype(f32)
            masks[k] = jnp.where(spot < length, 0.0, -1e30)

    @pl.when(h == 0)
    def _():
        unit, _ = centre_rows(lt[r].astype(f32))
        out = (unit * small[3:4]).astype(bf16)
        nrm[r] = out
        normed[0] = out
        v = dot_nn(out, wv[...]).astype(bf16)
        val[r] = v
        values[0] = v

    row = lax.broadcasted_iota(jnp.int32, (8, width), 0)
    b1 = jnp.sum(jnp.where(row == h, small[...], 0.0), axis=0, keepdims=True)
    shift = b2[h, 0:1] + masks[r, 0:1]
    tile = pl.ds(pl.multiple_of((h // 2) * 128, 128), 128)
    step = 256
    for m in range(0, 512, step):
        at = slice(m, m + step)
        before = dot_nn(nrm[r, at, :], wf[0]) + b1
        out, grad = gelu_pair(before)
        hidden = out.astype(bf16)
        hid[0, 0, at, :] = hidden
        slope[0, 0, at, :] = grad.astype(bf16)
        logits = dot_nn(hidden, ws[0]) + shift
        e = jnp.exp(logits - jnp.max(logits, axis=-1, keepdims=True))
        p = (e * (1.0 / jnp.sum(e, axis=-1, keepdims=True))).astype(bf16)
        prob[0, 0, at, :] = p
        mix = dot_nn(p, val[r, :, tile])
        lane = lax.broadcasted_iota(jnp.int32, mix.shape, 1)
        old = join[r, at, tile].astype(f32)
        join[r, at, tile] = jnp.where((h == 1) & (lane < 64), old, mix).astype(bf16)

    for k in range(3):

        @at_step(2, k)
        def _():
            start(out_j(k))

    @at_step(2, 2)
    def _():
        wait(f3(1))
        start(f5(1))

    @at_step(2, 3)
    def _():
        start(mine_j())
        for k in range(2):
            wait(f4(k) + f5(k))
        for k in range(3):
            wait(out_j(k))
        wait(mine_j())


def attend_call(tokens, extra, w_first, w_second, w_out, w_up, w_down):
    _, slots, width = tokens.shape
    heads = w_first.shape[0] // GROUP
    by_row = lambda h, r: (jnp.where(h == 0, r, GROUP - 1), 0, 0)
    by_head = lambda h, r: (h, 0, 0)
    both = lambda h, r: (h, r, 0, 0)
    rows_f = 2 * w_down.shape[0] + 32
    return pl.pallas_call(
        attend_kernel,
        grid=(heads, GROUP),
        out_shape=(
            shape_of((heads, width, width), bf16),
            shape_of((heads, width, slots), bf16),
            shape_of((width, 256), bf16),
            shape_of((8, width), f32),
            shape_of((GROUP, slots, width), bf16),
            shape_of((GROUP, slots, 256), bf16),
            shape_of((heads, GROUP, slots, width), bf16),
            shape_of((heads, GROUP, slots, width), bf16),
            shape_of((heads, GROUP, slots, slots), bf16),
            shape_of((GROUP, slots, 256), bf16),
            shape_of((2, 2, 2, 4, rows_f, width), bf16),
        ),
        in_specs=[ANY] + [FULL] * 6,
        out_specs=(
            pl.BlockSpec((1, width, width), by_head),
            pl.BlockSpec((1, width, slots), by_head),
            pl.BlockSpec((width, 256), lambda h, r: (0, 0)),
            pl.BlockSpec((8, width), lambda h, r: (0, 0)),
            pl.BlockSpec((1, slots, width), by_row),
            pl.BlockSpec((1, slots, 256), by_row),
            pl.BlockSpec((1, 1, slots, width), both),
            pl.BlockSpec((1, 1, slots, width), both),
            pl.BlockSpec((1, 1, slots, slots), both),
            ANY,
            ANY,
        ),
        scratch_shapes=[
            pltpu.VMEM((GROUP, 384, 256), bf16),
            pltpu.VMEM((rows_f, width), bf16),
            pltpu.VMEM((2, 4, GROUP, 384, 256), bf16),
            pltpu.VMEM((GROUP, slots, width), bf16),
            pltpu.VMEM((GROUP, slots, width), bf16),
            pltpu.VMEM((GROUP, slots, 256), bf16),
            pltpu.VMEM((width, 128), f32),
            pltpu.VMEM((heads, 8, slots), f32),
            pltpu.VMEM((GROUP, 8, slots), f32),
            pltpu.VMEM((GROUP, slots, 256), bf16),
            DMA((heads + 3,)),
            DMA((heads, 3)),
            DMA((heads, 3)),
            DMA((heads, 4)),
            DMA((heads, 4)),
            DMA((heads,)),
            DMA((heads,)),
            DMA((3,)),
            DMA((3,)),
            DMA((2, 4)),
            DMA((2, 4)),
            DMA((2, 4)),
            DMA((2, 4)),
            DMA((3,)),
            DMA((3,)),
        ],
        compiler_params=pltpu.CompilerParams(collective_id=1, has_side_effects=True, vmem_limit_bytes=VMEM_LIMIT),
    )(tokens, extra, w_first, w_second, w_out, w_up, w_down)


def slab(t, c, z):
    y, x = t // 2, t % 2
    return (0, y, x, z) if c == 0 else (1, x, y, z)


CUTS = ((0, 128), (128, 224))


def cut(k):
    return slice(*CUTS[k])


def ffn_kernel(
    lf_far, joined, tokens, small, gout, result, gmid, gmix, half, gg2,
    lf, gf, gj, more, meet_b, acts, slopes, wu, wo, n2, gn2, gwu, loads, own, sg, rg, sx, rx, sb, rb,
):
    width = tokens.shape[-1]
    me, core, z_me = place()
    tps = group_peers()
    slow, fast, slow_dev, fast_dev = square()
    sibling = (me, 1 - core, z_me)
    parts = (slice(0, 96), slice(128, 224), slice(96, 128))
    cross = lambda k: [
        remote(
            gf.at[1 - core, :, :, :, parts[k], :], more.at[:, :, :, parts[k], :], sx.at[k], rx.at[k], sibling
        )
    ]
    over = lambda: remote(gf.at[core, 1 - slow, :, :, cut(1), :], meet_b, sb, rb, slow_dev)
    out_g = lambda k: [remote(gj.at[tps[k]], gmix.at[k], sg.at[k], rg.at[k], (tps[k], core, z_me))]
    greet([(p, core, z_me) for p in tps] + [sibling])
    load = lambda k: local(lf_far.at[:, :, :, :, parts[k], :], lf.at[:, :, :, :, parts[k], :], loads.at[k])
    for k in (2, 0, 1):
        load(k).start()
    load(2).wait()
    wo[...] = jnp.zeros_like(wo)
    for t in range(GROUP):
        for c in range(2):
            for z in range(0, 4, 2):
                pair = [lf[slab(t, c, z + k) + (slice(96, 128),)].astype(f32)[0:24] for k in range(2)]
                wo[t, (c * 4 + z) * 24 : (c * 4 + z) * 24 + 48, :] = jnp.concatenate(pair, 0).astype(bf16)
    middle = tokens[...].astype(f32)
    for t in range(GROUP):
        middle = middle + dot_nn(joined[t], wo[t])
    result[...] = middle
    gmid[...] = middle
    g2 = small[4:5]
    unit, _ = centre_rows(middle)
    n2[...] = (unit * g2).astype(bf16)
    gn2[...] = jnp.zeros_like(gn2)
    load(0).wait()

    def fold(k):
        def one(i, carry):
            for j in range(2):
                for z in range(4):
                    spot = (i, j, z, parts[k])
                    gf[(core,) + spot] = (gf[(core,) + spot].astype(f32) + more[spot].astype(f32)).astype(bf16)
            return carry

        lax.fori_loop(0, 2, one, 0)

    def ahead(p, carry):
        rows = pl.ds(pl.multiple_of(p * 48, 16), 48)
        for t in range(GROUP):
            for c in range(2):
                for z in range(0, 4, 2):
                    ends = [lf[slab(t, c, z + k) + (rows,)].astype(f32) for k in range(2)]
                    at = (t * 8 + c * 4 + z) * 24
                    for k in range(2):
                        both = jnp.concatenate([e[24 * k : 24 * k + 24] for e in ends], 0)
                        wu[2 * p + k, at : at + 48, :] = both.astype(bf16)
        branch = gout[...].astype(bf16)
        for k in range(2):
            act, slope = gelu_pair(dot_nn(n2[...], wu[2 * p + k]))
            act = act.astype(bf16)
            acts[2 * p + k] = act
            slopes[2 * p + k] = slope.astype(bf16)
            gwd = dot_tn(act, branch).astype(bf16)
            gf[0, p, k, :, 128:224, :] = gwd[:384].reshape(4, 96, width)
            gf[1, k, p, :, 128:224, :] = gwd[384:].reshape(4, 96, width)
        return carry

    def behind(p, carry):
        rows = pl.ds(pl.multiple_of(p * 48, 16), 48)
        branch = gout[...].astype(bf16)
        for k in range(2):
            wd = jnp.concatenate(
                [lf[0, p, k, :, 128:224, :].reshape(384, width), lf[1, k, p, :, 128:224, :].reshape(384, width)], 0
            )
            gup = (dot_nt(branch, wd) * slopes[2 * p + k].astype(f32)).astype(bf16)
            gwu[k] = dot_tn(n2[...], gup)
            gn2[...] += dot_nt(gup, wu[2 * p + k])
            result[...] += dot_nn(acts[2 * p + k], wd)
        for t in range(GROUP):
            for c in range(2):
                for z in range(4):
                    at = (t * 8 + c * 4 + z) * 24
                    both = jnp.concatenate([gwu[0, at : at + 24, :], gwu[1, at : at + 24, :]], 0)
                    gf[slab(t, c, z) + (rows,)] = both.astype(bf16)
        return carry

    lax.fori_loop(0, 2, ahead, 0)
    met(4)
    start(cross(1))
    load(1).wait()

    def turn(p, carry):
        @pl.when(p == 1)
        def _():
            wait(cross(1))
            fold(1)
            over().start()

        return behind(p, carry)

    lax.fori_loop(0, 2, turn, 0)
    start(cross(0))
    unit, scale = centre_rows(gmid[...])
    gn = gn2[...]
    gg2[...] = jnp.sum((gn * unit).reshape(-1, 8, width), axis=0)
    gu = gn * g2
    back = scale * (
        gu - jnp.mean(gu, axis=-1, keepdims=True) - unit * jnp.mean(gu * unit, axis=-1, keepdims=True)
    )
    gm = gout[...] + back
    gmid[...] = gm
    ga = gm.astype(bf16)
    for t in range(GROUP):
        gj[t] = dot_nt(ga, wo[t]).astype(bf16)
    for k in range(3):
        start(out_g(k))
    mine = local(gj.at[me], gmix.at[3], own.at[0])
    mine.start()
    for t in range(GROUP):
        gwo = dot_tn(joined[t], ga)
        for c in range(2):
            for z in range(4):
                at = (c * 4 + z) * 24
                padded = jnp.concatenate([gwo[at : at + 24, :], jnp.zeros((8, width), f32)], 0)
                gf[slab(t, c, z) + (slice(96, 128),)] = padded.astype(bf16)
    start(cross(2))
    for k in (0, 2):
        wait(cross(k))
        fold(k)
    over().wait()

    def arrived(j, carry):
        for z in range(4):
            spot = (core, slow, j, z, cut(1))
            gf[spot] = (gf[spot].astype(f32) + meet_b[j, z].astype(f32)).astype(bf16)
        return carry

    lax.fori_loop(0, 2, arrived, 0)
    leave = local(gf.at[core], half, own.at[1])
    leave.start()
    for k in range(3):
        wait(out_g(k))
    mine.wait()
    leave.wait()


def ffn_call(lf, joined, tokens, small, gout):
    slots, width = tokens.shape
    return pl.pallas_call(
        ffn_kernel,
        out_shape=(
            shape_of((slots, width), f32),
            shape_of((slots, width), f32),
            shape_of(joined.shape, bf16),
            shape_of(lf.shape[1:], bf16),
            shape_of((8, width), f32),
        ),
        in_specs=[ANY] + [FULL] * 4,
        out_specs=(FULL, FULL, ANY, ANY, FULL),
        scratch_shapes=[
            pltpu.VMEM(lf.shape, bf16),
            pltpu.VMEM(lf.shape, bf16),
            pltpu.VMEM(joined.shape, bf16),
            pltpu.VMEM(lf.shape[1:], bf16),
            pltpu.VMEM((2, 4, 96, width), bf16),
            pltpu.VMEM((4, slots, width), bf16),
            pltpu.VMEM((4, slots, width), bf16),
            pltpu.VMEM((4, width, width), bf16),
            pltpu.VMEM((GROUP, 256, width), bf16),
            pltpu.VMEM((slots, width), bf16),
            pltpu.VMEM((slots, width), f32),
            pltpu.VMEM((2, width, width), f32),
            DMA((3,)),
            DMA((2,)),
            DMA((3,)),
            DMA((3,)),
            DMA((3,)),
            DMA((3,)),
            DMA,
            DMA,
        ],
        compiler_params=pltpu.CompilerParams(collective_id=2, has_side_effects=True, vmem_limit_bytes=VMEM_LIMIT),
    )(lf, joined, tokens, small, gout)


def back_kernel(
    wf, ws, wv, normed, values, hid, slope, prob, gmix, gg2, half, tokens, gmid, small, out_f, out_a, out_s, gtok,
    wcat, gb_all, awf, aws, ab1, ab2, gn, gv, awv, stash, ga, gs, nb, tok, fs, fb2, fb3, fb4, cb1, cb2, sb1, sb2,
    own, s1, r1, s2, r2, s3, r3, sn, rn, sf, rf, s4, r4, sv, rv,
):
    step, r = pl.program_id(0), pl.program_id(1)
    width = ws.shape[1]
    heads = ab1.shape[0]
    h = jnp.maximum(heads - 1 - step, 0)
    t, c, z = place()
    sibling = (t, 1 - c, z)
    tps, zs = group_peers(), line_peers()
    slow, fast, slow_dev, fast_dev = square()

    a1 = lambda i: [remote(ga.at[1 - c, :, :, part(i)], cb1.at[:, :, part(i)], s1.at[i], r1.at[i], sibling)]

    def add_heads(i):
        def add(o, slot):
            def one(j, carry):
                here = ga[c, o, j, part(i)].astype(f32) + cb2[slot, j, part(i)].astype(f32)
                ga[c, o, j, part(i)] = here.astype(bf16)
                return carry

            lax.fori_loop(0, GROUP, one, 0)

        return add

    def add_f(k):
        def add(o, slot):
            fs[fast, o, cut(k)] = (fs[fast, o, cut(k)].astype(f32) + fb4[slot, cut(k)].astype(f32)).astype(bf16)

        return add

    a2 = lambda i: Gather(
        lambda o: ga.at[c, o, :, part(i)], lambda k: cb2.at[k, :, part(i)], add_heads(i), s2.at[i], r2.at[i]
    )
    a3 = lambda i: [
        remote(ga.at[c, z, p, part(i)], out_a.at[t, part(i)], s3.at[i, k], r3.at[i, k], (p, c, z))
        for k, p in enumerate(tps)
    ]
    mine = lambda i: [local(ga.at[c, z, t, part(i)], out_a.at[t, part(i)], own.at[i])]
    mine_f = lambda: [local(half.at[slow], fs, own.at[heads])]
    mine_t = lambda: [local(tokens, tok, own.at[heads + 1]), local(gmid, gtok, own.at[heads + 2])]
    mine_w = lambda: [
        local(wf.at[i], wcat.at[:, i * width : (i + 1) * width], own.at[heads + 3 + i]) for i in range(heads)
    ]
    v1 = lambda: [remote(gs.at[1 - c], sb1, sv.at[0], rv.at[0], sibling)]
    v2 = lambda: [remote(gs.at[c, p], sb2.at[k], sv.at[1 + k], rv.at[1 + k], (t, c, p)) for k, p in enumerate(zs)]
    f2 = lambda: [remote(half.at[1 - slow, :, :, cut(0), :], fb2, sf.at[0], rf.at[0], slow_dev)]
    f3 = lambda k: [remote(fs.at[1 - fast, :, cut(k)], fb3.at[:, cut(k)], sf.at[1 + k], rf.at[1 + k], fast_dev)]
    f4 = lambda k: Gather(
        lambda o: fs.at[fast, o, cut(k)], lambda n: fb4.at[n, cut(k)], add_f(k), s4.at[k], r4.at[k]
    )
    line_n = lambda k: gb_all.at[k, :, 0:width]
    out_n = lambda k: remote(line_n(k), nb.at[k], sn.at[k], rn.at[k], (fast_dev, fast_dev, slow_dev)[k])

    def at_step(i, j):
        return pl.when((step == i) & (r == j))

    def meet(i):
        wait(a1(i))

        def line(k, carry):
            for j in range(GROUP):
                here = ga[c, k, j, part(i)].astype(f32) + cb1[k, j, part(i)].astype(f32)
                ga[c, k, j, part(i)] = here.astype(bf16)
            return carry

        lax.fori_loop(0, 4, line, 0)
        a2(i).begin()

    def deal(i):
        a2(i).finish()
        start(mine(i) + a3(i))

    def add_slabs(total, more, k):
        def one(i, carry):
            here = fs[total, i, cut(k)].astype(f32) + more(i).astype(f32)
            fs[total, i, cut(k)] = here.astype(bf16)
            return carry

        lax.fori_loop(0, 4, one, 0)

    @at_step(0, 0)
    def _():
        greet([(p, c, z) for p in tps] + [(t, c, p) for p in zs] + [sibling])
        start(mine_f() + mine_w() + mine_t())
        met(7)
        start(f2())
        wait(mine_f())
        start(f3(1))

    @at_step(0, 3)
    def _():
        wait(f3(1))
        add_slabs(fast, lambda i: fb3[i, cut(1)], 1)
        f4(1).begin()

    @at_step(1, 0)
    def _():
        meet(2)

    @at_step(1, 2)
    def _():
        f4(1).forward()

    @at_step(1, 3)
    def _():
        wait(f2())
        add_slabs(1 - fast, lambda i: fb2[1 - fast, i], 0)
        start(f3(0))
        add_slabs(fast, lambda i: fb2[fast, i], 0)

    @at_step(2, 0)
    def _():
        a2(2).forward()
        meet(1)

    @at_step(2, 2)
    def _():
        wait(f3(0))
        add_slabs(fast, lambda i: fb3[i, cut(0)], 0)
        f4(0).begin()

    @at_step(2, 3)
    def _():
        deal(2)

    @at_step(3, 0)
    def _():
        wait(mine_w())

    @pl.when((r == 0) & (step < heads))
    def _():
        awf[...] = jnp.zeros_like(awf)
        aws[...] = jnp.zeros_like(aws)
        ab1[h] = jnp.zeros(ab1.shape[1:], f32)
        ab2[h] = jnp.zeros(ab2.shape[1:], f32)

    @pl.when(step < heads)
    def _():
        tile = pl.ds(pl.multiple_of((h // 2) * 128, 128), 128)
        lane = lax.broadcasted_iota(jnp.int32, (512, 128), 1)
        gm = jnp.where(lane // 64 == h % 2, gmix[0, :, tile].astype(f32), 0.0).astype(bf16)
        gw = dot_nt(gm, values[0, :, tile])
        p = prob[0, 0]
        p32 = p.astype(f32)
        gl = (p32 * (gw - jnp.sum(p32 * gw, axis=-1, keepdims=True))).astype(bf16)
        ab2[h] += jnp.sum(gl.astype(f32).reshape(-1, 8, 512), axis=0)
        gvh = dot_tn(p, gm)

        @pl.when(h != 0)
        def _():
            gv[r, :, tile] = gvh.astype(bf16)

        @pl.when(h == 0)
        def _():
            gv[r, :, tile] = (gv[r, :, tile].astype(f32) + gvh).astype(bf16)

        aws[...] += dot_tn(hid[0, 0], gl)
        gb = (dot_nt(gl, ws[0]) * slope[0, 0].astype(f32)).astype(bf16)
        gb_all[r, :, pl.ds(pl.multiple_of(h * width, 128), width)] = gb
        ab1[h] += jnp.sum(gb.astype(f32).reshape(-1, 8, width), axis=0)
        awf[...] += dot_tn(normed[0], gb)

    @pl.when(step == heads - 1)
    def _():
        more = dot_tn(normed[0], gv[r])

        @pl.when(r == 0)
        def _():
            awv[...] = more

        @pl.when(r != 0)
        def _():
            awv[...] += more

    def pack(i):
        def one(tt, carry):
            for cc in range(2):
                for zz in range(4):
                    at = pl.ds(pl.multiple_of((tt * 8 + cc * 4 + zz) * 24, 8), 24)
                    stack = [awf[at, 256 * j : 256 * j + 256] for j in range(3)]
                    stack += [aws[at, 256 * j : 256 * j + 256] for j in range(2)]
                    if i == 0:
                        stack = [awv[at, :]] + stack
                    if i == 1:
                        stack = stack + [stash[cc, zz, tt]]
                    whole = jnp.concatenate(stack, 0)
                    if i == 2:
                        stash[cc, zz, tt] = whole[0:8]
                        whole = whole[8:]
                    ga[cc, zz, tt, part(i)] = whole.astype(bf16)
            return carry

        lax.fori_loop(0, GROUP, one, 0)
        start(a1(i))

    @at_step(0, 3)
    def _():
        pack(2)

    @at_step(1, 3)
    def _():
        pack(1)

    @at_step(2, 3)
    def _():
        row = lax.broadcasted_iota(jnp.int32, (128, width), 0)
        stack = jnp.zeros((128, width), f32)
        lines = [jnp.sum(ab1[i], axis=0, keepdims=True) for i in range(heads)]
        for k, line in enumerate(lines + [jnp.sum(gg2[...], axis=0, keepdims=True)]):
            stack = jnp.where(row == 64 + k, line, stack)
        lane = lax.broadcasted_iota(jnp.int32, (width, 128), 1)
        awv[:, 128:256] = jnp.where(lane < 64, awv[:, 128:256], stack.T)
        pack(0)

    @pl.when(step == heads)
    def _():
        total = dot_nt(gb_all[r], wcat[...]) + dot_nt(gv[r], wv[...])

        @pl.when(r < 3)
        def _():
            gb_all[r, :, 0:width] = total.astype(bf16)

        @pl.when(r == 3)
        def _():
            gn[...] = total

    @at_step(3, 0)
    def _():
        out_n(0).start()
        meet(0)

    @at_step(3, 1)
    def _():
        out_n(1).start()
        a2(1).forward()

    @at_step(2, 3)
    def _():
        flat = jnp.concatenate([jnp.sum(ab2[k], axis=0, keepdims=True) for k in range(3)], 1)
        flat = jnp.broadcast_to(flat, (8, 1536))
        for cc in range(2):
            for zz in range(4):
                s = (cc * 4 + zz) * 192
                gs[cc, zz] = (pltpu.roll(flat, 1536 - s, 1) if s else flat)[:, 0:256]
        start(v1())

    @at_step(3, 2)
    def _():
        f4(0).forward()
        wait(v1())
        gs[c] += sb1[...]
        start(v2())

    @at_step(3, 3)
    def _():
        out_n(0).wait()

        def join(i, carry):
            at = pl.ds(pl.multiple_of(i * 128, 128), 128)
            here = gb_all[2, at, 0:width].astype(f32) + nb[0, at, :].astype(f32)
            gb_all[2, at, 0:width] = here.astype(bf16)
            return carry

        lax.fori_loop(0, 4, join, 0)
        out_n(2).start()
        deal(1)
        a2(0).forward()
        f4(1).finish()
        f4(0).finish()
        out_f[...] = fs[fast, z].astype(f32)
        out_n(1).wait()
        out_n(2).wait()
        wait(mine_t())

        def ln_back(i, carry):
            at = pl.ds(pl.multiple_of(i * 128, 128), 128)
            g = gn[at, :] + nb[1, at, :].astype(f32) + nb[2, at, :].astype(f32)
            unit, scale = centre_rows(tok[at, :].astype(f32))
            gu = g * small[3:4]
            back = scale * (
                gu - jnp.mean(gu, axis=-1, keepdims=True) - unit * jnp.mean(gu * unit, axis=-1, keepdims=True)
            )
            gtok[at, :] += back
            return carry

        lax.fori_loop(0, 4, ln_back, 0)
        wait(v2())
        out_s[...] = gs[c, z] + sb2[0] + sb2[1] + sb2[2]
        deal(0)
        for i in range(heads):
            wait(mine(i) + a3(i))


def back_call(wf, ws, wv, normed, values, hid, slope, prob, gmix, gg2, half, tokens, gmid, small):
    heads, width, slots = ws.shape
    rows = half.shape[-2]
    head = lambda h: jnp.maximum(heads - 1 - h, 0)
    held = lambda h, r: jnp.where(h < heads, r, GROUP - 1)
    by_head = lambda h, r: (head(h), 0, 0)
    row = lambda h, r: (r, 0, 0)
    early = lambda h, r: (held(h, r), 0, 0)
    both = lambda h, r: (head(h), held(h, r), 0, 0)
    flat = lambda h, r: (0, 0)
    return pl.pallas_call(
        back_kernel,
        grid=(heads + 1, GROUP),
        out_shape=(
            shape_of((rows, width), f32),
            shape_of((GROUP, 384, 256), bf16),
            shape_of((8, 256), f32),
            shape_of(tokens.shape, f32),
        ),
        in_specs=[
            ANY,
            pl.BlockSpec((1, width, slots), by_head),
            pl.BlockSpec((width, 256), flat),
            pl.BlockSpec((1, slots, width), row),
            pl.BlockSpec((1, slots, 256), early),
            pl.BlockSpec((1, 1, slots, width), both),
            pl.BlockSpec((1, 1, slots, width), both),
            pl.BlockSpec((1, 1, slots, slots), both),
            pl.BlockSpec((1, slots, 256), early),
            pl.BlockSpec((8, width), flat),
            ANY,
            ANY,
            ANY,
            pl.BlockSpec((8, width), flat),
        ],
        out_specs=(FULL, ANY, FULL, FULL),
        scratch_shapes=[
            pltpu.VMEM((width, heads * width), bf16),
            pltpu.VMEM((GROUP, slots, heads * width), bf16),
            pltpu.VMEM((width, width), f32),
            pltpu.VMEM((width, slots), f32),
            pltpu.VMEM((heads, 8, width), f32),
            pltpu.VMEM((heads, 8, slots), f32),
            pltpu.VMEM((slots, width), f32),
            pltpu.VMEM((GROUP, slots, 256), bf16),
            pltpu.VMEM((width, 256), f32),
            pltpu.VMEM((2, 4, GROUP, 8, 256), f32),
            pltpu.VMEM((2, 4, GROUP, 384, 256), bf16),
            pltpu.VMEM((2, 4, 8, 256), f32),
            pltpu.VMEM((3, slots, width), bf16),
            pltpu.VMEM((slots, width), bf16),
            pltpu.VMEM((2, 4, rows, width), bf16),
            pltpu.VMEM((2, 4, 128, width), bf16),
            pltpu.VMEM((4, rows, width), bf16),
            pltpu.VMEM((4, rows, width), bf16),
            pltpu.VMEM((4, GROUP, 384, 256), bf16),
            pltpu.VMEM((4, GROUP, 384, 256), bf16),
            pltpu.VMEM((4, 8, 256), f32),
            pltpu.VMEM((3, 8, 256), f32),
            DMA((2 * heads + 3,)),
            DMA((heads,)),
            DMA((heads,)),
            DMA((heads, 3)),
            DMA((heads, 4)),
            DMA((heads, 3)),
            DMA((heads, 3)),
            DMA((3,)),
            DMA((3,)),
            DMA((3,)),
            DMA((3,)),
            DMA((2, 3)),
            DMA((2, 4)),
            DMA((4,)),
            DMA((4,)),
        ],
        compiler_params=pltpu.CompilerParams(collective_id=3, has_side_effects=True, vmem_limit_bytes=VMEM_LIMIT),
    )(wf, ws, wv, normed, values, hid, slope, prob, gmix, gg2, half, tokens, gmid, small)


def finish_kernel(sums_a, sums_f, w_first, w_value, out_first, out_second, out_value, out_up, out_out, out_down, dots):
    heads_all, depth, width = w_first.shape
    heads = heads_all // GROUP
    total = jnp.zeros((depth, 256), f32)
    for t in range(GROUP):
        whole = sums_a[t].astype(f32)
        out_value[t] = whole[0:depth]
        total += jnp.where(
            lax.broadcasted_iota(jnp.int32, (depth, 256), 1) < 192, whole[0:depth] * w_value[t].astype(f32), 0.0
        )
        for i in range(heads):
            block = lambda j: whole[depth * (1 + 5 * i + j) : depth * (2 + 5 * i + j)]
            weight = w_first[heads * t + i].astype(f32)
            for j in range(3):
                at = slice(256 * j, 256 * j + 256)
                out_first[heads * t + i, :, at] = block(j)
                total += block(j) * weight[:, at]
            for j in range(2):
                out_second[heads * t + i, :, 256 * j : 256 * j + 256] = block(3 + j)
    dots[...] = jnp.broadcast_to(jnp.sum(total, axis=1, keepdims=True), dots.shape)
    for k in range(4):
        out_up[:, width * k : width * k + width] = sums_f[depth * k : depth * k + depth]
    out_out[...] = sums_f[4 * depth : 5 * depth]
    out_down[...] = sums_f[128:224]


def finish_call(sums_a, sums_f, w_first, w_value, slots):
    heads_all, depth, width = w_first.shape
    return pl.pallas_call(
        finish_kernel,
        out_shape=(
            shape_of((heads_all, depth, width), f32),
            shape_of((heads_all, depth, slots), f32),
            shape_of((GROUP, depth, 256), f32),
            shape_of((depth, 4 * width), f32),
            shape_of((depth, width), f32),
            shape_of((4 * depth, width), f32),
            shape_of((depth, 128), f32),
        ),
        in_specs=[FULL] * 4,
        out_specs=(FULL,) * 7,
        compiler_params=pltpu.CompilerParams(vmem_limit_bytes=VMEM_LIMIT),
    )(sums_a, sums_f, w_first, w_value)


def on_device_fast(tokens, lengths, gain_one, w_value, w_first, b_first, w_second, b_second, w_out, gain_two, w_up, w_down, grad_out):
    _, slots, width = tokens.shape
    heads_all, depth, _ = w_first.shape
    heads = heads_all // GROUP
    digits = jnp.stack([lengths[0] // 16, lengths[0] % 16]).astype(bf16)
    extra = jnp.concatenate(
        [
            w_value.reshape(depth, GROUP, -1).transpose(1, 0, 2),
            b_first.reshape(GROUP, heads, depth).transpose(0, 2, 1),
            jnp.broadcast_to(jnp.stack([gain_one, gain_two], 1), (GROUP, depth, 2)),
            jnp.broadcast_to(b_second.reshape(depth, 8), (GROUP, depth, 8)),
            jnp.broadcast_to(digits, (GROUP, depth, 2)),
            jnp.zeros((GROUP, depth, 49), bf16),
        ],
        2,
    )
    wf, ws, wv, small, normed, values, hid, slope, prob, joined, lf = attend_call(
        tokens, extra, w_first, w_second, w_out, w_up, w_down
    )
    result, gmid, gmix, half, gg2 = ffn_call(lf, joined, tokens[0], small, grad_out[0])
    out_f, out_a, out_s, gtok = back_call(
        wf, ws, wv, normed, values, hid, slope, prob, gmix, gg2, half, tokens[0], gmid, small
    )
    grad_first, grad_second, side, grad_up, grad_out_w, grad_down, dots = finish_call(
        out_a, out_f, w_first, extra, slots
    )
    return (
        result[None],
        gtok[None],
        dots[:, 0] / gain_one.astype(f32),
        side[:, :, :192].transpose(1, 0, 2).reshape(depth, width),
        grad_first,
        side[:, :, 192:195].transpose(0, 2, 1).reshape(heads_all, depth),
        grad_second,
        out_s[0, : b_second.shape[0]],
        grad_out_w,
        jnp.sum(side[:, :, 195], axis=0),
        grad_up,
        grad_down,
    )


def solution(mesh):
    wide, narrow = mesh.shape["wide"], mesh.shape["narrow"]
    grouped = Mesh(mesh.devices.reshape(GROUP, wide // GROUP, narrow), ALL)
    vec = P(ALL)
    flat = P(ALL, None)
    mid = P(None, ALL, None)
    row = P(ALL, None, None)
    body = on_device_fast if (wide, narrow) == (8, 4) else on_device
    return jax.shard_map(
        body,
        mesh=grouped,
        in_specs=(row, vec, vec, flat, mid, P(None, ALL), mid, vec, flat, vec, flat, flat, row),
        out_specs=(row, row, vec, flat, mid, P(None, ALL), mid, vec, flat, vec, flat, flat),
        check_vma=False,
    )
```

```python
import jax
import jax.numpy as jnp
from jax import lax
from jax.experimental import pallas as pl
from jax.experimental.pallas import tpu as pltpu
from jax.sharding import Mesh
from jax.sharding import PartitionSpec as P

epsilon = 1e-05
f32 = jnp.float32
bf16 = jnp.bfloat16
GROUP = 4


def norm_rows(values, factor):
    average = jnp.mean(values, axis=-1, keepdims=True)
    centred = values - average
    spread = jnp.mean(centred * centred, axis=-1, keepdims=True)
    return centred * lax.rsqrt(spread + epsilon) * factor


def smooth(values):
    return jax.nn.gelu(values, approximate=False)


def mm(spec, a, b):
    return jnp.einsum(spec, a, b, preferred_element_type=f32)


REST = ("rep", "narrow")
ALL = ("tp", "rep", "narrow")


def to_heads(shard):
    heads, depth, width = shard.shape
    pieces = lax.all_to_all(shard.reshape(GROUP, heads // GROUP, depth, width), "tp", 0, 0)
    whole = lax.all_gather(pieces, REST, axis=0)
    return whole.transpose(2, 1, 0, 3, 4).reshape(heads // GROUP, -1, width)


def from_heads(grad):
    heads, depth, width = grad.shape
    n = lax.axis_size("rep") * lax.axis_size("narrow")
    pieces = grad.astype(bf16).reshape(heads, GROUP, n, depth // (GROUP * n), width).transpose(2, 1, 0, 3, 4)
    pieces = pieces.reshape((n * GROUP,) + pieces.shape[2:])
    share = lax.psum_scatter(pieces, REST, scatter_dimension=0, tiled=True)
    share = lax.all_to_all(share, "tp", 0, 0)
    return share.reshape(heads * GROUP, depth // (GROUP * n), width).astype(f32)


def on_device(tokens, lengths, gain_one, w_value, w_first, b_first, w_second, b_second, w_out, gain_two, w_up, w_down, grad_out):
    row_count, slots, width = tokens.shape
    heads_all = w_first.shape[0]
    heads = heads_all // GROUP
    head_size = width // heads_all
    me = lax.axis_index("tp")
    depth = w_value.shape[0]

    small = [gain_one, gain_two, b_second, b_first.reshape(-1)]
    gathered = lax.all_gather(jnp.concatenate(small), ALL, axis=0)
    n_all = gathered.shape[0]
    g1 = gathered[:, :depth].reshape(-1).astype(f32)
    g2 = gathered[:, depth : 2 * depth].reshape(-1).astype(f32)
    b2_len = b_second.shape[0]
    b2 = gathered[:, 2 * depth : 2 * depth + b2_len].reshape(heads_all, slots).astype(f32)
    b1 = gathered[:, 2 * depth + b2_len :].reshape(n_all, heads_all, depth).transpose(1, 0, 2).reshape(heads_all, width).astype(f32)
    b1 = lax.dynamic_slice_in_dim(b1, me * heads, heads, 0)
    b2 = lax.dynamic_slice_in_dim(b2, me * heads, heads, 0)

    wf = to_heads(w_first)
    ws = to_heads(w_second)
    wv = to_heads(w_value.reshape(depth, GROUP, width // GROUP).transpose(1, 0, 2))[0]
    rows = lax.all_gather(tokens, "tp", axis=0, tiled=True)
    lens = lax.all_gather(lengths, "tp", axis=0, tiled=True)
    n_rows = rows.shape[0]

    normed = norm_rows(rows.astype(f32), g1).astype(bf16)
    values = mm("rsd,de->rse", normed, wv).astype(bf16)
    per_head = values.reshape(n_rows, slots, heads, head_size).transpose(2, 0, 1, 3)
    before = mm("rsd,hde->hrse", normed, wf) + b1[:, None, None, :]
    hidden = smooth(before).astype(bf16)
    logits = mm("hrse,hej->hrsj", hidden, ws) + b2[:, None, None, :]
    visible = lax.broadcasted_iota(jnp.int32, (1, n_rows, 1, slots), 3) < lens[None, :, None, None]
    masked = jnp.where(visible, logits, f32(-1e30))
    scaled = jnp.exp(masked - jnp.max(masked, axis=-1, keepdims=True))
    probabilities = scaled / jnp.sum(scaled, axis=-1, keepdims=True)
    weights = probabilities.astype(bf16)
    mixture = mm("hrsj,hrjc->rshc", weights, per_head).astype(bf16)
    mixture = mixture.reshape(GROUP, row_count, slots, heads * head_size)
    joined = lax.all_to_all(mixture, "tp", 0, 0).transpose(1, 2, 0, 3).reshape(row_count * slots, width)

    wo = lax.all_gather(w_out, ALL, axis=0, tiled=True)
    wu = lax.all_gather(w_up, ALL, axis=0, tiled=True)
    wd = lax.all_gather(w_down, ALL, axis=0, tiled=True)
    inputs = tokens.astype(f32).reshape(-1, width)
    middle = inputs + mm("sd,de->se", joined, wo)
    normed_two, norm_two_back = jax.vjp(norm_rows, middle, g2)
    normed_two = normed_two.astype(bf16)
    upward = mm("td,df->tf", normed_two, wu)
    active, smooth_up_back = jax.vjp(smooth, upward)
    active = active.astype(bf16)
    result = middle + mm("tf,fd->td", active, wd)

    g_out = grad_out.reshape(-1, width)
    grad_branch = g_out.astype(bf16)
    grad_w_down = mm("tf,td->fd", active, grad_branch)
    grad_upward = smooth_up_back(mm("td,fd->tf", grad_branch, wd))[0].astype(bf16)
    grad_w_up = mm("td,tf->df", normed_two, grad_upward)
    grad_middle_norm, grad_gain_two = norm_two_back(mm("tf,df->td", grad_upward, wu))
    grad_middle = g_out + grad_middle_norm
    grad_attn = grad_middle.astype(bf16)
    grad_w_out = mm("sd,se->de", joined, grad_attn)
    grad_joined = mm("se,de->sd", grad_attn, wo).astype(bf16)

    grad_mixture = grad_joined.reshape(row_count, slots, GROUP, heads * head_size).transpose(2, 0, 1, 3)
    grad_mixture = lax.all_to_all(grad_mixture, "tp", 0, 0).reshape(n_rows, slots, heads, head_size).transpose(2, 0, 1, 3)
    grad_weights = mm("hrsc,hrjc->hrsj", grad_mixture, per_head)
    grad_values = mm("hrsj,hrsc->rjhc", weights, grad_mixture).astype(bf16).reshape(n_rows, slots, heads * head_size)
    centre = jnp.sum(probabilities * grad_weights, axis=-1, keepdims=True)
    grad_logits = (probabilities * (grad_weights - centre)).astype(bf16)
    grad_b_second = jnp.sum(grad_logits.astype(f32), axis=(1, 2))
    grad_w_second = mm("hrse,hrsj->hej", hidden, grad_logits)
    grad_hidden = mm("hrsj,hej->hrse", grad_logits, ws)
    smooth_value, smooth_back = jax.vjp(smooth, before)
    grad_before = smooth_back(grad_hidden)[0].astype(bf16)
    grad_b_first = jnp.sum(grad_before.astype(f32), axis=(1, 2))
    grad_w_first = mm("rsd,hrse->hde", normed, grad_before)
    grad_w_value = mm("rsd,rse->de", normed, grad_values)
    grad_normed = mm("hrse,hde->rsd", grad_before, wf) + mm("rse,de->rsd", grad_values, wv)
    grad_normed = lax.psum_scatter(grad_normed.astype(bf16), "tp", scatter_dimension=0, tiled=True)
    value, norm_one_back = jax.vjp(norm_rows, inputs, g1)
    grad_inputs_norm, grad_gain_one = norm_one_back(grad_normed.astype(f32).reshape(-1, width))
    grad_tokens = grad_middle + grad_inputs_norm

    out_first = from_heads(grad_w_first)
    out_second = from_heads(grad_w_second)
    out_value = from_heads(grad_w_value[None]).transpose(1, 0, 2).reshape(depth, width)

    def share(grad):
        return lax.psum_scatter(grad.astype(bf16), ALL, scatter_dimension=0, tiled=True).astype(f32)

    vec_tp = jnp.concatenate([grad_b_first.reshape(-1), grad_b_second.reshape(-1)])
    vec_tp = lax.dynamic_update_slice_in_dim(jnp.zeros((GROUP, vec_tp.shape[0]), f32), vec_tp[None], me, 0)
    vec = jnp.concatenate([vec_tp.reshape(-1), grad_gain_one, grad_gain_two])
    vec = lax.psum(vec, ALL)
    index = (me * lax.axis_size("rep") + lax.axis_index("rep")) * lax.axis_size("narrow") + lax.axis_index("narrow")
    n_tp = GROUP * (heads * width + heads * slots)
    tp_part = vec[:n_tp].reshape(GROUP, -1)
    gb1 = tp_part[:, : heads * width].reshape(heads_all, width)
    gb2 = tp_part[:, heads * width :].reshape(-1)
    gb1 = lax.dynamic_slice_in_dim(gb1, index * depth, depth, 1)
    gb2 = lax.dynamic_slice_in_dim(gb2, index * b2_len, b2_len, 0)
    gg1 = lax.dynamic_slice_in_dim(vec[n_tp : n_tp + width], index * depth, depth, 0)
    gg2 = lax.dynamic_slice_in_dim(vec[n_tp + width :], index * depth, depth, 0)
    shape = tokens.shape
    return (
        result.reshape(shape),
        grad_tokens.reshape(shape),
        gg1,
        out_value,
        out_first,
        gb1,
        out_second,
        gb2,
        share(grad_w_out),
        gg2,
        share(grad_w_up),
        share(grad_w_down),
    )


MESH = pl.DeviceIdType.MESH
VMEM_LIMIT = 60 * 2**20
ANY = pl.BlockSpec(memory_space=pl.ANY)
FULL = pl.BlockSpec(memory_space=pltpu.VMEM)
DMA = pltpu.SemaphoreType.DMA


def shape_of(dims, kind):
    return jax.ShapeDtypeStruct(dims, kind)


def dot_nt(a, b):
    return lax.dot_general(a, b, (((1,), (1,)), ((), ())), preferred_element_type=f32)


def dot_tn(a, b):
    return lax.dot_general(a, b, (((0,), (0,)), ((), ())), preferred_element_type=f32)


def dot_nn(a, b):
    return lax.dot_general(a, b, (((1,), (0,)), ((), ())), preferred_element_type=f32)


def place():
    return lax.axis_index("tp"), lax.axis_index("rep"), lax.axis_index("narrow")


def group_peers():
    t, c, z = place()
    along_x = t + 1 - 2 * (t % 2)
    along_y = (t + 2) % GROUP
    return [GROUP - 1 - t, (1 - c) * along_x + c * along_y, (1 - c) * along_y + c * along_x]


def line_peers():
    z = lax.axis_index("narrow")
    return [(z + k) % 4 for k in (1, 2, 3)]


def line_place():
    z = lax.axis_index("narrow")
    side = z // 2
    end, inner = 3 * side, 1 + side
    return end, inner, 2 - side, 3 - 3 * side, end + inner - z, z == inner


class Spread:
    def __init__(self, slabs, send, recv, source=None):
        t, c, z = place()
        end, inner, other, far, near, is_inner = line_place()
        self.is_inner = is_inner
        move = lambda o, k, to: remote(slabs(o), slabs(o), send.at[k], recv.at[o], (t, c, to))
        source = slabs(z) if source is None else source
        give = lambda k, to: remote(source, slabs(z), send.at[k], recv.at[z], (t, c, to))
        self.own = lambda: [give(0, other), give(1, near)]
        self.on = lambda: [move(other, 2, end), move(far, 3, end)]
        self.near = lambda: move(near, 0, near)

    def begin(self):
        start(self.own())

    def forward(self):
        @pl.when(self.is_inner)
        def _():
            for copy in self.on():
                copy.wait_recv()
            start(self.on())

    def finish(self):
        self.near().wait_recv()

        @pl.when(jnp.logical_not(self.is_inner))
        def _():
            for copy in self.on():
                copy.wait_recv()

        for copy in self.own():
            copy.wait_send()

        @pl.when(self.is_inner)
        def _():
            for copy in self.on():
                copy.wait_send()


class Gather:
    def __init__(self, slabs, land, add, send, recv):
        t, c, z = place()
        end, inner, other, far, near, is_inner = line_place()
        self.is_inner, self.add, self.z = is_inner, add, z
        self.other, self.far = other, far
        move = lambda o, slot, k, to: remote(slabs(o), land(slot), send.at[k], recv.at[slot], (t, c, to))
        self.out = lambda: [move(far, 2, 0, inner), move(other, 1, 1, inner), move(inner, 0, 2, inner)]
        self.back = lambda: [move(end, 0, 2, end)]
        self.on_far = lambda: [move(far, 1, 0, far)]
        self.on_other = lambda: [move(other, 3, 1, other)]
        self.got = lambda slot: move(z, slot, 0, near).wait_recv()

    def begin(self):
        @pl.when(self.is_inner)
        def _():
            start(self.back())

        @pl.when(jnp.logical_not(self.is_inner))
        def _():
            start(self.out())

    def forward(self):
        @pl.when(self.is_inner)
        def _():
            self.got(2)
            self.add(self.far, 2)
            start(self.on_far())
            self.got(1)
            self.add(self.other, 1)
            start(self.on_other())

    def finish(self):
        self.got(0)
        self.add(self.z, 0)

        @pl.when(self.is_inner)
        def _():
            self.got(3)
            self.add(self.z, 3)
            for copy in self.back() + self.on_far() + self.on_other():
                copy.wait_send()

        @pl.when(jnp.logical_not(self.is_inner))
        def _():
            self.got(1)
            self.add(self.z, 1)
            for copy in self.out():
                copy.wait_send()


def greet(devices):
    barrier = pltpu.get_barrier_semaphore()
    for device in devices:
        pl.semaphore_signal(barrier, inc=1, device_id=device, device_id_type=MESH)


def met(count):
    pl.semaphore_wait(pltpu.get_barrier_semaphore(), count)


def remote(src, dst, send, recv, device):
    return pltpu.make_async_remote_copy(
        src_ref=src, dst_ref=dst, send_sem=send, recv_sem=recv, device_id=device, device_id_type=MESH
    )


def local(src, dst, sem):
    return pltpu.make_async_copy(src, dst, sem)


def start(copies):
    for copy in copies:
        copy.start()


def wait(copies):
    for copy in copies:
        copy.wait()


def square():
    t, c, z = place()
    y, x = t // 2, t % 2
    tps = group_peers()
    slow, fast = (1 - c) * y + c * x, (1 - c) * x + c * y
    return slow, fast, (tps[2], c, z), (tps[1], c, z)


def gelu_pair(v):
    cdf = 0.5 * (1.0 + lax.erf(v * 0.7071067811865476))
    return v * cdf, cdf + v * (jnp.exp(-0.5 * v * v) * 0.3989422804014327)


def centre_rows(v):
    shifted = v - jnp.mean(v, axis=-1, keepdims=True)
    scale = lax.rsqrt(jnp.mean(shifted * shifted, axis=-1, keepdims=True) + epsilon)
    return shifted * scale, scale


ROWS = ((0, 144), (144, 272), (272, 384))


def part(i):
    return slice(*ROWS[i])


def attend_kernel(
    tokens, extra, w_first, w_second, w_out, w_up, w_down,
    wf, ws, wv, small, normed, values, hid, slope, prob, joined, lf,
    pa, pf, la, lt, nrm, val, cols, b2, masks, join, own, s1, r1, s2, r2, s3, r3, st, rt, s1f, r1f, sf, rf, sj, rj,
):
    h, r = pl.program_id(0), pl.program_id(1)
    width = wf.shape[-1]
    heads = w_first.shape[0] // GROUP
    t, c, z = place()
    sibling = (t, 1 - c, z)
    tps, zs = group_peers(), line_peers()
    slow, fast, slow_dev, fast_dev = square()

    a1 = lambda i: [
        remote(pa.at[p, part(i)], la.at[c, z, t, part(i)], s1.at[i, k], r1.at[i, k], (p, c, z))
        for k, p in enumerate(tps)
    ]
    a2 = lambda i: Spread(lambda o: la.at[c, o, :, part(i)], s2.at[i], r2.at[i])
    a3 = lambda i: [remote(la.at[c, :, :, part(i)], la.at[c, :, :, part(i)], s3.at[i], r3.at[i], sibling)]
    mine = lambda i: [local(pa.at[t, part(i)], la.at[c, z, t, part(i)], own.at[i])]
    mine_t = lambda: [local(tokens.at[0], lt.at[3], own.at[heads])]
    mine_f = lambda: [local(pf, lf.at[c, slow, fast, z], own.at[heads + 1])]
    mine_j = lambda: [local(join.at[3], joined.at[t], own.at[heads + 2])]
    tok_fast = lambda: remote(tokens.at[0], lt.at[1], st.at[0], rt.at[0], fast_dev)
    tok_slow = lambda: remote(tokens.at[0], lt.at[2], st.at[1], rt.at[1], slow_dev)
    tok_on = lambda: remote(lt.at[1], lt.at[0], st.at[2], rt.at[2], slow_dev)
    f1 = lambda k: Spread(lambda o: lf.at[c, slow, fast, o, cut(k)], s1f.at[k], r1f.at[k], pf.at[cut(k)])

    def whole(k, spot, n, device):
        piece = lf.at[spot + (slice(None),) * (4 - len(spot)) + (cut(k),)]
        return [remote(piece, piece, sf.at[k, n], rf.at[k, n], device)]

    f2 = lambda k: whole(k, (c, slow, fast), 0, fast_dev)
    f3 = lambda k: whole(k, (c, slow), 1, slow_dev)
    f4 = lambda k: whole(k, (c, slow), 2, sibling)
    f5 = lambda k: whole(k, (c, 1 - slow), 3, sibling)
    out_j = lambda k: [remote(join.at[k], joined.at[t], sj.at[k], rj.at[k], (tps[k], c, z))]

    def at_step(i, j):
        return pl.when((h == i) & (r == j))

    @at_step(0, 0)
    def _():
        greet([(p, c, z) for p in tps] + [(t, c, p) for p in zs] + [sibling])
        blocks = lambda v: [v[:, k : k + 256] for k in range(0, v.shape[1], 256)]
        ups = [w_up[:, k : k + width].astype(f32) for k in range(0, w_up.shape[1], width)]
        pf[0:96] = jnp.concatenate(ups, 0).astype(bf16)
        pf[96:128] = jnp.concatenate([w_out[...].astype(f32), jnp.zeros((8, width), f32)], 0).astype(bf16)
        pf[128:224] = w_down[...]
        for p in range(GROUP):
            stack = [extra[p].astype(f32)]
            for i in range(heads):
                stack += blocks(w_first[heads * p + i].astype(f32)) + blocks(w_second[heads * p + i].astype(f32))
            pa[p] = jnp.concatenate(stack, 0).astype(bf16)
        met(7)
        f1(0).begin()
        for i in range(heads):
            start(mine(i) + a1(i))
        start(mine_f() + mine_t())
        wait(mine(0) + a1(0))
        a2(0).begin()
        wait(mine(1) + a1(1))
        wait(mine(2) + a1(2))
        start([tok_fast(), tok_slow()])
        f1(0).forward()
        f1(1).begin()
        a2(0).forward()
        a2(1).begin()
        tok_fast().wait_recv()
        tok_on().start()
        f1(0).finish()
        wait(mine_f())
        start(f2(0))
        a2(0).finish()
        start(a3(0))
        f1(1).forward()
        a2(1).forward()
        a2(2).begin()
        wait(mine_t() + a3(0))
        tok_fast().wait_send()
        tok_slow().wait()
        tok_on().wait()

    @at_step(0, 1)
    def _():
        wait(f2(0))
        start(f3(0) + f4(0))
        f1(1).finish()
        start(f2(1))

    @at_step(0, 3)
    def _():
        a2(2).forward()

    @at_step(1, 0)
    def _():
        a2(1).finish()
        start(a3(1))
        wait(a3(1))

    @at_step(1, 1)
    def _():
        wait(f2(1))
        start(f3(1) + f4(1))

    @at_step(2, 0)
    def _():
        a2(2).finish()
        start(a3(2))
        wait(f3(0))
        start(f5(0))
        wait(a3(2))

    def unpack(i):
        def one(tt, carry):
            for cc in range(2):
                for zz in range(0, 4, 2):
                    at = pl.ds(pl.multiple_of((tt * 8 + cc * 4 + zz) * 24, 48), 48)

                    def block(first):
                        low = first // 16 * 16
                        both = [la[cc, zz + k, tt, low : low + 32].astype(f32)[first - low :][:24] for k in range(2)]
                        return jnp.concatenate(both, 0)

                    base = 24 + 120 * i
                    for j in range(3):
                        wf[0, at, 256 * j : 256 * j + 256] = block(base + 24 * j).astype(bf16)
                    for j in range(2):
                        ws[0, at, 256 * j : 256 * j + 256] = block(base + 72 + 24 * j).astype(bf16)
                    if i == 0:
                        both = block(0)
                        cols[at, :] = both[:, 128:256]
                        lane = lax.broadcasted_iota(jnp.int32, both.shape, 1)
                        wv[at, :] = jnp.where(lane < 192, both, 0.0).astype(bf16)

            return carry

        lax.fori_loop(0, GROUP, one, 0)

    for i in range(heads):

        @at_step(i, 0)
        def _():
            unpack(i)

    @at_step(0, 0)
    def _():
        small[...] = cols[...].T[64:72]
        mine_rows = cols[pl.ds(pl.multiple_of(t * 192, 192), 192), :].astype(bf16)
        lane = lax.broadcasted_iota(jnp.int32, (128, 512), 0)
        spot = lax.broadcasted_iota(jnp.int32, (128, 512), 1)
        spread = dot_nn(mine_rows, jnp.where(lane - 69 == spot % 8, 1.0, 0.0).astype(bf16))
        row = lax.broadcasted_iota(jnp.int32, (64, 512), 0)
        spot = lax.broadcasted_iota(jnp.int32, (64, 512), 1)
        for i in range(heads):
            picked = jnp.where(row == spot // 8, spread[64 * i : 64 * i + 64], 0.0)
            b2[i] = jnp.broadcast_to(jnp.sum(picked, axis=0, keepdims=True), (8, 512))
        for k, p in enumerate(tps + [t]):
            line = cols[pl.ds(pl.multiple_of((p * 8 + c * 4 + z) * 24, 8), 8), :]
            lane = lax.broadcasted_iota(jnp.int32, line.shape, 1)
            digits = jnp.where(lane == 77, 16.0 * line, jnp.where(lane == 78, line, 0.0))
            length = jnp.sum(digits, axis=1, keepdims=True)
            spot = lax.broadcasted_iota(jnp.int32, (8, 512), 1).astype(f32)
            masks[k] = jnp.where(spot < length, 0.0, -1e30)

    @pl.when(h == 0)
    def _():
        unit, _ = centre_rows(lt[r].astype(f32))
        out = (unit * small[3:4]).astype(bf16)
        nrm[r] = out
        normed[0] = out
        v = dot_nn(out, wv[...]).astype(bf16)
        val[r] = v
        values[0] = v

    row = lax.broadcasted_iota(jnp.int32, (8, width), 0)
    b1 = jnp.sum(jnp.where(row == h, small[...], 0.0), axis=0, keepdims=True)
    shift = b2[h, 0:1] + masks[r, 0:1]
    tile = pl.ds(pl.multiple_of((h // 2) * 128, 128), 128)
    step = 256
    for m in range(0, 512, step):
        at = slice(m, m + step)
        before = dot_nn(nrm[r, at, :], wf[0]) + b1
        out, grad = gelu_pair(before)
        hidden = out.astype(bf16)
        hid[0, 0, at, :] = hidden
        slope[0, 0, at, :] = grad.astype(bf16)
        logits = dot_nn(hidden, ws[0]) + shift
        e = jnp.exp(logits - jnp.max(logits, axis=-1, keepdims=True))
        p = (e * (1.0 / jnp.sum(e, axis=-1, keepdims=True))).astype(bf16)
        prob[0, 0, at, :] = p
        mix = dot_nn(p, val[r, :, tile])
        lane = lax.broadcasted_iota(jnp.int32, mix.shape, 1)
        old = join[r, at, tile].astype(f32)
        join[r, at, tile] = jnp.where((h == 1) & (lane < 64), old, mix).astype(bf16)

    for k in range(3):

        @at_step(2, k)
        def _():
            start(out_j(k))

    @at_step(2, 2)
    def _():
        wait(f3(1))
        start(f5(1))

    @at_step(2, 3)
    def _():
        start(mine_j())
        for k in range(2):
            wait(f4(k) + f5(k))
        for k in range(3):
            wait(out_j(k))
        wait(mine_j())


def attend_call(tokens, extra, w_first, w_second, w_out, w_up, w_down):
    _, slots, width = tokens.shape
    heads = w_first.shape[0] // GROUP
    by_row = lambda h, r: (jnp.where(h == 0, r, GROUP - 1), 0, 0)
    by_head = lambda h, r: (h, 0, 0)
    both = lambda h, r: (h, r, 0, 0)
    rows_f = 2 * w_down.shape[0] + 32
    return pl.pallas_call(
        attend_kernel,
        grid=(heads, GROUP),
        out_shape=(
            shape_of((heads, width, width), bf16),
            shape_of((heads, width, slots), bf16),
            shape_of((width, 256), bf16),
            shape_of((8, width), f32),
            shape_of((GROUP, slots, width), bf16),
            shape_of((GROUP, slots, 256), bf16),
            shape_of((heads, GROUP, slots, width), bf16),
            shape_of((heads, GROUP, slots, width), bf16),
            shape_of((heads, GROUP, slots, slots), bf16),
            shape_of((GROUP, slots, 256), bf16),
            shape_of((2, 2, 2, 4, rows_f, width), bf16),
        ),
        in_specs=[ANY] + [FULL] * 6,
        out_specs=(
            pl.BlockSpec((1, width, width), by_head),
            pl.BlockSpec((1, width, slots), by_head),
            pl.BlockSpec((width, 256), lambda h, r: (0, 0)),
            pl.BlockSpec((8, width), lambda h, r: (0, 0)),
            pl.BlockSpec((1, slots, width), by_row),
            pl.BlockSpec((1, slots, 256), by_row),
            pl.BlockSpec((1, 1, slots, width), both),
            pl.BlockSpec((1, 1, slots, width), both),
            pl.BlockSpec((1, 1, slots, slots), both),
            ANY,
            ANY,
        ),
        scratch_shapes=[
            pltpu.VMEM((GROUP, 384, 256), bf16),
            pltpu.VMEM((rows_f, width), bf16),
            pltpu.VMEM((2, 4, GROUP, 384, 256), bf16),
            pltpu.VMEM((GROUP, slots, width), bf16),
            pltpu.VMEM((GROUP, slots, width), bf16),
            pltpu.VMEM((GROUP, slots, 256), bf16),
            pltpu.VMEM((width, 128), f32),
            pltpu.VMEM((heads, 8, slots), f32),
            pltpu.VMEM((GROUP, 8, slots), f32),
            pltpu.VMEM((GROUP, slots, 256), bf16),
            DMA((heads + 3,)),
            DMA((heads, 3)),
            DMA((heads, 3)),
            DMA((heads, 4)),
            DMA((heads, 4)),
            DMA((heads,)),
            DMA((heads,)),
            DMA((3,)),
            DMA((3,)),
            DMA((2, 4)),
            DMA((2, 4)),
            DMA((2, 4)),
            DMA((2, 4)),
            DMA((3,)),
            DMA((3,)),
        ],
        compiler_params=pltpu.CompilerParams(collective_id=1, has_side_effects=True, vmem_limit_bytes=VMEM_LIMIT),
    )(tokens, extra, w_first, w_second, w_out, w_up, w_down)


def slab(t, c, z):
    y, x = t // 2, t % 2
    return (0, y, x, z) if c == 0 else (1, x, y, z)


CUTS = ((0, 128), (128, 224))


def cut(k):
    return slice(*CUTS[k])


def ffn_kernel(
    lf_far, joined, tokens, small, gout, result, gmid, gmix, half, gg2,
    lf, gf, gj, more, meet_b, acts, slopes, wu, wo, n2, gn2, gwu, loads, own, sg, rg, sx, rx, sb, rb,
):
    width = tokens.shape[-1]
    me, core, z_me = place()
    tps = group_peers()
    slow, fast, slow_dev, fast_dev = square()
    sibling = (me, 1 - core, z_me)
    parts = (slice(0, 48), slice(128, 224), slice(96, 128), slice(48, 96))
    wanted = (slice(0, 96), slice(128, 224), slice(96, 128))
    cross = lambda k: [
        remote(
            gf.at[1 - core, :, :, :, parts[k], :], more.at[:, :, :, parts[k], :], sx.at[k], rx.at[k], sibling
        )
    ]
    over = lambda: remote(gf.at[core, 1 - slow, :, :, cut(1), :], meet_b, sb, rb, slow_dev)
    out_g = lambda k: [remote(gj.at[tps[k]], gmix.at[k], sg.at[k], rg.at[k], (tps[k], core, z_me))]
    greet([(p, core, z_me) for p in tps] + [sibling])
    load = lambda k: local(lf_far.at[:, :, :, :, wanted[k], :], lf.at[:, :, :, :, wanted[k], :], loads.at[k])
    for k in (2, 0, 1):
        load(k).start()
    load(2).wait()
    wo[...] = jnp.zeros_like(wo)
    for t in range(GROUP):
        for c in range(2):
            for z in range(0, 4, 2):
                pair = [lf[slab(t, c, z + k) + (slice(96, 128),)].astype(f32)[0:24] for k in range(2)]
                wo[t, (c * 4 + z) * 24 : (c * 4 + z) * 24 + 48, :] = jnp.concatenate(pair, 0).astype(bf16)
    middle = tokens[...].astype(f32)
    for t in range(GROUP):
        middle = middle + dot_nn(joined[t], wo[t])
    result[...] = middle
    gmid[...] = middle
    g2 = small[4:5]
    unit, _ = centre_rows(middle)
    n2[...] = (unit * g2).astype(bf16)
    gn2[...] = jnp.zeros_like(gn2)
    load(0).wait()

    def fold(k):
        def one(i, carry):
            for j in range(2):
                for z in range(4):
                    spot = (i, j, z, parts[k])
                    gf[(core,) + spot] = (gf[(core,) + spot].astype(f32) + more[spot].astype(f32)).astype(bf16)
            return carry

        lax.fori_loop(0, 2, one, 0)

    def ahead(p, carry):
        rows = pl.ds(pl.multiple_of(p * 48, 16), 48)
        for t in range(GROUP):
            for c in range(2):
                for z in range(0, 4, 2):
                    ends = [lf[slab(t, c, z + k) + (rows,)].astype(f32) for k in range(2)]
                    at = (t * 8 + c * 4 + z) * 24
                    for k in range(2):
                        both = jnp.concatenate([e[24 * k : 24 * k + 24] for e in ends], 0)
                        wu[2 * p + k, at : at + 48, :] = both.astype(bf16)
        branch = gout[...].astype(bf16)
        for k in range(2):
            act, slope = gelu_pair(dot_nn(n2[...], wu[2 * p + k]))
            act = act.astype(bf16)
            acts[2 * p + k] = act
            slopes[2 * p + k] = slope.astype(bf16)
            gwd = dot_tn(act, branch).astype(bf16)
            gf[0, p, k, :, 128:224, :] = gwd[:384].reshape(4, 96, width)
            gf[1, k, p, :, 128:224, :] = gwd[384:].reshape(4, 96, width)
        return carry

    def down_block(p, k):
        return jnp.concatenate(
            [lf[0, p, k, :, 128:224, :].reshape(384, width), lf[1, k, p, :, 128:224, :].reshape(384, width)], 0
        )

    def behind(p, carry):
        @pl.when(p == 1)
        def _():
            wait(cross(1))
            fold(1)
            over().start()

        branch = gout[...].astype(bf16)
        for k in range(2):
            gup = (dot_nt(branch, down_block(p, k)) * slopes[2 * p + k].astype(f32)).astype(bf16)
            slopes[2 * p + k] = gup
            gn2[...] += dot_nt(gup, wu[2 * p + k])
        return carry

    def weights(p, carry):
        rows = pl.ds(pl.multiple_of(p * 48, 16), 48)
        for k in range(2):
            gwu[k] = dot_tn(n2[...], slopes[2 * p + k])
            result[...] += dot_nn(acts[2 * p + k], down_block(p, k))
        for t in range(GROUP):
            for c in range(2):
                for z in range(4):
                    at = (t * 8 + c * 4 + z) * 24
                    both = jnp.concatenate([gwu[0, at : at + 24, :], gwu[1, at : at + 24, :]], 0)
                    gf[slab(t, c, z) + (rows,)] = both.astype(bf16)
        for k, n in ((0, 0), (1, 3)):

            @pl.when(p == k)
            def _():
                start(cross(n))

        return carry

    lax.fori_loop(0, 2, ahead, 0)
    met(4)
    start(cross(1))
    load(1).wait()

    lax.fori_loop(0, 2, behind, 0)
    unit, scale = centre_rows(gmid[...])
    gn = gn2[...]
    gg2[...] = jnp.sum((gn * unit).reshape(-1, 8, width), axis=0)
    gu = gn * g2
    back = scale * (
        gu - jnp.mean(gu, axis=-1, keepdims=True) - unit * jnp.mean(gu * unit, axis=-1, keepdims=True)
    )
    gm = gout[...] + back
    gmid[...] = gm
    ga = gm.astype(bf16)
    for t in range(GROUP):
        gj[t] = dot_nt(ga, wo[t]).astype(bf16)
    for k in range(3):
        start(out_g(k))
    mine = local(gj.at[me], gmix.at[3], own.at[0])
    mine.start()
    for t in range(GROUP):
        gwo = dot_tn(joined[t], ga)
        for c in range(2):
            for z in range(4):
                at = (c * 4 + z) * 24
                padded = jnp.concatenate([gwo[at : at + 24, :], jnp.zeros((8, width), f32)], 0)
                gf[slab(t, c, z) + (slice(96, 128),)] = padded.astype(bf16)
    start(cross(2))
    lax.fori_loop(0, 2, weights, 0)
    over().wait()

    def arrived(j, carry):
        for z in range(4):
            spot = (core, slow, j, z, cut(1))
            gf[spot] = (gf[spot].astype(f32) + meet_b[j, z].astype(f32)).astype(bf16)
        return carry

    lax.fori_loop(0, 2, arrived, 0)
    leave = [local(gf.at[core, :, :, :, cut(k), :], half.at[:, :, :, cut(k), :], own.at[1 + k]) for k in range(2)]
    leave[1].start()
    for k in (2, 0, 3):
        wait(cross(k))
        fold(k)
    leave[0].start()
    for k in range(3):
        wait(out_g(k))
    mine.wait()
    wait(leave)


def ffn_call(lf, joined, tokens, small, gout):
    slots, width = tokens.shape
    return pl.pallas_call(
        ffn_kernel,
        out_shape=(
            shape_of((slots, width), f32),
            shape_of((slots, width), f32),
            shape_of(joined.shape, bf16),
            shape_of(lf.shape[1:], bf16),
            shape_of((8, width), f32),
        ),
        in_specs=[ANY] + [FULL] * 4,
        out_specs=(FULL, FULL, ANY, ANY, FULL),
        scratch_shapes=[
            pltpu.VMEM(lf.shape, bf16),
            pltpu.VMEM(lf.shape, bf16),
            pltpu.VMEM(joined.shape, bf16),
            pltpu.VMEM(lf.shape[1:], bf16),
            pltpu.VMEM((2, 4, 96, width), bf16),
            pltpu.VMEM((4, slots, width), bf16),
            pltpu.VMEM((4, slots, width), bf16),
            pltpu.VMEM((4, width, width), bf16),
            pltpu.VMEM((GROUP, 256, width), bf16),
            pltpu.VMEM((slots, width), bf16),
            pltpu.VMEM((slots, width), f32),
            pltpu.VMEM((2, width, width), f32),
            DMA((3,)),
            DMA((3,)),
            DMA((3,)),
            DMA((3,)),
            DMA((4,)),
            DMA((4,)),
            DMA,
            DMA,
        ],
        compiler_params=pltpu.CompilerParams(collective_id=2, has_side_effects=True, vmem_limit_bytes=VMEM_LIMIT),
    )(lf, joined, tokens, small, gout)


def back_kernel(
    wf, ws, wv, normed, values, hid, slope, prob, gmix, gg2, half, tokens, gmid, small, out_f, out_a, out_s, gtok,
    wcat, gb_all, awf, aws, ab1, ab2, gn, gv, awv, stash, ga, gs, nb, tok, fs, fb2, fb3, fb4, cb1, cb2, sb1, sb2,
    own, s1, r1, s2, r2, s3, r3, sn, rn, sf, rf, s4, r4, sv, rv,
):
    step, r = pl.program_id(0), pl.program_id(1)
    width = ws.shape[1]
    heads = ab1.shape[0]
    h = jnp.maximum(heads - 1 - step, 0)
    t, c, z = place()
    sibling = (t, 1 - c, z)
    tps, zs = group_peers(), line_peers()
    slow, fast, slow_dev, fast_dev = square()

    a1 = lambda i: [remote(ga.at[1 - c, :, :, part(i)], cb1.at[:, :, part(i)], s1.at[i], r1.at[i], sibling)]

    def add_heads(i):
        def add(o, slot):
            def one(j, carry):
                here = ga[c, o, j, part(i)].astype(f32) + cb2[slot, j, part(i)].astype(f32)
                ga[c, o, j, part(i)] = here.astype(bf16)
                return carry

            lax.fori_loop(0, GROUP, one, 0)

        return add

    def add_f(k):
        def add(o, slot):
            fs[fast, o, cut(k)] = (fs[fast, o, cut(k)].astype(f32) + fb4[slot, cut(k)].astype(f32)).astype(bf16)

        return add

    a2 = lambda i: Gather(
        lambda o: ga.at[c, o, :, part(i)], lambda k: cb2.at[k, :, part(i)], add_heads(i), s2.at[i], r2.at[i]
    )
    a3 = lambda i: [
        remote(ga.at[c, z, p, part(i)], out_a.at[t, part(i)], s3.at[i, k], r3.at[i, k], (p, c, z))
        for k, p in enumerate(tps)
    ]
    mine = lambda i: [local(ga.at[c, z, t, part(i)], out_a.at[t, part(i)], own.at[i])]
    mine_f = lambda: [local(half.at[slow], fs, own.at[heads])]
    mine_t = lambda: [local(tokens, tok, own.at[heads + 1]), local(gmid, gtok, own.at[heads + 2])]
    mine_w = lambda: [
        local(wf.at[i], wcat.at[:, i * width : (i + 1) * width], own.at[heads + 3 + i]) for i in range(heads)
    ]
    v1 = lambda: [remote(gs.at[1 - c], sb1, sv.at[0], rv.at[0], sibling)]
    v2 = lambda: [remote(gs.at[c, p], sb2.at[k], sv.at[1 + k], rv.at[1 + k], (t, c, p)) for k, p in enumerate(zs)]
    f2 = lambda: [remote(half.at[1 - slow, :, :, cut(0), :], fb2, sf.at[0], rf.at[0], slow_dev)]
    f3 = lambda k: [remote(fs.at[1 - fast, :, cut(k)], fb3.at[:, cut(k)], sf.at[1 + k], rf.at[1 + k], fast_dev)]
    f4 = lambda k: Gather(
        lambda o: fs.at[fast, o, cut(k)], lambda n: fb4.at[n, cut(k)], add_f(k), s4.at[k], r4.at[k]
    )
    line_n = lambda k: gb_all.at[k, :, 0:width]
    out_n = lambda k: remote(line_n(k), nb.at[k], sn.at[k], rn.at[k], (fast_dev, fast_dev, slow_dev)[k])

    def at_step(i, j):
        return pl.when((step == i) & (r == j))

    def meet(i):
        wait(a1(i))

        def line(k, carry):
            for j in range(GROUP):
                here = ga[c, k, j, part(i)].astype(f32) + cb1[k, j, part(i)].astype(f32)
                ga[c, k, j, part(i)] = here.astype(bf16)
            return carry

        lax.fori_loop(0, 4, line, 0)
        a2(i).begin()

    def deal(i):
        a2(i).finish()
        start(mine(i) + a3(i))

    def add_slabs(total, more, k):
        def one(i, carry):
            here = fs[total, i, cut(k)].astype(f32) + more(i).astype(f32)
            fs[total, i, cut(k)] = here.astype(bf16)
            return carry

        lax.fori_loop(0, 4, one, 0)

    @at_step(0, 0)
    def _():
        greet([(p, c, z) for p in tps] + [(t, c, p) for p in zs] + [sibling])
        start(mine_f() + mine_w() + mine_t())
        met(7)
        start(f2())
        wait(mine_f())
        start(f3(1))

    @at_step(0, 3)
    def _():
        wait(f3(1))
        add_slabs(fast, lambda i: fb3[i, cut(1)], 1)
        f4(1).begin()

    @at_step(1, 0)
    def _():
        meet(2)

    @at_step(1, 2)
    def _():
        f4(1).forward()

    @at_step(1, 3)
    def _():
        wait(f2())
        add_slabs(1 - fast, lambda i: fb2[1 - fast, i], 0)
        start(f3(0))
        add_slabs(fast, lambda i: fb2[fast, i], 0)

    @at_step(2, 0)
    def _():
        a2(2).forward()
        meet(1)

    @at_step(2, 2)
    def _():
        wait(f3(0))
        add_slabs(fast, lambda i: fb3[i, cut(0)], 0)
        f4(0).begin()

    @at_step(2, 3)
    def _():
        deal(2)

    @at_step(3, 0)
    def _():
        wait(mine_w())

    @pl.when((r == 0) & (step < heads))
    def _():
        awf[...] = jnp.zeros_like(awf)
        aws[...] = jnp.zeros_like(aws)
        ab1[h] = jnp.zeros(ab1.shape[1:], f32)
        ab2[h] = jnp.zeros(ab2.shape[1:], f32)

    @pl.when(step < heads)
    def _():
        tile = pl.ds(pl.multiple_of((h // 2) * 128, 128), 128)
        lane = lax.broadcasted_iota(jnp.int32, (512, 128), 1)
        gm = jnp.where(lane // 64 == h % 2, gmix[0, :, tile].astype(f32), 0.0).astype(bf16)
        gw = dot_nt(gm, values[0, :, tile])
        p = prob[0, 0]
        p32 = p.astype(f32)
        gl = (p32 * (gw - jnp.sum(p32 * gw, axis=-1, keepdims=True))).astype(bf16)
        ab2[h] += jnp.sum(gl.astype(f32).reshape(-1, 8, 512), axis=0)
        gvh = dot_tn(p, gm)

        @pl.when(h != 0)
        def _():
            gv[r, :, tile] = gvh.astype(bf16)

        @pl.when(h == 0)
        def _():
            gv[r, :, tile] = (gv[r, :, tile].astype(f32) + gvh).astype(bf16)

        aws[...] += dot_tn(hid[0, 0], gl)
        gb = (dot_nt(gl, ws[0]) * slope[0, 0].astype(f32)).astype(bf16)
        gb_all[r, :, pl.ds(pl.multiple_of(h * width, 128), width)] = gb
        ab1[h] += jnp.sum(gb.astype(f32).reshape(-1, 8, width), axis=0)
        awf[...] += dot_tn(normed[0], gb)

    @pl.when(step == heads - 1)
    def _():
        more = dot_tn(normed[0], gv[r])

        @pl.when(r == 0)
        def _():
            awv[...] = more

        @pl.when(r != 0)
        def _():
            awv[...] += more

    def pack(i):
        def one(tt, carry):
            for cc in range(2):
                for zz in range(4):
                    at = pl.ds(pl.multiple_of((tt * 8 + cc * 4 + zz) * 24, 8), 24)
                    stack = [awf[at, 256 * j : 256 * j + 256] for j in range(3)]
                    stack += [aws[at, 256 * j : 256 * j + 256] for j in range(2)]
                    if i == 0:
                        stack = [awv[at, :]] + stack
                    if i == 1:
                        stack = stack + [stash[cc, zz, tt]]
                    whole = jnp.concatenate(stack, 0)
                    if i == 2:
                        stash[cc, zz, tt] = whole[0:8]
                        whole = whole[8:]
                    ga[cc, zz, tt, part(i)] = whole.astype(bf16)
            return carry

        lax.fori_loop(0, GROUP, one, 0)
        start(a1(i))

    @at_step(0, 3)
    def _():
        pack(2)

    @at_step(1, 3)
    def _():
        pack(1)

    @at_step(2, 3)
    def _():
        row = lax.broadcasted_iota(jnp.int32, (128, width), 0)
        stack = jnp.zeros((128, width), f32)
        lines = [jnp.sum(ab1[i], axis=0, keepdims=True) for i in range(heads)]
        for k, line in enumerate(lines + [jnp.sum(gg2[...], axis=0, keepdims=True)]):
            stack = jnp.where(row == 64 + k, line, stack)
        lane = lax.broadcasted_iota(jnp.int32, (width, 128), 1)
        awv[:, 128:256] = jnp.where(lane < 64, awv[:, 128:256], stack.T)
        pack(0)

    @pl.when(step == heads)
    def _():
        total = dot_nt(gb_all[r], wcat[...]) + dot_nt(gv[r], wv[...])

        @pl.when(r < 3)
        def _():
            gb_all[r, :, 0:width] = total.astype(bf16)

        @pl.when(r == 3)
        def _():
            gn[...] = total

    @at_step(3, 0)
    def _():
        out_n(0).start()
        meet(0)
        a2(1).forward()

    @at_step(3, 1)
    def _():
        out_n(1).start()

    @at_step(2, 3)
    def _():
        flat = jnp.concatenate([jnp.sum(ab2[k], axis=0, keepdims=True) for k in range(3)], 1)
        flat = jnp.broadcast_to(flat, (8, 1536))
        for cc in range(2):
            for zz in range(4):
                s = (cc * 4 + zz) * 192
                gs[cc, zz] = (pltpu.roll(flat, 1536 - s, 1) if s else flat)[:, 0:256]
        start(v1())

    @at_step(3, 2)
    def _():
        f4(0).forward()
        wait(v1())
        gs[c] += sb1[...]
        start(v2())

    @at_step(3, 3)
    def _():
        out_n(0).wait()

        def join(i, carry):
            at = pl.ds(pl.multiple_of(i * 128, 128), 128)
            here = gb_all[2, at, 0:width].astype(f32) + nb[0, at, :].astype(f32)
            gb_all[2, at, 0:width] = here.astype(bf16)
            return carry

        lax.fori_loop(0, 4, join, 0)
        out_n(2).start()
        deal(1)
        a2(0).forward()
        f4(1).finish()
        f4(0).finish()
        out_f[...] = fs[fast, z].astype(f32)
        out_n(1).wait()
        out_n(2).wait()
        wait(mine_t())

        def ln_back(i, carry):
            at = pl.ds(pl.multiple_of(i * 128, 128), 128)
            g = gn[at, :] + nb[1, at, :].astype(f32) + nb[2, at, :].astype(f32)
            unit, scale = centre_rows(tok[at, :].astype(f32))
            gu = g * small[3:4]
            back = scale * (
                gu - jnp.mean(gu, axis=-1, keepdims=True) - unit * jnp.mean(gu * unit, axis=-1, keepdims=True)
            )
            gtok[at, :] += back
            return carry

        lax.fori_loop(0, 4, ln_back, 0)
        wait(v2())
        out_s[...] = gs[c, z] + sb2[0] + sb2[1] + sb2[2]
        deal(0)
        for i in range(heads):
            wait(mine(i) + a3(i))


def back_call(wf, ws, wv, normed, values, hid, slope, prob, gmix, gg2, half, tokens, gmid, small):
    heads, width, slots = ws.shape
    rows = half.shape[-2]
    head = lambda h: jnp.maximum(heads - 1 - h, 0)
    held = lambda h, r: jnp.where(h < heads, r, GROUP - 1)
    by_head = lambda h, r: (head(h), 0, 0)
    row = lambda h, r: (r, 0, 0)
    early = lambda h, r: (held(h, r), 0, 0)
    both = lambda h, r: (head(h), held(h, r), 0, 0)
    flat = lambda h, r: (0, 0)
    return pl.pallas_call(
        back_kernel,
        grid=(heads + 1, GROUP),
        out_shape=(
            shape_of((rows, width), f32),
            shape_of((GROUP, 384, 256), bf16),
            shape_of((8, 256), f32),
            shape_of(tokens.shape, f32),
        ),
        in_specs=[
            ANY,
            pl.BlockSpec((1, width, slots), by_head),
            pl.BlockSpec((width, 256), flat),
            pl.BlockSpec((1, slots, width), row),
            pl.BlockSpec((1, slots, 256), early),
            pl.BlockSpec((1, 1, slots, width), both),
            pl.BlockSpec((1, 1, slots, width), both),
            pl.BlockSpec((1, 1, slots, slots), both),
            pl.BlockSpec((1, slots, 256), early),
            pl.BlockSpec((8, width), flat),
            ANY,
            ANY,
            ANY,
            pl.BlockSpec((8, width), flat),
        ],
        out_specs=(FULL, ANY, FULL, FULL),
        scratch_shapes=[
            pltpu.VMEM((width, heads * width), bf16),
            pltpu.VMEM((GROUP, slots, heads * width), bf16),
            pltpu.VMEM((width, width), f32),
            pltpu.VMEM((width, slots), f32),
            pltpu.VMEM((heads, 8, width), f32),
            pltpu.VMEM((heads, 8, slots), f32),
            pltpu.VMEM((slots, width), f32),
            pltpu.VMEM((GROUP, slots, 256), bf16),
            pltpu.VMEM((width, 256), f32),
            pltpu.VMEM((2, 4, GROUP, 8, 256), f32),
            pltpu.VMEM((2, 4, GROUP, 384, 256), bf16),
            pltpu.VMEM((2, 4, 8, 256), f32),
            pltpu.VMEM((3, slots, width), bf16),
            pltpu.VMEM((slots, width), bf16),
            pltpu.VMEM((2, 4, rows, width), bf16),
            pltpu.VMEM((2, 4, 128, width), bf16),
            pltpu.VMEM((4, rows, width), bf16),
            pltpu.VMEM((4, rows, width), bf16),
            pltpu.VMEM((4, GROUP, 384, 256), bf16),
            pltpu.VMEM((4, GROUP, 384, 256), bf16),
            pltpu.VMEM((4, 8, 256), f32),
            pltpu.VMEM((3, 8, 256), f32),
            DMA((2 * heads + 3,)),
            DMA((heads,)),
            DMA((heads,)),
            DMA((heads, 3)),
            DMA((heads, 4)),
            DMA((heads, 3)),
            DMA((heads, 3)),
            DMA((3,)),
            DMA((3,)),
            DMA((3,)),
            DMA((3,)),
            DMA((2, 3)),
            DMA((2, 4)),
            DMA((4,)),
            DMA((4,)),
        ],
        compiler_params=pltpu.CompilerParams(collective_id=3, has_side_effects=True, vmem_limit_bytes=VMEM_LIMIT),
    )(wf, ws, wv, normed, values, hid, slope, prob, gmix, gg2, half, tokens, gmid, small)


def finish_kernel(
    sums_a, sums_f, sums_b, w_first, extra,
    out_one, out_value, out_first, out_b1, out_second, out_b2, out_out, out_two, out_up, out_down,
):
    heads_all, depth, width = w_first.shape
    heads = heads_all // GROUP
    total = jnp.zeros((depth, 256), f32)
    lane = lax.broadcasted_iota(jnp.int32, (depth, 256), 1)
    sides = []
    for t in range(GROUP):
        whole = sums_a[t].astype(f32)
        out_value[:, 192 * t : 192 * t + 192] = whole[0:depth, 0:192]
        sides.append(whole[0:depth, 128:256])
        total += jnp.where(lane < 192, whole[0:depth] * extra[t].astype(f32), 0.0)
        for i in range(heads):
            block = lambda j: whole[depth * (1 + 5 * i + j) : depth * (2 + 5 * i + j)]
            weight = w_first[heads * t + i].astype(f32)
            for j in range(3):
                at = slice(256 * j, 256 * j + 256)
                out_first[heads * t + i, :, at] = block(j)
                total += block(j) * weight[:, at]
            for j in range(2):
                out_second[heads * t + i, :, 256 * j : 256 * j + 256] = block(3 + j)
    gain = jnp.sum(jnp.where(lane == 195, extra[0].astype(f32), 0.0), axis=1, keepdims=True)
    gain_grad = jnp.sum(total, axis=1, keepdims=True) / gain
    low = lax.broadcasted_iota(jnp.int32, (depth, 128), 1)
    sides[0] = jnp.where(low == 68, gain_grad, sides[0])
    turned = jnp.concatenate(sides + [jnp.zeros((128 - GROUP * depth, 128), f32)], 0).T
    two = jnp.zeros((1, 128), f32)
    for t in range(GROUP):
        mine = pltpu.roll(turned, 128 - depth * t, 1) if t else turned
        out_b1[heads * t : heads * t + heads, :] = mine[64 : 64 + heads, 0:depth]
        two += mine[67:68]
    out_two[...] = two[:, 0:depth]
    out_one[...] = turned[68:69, 0:depth]
    out_b2[...] = sums_b[0:1, 0 : out_b2.shape[1]]
    for k in range(4):
        out_up[:, width * k : width * k + width] = sums_f[depth * k : depth * k + depth]
    out_out[...] = sums_f[4 * depth : 5 * depth]
    out_down[...] = sums_f[128:224]


def finish_call(sums_a, sums_f, sums_b, w_first, extra, slots, shard):
    heads_all, depth, width = w_first.shape
    return pl.pallas_call(
        finish_kernel,
        out_shape=(
            shape_of((1, depth), f32),
            shape_of((depth, width), f32),
            shape_of((heads_all, depth, width), f32),
            shape_of((heads_all, depth), f32),
            shape_of((heads_all, depth, slots), f32),
            shape_of((1, shard), f32),
            shape_of((depth, width), f32),
            shape_of((1, depth), f32),
            shape_of((depth, 4 * width), f32),
            shape_of((4 * depth, width), f32),
        ),
        in_specs=[FULL] * 5,
        out_specs=(FULL,) * 10,
        compiler_params=pltpu.CompilerParams(vmem_limit_bytes=VMEM_LIMIT),
    )(sums_a, sums_f, sums_b, w_first, extra)


def on_device_fast(tokens, lengths, gain_one, w_value, w_first, b_first, w_second, b_second, w_out, gain_two, w_up, w_down, grad_out):
    _, slots, width = tokens.shape
    heads_all, depth, _ = w_first.shape
    heads = heads_all // GROUP
    digits = jnp.stack([lengths[0] // 16, lengths[0] % 16]).astype(bf16)
    extra = jnp.concatenate(
        [
            w_value.reshape(depth, GROUP, -1).transpose(1, 0, 2),
            b_first.reshape(GROUP, heads, depth).transpose(0, 2, 1),
            jnp.broadcast_to(jnp.stack([gain_one, gain_two], 1), (GROUP, depth, 2)),
            jnp.broadcast_to(b_second.reshape(depth, 8), (GROUP, depth, 8)),
            jnp.broadcast_to(digits, (GROUP, depth, 2)),
            jnp.zeros((GROUP, depth, 49), bf16),
        ],
        2,
    )
    wf, ws, wv, small, normed, values, hid, slope, prob, joined, lf = attend_call(
        tokens, extra, w_first, w_second, w_out, w_up, w_down
    )
    result, gmid, gmix, half, gg2 = ffn_call(lf, joined, tokens[0], small, grad_out[0])
    out_f, out_a, out_s, gtok = back_call(
        wf, ws, wv, normed, values, hid, slope, prob, gmix, gg2, half, tokens[0], gmid, small
    )
    outs = finish_call(out_a, out_f, out_s, w_first, extra, slots, b_second.shape[0])
    return (result[None], gtok[None]) + tuple(v[0] if k in (0, 5, 7) else v for k, v in enumerate(outs))


def solution(mesh):
    wide, narrow = mesh.shape["wide"], mesh.shape["narrow"]
    grouped = Mesh(mesh.devices.reshape(GROUP, wide // GROUP, narrow), ALL)
    vec = P(ALL)
    flat = P(ALL, None)
    mid = P(None, ALL, None)
    row = P(ALL, None, None)
    body = on_device_fast if (wide, narrow) == (8, 4) else on_device
    return jax.shard_map(
        body,
        mesh=grouped,
        in_specs=(row, vec, vec, flat, mid, P(None, ALL), mid, vec, flat, vec, flat, flat, row),
        out_specs=(row, row, vec, flat, mid, P(None, ALL), mid, vec, flat, vec, flat, flat),
        check_vma=False,
    )
```

```python
import jax
import jax.numpy as jnp
from jax import lax
from jax.experimental import pallas as pl
from jax.experimental.pallas import tpu as pltpu
from jax.sharding import Mesh
from jax.sharding import PartitionSpec as P

epsilon = 1e-05
f32 = jnp.float32
bf16 = jnp.bfloat16
GROUP = 4


def norm_rows(values, factor):
    average = jnp.mean(values, axis=-1, keepdims=True)
    centred = values - average
    spread = jnp.mean(centred * centred, axis=-1, keepdims=True)
    return centred * lax.rsqrt(spread + epsilon) * factor


def smooth(values):
    return jax.nn.gelu(values, approximate=False)


def mm(spec, a, b):
    return jnp.einsum(spec, a, b, preferred_element_type=f32)


REST = ("rep", "narrow")
ALL = ("tp", "rep", "narrow")


def to_heads(shard):
    heads, depth, width = shard.shape
    pieces = lax.all_to_all(shard.reshape(GROUP, heads // GROUP, depth, width), "tp", 0, 0)
    whole = lax.all_gather(pieces, REST, axis=0)
    return whole.transpose(2, 1, 0, 3, 4).reshape(heads // GROUP, -1, width)


def from_heads(grad):
    heads, depth, width = grad.shape
    n = lax.axis_size("rep") * lax.axis_size("narrow")
    pieces = grad.astype(bf16).reshape(heads, GROUP, n, depth // (GROUP * n), width).transpose(2, 1, 0, 3, 4)
    pieces = pieces.reshape((n * GROUP,) + pieces.shape[2:])
    share = lax.psum_scatter(pieces, REST, scatter_dimension=0, tiled=True)
    share = lax.all_to_all(share, "tp", 0, 0)
    return share.reshape(heads * GROUP, depth // (GROUP * n), width).astype(f32)


def on_device(tokens, lengths, gain_one, w_value, w_first, b_first, w_second, b_second, w_out, gain_two, w_up, w_down, grad_out):
    row_count, slots, width = tokens.shape
    heads_all = w_first.shape[0]
    heads = heads_all // GROUP
    head_size = width // heads_all
    me = lax.axis_index("tp")
    depth = w_value.shape[0]

    small = [gain_one, gain_two, b_second, b_first.reshape(-1)]
    gathered = lax.all_gather(jnp.concatenate(small), ALL, axis=0)
    n_all = gathered.shape[0]
    g1 = gathered[:, :depth].reshape(-1).astype(f32)
    g2 = gathered[:, depth : 2 * depth].reshape(-1).astype(f32)
    b2_len = b_second.shape[0]
    b2 = gathered[:, 2 * depth : 2 * depth + b2_len].reshape(heads_all, slots).astype(f32)
    b1 = gathered[:, 2 * depth + b2_len :].reshape(n_all, heads_all, depth).transpose(1, 0, 2).reshape(heads_all, width).astype(f32)
    b1 = lax.dynamic_slice_in_dim(b1, me * heads, heads, 0)
    b2 = lax.dynamic_slice_in_dim(b2, me * heads, heads, 0)

    wf = to_heads(w_first)
    ws = to_heads(w_second)
    wv = to_heads(w_value.reshape(depth, GROUP, width // GROUP).transpose(1, 0, 2))[0]
    rows = lax.all_gather(tokens, "tp", axis=0, tiled=True)
    lens = lax.all_gather(lengths, "tp", axis=0, tiled=True)
    n_rows = rows.shape[0]

    normed = norm_rows(rows.astype(f32), g1).astype(bf16)
    values = mm("rsd,de->rse", normed, wv).astype(bf16)
    per_head = values.reshape(n_rows, slots, heads, head_size).transpose(2, 0, 1, 3)
    before = mm("rsd,hde->hrse", normed, wf) + b1[:, None, None, :]
    hidden = smooth(before).astype(bf16)
    logits = mm("hrse,hej->hrsj", hidden, ws) + b2[:, None, None, :]
    visible = lax.broadcasted_iota(jnp.int32, (1, n_rows, 1, slots), 3) < lens[None, :, None, None]
    masked = jnp.where(visible, logits, f32(-1e30))
    scaled = jnp.exp(masked - jnp.max(masked, axis=-1, keepdims=True))
    probabilities = scaled / jnp.sum(scaled, axis=-1, keepdims=True)
    weights = probabilities.astype(bf16)
    mixture = mm("hrsj,hrjc->rshc", weights, per_head).astype(bf16)
    mixture = mixture.reshape(GROUP, row_count, slots, heads * head_size)
    joined = lax.all_to_all(mixture, "tp", 0, 0).transpose(1, 2, 0, 3).reshape(row_count * slots, width)

    wo = lax.all_gather(w_out, ALL, axis=0, tiled=True)
    wu = lax.all_gather(w_up, ALL, axis=0, tiled=True)
    wd = lax.all_gather(w_down, ALL, axis=0, tiled=True)
    inputs = tokens.astype(f32).reshape(-1, width)
    middle = inputs + mm("sd,de->se", joined, wo)
    normed_two, norm_two_back = jax.vjp(norm_rows, middle, g2)
    normed_two = normed_two.astype(bf16)
    upward = mm("td,df->tf", normed_two, wu)
    active, smooth_up_back = jax.vjp(smooth, upward)
    active = active.astype(bf16)
    result = middle + mm("tf,fd->td", active, wd)

    g_out = grad_out.reshape(-1, width)
    grad_branch = g_out.astype(bf16)
    grad_w_down = mm("tf,td->fd", active, grad_branch)
    grad_upward = smooth_up_back(mm("td,fd->tf", grad_branch, wd))[0].astype(bf16)
    grad_w_up = mm("td,tf->df", normed_two, grad_upward)
    grad_middle_norm, grad_gain_two = norm_two_back(mm("tf,df->td", grad_upward, wu))
    grad_middle = g_out + grad_middle_norm
    grad_attn = grad_middle.astype(bf16)
    grad_w_out = mm("sd,se->de", joined, grad_attn)
    grad_joined = mm("se,de->sd", grad_attn, wo).astype(bf16)

    grad_mixture = grad_joined.reshape(row_count, slots, GROUP, heads * head_size).transpose(2, 0, 1, 3)
    grad_mixture = lax.all_to_all(grad_mixture, "tp", 0, 0).reshape(n_rows, slots, heads, head_size).transpose(2, 0, 1, 3)
    grad_weights = mm("hrsc,hrjc->hrsj", grad_mixture, per_head)
    grad_values = mm("hrsj,hrsc->rjhc", weights, grad_mixture).astype(bf16).reshape(n_rows, slots, heads * head_size)
    centre = jnp.sum(probabilities * grad_weights, axis=-1, keepdims=True)
    grad_logits = (probabilities * (grad_weights - centre)).astype(bf16)
    grad_b_second = jnp.sum(grad_logits.astype(f32), axis=(1, 2))
    grad_w_second = mm("hrse,hrsj->hej", hidden, grad_logits)
    grad_hidden = mm("hrsj,hej->hrse", grad_logits, ws)
    smooth_value, smooth_back = jax.vjp(smooth, before)
    grad_before = smooth_back(grad_hidden)[0].astype(bf16)
    grad_b_first = jnp.sum(grad_before.astype(f32), axis=(1, 2))
    grad_w_first = mm("rsd,hrse->hde", normed, grad_before)
    grad_w_value = mm("rsd,rse->de", normed, grad_values)
    grad_normed = mm("hrse,hde->rsd", grad_before, wf) + mm("rse,de->rsd", grad_values, wv)
    grad_normed = lax.psum_scatter(grad_normed.astype(bf16), "tp", scatter_dimension=0, tiled=True)
    value, norm_one_back = jax.vjp(norm_rows, inputs, g1)
    grad_inputs_norm, grad_gain_one = norm_one_back(grad_normed.astype(f32).reshape(-1, width))
    grad_tokens = grad_middle + grad_inputs_norm

    out_first = from_heads(grad_w_first)
    out_second = from_heads(grad_w_second)
    out_value = from_heads(grad_w_value[None]).transpose(1, 0, 2).reshape(depth, width)

    def share(grad):
        return lax.psum_scatter(grad.astype(bf16), ALL, scatter_dimension=0, tiled=True).astype(f32)

    vec_tp = jnp.concatenate([grad_b_first.reshape(-1), grad_b_second.reshape(-1)])
    vec_tp = lax.dynamic_update_slice_in_dim(jnp.zeros((GROUP, vec_tp.shape[0]), f32), vec_tp[None], me, 0)
    vec = jnp.concatenate([vec_tp.reshape(-1), grad_gain_one, grad_gain_two])
    vec = lax.psum(vec, ALL)
    index = (me * lax.axis_size("rep") + lax.axis_index("rep")) * lax.axis_size("narrow") + lax.axis_index("narrow")
    n_tp = GROUP * (heads * width + heads * slots)
    tp_part = vec[:n_tp].reshape(GROUP, -1)
    gb1 = tp_part[:, : heads * width].reshape(heads_all, width)
    gb2 = tp_part[:, heads * width :].reshape(-1)
    gb1 = lax.dynamic_slice_in_dim(gb1, index * depth, depth, 1)
    gb2 = lax.dynamic_slice_in_dim(gb2, index * b2_len, b2_len, 0)
    gg1 = lax.dynamic_slice_in_dim(vec[n_tp : n_tp + width], index * depth, depth, 0)
    gg2 = lax.dynamic_slice_in_dim(vec[n_tp + width :], index * depth, depth, 0)
    shape = tokens.shape
    return (
        result.reshape(shape),
        grad_tokens.reshape(shape),
        gg1,
        out_value,
        out_first,
        gb1,
        out_second,
        gb2,
        share(grad_w_out),
        gg2,
        share(grad_w_up),
        share(grad_w_down),
    )


MESH = pl.DeviceIdType.MESH
VMEM_LIMIT = 60 * 2**20
ANY = pl.BlockSpec(memory_space=pl.ANY)
FULL = pl.BlockSpec(memory_space=pltpu.VMEM)
DMA = pltpu.SemaphoreType.DMA


def shape_of(dims, kind):
    return jax.ShapeDtypeStruct(dims, kind)


def dot_nt(a, b):
    return lax.dot_general(a, b, (((1,), (1,)), ((), ())), preferred_element_type=f32)


def dot_tn(a, b):
    return lax.dot_general(a, b, (((0,), (0,)), ((), ())), preferred_element_type=f32)


def dot_nn(a, b):
    return lax.dot_general(a, b, (((1,), (0,)), ((), ())), preferred_element_type=f32)


def place():
    return lax.axis_index("tp"), lax.axis_index("rep"), lax.axis_index("narrow")


def group_peers():
    t, c, z = place()
    along_x = t + 1 - 2 * (t % 2)
    along_y = (t + 2) % GROUP
    return [GROUP - 1 - t, (1 - c) * along_x + c * along_y, (1 - c) * along_y + c * along_x]


def line_peers():
    z = lax.axis_index("narrow")
    return [(z + k) % 4 for k in (1, 2, 3)]


def line_place():
    z = lax.axis_index("narrow")
    side = z // 2
    end, inner = 3 * side, 1 + side
    return end, inner, 2 - side, 3 - 3 * side, end + inner - z, z == inner


class Spread:
    def __init__(self, slabs, send, recv, source=None):
        t, c, z = place()
        end, inner, other, far, near, is_inner = line_place()
        self.is_inner = is_inner
        move = lambda o, k, to: remote(slabs(o), slabs(o), send.at[k], recv.at[o], (t, c, to))
        source = slabs(z) if source is None else source
        give = lambda k, to: remote(source, slabs(z), send.at[k], recv.at[z], (t, c, to))
        self.own = lambda: [give(0, other), give(1, near)]
        self.on = lambda: [move(other, 2, end), move(far, 3, end)]
        self.near = lambda: move(near, 0, near)

    def begin(self):
        start(self.own())

    def forward(self):
        @pl.when(self.is_inner)
        def _():
            for copy in self.on():
                copy.wait_recv()
            start(self.on())

    def finish(self):
        self.near().wait_recv()

        @pl.when(jnp.logical_not(self.is_inner))
        def _():
            for copy in self.on():
                copy.wait_recv()

        for copy in self.own():
            copy.wait_send()

        @pl.when(self.is_inner)
        def _():
            for copy in self.on():
                copy.wait_send()


class Gather:
    def __init__(self, slabs, land, add, send, recv):
        t, c, z = place()
        end, inner, other, far, near, is_inner = line_place()
        self.is_inner, self.add, self.z = is_inner, add, z
        self.other, self.far = other, far
        move = lambda o, slot, k, to: remote(slabs(o), land(slot), send.at[k], recv.at[slot], (t, c, to))
        self.out = lambda: [move(far, 2, 0, inner), move(other, 1, 1, inner), move(inner, 0, 2, inner)]
        self.back = lambda: [move(end, 0, 2, end)]
        self.on_far = lambda: [move(far, 1, 0, far)]
        self.on_other = lambda: [move(other, 3, 1, other)]
        self.got = lambda slot: move(z, slot, 0, near).wait_recv()

    def begin(self):
        @pl.when(self.is_inner)
        def _():
            start(self.back())

        @pl.when(jnp.logical_not(self.is_inner))
        def _():
            start(self.out())

    def forward(self):
        @pl.when(self.is_inner)
        def _():
            self.got(2)
            self.add(self.far, 2)
            start(self.on_far())
            self.got(1)
            self.add(self.other, 1)
            start(self.on_other())

    def finish(self):
        self.got(0)
        self.add(self.z, 0)

        @pl.when(self.is_inner)
        def _():
            self.got(3)
            self.add(self.z, 3)
            for copy in self.back() + self.on_far() + self.on_other():
                copy.wait_send()

        @pl.when(jnp.logical_not(self.is_inner))
        def _():
            self.got(1)
            self.add(self.z, 1)
            for copy in self.out():
                copy.wait_send()


def greet(devices):
    barrier = pltpu.get_barrier_semaphore()
    for device in devices:
        pl.semaphore_signal(barrier, inc=1, device_id=device, device_id_type=MESH)


def met(count):
    pl.semaphore_wait(pltpu.get_barrier_semaphore(), count)


def remote(src, dst, send, recv, device):
    return pltpu.make_async_remote_copy(
        src_ref=src, dst_ref=dst, send_sem=send, recv_sem=recv, device_id=device, device_id_type=MESH
    )


def local(src, dst, sem):
    return pltpu.make_async_copy(src, dst, sem)


def start(copies):
    for copy in copies:
        copy.start()


def wait(copies):
    for copy in copies:
        copy.wait()


def square():
    t, c, z = place()
    y, x = t // 2, t % 2
    tps = group_peers()
    slow, fast = (1 - c) * y + c * x, (1 - c) * x + c * y
    return slow, fast, (tps[2], c, z), (tps[1], c, z)


def gelu_pair(v):
    cdf = 0.5 * (1.0 + lax.erf(v * 0.7071067811865476))
    return v * cdf, cdf + v * (jnp.exp(-0.5 * v * v) * 0.3989422804014327)


def centre_rows(v):
    shifted = v - jnp.mean(v, axis=-1, keepdims=True)
    scale = lax.rsqrt(jnp.mean(shifted * shifted, axis=-1, keepdims=True) + epsilon)
    return shifted * scale, scale


ROWS = ((0, 144), (144, 272), (272, 384))


def part(i):
    return slice(*ROWS[i])


def attend_kernel(
    tokens, extra, w_first, w_second, w_out, w_up, w_down,
    wf, ws, wv, small, normed, values, hid, slope, prob, joined, lf,
    pa, pf, la, lt, nrm, val, cols, b2, masks, join, own, s1, r1, s2, r2, s3, r3, st, rt, s1f, r1f, sf, rf, sj, rj,
):
    h, r = pl.program_id(0), pl.program_id(1)
    width = wf.shape[-1]
    heads = w_first.shape[0] // GROUP
    t, c, z = place()
    sibling = (t, 1 - c, z)
    tps, zs = group_peers(), line_peers()
    slow, fast, slow_dev, fast_dev = square()

    a1 = lambda i: [
        remote(pa.at[p, part(i)], la.at[c, z, t, part(i)], s1.at[i, k], r1.at[i, k], (p, c, z))
        for k, p in enumerate(tps)
    ]
    a2 = lambda i: Spread(lambda o: la.at[c, o, :, part(i)], s2.at[i], r2.at[i])
    a3 = lambda i: [remote(la.at[c, :, :, part(i)], la.at[c, :, :, part(i)], s3.at[i], r3.at[i], sibling)]
    mine = lambda i: [local(pa.at[t, part(i)], la.at[c, z, t, part(i)], own.at[i])]
    mine_t = lambda: [local(tokens.at[0], lt.at[3], own.at[heads])]
    mine_f = lambda: [local(pf, lf.at[c, slow, fast, z], own.at[heads + 1])]
    mine_j = lambda: [local(join.at[3], joined.at[t], own.at[heads + 2])]
    tok_fast = lambda: remote(tokens.at[0], lt.at[1], st.at[0], rt.at[0], fast_dev)
    tok_slow = lambda: remote(tokens.at[0], lt.at[2], st.at[1], rt.at[1], slow_dev)
    tok_on = lambda: remote(lt.at[1], lt.at[0], st.at[2], rt.at[2], slow_dev)
    f1 = lambda k: Spread(lambda o: lf.at[c, slow, fast, o, cut(k)], s1f.at[k], r1f.at[k], pf.at[cut(k)])

    def whole(k, spot, n, device):
        piece = lf.at[spot + (slice(None),) * (4 - len(spot)) + (cut(k),)]
        return [remote(piece, piece, sf.at[k, n], rf.at[k, n], device)]

    f2 = lambda k: whole(k, (c, slow, fast), 0, fast_dev)
    f3 = lambda k: whole(k, (c, slow), 1, slow_dev)
    f4 = lambda k: whole(k, (c, slow), 2, sibling)
    f5 = lambda k: whole(k, (c, 1 - slow), 3, sibling)
    out_j = lambda k: [remote(join.at[k], joined.at[t], sj.at[k], rj.at[k], (tps[k], c, z))]

    def at_step(i, j):
        return pl.when((h == i) & (r == j))

    @at_step(0, 0)
    def _():
        greet([(p, c, z) for p in tps] + [(t, c, p) for p in zs] + [sibling])
        blocks = lambda v: [v[:, k : k + 256] for k in range(0, v.shape[1], 256)]
        ups = [w_up[:, k : k + width].astype(f32) for k in range(0, w_up.shape[1], width)]
        pf[0:96] = jnp.concatenate(ups, 0).astype(bf16)
        pf[96:128] = jnp.concatenate([w_out[...].astype(f32), jnp.zeros((8, width), f32)], 0).astype(bf16)
        met(7)
        f1(0).begin()
        for p in range(GROUP):
            stack = [extra[p].astype(f32)]
            for i in range(heads):
                stack += blocks(w_first[heads * p + i].astype(f32)) + blocks(w_second[heads * p + i].astype(f32))
            pa[p] = jnp.concatenate(stack, 0).astype(bf16)
        for i in range(heads):
            start(mine(i) + a1(i))
        pf[128:224] = w_down[...]
        start(mine_f() + mine_t())
        wait(mine(0) + a1(0))
        a2(0).begin()
        wait(mine(1) + a1(1))
        wait(mine(2) + a1(2))
        start([tok_fast(), tok_slow()])
        f1(0).forward()
        f1(1).begin()
        a2(0).forward()
        a2(1).begin()
        tok_fast().wait_recv()
        tok_on().start()
        f1(0).finish()
        wait(mine_f())
        start(f2(0))
        a2(0).finish()
        start(a3(0))
        f1(1).forward()
        a2(1).forward()
        a2(2).begin()
        wait(mine_t() + a3(0))
        tok_fast().wait_send()
        tok_slow().wait()
        tok_on().wait()

    @at_step(0, 1)
    def _():
        wait(f2(0))
        start(f3(0) + f4(0))
        f1(1).finish()
        start(f2(1))

    @at_step(0, 3)
    def _():
        a2(2).forward()

    @at_step(1, 0)
    def _():
        a2(1).finish()
        start(a3(1))
        wait(a3(1))

    @at_step(1, 1)
    def _():
        wait(f2(1))
        start(f3(1) + f4(1))

    @at_step(2, 0)
    def _():
        a2(2).finish()
        start(a3(2))
        wait(f3(0))
        start(f5(0))
        wait(a3(2))

    def unpack(i):
        def one(tt, carry):
            for cc in range(2):
                for zz in range(0, 4, 2):
                    at = pl.ds(pl.multiple_of((tt * 8 + cc * 4 + zz) * 24, 48), 48)

                    def block(first):
                        low = first // 16 * 16
                        both = [la[cc, zz + k, tt, low : low + 32].astype(f32)[first - low :][:24] for k in range(2)]
                        return jnp.concatenate(both, 0)

                    base = 24 + 120 * i
                    for j in range(3):
                        wf[0, at, 256 * j : 256 * j + 256] = block(base + 24 * j).astype(bf16)
                    for j in range(2):
                        ws[0, at, 256 * j : 256 * j + 256] = block(base + 72 + 24 * j).astype(bf16)
                    if i == 0:
                        both = block(0)
                        cols[at, :] = both[:, 128:256]
                        lane = lax.broadcasted_iota(jnp.int32, both.shape, 1)
                        wv[at, :] = jnp.where(lane < 192, both, 0.0).astype(bf16)

            return carry

        lax.fori_loop(0, GROUP, one, 0)

    for i in range(heads):

        @at_step(i, 0)
        def _():
            unpack(i)

    @at_step(0, 0)
    def _():
        small[...] = cols[...].T[64:72]
        mine_rows = cols[pl.ds(pl.multiple_of(t * 192, 192), 192), :].astype(bf16)
        lane = lax.broadcasted_iota(jnp.int32, (128, 512), 0)
        spot = lax.broadcasted_iota(jnp.int32, (128, 512), 1)
        spread = dot_nn(mine_rows, jnp.where(lane - 69 == spot % 8, 1.0, 0.0).astype(bf16))
        row = lax.broadcasted_iota(jnp.int32, (64, 512), 0)
        spot = lax.broadcasted_iota(jnp.int32, (64, 512), 1)
        for i in range(heads):
            picked = jnp.where(row == spot // 8, spread[64 * i : 64 * i + 64], 0.0)
            b2[i] = jnp.broadcast_to(jnp.sum(picked, axis=0, keepdims=True), (8, 512))
        for k, p in enumerate(tps + [t]):
            line = cols[pl.ds(pl.multiple_of((p * 8 + c * 4 + z) * 24, 8), 8), :]
            lane = lax.broadcasted_iota(jnp.int32, line.shape, 1)
            digits = jnp.where(lane == 77, 16.0 * line, jnp.where(lane == 78, line, 0.0))
            length = jnp.sum(digits, axis=1, keepdims=True)
            spot = lax.broadcasted_iota(jnp.int32, (8, 512), 1).astype(f32)
            masks[k] = jnp.where(spot < length, 0.0, -1e30)

    @pl.when(h == 0)
    def _():
        unit, _ = centre_rows(lt[r].astype(f32))
        out = (unit * small[3:4]).astype(bf16)
        nrm[r] = out
        normed[0] = out
        v = dot_nn(out, wv[...]).astype(bf16)
        val[r] = v
        values[0] = v

    row = lax.broadcasted_iota(jnp.int32, (8, width), 0)
    b1 = jnp.sum(jnp.where(row == h, small[...], 0.0), axis=0, keepdims=True)
    shift = b2[h, 0:1] + masks[r, 0:1]
    tile = pl.ds(pl.multiple_of((h // 2) * 128, 128), 128)
    step = 512
    for m in range(0, 512, step):
        at = slice(m, m + step)
        before = dot_nn(nrm[r, at, :], wf[0]) + b1
        out, grad = gelu_pair(before)
        hidden = out.astype(bf16)
        hid[0, 0, at, :] = hidden
        slope[0, 0, at, :] = grad.astype(bf16)
        logits = dot_nn(hidden, ws[0]) + shift
        e = jnp.exp(logits - jnp.max(logits, axis=-1, keepdims=True))
        p = (e * (1.0 / jnp.sum(e, axis=-1, keepdims=True))).astype(bf16)
        prob[0, 0, at, :] = p
        mix = dot_nn(p, val[r, :, tile])
        lane = lax.broadcasted_iota(jnp.int32, mix.shape, 1)
        old = join[r, at, tile].astype(f32)
        join[r, at, tile] = jnp.where((h == 1) & (lane < 64), old, mix).astype(bf16)

    for k in range(3):

        @at_step(2, k)
        def _():
            start(out_j(k))

    @at_step(2, 2)
    def _():
        wait(f3(1))
        start(f5(1))

    @at_step(2, 3)
    def _():
        start(mine_j())
        for k in range(2):
            wait(f4(k) + f5(k))
        for k in range(3):
            wait(out_j(k))
        wait(mine_j())


def attend_call(tokens, extra, w_first, w_second, w_out, w_up, w_down):
    _, slots, width = tokens.shape
    heads = w_first.shape[0] // GROUP
    by_row = lambda h, r: (jnp.where(h == 0, r, GROUP - 1), 0, 0)
    by_head = lambda h, r: (h, 0, 0)
    both = lambda h, r: (h, r, 0, 0)
    rows_f = 2 * w_down.shape[0] + 32
    return pl.pallas_call(
        attend_kernel,
        grid=(heads, GROUP),
        out_shape=(
            shape_of((heads, width, width), bf16),
            shape_of((heads, width, slots), bf16),
            shape_of((width, 256), bf16),
            shape_of((8, width), f32),
            shape_of((GROUP, slots, width), bf16),
            shape_of((GROUP, slots, 256), bf16),
            shape_of((heads, GROUP, slots, width), bf16),
            shape_of((heads, GROUP, slots, width), bf16),
            shape_of((heads, GROUP, slots, slots), bf16),
            shape_of((GROUP, slots, 256), bf16),
            shape_of((2, 2, 2, 4, rows_f, width), bf16),
        ),
        in_specs=[ANY] + [FULL] * 6,
        out_specs=(
            pl.BlockSpec((1, width, width), by_head),
            pl.BlockSpec((1, width, slots), by_head),
            pl.BlockSpec((width, 256), lambda h, r: (0, 0)),
            pl.BlockSpec((8, width), lambda h, r: (0, 0)),
            pl.BlockSpec((1, slots, width), by_row),
            pl.BlockSpec((1, slots, 256), by_row),
            pl.BlockSpec((1, 1, slots, width), both),
            pl.BlockSpec((1, 1, slots, width), both),
            pl.BlockSpec((1, 1, slots, slots), both),
            ANY,
            ANY,
        ),
        scratch_shapes=[
            pltpu.VMEM((GROUP, 384, 256), bf16),
            pltpu.VMEM((rows_f, width), bf16),
            pltpu.VMEM((2, 4, GROUP, 384, 256), bf16),
            pltpu.VMEM((GROUP, slots, width), bf16),
            pltpu.VMEM((GROUP, slots, width), bf16),
            pltpu.VMEM((GROUP, slots, 256), bf16),
            pltpu.VMEM((width, 128), f32),
            pltpu.VMEM((heads, 8, slots), f32),
            pltpu.VMEM((GROUP, 8, slots), f32),
            pltpu.VMEM((GROUP, slots, 256), bf16),
            DMA((heads + 3,)),
            DMA((heads, 3)),
            DMA((heads, 3)),
            DMA((heads, 4)),
            DMA((heads, 4)),
            DMA((heads,)),
            DMA((heads,)),
            DMA((3,)),
            DMA((3,)),
            DMA((2, 4)),
            DMA((2, 4)),
            DMA((2, 4)),
            DMA((2, 4)),
            DMA((3,)),
            DMA((3,)),
        ],
        compiler_params=pltpu.CompilerParams(collective_id=1, has_side_effects=True, vmem_limit_bytes=VMEM_LIMIT),
    )(tokens, extra, w_first, w_second, w_out, w_up, w_down)


def slab(t, c, z):
    y, x = t // 2, t % 2
    return (0, y, x, z) if c == 0 else (1, x, y, z)


CUTS = ((0, 128), (128, 224))


def cut(k):
    return slice(*CUTS[k])


def ffn_kernel(
    lf_far, joined, tokens, small, gout, result, gmid, gmix, half, gg2,
    lf, gf, gj, more, meet_b, acts, slopes, wu, wo, n2, gn2, gwu, loads, own, sg, rg, sx, rx, sb, rb,
):
    width = tokens.shape[-1]
    me, core, z_me = place()
    tps = group_peers()
    slow, fast, slow_dev, fast_dev = square()
    sibling = (me, 1 - core, z_me)
    parts = (slice(0, 48), slice(128, 224), slice(96, 128), slice(48, 96))
    wanted = (slice(0, 96), slice(128, 224), slice(96, 128))
    cross = lambda k: [
        remote(
            gf.at[1 - core, :, :, :, parts[k], :], more.at[:, :, :, parts[k], :], sx.at[k], rx.at[k], sibling
        )
    ]
    over = lambda: remote(gf.at[core, 1 - slow, :, :, cut(1), :], meet_b, sb, rb, slow_dev)
    out_g = lambda k: [remote(gj.at[tps[k]], gmix.at[k], sg.at[k], rg.at[k], (tps[k], core, z_me))]
    greet([(p, core, z_me) for p in tps] + [sibling])
    load = lambda k: local(lf_far.at[:, :, :, :, wanted[k], :], lf.at[:, :, :, :, wanted[k], :], loads.at[k])
    for k in (2, 0, 1):
        load(k).start()
    load(2).wait()
    wo[...] = jnp.zeros_like(wo)
    for t in range(GROUP):
        for c in range(2):
            for z in range(0, 4, 2):
                pair = [lf[slab(t, c, z + k) + (slice(96, 128),)].astype(f32)[0:24] for k in range(2)]
                wo[t, (c * 4 + z) * 24 : (c * 4 + z) * 24 + 48, :] = jnp.concatenate(pair, 0).astype(bf16)
    middle = tokens[...].astype(f32)
    for t in range(GROUP):
        middle = middle + dot_nn(joined[t], wo[t])
    result[...] = middle
    gmid[...] = middle
    g2 = small[4:5]
    unit, _ = centre_rows(middle)
    n2[...] = (unit * g2).astype(bf16)
    gn2[...] = jnp.zeros_like(gn2)
    load(0).wait()

    def fold(k):
        def one(i, carry):
            for j in range(2):
                for z in range(4):
                    spot = (i, j, z, parts[k])
                    gf[(core,) + spot] = (gf[(core,) + spot].astype(f32) + more[spot].astype(f32)).astype(bf16)
            return carry

        lax.fori_loop(0, 2, one, 0)

    def ahead(p, carry):
        rows = pl.ds(pl.multiple_of(p * 48, 16), 48)
        for t in range(GROUP):
            for c in range(2):
                for z in range(0, 4, 2):
                    ends = [lf[slab(t, c, z + k) + (rows,)].astype(f32) for k in range(2)]
                    at = (t * 8 + c * 4 + z) * 24
                    for k in range(2):
                        both = jnp.concatenate([e[24 * k : 24 * k + 24] for e in ends], 0)
                        wu[2 * p + k, at : at + 48, :] = both.astype(bf16)
        branch = gout[...].astype(bf16)
        for k in range(2):
            act, slope = gelu_pair(dot_nn(n2[...], wu[2 * p + k]))
            act = act.astype(bf16)
            acts[2 * p + k] = act
            slopes[2 * p + k] = slope.astype(bf16)
            gwd = dot_tn(act, branch).astype(bf16)
            gf[0, p, k, :, 128:224, :] = gwd[:384].reshape(4, 96, width)
            gf[1, k, p, :, 128:224, :] = gwd[384:].reshape(4, 96, width)
        return carry

    def down_block(p, k):
        return jnp.concatenate(
            [lf[0, p, k, :, 128:224, :].reshape(384, width), lf[1, k, p, :, 128:224, :].reshape(384, width)], 0
        )

    def behind(p, carry):
        @pl.when(p == 1)
        def _():
            wait(cross(1))
            fold(1)
            over().start()

        branch = gout[...].astype(bf16)
        for k in range(2):
            gup = (dot_nt(branch, down_block(p, k)) * slopes[2 * p + k].astype(f32)).astype(bf16)
            slopes[2 * p + k] = gup
            gn2[...] += dot_nt(gup, wu[2 * p + k])
        return carry

    def weights(p, carry):
        rows = pl.ds(pl.multiple_of(p * 48, 16), 48)
        for k in range(2):
            gwu[k] = dot_tn(n2[...], slopes[2 * p + k])
            result[...] += dot_nn(acts[2 * p + k], down_block(p, k))
        for t in range(GROUP):
            for c in range(2):
                for z in range(4):
                    at = (t * 8 + c * 4 + z) * 24
                    both = jnp.concatenate([gwu[0, at : at + 24, :], gwu[1, at : at + 24, :]], 0)
                    gf[slab(t, c, z) + (rows,)] = both.astype(bf16)
        for k, n in ((0, 0), (1, 3)):

            @pl.when(p == k)
            def _():
                start(cross(n))

        return carry

    lax.fori_loop(0, 2, ahead, 0)
    met(4)
    start(cross(1))
    load(1).wait()

    lax.fori_loop(0, 2, behind, 0)
    unit, scale = centre_rows(gmid[...])
    gn = gn2[...]
    gg2[...] = jnp.sum((gn * unit).reshape(-1, 8, width), axis=0)
    gu = gn * g2
    back = scale * (
        gu - jnp.mean(gu, axis=-1, keepdims=True) - unit * jnp.mean(gu * unit, axis=-1, keepdims=True)
    )
    gm = gout[...] + back
    gmid[...] = gm
    ga = gm.astype(bf16)
    for t in range(GROUP):
        gj[t] = dot_nt(ga, wo[t]).astype(bf16)
    for k in range(3):
        start(out_g(k))
    mine = local(gj.at[me], gmix.at[3], own.at[0])
    mine.start()
    for t in range(GROUP):
        gwo = dot_tn(joined[t], ga)
        for c in range(2):
            for z in range(4):
                at = (c * 4 + z) * 24
                padded = jnp.concatenate([gwo[at : at + 24, :], jnp.zeros((8, width), f32)], 0)
                gf[slab(t, c, z) + (slice(96, 128),)] = padded.astype(bf16)
    start(cross(2))
    lax.fori_loop(0, 2, weights, 0)
    over().wait()

    def arrived(j, carry):
        for z in range(4):
            spot = (core, slow, j, z, cut(1))
            gf[spot] = (gf[spot].astype(f32) + meet_b[j, z].astype(f32)).astype(bf16)
        return carry

    lax.fori_loop(0, 2, arrived, 0)
    leave = [local(gf.at[core, :, :, :, cut(k), :], half.at[:, :, :, cut(k), :], own.at[1 + k]) for k in range(2)]
    leave[1].start()
    for k in (2, 0, 3):
        wait(cross(k))
        fold(k)
    leave[0].start()
    for k in range(3):
        wait(out_g(k))
    mine.wait()
    wait(leave)


def ffn_call(lf, joined, tokens, small, gout):
    slots, width = tokens.shape
    return pl.pallas_call(
        ffn_kernel,
        out_shape=(
            shape_of((slots, width), f32),
            shape_of((slots, width), f32),
            shape_of(joined.shape, bf16),
            shape_of(lf.shape[1:], bf16),
            shape_of((8, width), f32),
        ),
        in_specs=[ANY] + [FULL] * 4,
        out_specs=(FULL, FULL, ANY, ANY, FULL),
        scratch_shapes=[
            pltpu.VMEM(lf.shape, bf16),
            pltpu.VMEM(lf.shape, bf16),
            pltpu.VMEM(joined.shape, bf16),
            pltpu.VMEM(lf.shape[1:], bf16),
            pltpu.VMEM((2, 4, 96, width), bf16),
            pltpu.VMEM((4, slots, width), bf16),
            pltpu.VMEM((4, slots, width), bf16),
            pltpu.VMEM((4, width, width), bf16),
            pltpu.VMEM((GROUP, 256, width), bf16),
            pltpu.VMEM((slots, width), bf16),
            pltpu.VMEM((slots, width), f32),
            pltpu.VMEM((2, width, width), f32),
            DMA((3,)),
            DMA((3,)),
            DMA((3,)),
            DMA((3,)),
            DMA((4,)),
            DMA((4,)),
            DMA,
            DMA,
        ],
        compiler_params=pltpu.CompilerParams(collective_id=2, has_side_effects=True, vmem_limit_bytes=VMEM_LIMIT),
    )(lf, joined, tokens, small, gout)


def back_kernel(
    wf, ws, wv, normed, values, hid, slope, prob, gmix, gg2, half, tokens, gmid, small, out_f, out_a, out_s, gtok,
    wcat, gb_all, awf, aws, ab1, ab2, gn, gv, awv, stash, ga, gs, nb, tok, fs, fb2, fb3, fb4, cb1, cb2, sb1, sb2,
    own, s1, r1, s2, r2, s3, r3, sn, rn, sf, rf, s4, r4, sv, rv,
):
    step, r = pl.program_id(0), pl.program_id(1)
    width = ws.shape[1]
    heads = ab1.shape[0]
    h = jnp.maximum(heads - 1 - step, 0)
    t, c, z = place()
    sibling = (t, 1 - c, z)
    tps, zs = group_peers(), line_peers()
    slow, fast, slow_dev, fast_dev = square()

    a1 = lambda i: [remote(ga.at[1 - c, :, :, part(i)], cb1.at[:, :, part(i)], s1.at[i], r1.at[i], sibling)]

    def add_heads(i):
        def add(o, slot):
            def one(j, carry):
                here = ga[c, o, j, part(i)].astype(f32) + cb2[slot, j, part(i)].astype(f32)
                ga[c, o, j, part(i)] = here.astype(bf16)
                return carry

            lax.fori_loop(0, GROUP, one, 0)

        return add

    def add_f(k):
        def add(o, slot):
            fs[fast, o, cut(k)] = (fs[fast, o, cut(k)].astype(f32) + fb4[slot, cut(k)].astype(f32)).astype(bf16)

        return add

    a2 = lambda i: Gather(
        lambda o: ga.at[c, o, :, part(i)], lambda k: cb2.at[k, :, part(i)], add_heads(i), s2.at[i], r2.at[i]
    )
    a3 = lambda i: [
        remote(ga.at[c, z, p, part(i)], out_a.at[t, part(i)], s3.at[i, k], r3.at[i, k], (p, c, z))
        for k, p in enumerate(tps)
    ]
    mine = lambda i: [local(ga.at[c, z, t, part(i)], out_a.at[t, part(i)], own.at[i])]
    mine_f = lambda: [local(half.at[slow], fs, own.at[heads])]
    mine_t = lambda: [local(tokens, tok, own.at[heads + 1]), local(gmid, gtok, own.at[heads + 2])]
    mine_w = lambda: [
        local(wf.at[i], wcat.at[:, i * width : (i + 1) * width], own.at[heads + 3 + i]) for i in range(heads)
    ]
    v1 = lambda: [remote(gs.at[1 - c], sb1, sv.at[0], rv.at[0], sibling)]
    v2 = lambda: [remote(gs.at[c, p], sb2.at[k], sv.at[1 + k], rv.at[1 + k], (t, c, p)) for k, p in enumerate(zs)]
    f2 = lambda: [remote(half.at[1 - slow, :, :, cut(0), :], fb2, sf.at[0], rf.at[0], slow_dev)]
    f3 = lambda k: [remote(fs.at[1 - fast, :, cut(k)], fb3.at[:, cut(k)], sf.at[1 + k], rf.at[1 + k], fast_dev)]
    f4 = lambda k: Gather(
        lambda o: fs.at[fast, o, cut(k)], lambda n: fb4.at[n, cut(k)], add_f(k), s4.at[k], r4.at[k]
    )
    line_n = lambda k: gb_all.at[k, :, 0:width]
    out_n = lambda k: remote(line_n(k), nb.at[k], sn.at[k], rn.at[k], (fast_dev, fast_dev, slow_dev)[k])

    def at_step(i, j):
        return pl.when((step == i) & (r == j))

    def meet(i):
        wait(a1(i))

        def line(k, carry):
            for j in range(GROUP):
                here = ga[c, k, j, part(i)].astype(f32) + cb1[k, j, part(i)].astype(f32)
                ga[c, k, j, part(i)] = here.astype(bf16)
            return carry

        lax.fori_loop(0, 4, line, 0)
        a2(i).begin()

    def deal(i):
        a2(i).finish()
        start(mine(i) + a3(i))

    def add_slabs(total, more, k):
        def one(i, carry):
            here = fs[total, i, cut(k)].astype(f32) + more(i).astype(f32)
            fs[total, i, cut(k)] = here.astype(bf16)
            return carry

        lax.fori_loop(0, 4, one, 0)

    @at_step(0, 0)
    def _():
        greet([(p, c, z) for p in tps] + [(t, c, p) for p in zs] + [sibling])
        start(mine_f() + mine_w() + mine_t())
        met(7)
        start(f2())
        wait(mine_f())
        start(f3(1))

    @at_step(0, 3)
    def _():
        wait(f3(1))
        add_slabs(fast, lambda i: fb3[i, cut(1)], 1)
        f4(1).begin()

    @at_step(1, 0)
    def _():
        meet(2)

    @at_step(1, 2)
    def _():
        f4(1).forward()

    @at_step(1, 3)
    def _():
        wait(f2())
        add_slabs(1 - fast, lambda i: fb2[1 - fast, i], 0)
        start(f3(0))
        add_slabs(fast, lambda i: fb2[fast, i], 0)

    @at_step(2, 0)
    def _():
        a2(2).forward()
        meet(1)

    @at_step(2, 2)
    def _():
        wait(f3(0))
        add_slabs(fast, lambda i: fb3[i, cut(0)], 0)
        f4(0).begin()

    @at_step(2, 3)
    def _():
        deal(2)

    @at_step(3, 0)
    def _():
        wait(mine_w())

    @pl.when((r == 0) & (step < heads))
    def _():
        awf[...] = jnp.zeros_like(awf)
        aws[...] = jnp.zeros_like(aws)
        ab1[h] = jnp.zeros(ab1.shape[1:], f32)
        ab2[h] = jnp.zeros(ab2.shape[1:], f32)

    @pl.when(step < heads)
    def _():
        tile = pl.ds(pl.multiple_of((h // 2) * 128, 128), 128)
        lane = lax.broadcasted_iota(jnp.int32, (512, 128), 1)
        gm = jnp.where(lane // 64 == h % 2, gmix[0, :, tile].astype(f32), 0.0).astype(bf16)
        gw = dot_nt(gm, values[0, :, tile])
        p = prob[0, 0]
        p32 = p.astype(f32)
        gl = (p32 * (gw - jnp.sum(p32 * gw, axis=-1, keepdims=True))).astype(bf16)
        ab2[h] += jnp.sum(gl.astype(f32).reshape(-1, 8, 512), axis=0)
        gvh = dot_tn(p, gm)

        @pl.when(h != 0)
        def _():
            gv[r, :, tile] = gvh.astype(bf16)

        @pl.when(h == 0)
        def _():
            gv[r, :, tile] = (gv[r, :, tile].astype(f32) + gvh).astype(bf16)

        aws[...] += dot_tn(hid[0, 0], gl)
        gb = (dot_nt(gl, ws[0]) * slope[0, 0].astype(f32)).astype(bf16)
        gb_all[r, :, pl.ds(pl.multiple_of(h * width, 128), width)] = gb
        ab1[h] += jnp.sum(gb.astype(f32).reshape(-1, 8, width), axis=0)
        awf[...] += dot_tn(normed[0], gb)

    @pl.when(step == heads - 1)
    def _():
        more = dot_tn(normed[0], gv[r])

        @pl.when(r == 0)
        def _():
            awv[...] = more

        @pl.when(r != 0)
        def _():
            awv[...] += more

    def pack(i):
        def one(tt, carry):
            for cc in range(2):
                for zz in range(4):
                    at = pl.ds(pl.multiple_of((tt * 8 + cc * 4 + zz) * 24, 8), 24)
                    stack = [awf[at, 256 * j : 256 * j + 256] for j in range(3)]
                    stack += [aws[at, 256 * j : 256 * j + 256] for j in range(2)]
                    if i == 0:
                        stack = [awv[at, :]] + stack
                    if i == 1:
                        stack = stack + [stash[cc, zz, tt]]
                    whole = jnp.concatenate(stack, 0)
                    if i == 2:
                        stash[cc, zz, tt] = whole[0:8]
                        whole = whole[8:]
                    ga[cc, zz, tt, part(i)] = whole.astype(bf16)
            return carry

        lax.fori_loop(0, GROUP, one, 0)
        start(a1(i))

    @at_step(0, 3)
    def _():
        pack(2)

    @at_step(1, 3)
    def _():
        pack(1)

    @at_step(2, 3)
    def _():
        row = lax.broadcasted_iota(jnp.int32, (128, width), 0)
        stack = jnp.zeros((128, width), f32)
        lines = [jnp.sum(ab1[i], axis=0, keepdims=True) for i in range(heads)]
        for k, line in enumerate(lines + [jnp.sum(gg2[...], axis=0, keepdims=True)]):
            stack = jnp.where(row == 64 + k, line, stack)
        lane = lax.broadcasted_iota(jnp.int32, (width, 128), 1)
        awv[:, 128:256] = jnp.where(lane < 64, awv[:, 128:256], stack.T)
        pack(0)

    @pl.when(step == heads)
    def _():
        total = dot_nt(gb_all[r], wcat[...]) + dot_nt(gv[r], wv[...])

        @pl.when(r < 3)
        def _():
            gb_all[r, :, 0:width] = total.astype(bf16)

        @pl.when(r == 3)
        def _():
            gn[...] = total

    @at_step(3, 0)
    def _():
        out_n(0).start()
        meet(0)
        a2(1).forward()

    @at_step(3, 1)
    def _():
        out_n(1).start()

    @at_step(2, 3)
    def _():
        flat = jnp.concatenate([jnp.sum(ab2[k], axis=0, keepdims=True) for k in range(3)], 1)
        flat = jnp.broadcast_to(flat, (8, 1536))
        for cc in range(2):
            for zz in range(4):
                s = (cc * 4 + zz) * 192
                gs[cc, zz] = (pltpu.roll(flat, 1536 - s, 1) if s else flat)[:, 0:256]
        start(v1())

    @at_step(3, 2)
    def _():
        f4(0).forward()
        wait(v1())
        gs[c] += sb1[...]
        start(v2())

    @at_step(3, 3)
    def _():
        out_n(0).wait()

        def join(i, carry):
            at = pl.ds(pl.multiple_of(i * 128, 128), 128)
            here = gb_all[2, at, 0:width].astype(f32) + nb[0, at, :].astype(f32)
            gb_all[2, at, 0:width] = here.astype(bf16)
            return carry

        lax.fori_loop(0, 4, join, 0)
        out_n(2).start()
        deal(1)
        a2(0).forward()
        f4(1).finish()
        f4(0).finish()
        out_f[...] = fs[fast, z].astype(f32)
        out_n(1).wait()
        out_n(2).wait()
        wait(mine_t())

        def ln_back(i, carry):
            at = pl.ds(pl.multiple_of(i * 128, 128), 128)
            g = gn[at, :] + nb[1, at, :].astype(f32) + nb[2, at, :].astype(f32)
            unit, scale = centre_rows(tok[at, :].astype(f32))
            gu = g * small[3:4]
            back = scale * (
                gu - jnp.mean(gu, axis=-1, keepdims=True) - unit * jnp.mean(gu * unit, axis=-1, keepdims=True)
            )
            gtok[at, :] += back
            return carry

        lax.fori_loop(0, 4, ln_back, 0)
        wait(v2())
        out_s[...] = gs[c, z] + sb2[0] + sb2[1] + sb2[2]
        deal(0)
        for i in range(heads):
            wait(mine(i) + a3(i))


def back_call(wf, ws, wv, normed, values, hid, slope, prob, gmix, gg2, half, tokens, gmid, small):
    heads, width, slots = ws.shape
    rows = half.shape[-2]
    head = lambda h: jnp.maximum(heads - 1 - h, 0)
    held = lambda h, r: jnp.where(h < heads, r, GROUP - 1)
    by_head = lambda h, r: (head(h), 0, 0)
    row = lambda h, r: (r, 0, 0)
    early = lambda h, r: (held(h, r), 0, 0)
    both = lambda h, r: (head(h), held(h, r), 0, 0)
    flat = lambda h, r: (0, 0)
    return pl.pallas_call(
        back_kernel,
        grid=(heads + 1, GROUP),
        out_shape=(
            shape_of((rows, width), f32),
            shape_of((GROUP, 384, 256), bf16),
            shape_of((8, 256), f32),
            shape_of(tokens.shape, f32),
        ),
        in_specs=[
            ANY,
            pl.BlockSpec((1, width, slots), by_head),
            pl.BlockSpec((width, 256), flat),
            pl.BlockSpec((1, slots, width), row),
            pl.BlockSpec((1, slots, 256), early),
            pl.BlockSpec((1, 1, slots, width), both),
            pl.BlockSpec((1, 1, slots, width), both),
            pl.BlockSpec((1, 1, slots, slots), both),
            pl.BlockSpec((1, slots, 256), early),
            pl.BlockSpec((8, width), flat),
            ANY,
            ANY,
            ANY,
            pl.BlockSpec((8, width), flat),
        ],
        out_specs=(FULL, ANY, FULL, FULL),
        scratch_shapes=[
            pltpu.VMEM((width, heads * width), bf16),
            pltpu.VMEM((GROUP, slots, heads * width), bf16),
            pltpu.VMEM((width, width), f32),
            pltpu.VMEM((width, slots), f32),
            pltpu.VMEM((heads, 8, width), f32),
            pltpu.VMEM((heads, 8, slots), f32),
            pltpu.VMEM((slots, width), f32),
            pltpu.VMEM((GROUP, slots, 256), bf16),
            pltpu.VMEM((width, 256), f32),
            pltpu.VMEM((2, 4, GROUP, 8, 256), f32),
            pltpu.VMEM((2, 4, GROUP, 384, 256), bf16),
            pltpu.VMEM((2, 4, 8, 256), f32),
            pltpu.VMEM((3, slots, width), bf16),
            pltpu.VMEM((slots, width), bf16),
            pltpu.VMEM((2, 4, rows, width), bf16),
            pltpu.VMEM((2, 4, 128, width), bf16),
            pltpu.VMEM((4, rows, width), bf16),
            pltpu.VMEM((4, rows, width), bf16),
            pltpu.VMEM((4, GROUP, 384, 256), bf16),
            pltpu.VMEM((4, GROUP, 384, 256), bf16),
            pltpu.VMEM((4, 8, 256), f32),
            pltpu.VMEM((3, 8, 256), f32),
            DMA((2 * heads + 3,)),
            DMA((heads,)),
            DMA((heads,)),
            DMA((heads, 3)),
            DMA((heads, 4)),
            DMA((heads, 3)),
            DMA((heads, 3)),
            DMA((3,)),
            DMA((3,)),
            DMA((3,)),
            DMA((3,)),
            DMA((2, 3)),
            DMA((2, 4)),
            DMA((4,)),
            DMA((4,)),
        ],
        compiler_params=pltpu.CompilerParams(collective_id=3, has_side_effects=True, vmem_limit_bytes=VMEM_LIMIT),
    )(wf, ws, wv, normed, values, hid, slope, prob, gmix, gg2, half, tokens, gmid, small)


def finish_kernel(
    sums_a, sums_f, sums_b, w_first, extra,
    out_one, out_value, out_first, out_b1, out_second, out_b2, out_out, out_two, out_up, out_down,
):
    heads_all, depth, width = w_first.shape
    heads = heads_all // GROUP
    total = jnp.zeros((depth, 256), f32)
    lane = lax.broadcasted_iota(jnp.int32, (depth, 256), 1)
    sides = []
    for t in range(GROUP):
        whole = sums_a[t].astype(f32)
        out_value[:, 192 * t : 192 * t + 192] = whole[0:depth, 0:192]
        sides.append(whole[0:depth, 128:256])
        total += jnp.where(lane < 192, whole[0:depth] * extra[t].astype(f32), 0.0)
        for i in range(heads):
            block = lambda j: whole[depth * (1 + 5 * i + j) : depth * (2 + 5 * i + j)]
            weight = w_first[heads * t + i].astype(f32)
            for j in range(3):
                at = slice(256 * j, 256 * j + 256)
                out_first[heads * t + i, :, at] = block(j)
                total += block(j) * weight[:, at]
            for j in range(2):
                out_second[heads * t + i, :, 256 * j : 256 * j + 256] = block(3 + j)
    gain = jnp.sum(jnp.where(lane == 195, extra[0].astype(f32), 0.0), axis=1, keepdims=True)
    gain_grad = jnp.sum(total, axis=1, keepdims=True) / gain
    low = lax.broadcasted_iota(jnp.int32, (depth, 128), 1)
    sides[0] = jnp.where(low == 68, gain_grad, sides[0])
    turned = jnp.concatenate(sides + [jnp.zeros((128 - GROUP * depth, 128), f32)], 0).T
    two = jnp.zeros((1, 128), f32)
    for t in range(GROUP):
        mine = pltpu.roll(turned, 128 - depth * t, 1) if t else turned
        out_b1[heads * t : heads * t + heads, :] = mine[64 : 64 + heads, 0:depth]
        two += mine[67:68]
    out_two[...] = two[:, 0:depth]
    out_one[...] = turned[68:69, 0:depth]
    out_b2[...] = sums_b[0:1, 0 : out_b2.shape[1]]
    for k in range(4):
        out_up[:, width * k : width * k + width] = sums_f[depth * k : depth * k + depth]
    out_out[...] = sums_f[4 * depth : 5 * depth]
    out_down[...] = sums_f[128:224]


def finish_call(sums_a, sums_f, sums_b, w_first, extra, slots, shard):
    heads_all, depth, width = w_first.shape
    return pl.pallas_call(
        finish_kernel,
        out_shape=(
            shape_of((1, depth), f32),
            shape_of((depth, width), f32),
            shape_of((heads_all, depth, width), f32),
            shape_of((heads_all, depth), f32),
            shape_of((heads_all, depth, slots), f32),
            shape_of((1, shard), f32),
            shape_of((depth, width), f32),
            shape_of((1, depth), f32),
            shape_of((depth, 4 * width), f32),
            shape_of((4 * depth, width), f32),
        ),
        in_specs=[FULL] * 5,
        out_specs=(FULL,) * 10,
        compiler_params=pltpu.CompilerParams(vmem_limit_bytes=VMEM_LIMIT),
    )(sums_a, sums_f, sums_b, w_first, extra)


def on_device_fast(tokens, lengths, gain_one, w_value, w_first, b_first, w_second, b_second, w_out, gain_two, w_up, w_down, grad_out):
    _, slots, width = tokens.shape
    heads_all, depth, _ = w_first.shape
    heads = heads_all // GROUP
    digits = jnp.stack([lengths[0] // 16, lengths[0] % 16]).astype(bf16)
    extra = jnp.concatenate(
        [
            w_value.reshape(depth, GROUP, -1).transpose(1, 0, 2),
            b_first.reshape(GROUP, heads, depth).transpose(0, 2, 1),
            jnp.broadcast_to(jnp.stack([gain_one, gain_two], 1), (GROUP, depth, 2)),
            jnp.broadcast_to(b_second.reshape(depth, 8), (GROUP, depth, 8)),
            jnp.broadcast_to(digits, (GROUP, depth, 2)),
            jnp.zeros((GROUP, depth, 49), bf16),
        ],
        2,
    )
    wf, ws, wv, small, normed, values, hid, slope, prob, joined, lf = attend_call(
        tokens, extra, w_first, w_second, w_out, w_up, w_down
    )
    result, gmid, gmix, half, gg2 = ffn_call(lf, joined, tokens[0], small, grad_out[0])
    out_f, out_a, out_s, gtok = back_call(
        wf, ws, wv, normed, values, hid, slope, prob, gmix, gg2, half, tokens[0], gmid, small
    )
    outs = finish_call(out_a, out_f, out_s, w_first, extra, slots, b_second.shape[0])
    return (result[None], gtok[None]) + tuple(v[0] if k in (0, 5, 7) else v for k, v in enumerate(outs))


def solution(mesh):
    wide, narrow = mesh.shape["wide"], mesh.shape["narrow"]
    grouped = Mesh(mesh.devices.reshape(GROUP, wide // GROUP, narrow), ALL)
    vec = P(ALL)
    flat = P(ALL, None)
    mid = P(None, ALL, None)
    row = P(ALL, None, None)
    body = on_device_fast if (wide, narrow) == (8, 4) else on_device
    return jax.shard_map(
        body,
        mesh=grouped,
        in_specs=(row, vec, vec, flat, mid, P(None, ALL), mid, vec, flat, vec, flat, flat, row),
        out_specs=(row, row, vec, flat, mid, P(None, ALL), mid, vec, flat, vec, flat, flat),
        check_vma=False,
    )
```
